32 devices in a mesh: seg: 4 (over y, x), seq: 8 (over z, core).
Axes of the slice: x: 2, y: 2, z: 4, core: 2. Of those that a mesh axis runs over, the one named last changes fastest.
Arguments:
- sublevel_arguments: bfloat16 [4, 1024, 2048], P('seg', 'seq'), may hold values from -6 to 6
- upstream_derivative: bfloat16 [4, 1024, 2048], P('seg', 'seq'), may hold values from -6 to 6
- piece_starting_memories: float32 [4, 32, 64, 64], P('seg'), may hold values from -6 to 6
- initial_standardize_scaling: bfloat16 [2048], P(('seg', 'seq')), may hold values from 0.099609375 to 1.8984375
- initial_standardize_offset: bfloat16 [2048], P(('seg', 'seq')), may hold values from -1.1953125 to 1.1953125
- acceptor_lerp_fraction: bfloat16 [2048], P(('seg', 'seq')), may hold values from 0 to 1
- lookup_lerp_fraction: bfloat16 [2048], P(('seg', 'seq')), may hold values from 0 to 1
- payload_lerp_fraction: bfloat16 [2048], P(('seg', 'seq')), may hold values from 0 to 1
- valve_lerp_fraction: bfloat16 [2048], P(('seg', 'seq')), may hold values from 0 to 1
- lane_fading_speed: bfloat16 [2048], P(('seg', 'seq')), may hold values from 9.727478e-05 to 0.024902344
- current_step_reward: bfloat16 [2048], P(('seg', 'seq')), may hold values from -2 to 2
- cluster_standardize_scaling: bfloat16 [2048], P(('seg', 'seq')), may hold values from 0.099609375 to 1.8984375
- cluster_standardize_offset: bfloat16 [2048], P(('seg', 'seq')), may hold values from -1.1953125 to 1.1953125
- acceptor_weights: bfloat16 [2048, 2048], P(('seg', 'seq')), may hold values from -0.125 to 0.125
- lookup_weights: bfloat16 [2048, 2048], P(('seg', 'seq')), may hold values from -0.125 to 0.125
- payload_weights: bfloat16 [2048, 2048], P(('seg', 'seq')), may hold values from -0.125 to 0.125
- valve_weights: bfloat16 [2048, 2048], P(('seg', 'seq')), may hold values from -0.125 to 0.125
- emission_weights: bfloat16 [2048, 2048], P(('seg', 'seq')), may hold values from -0.25 to 0.25
- latter_standardize_scaling: bfloat16 [2048], P(('seg', 'seq')), may hold values from 0.099609375 to 1.8984375
- latter_standardize_offset: bfloat16 [2048], P(('seg', 'seq')), may hold values from -1.1953125 to 1.1953125
- feedforward_lookup_lerp: bfloat16 [2048], P(('seg', 'seq')), may hold values from 0 to 1
- feedforward_acceptor_lerp: bfloat16 [2048], P(('seg', 'seq')), may hold values from 0 to 1
- feedforward_lookup_weights: bfloat16 [2048, 7168], P(('seg', 'seq')), may hold values from -0.125 to 0.125
- feedforward_payload_weights: bfloat16 [7168, 2048], P(('seg', 'seq')), may hold values from -0.125 to 0.125
- feedforward_acceptor_weights: bfloat16 [2048, 2048], P(('seg', 'seq')), may hold values from -0.125 to 0.125
Outputs:
- layer_output: bfloat16 [4, 1024, 2048], P('seg', 'seq')
- input_grad: float32 [4, 1024, 2048], P('seg', 'seq')
- final_states: float32 [4, 32, 64, 64], P('seg', 'seq')
- grad_first_gain: float32 [2048], P(('seg', 'seq'))
- grad_first_bias: float32 [2048], P(('seg', 'seq'))
- grad_mix_recept: float32 [2048], P(('seg', 'seq'))
- grad_mix_key: float32 [2048], P(('seg', 'seq'))
- grad_mix_value: float32 [2048], P(('seg', 'seq'))
- grad_mix_gate: float32 [2048], P(('seg', 'seq'))
- grad_decay_rate: float32 [2048], P(('seg', 'seq'))
- grad_current_bonus: float32 [2048], P(('seg', 'seq'))
- grad_group_gain: float32 [2048], P(('seg', 'seq'))
- grad_group_bias: float32 [2048], P(('seg', 'seq'))
- grad_recept_weight: float32 [2048, 2048], P(('seg', 'seq'))
- grad_key_weight: float32 [2048, 2048], P(('seg', 'seq'))
- grad_value_weight: float32 [2048, 2048], P(('seg', 'seq'))
- grad_gate_weight: float32 [2048, 2048], P(('seg', 'seq'))
- grad_output_weight: float32 [2048, 2048], P(('seg', 'seq'))
- grad_second_gain: float32 [2048], P(('seg', 'seq'))
- grad_second_bias: float32 [2048], P(('seg', 'seq'))
- grad_shift_key: float32 [2048], P(('seg', 'seq'))
- grad_shift_recept: float32 [2048], P(('seg', 'seq'))
- grad_channel_key: float32 [2048, 7168], P(('seg', 'seq'))
- grad_channel_value: float32 [7168, 2048], P(('seg', 'seq'))
- grad_channel_recept: float32 [2048, 2048], P(('seg', 'seq'))
The draws below stay inside these ranges and needn't reach their ends.
All inputs are finite; a program needn't handle non-finite values.
Results may differ from the reference program's by a relative error of at most 0.029.
Values may be sent and summed in bfloat16 or wider, within the bound.
A program may use at most 272 MiB of HBM per device.

```python
import math
import jax
import jax.numpy as jnp
from jax import lax

MIXING_LANES = 32
LANE_DIMENSION = 64
EMBEDDING_SIZE = 2048
FF = 7168
BLOCK_LEN = 64
SEGS = 4
LENGTH = 1024


def levels(key, dims, cuts, low, high):
    loudness, own = 1.0, jax.random.fold_in(key, 6)
    for dim, parts in cuts:
        heights = jnp.exp(jax.random.uniform(jax.random.fold_in(own, dim), (parts,), jnp.float32, low / len(cuts), high / len(cuts)))
        loudness = loudness * jnp.repeat(heights, dims[dim] // parts).reshape([-1 if axis == dim else 1 for axis in range(len(dims))])
    return loudness


def gaussian(own_key, shape, scale, limit, split=(), kind=jnp.bfloat16):
    array = scale * jax.random.normal(own_key, shape, jnp.float32)
    if split:
        array = array * levels(own_key, shape, split, -0.22, 0.18)
    return jnp.clip(array, -limit, limit).astype(kind)


def setup_inputs(seed: int = 0) -> dict:
    keys = jax.random.split(jax.random.key(seed), 26)
    return {
        "sublevel_arguments": gaussian(keys[0], (SEGS, LENGTH, EMBEDDING_SIZE), 1.0, 6.0, ((0, 4), (1, 8))),
        "upstream_derivative": gaussian(keys[1], (SEGS, LENGTH, EMBEDDING_SIZE), 1.0, 6.0, ((0, 4), (1, 8))),
        "piece_starting_memories": gaussian(keys[2], (SEGS, MIXING_LANES, LANE_DIMENSION, LANE_DIMENSION), 1.0, 6.0, ((0, 4),), jnp.float32),
        "initial_standardize_scaling": jnp.clip(1.0 + 0.18 * jax.random.normal(keys[3], (EMBEDDING_SIZE,), jnp.float32), 0.099609375, 1.8984375).astype(jnp.bfloat16),
        "initial_standardize_offset": gaussian(keys[4], (EMBEDDING_SIZE,), 0.3, 1.1953125, ((0, 32),)),
        "acceptor_lerp_fraction": jnp.clip(1.0 * jax.random.uniform(keys[5], (EMBEDDING_SIZE,), jnp.float32) ** levels(keys[5], (EMBEDDING_SIZE,), ((0, 32),), -0.2, 0.2), 0.0, 1.0).astype(jnp.bfloat16),
        "lookup_lerp_fraction": jnp.clip(1.0 * jax.random.uniform(keys[6], (EMBEDDING_SIZE,), jnp.float32) ** levels(keys[6], (EMBEDDING_SIZE,), ((0, 32),), -0.2, 0.2), 0.0, 1.0).astype(jnp.bfloat16),
        "payload_lerp_fraction": jnp.clip(1.0 * jax.random.uniform(keys[7], (EMBEDDING_SIZE,), jnp.float32) ** levels(keys[7], (EMBEDDING_SIZE,), ((0, 32),), -0.2, 0.2), 0.0, 1.0).astype(jnp.bfloat16),
        "valve_lerp_fraction": jnp.clip(1.0 * jax.random.uniform(keys[8], (EMBEDDING_SIZE,), jnp.float32) ** levels(keys[8], (EMBEDDING_SIZE,), ((0, 32),), -0.2, 0.2), 0.0, 1.0).astype(jnp.bfloat16),
        "lane_fading_speed": jnp.clip(jnp.exp(math.log(0.024902344) - 5.5451774 * jax.random.uniform(keys[9], (EMBEDDING_SIZE,), jnp.float32) ** levels(keys[9], (EMBEDDING_SIZE,), ((0, 32),), -0.2, 0.2)), 9.72747802734375e-05, 0.024902344).astype(jnp.bfloat16),
        "current_step_reward": gaussian(keys[10], (EMBEDDING_SIZE,), 0.5, 2.0, ((0, 32),)),
        "cluster_standardize_scaling": jnp.clip(1.0 + 0.18 * jax.random.normal(keys[11], (EMBEDDING_SIZE,), jnp.float32), 0.099609375, 1.8984375).astype(jnp.bfloat16),
        "cluster_standardize_offset": gaussian(keys[12], (EMBEDDING_SIZE,), 0.3, 1.1953125, ((0, 32),)),
        "acceptor_weights": gaussian(keys[13], (EMBEDDING_SIZE, EMBEDDING_SIZE), EMBEDDING_SIZE ** -0.5, 0.125, ((0, 32),)),
        "lookup_weights": gaussian(keys[14], (EMBEDDING_SIZE, EMBEDDING_SIZE), EMBEDDING_SIZE ** -0.5, 0.125, ((0, 32),)),
        "payload_weights": gaussian(keys[15], (EMBEDDING_SIZE, EMBEDDING_SIZE), EMBEDDING_SIZE ** -0.5, 0.125, ((0, 32),)),
        "valve_weights": gaussian(keys[16], (EMBEDDING_SIZE, EMBEDDING_SIZE), EMBEDDING_SIZE ** -0.5, 0.125, ((0, 32),)),
        "emission_weights": gaussian(keys[17], (EMBEDDING_SIZE, EMBEDDING_SIZE), (EMBEDDING_SIZE // 4) ** -0.5, 0.25, ((0, 32),)),
        "latter_standardize_scaling": jnp.clip(1.0 + 0.18 * jax.random.normal(keys[18], (EMBEDDING_SIZE,), jnp.float32), 0.099609375, 1.8984375).astype(jnp.bfloat16),
        "latter_standardize_offset": gaussian(keys[19], (EMBEDDING_SIZE,), 0.3, 1.1953125, ((0, 32),)),
        "feedforward_lookup_lerp": jnp.clip(1.0 * jax.random.uniform(keys[20], (EMBEDDING_SIZE,), jnp.float32) ** levels(keys[20], (EMBEDDING_SIZE,), ((0, 32),), -0.2, 0.2), 0.0, 1.0).astype(jnp.bfloat16),
        "feedforward_acceptor_lerp": jnp.clip(1.0 * jax.random.uniform(keys[21], (EMBEDDING_SIZE,), jnp.float32) ** levels(keys[21], (EMBEDDING_SIZE,), ((0, 32),), -0.2, 0.2), 0.0, 1.0).astype(jnp.bfloat16),
        "feedforward_lookup_weights": gaussian(keys[22], (EMBEDDING_SIZE, FF), EMBEDDING_SIZE ** -0.5, 0.125, ((0, 32),)),
        "feedforward_payload_weights": gaussian(keys[23], (FF, EMBEDDING_SIZE), (FF // 4) ** -0.5, 0.125, ((0, 32),)),
        "feedforward_acceptor_weights": gaussian(keys[24], (EMBEDDING_SIZE, EMBEDDING_SIZE), EMBEDDING_SIZE ** -0.5, 0.125, ((0, 32),)),
    }


@jax.custom_vjp
def low(v):
    return lax.optimization_barrier(v.astype(jnp.bfloat16)).astype(jnp.float32)

@jax.custom_vjp
def low_back(v):
    return v

def low_keep(v):
    return (low(v), None)

def low_pass(kept, grad):
    return (grad,)

def back_keep(v):
    return (v, None)

def back_low(kept, grad):
    return (low(grad),)
low.defvjp(low_keep, low_pass)
low_back.defvjp(back_keep, back_low)
EPS = 1e-05
GROUP_EPS = 0.00064
EXACT_ARITHMETIC = lax.Precision.HIGHEST

def layer_norm(values, gain_vec, bias_vec):
    average = lax.optimization_barrier(jnp.mean(values, axis=-1, keepdims=True))
    centred = values - average
    spread = lax.optimization_barrier(jnp.mean(centred * centred, axis=-1, keepdims=True))
    return centred * lax.rsqrt(spread + EPS) * gain_vec + bias_vec

def group_norm(values, gain_vec, bias_vec):
    row_total = values.shape[0]
    piece_partition = values.reshape(row_total, MIXING_LANES, LANE_DIMENSION)
    average = lax.optimization_barrier(jnp.mean(piece_partition, axis=-1, keepdims=True))
    centred = piece_partition - average
    spread = lax.optimization_barrier(jnp.mean(centred * centred, axis=-1, keepdims=True))
    return (centred * lax.rsqrt(spread + GROUP_EPS)).reshape(row_total, -1) * gain_vec + bias_vec

def product(left, right):
    return jnp.dot(left, right, precision=EXACT_ARITHMETIC, preferred_element_type=jnp.float32)

def shifted(values):
    return jnp.concatenate([jnp.zeros_like(values[:1]), values[:-1]], axis=0)

def tile_stepping(passed_memory, tile_elements, fading_speeds, reward_array):
    acceptor_tile, lookup_tile, payload_tile = tile_elements
    block_len = acceptor_tile.shape[0]
    offsets = jnp.arange(block_len, dtype=jnp.float32)[:, None, None]
    decayed_recept = acceptor_tile * jnp.exp(-fading_speeds[None] * offsets)
    grown_keys = lookup_tile * jnp.exp(fading_speeds[None] * (offsets + 1.0))
    affinity_table = jnp.einsum('thc,shc->hts', decayed_recept, grown_keys, precision=EXACT_ARITHMETIC)
    below_mask = jnp.arange(block_len)[:, None] > jnp.arange(block_len)[None, :]
    affinity_table = jnp.where(below_mask[None], affinity_table, 0.0)
    reward_addend = lax.optimization_barrier(jnp.sum(acceptor_tile * reward_array[None] * lookup_tile, axis=-1, keepdims=True))
    sublevel_answer = jnp.einsum('csk,kcd->scd', affinity_table, payload_tile, precision=EXACT_ARITHMETIC) + reward_addend * payload_tile
    sublevel_answer = sublevel_answer + jnp.einsum('thc,hcv->thv', decayed_recept, passed_memory, precision=EXACT_ARITHMETIC)
    tail_keys = lookup_tile * jnp.exp(-fading_speeds[None] * (block_len - 1.0 - offsets))
    new_state = jnp.exp(-fading_speeds * block_len)[:, :, None] * passed_memory
    new_state = new_state + jnp.einsum('shc,shv->hcv', tail_keys, payload_tile, precision=EXACT_ARITHMETIC)
    return (new_state, sublevel_answer)

def repeating_refresh(acceptor_numbers, arriving_lookups, arriving_payloads, fading_speeds, reward_array, starting_memory):
    length_all = acceptor_numbers.shape[0]
    blocks = length_all // BLOCK_LEN
    checked_answer = jax.checkpoint(tile_stepping)

    def stepper(passed_memory, tile_elements):
        return checked_answer(passed_memory, tile_elements, fading_speeds, reward_array)
    shape = (blocks, BLOCK_LEN, MIXING_LANES, LANE_DIMENSION)
    final_memory, outputs = lax.scan(stepper, starting_memory, (acceptor_numbers.reshape(shape), arriving_lookups.reshape(shape), arriving_payloads.reshape(shape)))
    return (outputs.reshape(length_all, MIXING_LANES * LANE_DIMENSION), final_memory)

def segment_forward(inputs, starting_memory, learnable_collection):
    initial_standardize_scaling, initial_standardize_offset, acceptor_lerp_fraction, lookup_lerp_fraction, payload_lerp_fraction, valve_lerp_fraction, lane_fading_speed, current_step_reward, cluster_standardize_scaling, cluster_standardize_offset, acceptor_weights, lookup_weights, payload_weights, valve_weights, emission_weights, latter_standardize_scaling, latter_standardize_offset, feedforward_lookup_lerp, feedforward_acceptor_lerp, feedforward_lookup_weights, feedforward_payload_weights, feedforward_acceptor_weights = learnable_collection
    normed_one = layer_norm(inputs, initial_standardize_scaling, initial_standardize_offset)
    before_one = shifted(normed_one)

    def mixed(share):
        return low(before_one + share * (normed_one - before_one))
    acceptor_numbers = low(low_back(product(mixed(acceptor_lerp_fraction), acceptor_weights)))
    lookup_arrays = low(low_back(product(mixed(lookup_lerp_fraction), lookup_weights)))
    payload_arrays = low(low_back(product(mixed(payload_lerp_fraction), payload_weights)))
    gate_pre = low_back(product(mixed(valve_lerp_fraction), valve_weights))
    piece_partition = (inputs.shape[0], MIXING_LANES, LANE_DIMENSION)
    blender_emission_linear, final_memory = repeating_refresh(acceptor_numbers.reshape(piece_partition), lookup_arrays.reshape(piece_partition), payload_arrays.reshape(piece_partition), lane_fading_speed.reshape(MIXING_LANES, LANE_DIMENSION), current_step_reward.reshape(MIXING_LANES, LANE_DIMENSION), starting_memory)
    gated = low(group_norm(blender_emission_linear, cluster_standardize_scaling, cluster_standardize_offset) * jax.nn.silu(gate_pre))
    middle = inputs + low_back(product(gated, emission_weights))
    normed_two = layer_norm(middle, latter_standardize_scaling, latter_standardize_offset)
    before_two = shifted(normed_two)
    pre_act = low_back(product(low(before_two + feedforward_lookup_lerp * (normed_two - before_two)), feedforward_lookup_weights))
    activation = low(jnp.square(jax.nn.relu(pre_act)))
    value_out = low_back(product(activation, feedforward_payload_weights))
    pre_gate = low_back(product(low(before_two + feedforward_acceptor_lerp * (normed_two - before_two)), feedforward_acceptor_weights))
    return (middle + jax.nn.sigmoid(pre_gate) * value_out, final_memory)

def reference(sublevel_arguments, upstream_derivative, piece_starting_memories, initial_standardize_scaling, initial_standardize_offset, acceptor_lerp_fraction, lookup_lerp_fraction, payload_lerp_fraction, valve_lerp_fraction, lane_fading_speed, current_step_reward, cluster_standardize_scaling, cluster_standardize_offset, acceptor_weights, lookup_weights, payload_weights, valve_weights, emission_weights, latter_standardize_scaling, latter_standardize_offset, feedforward_lookup_lerp, feedforward_acceptor_lerp, feedforward_lookup_weights, feedforward_payload_weights, feedforward_acceptor_weights):
    learnable_collection = (initial_standardize_scaling, initial_standardize_offset, acceptor_lerp_fraction, lookup_lerp_fraction, payload_lerp_fraction, valve_lerp_fraction, lane_fading_speed, current_step_reward, cluster_standardize_scaling, cluster_standardize_offset, acceptor_weights, lookup_weights, payload_weights, valve_weights, emission_weights, latter_standardize_scaling, latter_standardize_offset, feedforward_lookup_lerp, feedforward_acceptor_lerp, feedforward_lookup_weights, feedforward_payload_weights, feedforward_acceptor_weights)
    learnable_collection = tuple((item.astype(jnp.float32) for item in learnable_collection))

    def one_segment(totals, items):
        inputs, upstream, starting_memory = items

        def forward(values, weights):
            return segment_forward(values, starting_memory, weights)
        (sublevel_answer, final_memory), pull = jax.vjp(forward, inputs.astype(jnp.float32), learnable_collection)
        input_grad, weight_grads = pull((upstream.astype(jnp.float32), jnp.zeros_like(final_memory)))
        totals = jax.tree.map(jnp.add, totals, weight_grads)
        return (totals, (sublevel_answer.astype(jnp.bfloat16), input_grad, final_memory))
    zeros = tuple((jnp.zeros_like(item) for item in learnable_collection))
    grads, (outputs, input_grads, finals) = lax.scan(one_segment, zeros, (sublevel_arguments, upstream_derivative, piece_starting_memories))
    return (outputs, input_grads, finals, grads[0], grads[1], grads[2], grads[3], grads[4], grads[5], grads[6], grads[7], grads[8], grads[9], grads[10], grads[11], grads[12], grads[13], grads[14], grads[15], grads[16], grads[17], grads[18], grads[19], grads[20], grads[21])
```

```python
import jax
import jax.numpy as jnp
from jax import lax
from jax.sharding import Mesh, PartitionSpec as P

TEAM = ("b", "l", "c")
TEAMS = ("a", "h")
SEQ = ("h", "l", "c")
ALL = ("a", "b", "h", "l", "c")
HEAD = 64
CHUNK = 128
EPS = 1e-05
GROUP_EPS = 0.00064
BF = jnp.bfloat16
F32 = jnp.float32


def dot(a, b, dims):
    return lax.dot_general(a, b, (dims, ((), ())), preferred_element_type=F32)


def mm(a, b):
    return dot(a, b, ((1,), (0,)))


def mm_nt(a, b):
    return dot(a, b, ((1,), (1,)))


def mm_tn(a, b):
    return dot(a, b, ((0,), (0,)))


class Layout:
    def __init__(self, mesh_shape):
        self.A, self.B, self.H, self.L, self.C = mesh_shape
        self.team = self.B * self.L * self.C
        self.n = self.team * self.A * self.H

    def spread(self, v, whole):
        w = v.shape[-1] // self.n
        lead = v.shape[:-1]
        if w % whole:
            return v.reshape(*lead, self.team, -1)
        k = len(lead)
        v = v.reshape(*lead, self.A, self.B, self.H, self.L, self.C, w)
        v = v.transpose(*range(k), k + 1, k + 3, k + 4, k, k + 2, k + 5)
        return v.reshape(*lead, self.team, -1)

    def unspread(self, v, whole):
        lead = v.shape[:-2]
        w = v.shape[-1] * self.team // self.n
        if w % whole:
            return v.reshape(*lead, -1)
        k = len(lead)
        v = v.reshape(*lead, self.B, self.L, self.C, self.A, self.H, w)
        v = v.transpose(*range(k), k + 3, k, k + 4, k + 1, k + 2, k + 5)
        return v.reshape(*lead, -1)

    def rows_in(self, g):
        m = g.shape[-1]
        g = g.reshape(self.A, self.H, self.B, self.L, self.C, -1, m)
        return g.transpose(0, 2, 1, 3, 4, 5, 6).reshape(-1, m)

    def rows_out(self, g):
        m = g.shape[-1]
        g = g.reshape(self.A, self.B, self.H, self.L, self.C, -1, m)
        return g.transpose(0, 2, 1, 3, 4, 5, 6).reshape(self.A * self.H, self.team, -1, m)


def column_weights(lay, pieces):
    parts = [lay.spread(w, unit) for w, unit in pieces]
    widths = [p.shape[-1] for p in parts]
    sent = jnp.concatenate(parts, axis=-1)
    got = lax.all_to_all(sent, TEAM, split_axis=1, concat_axis=0, tiled=False)
    full = lay.rows_in(lax.all_gather(got, TEAMS, axis=0))
    out, at = [], 0
    for w in widths:
        out.append(full[:, at : at + w])
        at += w
    return out


def column_grads(lay, pieces):
    sent = jnp.concatenate([g.astype(BF) for g, _ in pieces], axis=1)
    part = lax.psum_scatter(lay.rows_out(sent), TEAMS, scatter_dimension=0, tiled=False)
    got = lax.all_to_all(part, TEAM, split_axis=0, concat_axis=1, tiled=False)
    out, at = [], 0
    for g, unit in pieces:
        w = g.shape[1]
        out.append(lay.unspread(got[:, :, at : at + w], unit).astype(F32))
        at += w
    return out


def from_left(row, n):
    return lax.ppermute(row, SEQ, [(i, i + 1) for i in range(n - 1)])


def from_right(row, n):
    return lax.ppermute(row, SEQ, [(i + 1, i) for i in range(n - 1)])


def normed(v):
    mean = jnp.mean(v, axis=-1, keepdims=True)
    cent = v - mean
    rstd = lax.rsqrt(jnp.mean(cent * cent, axis=-1, keepdims=True) + EPS)
    return cent * rstd, rstd


def norm_back(e, xhat, rstd):
    m1 = jnp.mean(e, axis=-1, keepdims=True)
    m2 = jnp.mean(e * xhat, axis=-1, keepdims=True)
    return (e - m1 - xhat * m2) * rstd


def with_before(rows, halo, segs):
    v = rows.reshape(segs, -1, rows.shape[-1])
    return jnp.concatenate([halo, v[:, :-1]], axis=1).reshape(rows.shape)


def with_after(rows, segs):
    v = rows.reshape(segs, -1, rows.shape[-1])
    return (
        jnp.concatenate([v[:, 1:], jnp.zeros_like(v[:, :1])], axis=1).reshape(rows.shape),
        v[:, :1],
    )


EX = lax.Precision.HIGHEST


def ein(spec, a, b):
    return jnp.einsum(spec, a, b, precision=EX, preferred_element_type=F32)


class Wkv:
    def __init__(self, r, k, v, lam, u):
        c = r.shape[2]
        self.c = c
        i = jnp.arange(c, dtype=F32)[:, None, None]
        self.i = i
        self.down = jnp.exp(-lam[None] * i)
        self.up = jnp.exp(lam[None] * (i + 1.0))
        self.tail = jnp.exp(-lam[None] * (c - 1.0 - i))
        self.span = jnp.exp(-lam * c)
        self.r, self.k, self.v, self.u = r, k, v, u
        self.rd, self.kg, self.kt = r * self.down, k * self.up, k * self.tail
        self.low = jnp.arange(c)[:, None] > jnp.arange(c)[None, :]
        self.add = ein("znsgc,znsgv->zngcv", self.kt, v)

    def closing(self):
        s = 0.0
        for n in range(self.r.shape[1]):
            s = self.span[..., None] * s + self.add[:, n]
        return s

    def forward(self, s):
        states = []
        for n in range(self.r.shape[1]):
            states.append(s)
            s = self.span[..., None] * s + self.add[:, n]
        self.states = jnp.stack(states, 1)
        att = jnp.where(self.low, ein("zntgc,znsgc->zngts", self.rd, self.kg), 0.0)
        self.att = att
        self.diag = jnp.sum(self.r * self.u * self.k, axis=-1, keepdims=True)
        y = ein("zngts,znsgv->zntgv", att, self.v) + self.diag * self.v
        y = y + ein("zntgc,zngcv->zntgv", self.rd, self.states)
        return y, s

    def back_add(self, dy):
        return ein("zntgc,zntgv->zngcv", self.rd, dy)

    def back_closing(self, adds):
        g = 0.0
        for n in reversed(range(self.r.shape[1])):
            g = self.span[..., None] * g + adds[:, n]
        return g

    def backward(self, dy, adds, g):
        ends = []
        for n in reversed(range(self.r.shape[1])):
            ends.append(g)
            g = self.span[..., None] * g + adds[:, n]
        ends = jnp.stack(ends[::-1], 1)
        datt = jnp.where(self.low, ein("zntgv,znsgv->zngts", dy, self.v), 0.0)
        ddiag = jnp.sum(dy * self.v, axis=-1, keepdims=True)
        d_rd = ein("zngts,znsgc->zntgc", datt, self.kg) + ein("zntgv,zngcv->zntgc", dy, self.states)
        d_kg = ein("zngts,zntgc->znsgc", datt, self.rd)
        d_kt = ein("znsgv,zngcv->znsgc", self.v, ends)
        d_v = ein("zngts,zntgv->znsgv", self.att, dy) + self.diag * dy
        d_v = d_v + ein("znsgc,zngcv->znsgv", self.kt, ends)
        d_r = d_rd * self.down + ddiag * self.u * self.k
        d_k = d_kg * self.up + d_kt * self.tail + ddiag * self.u * self.r
        d_u = jnp.sum(ddiag * self.r * self.k, axis=(0, 1, 2))
        i = self.i
        d_l = jnp.sum(
            (i + 1.0) * self.kg * d_kg
            - i * self.rd * d_rd
            - (self.c - 1.0 - i) * self.kt * d_kt,
            axis=(0, 1, 2),
        )
        d_l = d_l - self.c * self.span * jnp.sum(self.states * ends, axis=(0, 1, 4))
        return d_r, d_k, d_v, d_u, d_l


def chain(first, add, span, n, ahead):
    place = lax.axis_index("h")
    state = jnp.where(place == (0 if ahead else n - 1), first, 0.0)
    for i in range(n - 1):
        pairs = [(j, j + 1) for j in range(n - 1)] if ahead else [(j + 1, j) for j in range(n - 1)]
        arrived = lax.ppermute(span * state + add, "h", pairs)
        state = jnp.where(place == (i + 1 if ahead else n - 2 - i), arrived, state)
    return state


def per_device(lay, *args):
    (x_in, up_in, start_in) = args[:3]
    vec = args[3:13]
    w_r, w_k, w_v, w_g, w_o = args[13:18]
    vec2 = args[18:22]
    w_ck, w_cv, w_cr = args[22:]
    rank = (lax.axis_index("b") * lay.L + lax.axis_index("l")) * lay.C + lax.axis_index("c")
    h_at = lax.axis_index("h")
    nseq = lay.H * lay.L * lay.C
    segs = lay.B
    D = x_in.shape[-1]
    x_own = x_in[0]
    rows = x_own.shape[0]
    T = rows * lay.team
    dcol = D // lay.team
    heads = dcol // HEAD
    half = lay.L * lay.C

    stacked = jnp.stack([*vec, *vec2])
    every = lax.all_gather(stacked, ALL, axis=0)
    every = every.transpose(1, 0, 2).reshape(stacked.shape[0], D).astype(F32)
    g1, b1, s_r, s_k, s_v, s_g, lam, bonus, gn_g, gn_b, g2, b2, s_ck, s_cr = every

    def mine(v):
        return lax.dynamic_index_in_dim(lay.spread(v, HEAD), rank, 0, False)

    lam_m, u_m, gs_m, gb_m = (mine(v) for v in (lam, bonus, gn_g, gn_b))

    W_r, W_k, W_v, W_g = column_weights(lay, [(w, HEAD) for w in (w_r, w_k, w_v, w_g)])
    if (D // lay.n) % HEAD:
        W_o = lax.all_gather(w_o, ALL, axis=0, tiled=True)
        W_o = lax.dynamic_slice_in_dim(W_o, rank * dcol, dcol, 0)
    else:
        W_o = lax.all_gather(w_o, TEAMS, axis=0, tiled=True)

    halo_x = from_left(x_own[-1:], nseq)
    xg = lax.all_gather(x_own, TEAM, axis=0, tiled=True).astype(F32)
    halo_all = lax.all_gather(halo_x, TEAM, axis=0)[::half].astype(F32)
    n1 = normed(xg)[0] * g1 + b1
    halo_1 = (normed(halo_all)[0] * g1 + b1) * jnp.where(h_at > 0, 1.0, 0.0)
    before = with_before(n1, halo_1, segs)
    diff1 = n1 - before
    m_r, m_k, m_v, m_g = ((before + s * diff1).astype(BF) for s in (s_r, s_k, s_v, s_g))
    r = mm(m_r, W_r).astype(BF)
    k = mm(m_k, W_k).astype(BF)
    v = mm(m_v, W_v).astype(BF)
    gate = mm(m_g, W_g)
    shape = (segs, T // segs // CHUNK, CHUNK, heads, HEAD)
    lam_h, u_h = lam_m.reshape(heads, HEAD), u_m.reshape(heads, HEAD)
    wkv = Wkv(*(t.astype(F32).reshape(shape) for t in (r, k, v)), lam_h, u_h)
    span_all = jnp.exp(-lam_h * (T // segs))[..., None]
    nh = start_in.shape[1]
    head_ids = jnp.arange(nh * HEAD, dtype=jnp.int32)
    my_heads = lax.dynamic_index_in_dim(lay.spread(head_ids, HEAD), rank, 0, False)[::HEAD] // HEAD
    b_at = lax.axis_index("b")
    other_rank = rank + jnp.where(b_at == 0, 1, -1) * (lay.L * lay.C)
    other_heads = (
        lax.dynamic_index_in_dim(lay.spread(head_ids, HEAD), other_rank, 0, False)[::HEAD] // HEAD
    )
    own_start = jnp.take(start_in[0], my_heads, axis=0)
    got_start = lax.ppermute(jnp.take(start_in[0], other_heads, axis=0), "b", [(0, 1), (1, 0)])
    start = jnp.where(b_at == 0, jnp.stack([own_start, got_start]), jnp.stack([got_start, own_start]))
    s_in = chain(start, wkv.closing(), span_all, lay.H, True)
    mixer, s_out = wkv.forward(s_in)
    mix = mixer.reshape(T, heads, HEAD)
    cent = mix - jnp.mean(mix, axis=-1, keepdims=True)
    g_rstd = lax.rsqrt(jnp.mean(cent * cent, axis=-1, keepdims=True) + GROUP_EPS)
    g_hat = (cent * g_rstd).reshape(T, dcol)
    n_mix = g_hat * gs_m + gb_m
    sig = jax.nn.sigmoid(gate)
    silu = gate * sig
    gated = (n_mix * silu).astype(BF)
    part = mm(gated, W_o).astype(BF)
    out = lax.psum_scatter(part, TEAM, scatter_dimension=0, tiled=True)
    middle = x_own.astype(F32) + out.astype(F32)

    placed = jnp.zeros((segs, nh, HEAD, HEAD), BF)
    s_fin = jnp.where(h_at == lay.H - 1, s_out, 0.0).astype(BF)
    placed = placed.at[:, my_heads].set(s_fin)
    final = lax.psum_scatter(placed, "b", scatter_dimension=0, tiled=True)
    final = lax.psum_scatter(final, SEQ, scatter_dimension=1, tiled=True).astype(F32)

    W_ck, W_cr = column_weights(lay, [(w_ck, 1), (w_cr, D)])
    W_cv = lax.all_gather(w_cv, TEAMS, axis=0, tiled=True)
    hat2, rstd2 = normed(middle)
    n2_own = (hat2 * g2 + b2).astype(BF)
    halo_2 = from_left(n2_own[-1:], nseq)
    n2 = lax.all_gather(n2_own, TEAM, axis=0, tiled=True).astype(F32)
    halo_2 = lax.all_gather(halo_2, TEAM, axis=0)[::half].astype(F32)
    before2 = with_before(n2, halo_2, segs)
    diff2 = n2 - before2
    m_ck, m_cr = ((before2 + s * diff2).astype(BF) for s in (s_ck, s_cr))
    relu = jax.nn.relu(mm(m_ck, W_ck))
    act = (relu * relu).astype(BF)
    vpart = mm(act, W_cv).astype(BF)
    val = lax.psum_scatter(vpart, TEAM, scatter_dimension=1, tiled=True).astype(F32)
    sigma = jax.nn.sigmoid(mm(m_cr, W_cr))
    upc = lax.all_to_all(up_in[0].reshape(rows, lay.team, dcol), TEAM, 1, 0).reshape(T, dcol)
    upc = upc.astype(F32)
    add = (sigma * val).astype(BF).reshape(lay.team, rows, dcol)
    add = lax.all_to_all(add, TEAM, 0, 1).reshape(rows, D)
    layer_output = (middle + add.astype(F32)).astype(BF)

    d_value = (sigma * upc).astype(BF)
    d_pregate = (upc * val * sigma * (1.0 - sigma)).astype(BF)
    d_val = lax.all_gather(d_value, TEAM, axis=1, tiled=True)
    g_cv = mm_tn(act, d_val)
    d_pre = (mm_nt(d_val, W_cv) * 2.0 * relu).astype(BF)
    g_ck = mm_tn(m_ck, d_pre)
    g_cr = mm_tn(m_cr, d_pregate)
    d_mck = mm_nt(d_pre, W_ck)
    d_mcr = mm_nt(d_pregate, W_cr)
    g_s_ck = jnp.sum(d_mck * diff2, axis=0)
    g_s_cr = jnp.sum(d_mcr * diff2, axis=0)
    nxt, first = with_after((1.0 - s_ck) * d_mck + (1.0 - s_cr) * d_mcr, segs)
    dn2_part = (s_ck * d_mck + s_cr * d_mcr + nxt).astype(BF)

    def to_rows(part, first):
        mine = lax.psum_scatter(part, TEAM, scatter_dimension=0, tiled=True).astype(F32)
        spread = jnp.zeros((segs, half, D), BF).at[:, :1].set(first.astype(BF))
        edge = lax.psum_scatter(spread.reshape(-1, D), TEAM, scatter_dimension=0, tiled=True)
        return mine.at[-1:].add(from_right(edge, nseq).astype(F32))

    dn2 = to_rows(dn2_part, first)
    g_g2 = jnp.sum(dn2 * hat2, axis=0)
    g_b2 = jnp.sum(dn2, axis=0)
    d_mid = up_in[0].astype(F32) + norm_back(dn2 * g2, hat2, rstd2)

    d_br = lax.all_gather(d_mid.astype(BF), TEAM, axis=0, tiled=True)
    g_o = mm_tn(gated, d_br)
    d_gated = mm_nt(d_br, W_o)
    dn = d_gated * silu
    g_gs = jnp.sum(dn * g_hat, axis=0)
    g_gb = jnp.sum(dn, axis=0)
    d_gate = (d_gated * n_mix * sig * (1.0 + gate * (1.0 - sig))).astype(BF)
    d_mix = norm_back(
        (dn * gs_m).reshape(T, heads, HEAD), g_hat.reshape(T, heads, HEAD), g_rstd
    ).reshape(shape)
    adds = wkv.back_add(d_mix)
    g_in = chain(0.0, wkv.back_closing(adds), span_all, lay.H, False)
    d_r, d_k, d_v, d_u, d_l = wkv.backward(d_mix, adds, g_in)
    d_r, d_k, d_v = (t.reshape(T, dcol).astype(BF) for t in (d_r, d_k, d_v))
    g_r, g_k, g_v, g_w = (
        mm_tn(m, d) for m, d in ((m_r, d_r), (m_k, d_k), (m_v, d_v), (m_g, d_gate))
    )
    d_m = [mm_nt(d, w) for d, w in ((d_r, W_r), (d_k, W_k), (d_v, W_v), (d_gate, W_g))]
    shares = (s_r, s_k, s_v, s_g)
    g_shares = [jnp.sum(d * diff1, axis=0) for d in d_m]
    nxt, first = with_after(sum((1.0 - s) * d for s, d in zip(shares, d_m)), segs)
    dn1_part = (sum(s * d for s, d in zip(shares, d_m)) + nxt).astype(BF)
    dn1 = to_rows(dn1_part, first)
    hat1, rstd1 = normed(x_own.astype(F32))
    g_g1 = jnp.sum(dn1 * hat1, axis=0)
    g_b1 = jnp.sum(dn1, axis=0)
    input_grad = d_mid + norm_back(dn1 * g1, hat1, rstd1)

    g_r, g_k, g_v, g_w, g_ck, g_cr = column_grads(
        lay, [(g_r, HEAD), (g_k, HEAD), (g_v, HEAD), (g_w, HEAD), (g_ck, 1), (g_cr, D)]
    )
    g_cv = lax.psum_scatter(g_cv.astype(BF), TEAMS, scatter_dimension=0, tiled=True).astype(F32)
    if (D // lay.n) % HEAD:
        g_o = jnp.zeros((D, D), BF).at[rank * dcol + jnp.arange(dcol)].set(g_o.astype(BF))
        g_o = lax.psum_scatter(g_o, ALL, scatter_dimension=0, tiled=True).astype(F32)
    else:
        g_o = lax.psum_scatter(g_o.astype(BF), TEAMS, scatter_dimension=0, tiled=True).astype(F32)

    def in_place(v):
        spread = jnp.where(jnp.arange(lay.team)[:, None] == rank, v.reshape(1, -1), 0.0)
        return lay.unspread(spread, HEAD)

    small = jnp.stack(
        [g_g1, g_b1, *g_shares, in_place(d_l), in_place(d_u), in_place(g_gs), in_place(g_gb)]
        + [g_g2, g_b2, g_s_ck, g_s_cr]
    )
    ns = small.shape[0]
    small = small.reshape(ns, lay.n, D // lay.n).transpose(1, 0, 2).reshape(-1)
    small = lax.psum_scatter(small, ALL, scatter_dimension=0, tiled=True).reshape(ns, -1)
    return (
        layer_output[None],
        input_grad[None],
        final,
        *(small[i] for i in range(10)),
        g_r,
        g_k,
        g_v,
        g_w,
        g_o,
        *(small[i] for i in range(10, 14)),
        g_ck,
        g_cv,
        g_cr,
    )


def solution(mesh):
    n_seg, n_seq = mesh.devices.shape
    shape = (n_seg // 2, 2, n_seq // 4, 2, 2)
    view = Mesh(mesh.devices.reshape(shape), ALL)
    lay = Layout(shape)
    seg = ("a", "b")
    vec, mat = P(ALL), P(ALL, None)
    tok = P(seg, SEQ, None)

    def step(*args):
        return per_device(lay, *args)

    return jax.shard_map(
        step,
        mesh=view,
        in_specs=(tok, tok, P(seg, None, None, None), *[vec] * 10, *[mat] * 5, *[vec] * 4, *[mat] * 3),
        out_specs=(tok, tok, P(seg, SEQ, None, None), *[vec] * 10, *[mat] * 5, *[vec] * 4, *[mat] * 3),
        check_vma=False,
    )
```

```python
import jax
import jax.numpy as jnp
from jax import lax
from jax.experimental import pallas as pl
from jax.experimental.pallas import tpu as pltpu
from jax.sharding import Mesh, PartitionSpec as P

TEAM = ("b", "l", "c")
TEAMS = ("a", "h")
SEQ = ("h", "l", "c")
ALL = ("a", "b", "h", "l", "c")
HEAD = 64
CHUNK = 128
EPS = 1e-05
GROUP_EPS = 0.00064
BF = jnp.bfloat16
F32 = jnp.float32


MESH = pl.DeviceIdType.MESH
DMA = pltpu.SemaphoreType.DMA
VMEM_BYTES = 56 << 20


def coords():
    return {name: lax.axis_index(name) for name in ALL}


def rank_of(b, l, c):
    return (b * 2 + l) * 2 + c


def remote(src, dst, sent, landed, to):
    return pltpu.make_async_remote_copy(
        src_ref=src,
        dst_ref=dst,
        send_sem=sent,
        recv_sem=landed,
        device_id=to,
        device_id_type=MESH,
    )


def mates(me):
    for m in range(1, 8):
        yield m, {"b": me["b"] ^ (m >> 2), "l": me["l"] ^ ((m >> 1) & 1), "c": me["c"] ^ (m & 1)}


def greet(me, H, column, across):
    sem = pltpu.get_barrier_semaphore()
    count = 0
    for dh in range(H if column else 1):
        h = lax.rem(me["h"] + dh, H)
        for m in range(8):
            if dh == 0 and m == 0:
                continue
            to = {
                "b": me["b"] ^ (m >> 2),
                "h": h if column else me["h"],
                "l": me["l"] ^ ((m >> 1) & 1),
                "c": me["c"] ^ (m & 1),
            }
            pl.semaphore_signal(sem, inc=1, device_id=to, device_id_type=MESH)
            count += 1
    if across:
        pl.semaphore_signal(sem, inc=1, device_id={"a": 1 - me["a"]}, device_id_type=MESH)
        count += 1
    pl.semaphore_wait(sem, count)


class Copies:
    def __init__(self, sems):
        self.sems, self.k, self.open = sems, 0, []

    def go(self, src, dst, landed, to):
        copy = remote(src, dst, self.sems.at[self.k], landed, to)
        self.k += 1
        copy.start()
        self.open.append(copy)

    def drain(self):
        for copy in self.open:
            copy.wait_send()


def landed(ref, sem):
    remote(ref, ref, sem, sem, {"c": 1 - lax.axis_index("c")}).wait_recv()


def upper(ref, half):
    n = ref.shape[0] // 2
    return ref.at[pl.ds(half * n, n)]


class TeamGather:
    SENDS = 14

    def __init__(self, me, own, view, send, recv):
        self.me, self.own, self.view, self.recv = me, own, view, recv
        self.copies = Copies(send)
        self.tx, self.tz, self.ts = {"b": 1 - me["b"]}, {"l": 1 - me["l"]}, {"c": 1 - me["c"]}

    def put(self, src, p, half, to):
        self.copies.go(src, upper(self.view(p), half), self.recv.at[p, half], to)

    def start(self):
        mine = rank_of(self.me["b"], self.me["l"], self.me["c"])
        for half, to in ((0, self.tx), (1, self.tz), (1, self.tx), (0, self.tz), (0, self.ts), (1, self.ts)):
            self.put(upper(self.own, half), mine, half, to)

    def finish(self):
        b, l, c = self.me["b"], self.me["l"], self.me["c"]
        px, pz, pd = rank_of(1 - b, l, c), rank_of(b, 1 - l, c), rank_of(1 - b, 1 - l, c)
        for p, half, on in (
            (px, 0, self.tz),
            (pz, 1, self.tx),
            (px, 1, None),
            (pz, 0, None),
            (pd, 0, None),
            (pd, 1, None),
        ):
            block = upper(self.view(p), half)
            landed(block, self.recv.at[p, half])
            if on is not None:
                self.put(block, p, half, on)
            self.put(block, p, half, self.ts)
        for q in range(4):
            p = q * 2 + 1 - c
            for half in range(2):
                landed(upper(self.view(p), half), self.recv.at[p, half])
        self.copies.drain()


class TeamSum:
    SENDS = 10

    def __init__(self, me, part, near, acc, mid, far, send, recv):
        self.me, self.part, self.near, self.acc, self.mid, self.far = me, part, near, acc, mid, far
        self.recv = recv
        self.copies = Copies(send)

    def start(self):
        b, l, c = self.me["b"], self.me["l"], self.me["c"]
        self.spots = [(b, l), (1 - b, l), (b, 1 - l), (1 - b, 1 - l)]
        for i in (3, 1, 2, 0):
            bb, ll = self.spots[i]
            self.copies.go(
                self.part(rank_of(bb, ll, 1 - c)), self.near.at[i], self.recv.at[i], {"c": 1 - c}
            )

    def pair(self, i):
        bb, ll = self.spots[i]
        landed(self.near.at[i], self.recv.at[i])
        return self.part(rank_of(bb, ll, self.me["c"]))[...].astype(F32) + self.near[i].astype(F32)

    def finish(self):
        b, l = self.me["b"], self.me["l"]
        tx, tz = {"b": 1 - b}, {"l": 1 - l}
        acc, mid, far, recv, go = self.acc, self.mid, self.far, self.recv, self.copies.go
        for i in (3, 1, 2):
            acc[i - 1] = self.pair(i).astype(BF)
            if i == 3:
                go(upper(acc.at[2], 0), mid.at[0], recv.at[4], tx)
                go(upper(acc.at[2], 1), mid.at[1], recv.at[5], tz)
            elif i == 1:
                go(upper(acc.at[0], 0), upper(far.at[0], 0), recv.at[6], tx)
            else:
                go(upper(acc.at[1], 1), upper(far.at[1], 1), recv.at[7], tz)
        n = mid.shape[1]
        landed(mid.at[0], recv.at[4])
        acc[1, :n] = (acc[1, :n].astype(F32) + mid[0].astype(F32)).astype(BF)
        go(upper(acc.at[1], 0), upper(far.at[1], 0), recv.at[8], tz)
        landed(mid.at[1], recv.at[5])
        acc[0, n:] = (acc[0, n:].astype(F32) + mid[1].astype(F32)).astype(BF)
        go(upper(acc.at[0], 1), upper(far.at[0], 1), recv.at[9], tx)
        own = self.pair(0)
        landed(upper(far.at[0], 0), recv.at[6])
        landed(upper(far.at[1], 1), recv.at[7])
        landed(upper(far.at[1], 0), recv.at[8])
        landed(upper(far.at[0], 1), recv.at[9])
        total = own + far[0].astype(F32) + far[1].astype(F32)
        self.copies.drain()
        return total

    @staticmethod
    def scratch(R, C):
        return [
            pltpu.VMEM((4, R, C), BF),
            pltpu.VMEM((3, R, C), BF),
            pltpu.VMEM((2, R // 2, C), BF),
            pltpu.VMEM((2, R, C), BF),
            DMA((10,)),
            DMA((10,)),
        ]


class TeamsGather:
    def __init__(self, me, H, source, out, send, near, far):
        self.me, self.H, self.source, self.out = me, H, source, out
        self.near, self.far = near, far
        self.copies = Copies(send)

    @staticmethod
    def sems(H):
        return [DMA((9 + 4 * (H - 1),)), DMA((8,)), DMA((2 * H, 2))]

    def start(self):
        me = self.me
        a, b, h, l, c = (me[n] for n in ALL)
        mine = rank_of(b, l, c)
        for m, to in mates(me):
            p = rank_of(to["b"], to["l"], to["c"])
            self.copies.go(self.source(p), self.out.at[a, b, h, l, c], self.near.at[mine], to)

    def spread(self, local):
        me = self.me
        a, b, h, l, c = (me[n] for n in ALL)
        local.wait()
        for g in range(2):
            bb = b if g == 0 else 1 - b
            for m in range(4):
                if g == 0 and m == 0:
                    continue
                ll, cc = l ^ (m >> 1), c ^ (m & 1)
                landed(self.out.at[a, bb, h, ll, cc], self.near.at[rank_of(bb, ll, cc)])
            block = self.out.at[a, bb, h]
            for dh in range(1, self.H):
                to = lax.rem(h + dh, self.H)
                self.copies.go(block, block, self.far.at[dh, g], {"h": to})
            self.copies.go(block, block, self.far.at[0, g], {"a": 1 - a})

    def forward(self):
        me = self.me
        a, b, h, l, c = (me[n] for n in ALL)
        H = self.H
        for g in range(2):
            bb = b if g == 0 else 1 - b
            for dh in range(1, H):
                came = lax.rem(h - dh + H, H)
                block = self.out.at[a, bb, came]
                landed(block, self.far.at[dh, g])
                self.copies.go(block, block, self.far.at[H - 1 + dh, g], {"a": 1 - a})

    def finish(self):
        me = self.me
        a, b, h, l, c = (me[n] for n in ALL)
        H = self.H
        for g in range(2):
            bb = b if g == 0 else 1 - b
            landed(self.out.at[1 - a, bb, h], self.far.at[0, g])
            for dh in range(1, H):
                came = lax.rem(h - dh + H, H)
                landed(self.out.at[1 - a, bb, came], self.far.at[H - 1 + dh, g])
        self.copies.drain()


class Halo:
    def __init__(self, me, H, own, out, send, recv):
        self.me, self.H, self.own, self.out, self.send, self.recv = me, H, own, out, send, recv
        self.last = (me["l"] == 1) & (me["c"] == 1) & (me["h"] < H - 1)

    def each(self):
        me = self.me
        n = self.own.shape[0]
        for p in range(8):
            to = {
                "b": p >> 2,
                "h": jnp.minimum(me["h"] + 1, self.H - 1),
                "l": (p >> 1) & 1,
                "c": p & 1,
            }
            src = self.own.at[pl.ds(n - 16, 16)]
            yield remote(src, self.out.at[me["b"]], self.send.at[p], self.recv.at[me["b"]], to)

    def start(self):
        if self.H == 1:
            return

        @pl.when(self.last)
        def _():
            for copy in self.each():
                copy.start()

    def finish(self):
        if self.H == 1:
            return

        @pl.when(self.me["h"] > 0)
        def _():
            for b in range(2):
                landed(self.out.at[b], self.recv.at[b])

        @pl.when(self.last)
        def _():
            for copy in self.each():
                copy.wait_send()


class Edge:
    def __init__(self, me, H, first, got, send, recv):
        self.me, self.H, self.first, self.got, self.send, self.recv = me, H, first, got, send, recv

    def each(self):
        me = self.me
        mine = rank_of(me["b"], me["l"], me["c"])
        for b in range(2):
            to = {"b": b, "h": jnp.maximum(me["h"] - 1, 0), "l": 1, "c": 1}
            yield remote(self.first.at[b], self.got.at[mine], self.send.at[b], self.recv.at[mine], to)

    def start(self):
        if self.H == 1:
            return

        @pl.when(self.me["h"] > 0)
        def _():
            for copy in self.each():
                copy.start()

    def finish(self, out):
        if self.H == 1:
            return
        me = self.me

        @pl.when((me["l"] == 1) & (me["c"] == 1) & (me["h"] < self.H - 1))
        def _():
            for p in range(8):
                landed(self.got.at[p], self.recv.at[p])
            total = self.got[0, 0:1].astype(F32)
            for p in range(1, 8):
                total = total + self.got[p, 0:1].astype(F32)
            n = out.shape[0]
            out[n - 1 : n] = out[n - 1 : n] + total

        @pl.when(me["h"] > 0)
        def _():
            for copy in self.each():
                copy.wait_send()


class Exchange:
    def __init__(self, me, source, out, send, recv):
        self.me, self.source, self.out, self.recv = me, source, out, recv
        self.copies = Copies(send)

    def start(self):
        mine = rank_of(self.me["b"], self.me["l"], self.me["c"])
        for m, to in mates(self.me):
            p = rank_of(to["b"], to["l"], to["c"])
            self.copies.go(self.source(p), self.out(mine), self.recv.at[mine], to)

    def finish(self):
        for m, to in mates(self.me):
            p = rank_of(to["b"], to["l"], to["c"])
            landed(self.out(p), self.recv.at[p])
        self.copies.drain()


ANY = pl.BlockSpec(memory_space=pl.ANY)
VM = pl.BlockSpec(memory_space=pltpu.VMEM)


def comm_call(body, outs, in_specs, out_specs, scratch, cid):
    return pl.pallas_call(
        body,
        out_shape=outs,
        in_specs=in_specs,
        out_specs=out_specs,
        scratch_shapes=scratch,
        compiler_params=pltpu.CompilerParams(
            collective_id=cid, has_side_effects=True, vmem_limit_bytes=VMEM_BYTES
        ),
    )


def opening(H, vecs, x, up, w, later):
    A = lax.axis_size("a")
    grid = (A, 2, H, 2, 2)
    rows, D = x.shape
    dcol = D // 8

    def body(
        vecs, x, up, w, later, va, xg, halo, upc, wa, team, *sems
    ):
        vs, vn, vf, xs, xr, hs, hr, us, ur, ws, wn, wf, qs, qr, ls = sems
        me = coords()
        a, b, h, l, c = (me[n] for n in ALL)
        mine = rank_of(b, l, c)
        local = [
            pltpu.make_async_copy(w.at[mine], wa.at[a, b, h, l, c], ls.at[0]),
            pltpu.make_async_copy(vecs, va.at[a, b, h, l, c], ls.at[1]),
            pltpu.make_async_copy(x, xg.at[mine], ls.at[2]),
            pltpu.make_async_copy(
                up.at[:, pl.ds(pl.multiple_of(mine * dcol, dcol), dcol)], upc.at[mine], ls.at[3]
            ),
            pltpu.make_async_copy(later.at[mine], team.at[mine], ls.at[4]),
        ]
        for copy in local:
            copy.start()
        greet(me, H, True, True)
        gw = TeamsGather(me, H, lambda p: w.at[p], wa, ws, wn, wf)
        gv = TeamsGather(me, H, lambda p: vecs, va, vs, vn, vf)
        gx = TeamGather(me, x, lambda p: xg.at[p], xs, xr)
        gh = Halo(me, H, x, halo, hs, hr)
        gu = Exchange(
            me,
            lambda p: up.at[:, pl.ds(pl.multiple_of(p * dcol, dcol), dcol)],
            lambda p: upc.at[p],
            us,
            ur,
        )
        gq = Exchange(me, lambda p: later.at[p], lambda p: team.at[p], qs, qr)
        gv.start()
        gw.start()
        gx.start()
        gh.start()
        gw.spread(local[0])
        gv.spread(local[1])
        gx.finish()
        gu.start()
        gq.start()
        gv.forward()
        gw.forward()
        gu.finish()
        gh.finish()
        gv.finish()
        gw.finish()
        gq.finish()
        for copy in local[2:]:
            copy.wait()

    gsems = TeamsGather.sems(H)
    return comm_call(
        body,
        (
            jax.ShapeDtypeStruct((*grid, *vecs.shape), BF),
            jax.ShapeDtypeStruct((8, rows, D), BF),
            jax.ShapeDtypeStruct((2, 16, D), BF),
            jax.ShapeDtypeStruct((8, rows, dcol), BF),
            jax.ShapeDtypeStruct((*grid, *w.shape[1:]), BF),
            jax.ShapeDtypeStruct(later.shape, BF),
        ),
        [ANY] * 5,
        [ANY] * 6,
        [*gsems, DMA((14,)), DMA((8, 2)), DMA((8,)), DMA((2,)), DMA((7,)), DMA((8,)), *gsems]
        + [DMA((7,)), DMA((8,)), DMA((5,))],
        0,
    )(vecs, x, up, w, later)


def gather_rows(H, x, cid, with_halo, move=None):
    rows, D = x.shape

    def body(*refs):
        refs = list(refs)
        x = refs.pop(0)
        src = refs.pop(0) if move is not None else None
        out = refs.pop(0)
        halo = refs.pop(0) if with_halo else None
        moved = refs.pop(0) if move is not None else None
        xs, xr, ls = refs[:3]
        rest = refs[3:]
        me = coords()
        mine = rank_of(me["b"], me["l"], me["c"])
        local = pltpu.make_async_copy(x, out.at[mine], ls.at[0])
        local.start()
        if move is not None:
            keep = pltpu.make_async_copy(src.at[mine], moved.at[mine], ls.at[1])
            keep.start()
        greet(me, H, with_halo, False)
        gx = TeamGather(me, x, lambda p: out.at[p], xs, xr)
        gx.start()
        if with_halo:
            gh = Halo(me, H, x, halo, rest[0], rest[1])
            gh.start()
        if move is not None:
            gm = Exchange(me, lambda p: src.at[p], lambda p: moved.at[p], rest[-2], rest[-1])
            gm.start()
        gx.finish()
        if with_halo:
            gh.finish()
        if move is not None:
            gm.finish()
            keep.wait()
        local.wait()

    outs = [jax.ShapeDtypeStruct((8, rows, D), BF)]
    scratch = [DMA((14,)), DMA((8, 2)), DMA((2,))]
    args = [x]
    if with_halo:
        outs.append(jax.ShapeDtypeStruct((2, 16, D), BF))
        scratch += [DMA((8,)), DMA((2,))]
    if move is not None:
        outs.append(jax.ShapeDtypeStruct(move.shape, BF))
        scratch += [DMA((7,)), DMA((8,))]
        args.append(move)
    out = comm_call(body, tuple(outs), [ANY] * len(args), [ANY] * len(outs), scratch, cid)(*args)
    return out if len(outs) > 1 else out[0]


def gather_columns(x, cid):
    T, m = x.shape

    def body(x, out, xs, xr, ls):
        me = coords()
        mine = rank_of(me["b"], me["l"], me["c"])

        def view(p):
            return out.at[:, pl.ds(pl.multiple_of(p * m, m), m)]

        local = pltpu.make_async_copy(x, view(mine), ls)
        local.start()
        greet(me, 1, False, False)
        gx = TeamGather(me, x, view, xs, xr)
        gx.start()
        gx.finish()
        local.wait()

    return comm_call(
        body,
        jax.ShapeDtypeStruct((T, 8 * m), BF),
        [ANY],
        ANY,
        [DMA((14,)), DMA((8, 2)), DMA],
        cid,
    )(x)


def sum_rows(H, part, first, cid):
    _, rows, D = part.shape
    n = len(TeamSum.scratch(rows, D))

    def body(*refs):
        refs = list(refs)
        part = refs.pop(0)
        fst = refs.pop(0) if first is not None else None
        out = refs.pop(0)
        me = coords()
        greet(me, H, first is not None, False)
        s = TeamSum(me, lambda p: part.at[p], *refs[:n])
        s.start()
        if first is not None:
            e = Edge(me, H, fst, *refs[n:])
            e.start()
        out[...] = s.finish()
        if first is not None:
            e.finish(out)

    scratch = TeamSum.scratch(rows, D)
    args = [part]
    if first is not None:
        scratch += [pltpu.VMEM((8, 16, D), BF), DMA((2,)), DMA((8,))]
        args.append(first)
    return comm_call(
        body, jax.ShapeDtypeStruct((rows, D), F32), [VM] * len(args), VM, scratch, cid
    )(*args)


def sum_columns(part, cid):
    T, m = part.shape[0], part.shape[1] // 8

    def body(part, out, *scratch):
        me = coords()
        greet(me, 1, False, False)
        s = TeamSum(
            me, lambda p: part.at[:, pl.ds(pl.multiple_of(p * m, m), m)], *scratch
        )
        s.start()
        out[...] = s.finish()

    return comm_call(
        body, jax.ShapeDtypeStruct((T, m), F32), [VM], VM, TeamSum.scratch(T, m), cid
    )(part)


def closing(H, small, cols):
    A = lax.axis_size("a")
    n = small.shape[0]
    grid = (A, 2, H, 2, 2)

    def body(small, cols, total, moved, got, ss, sr, ms, mr, ls):
        me = coords()
        a, b, h, l, c = (me[k] for k in ALL)
        mine = rank_of(b, l, c)
        keep = pltpu.make_async_copy(cols.at[mine], moved.at[mine], ls)
        keep.start()
        sem = pltpu.get_barrier_semaphore()
        others = []
        for i in range(1, n):
            k = i
            dc, k = k % 2, k // 2
            dl, k = k % 2, k // 2
            dh, k = k % H, k // H
            db, da = k % 2, k // 2
            to = {
                "a": lax.rem(a + da, A),
                "b": b ^ db,
                "h": lax.rem(h + dh, H),
                "l": l ^ dl,
                "c": c ^ dc,
            }
            others.append((i, to))
            pl.semaphore_signal(sem, inc=1, device_id=to, device_id_type=MESH)
        pl.semaphore_wait(sem, n - 1)
        copies = Copies(ss)

        def at(d):
            return (((d["a"] * 2 + d["b"]) * H + d["h"]) * 2 + d["l"]) * 2 + d["c"]

        for i, to in others:
            copies.go(small.at[at(to)], got.at[i], sr.at[i], to)
        gm = Exchange(me, lambda p: cols.at[p], lambda p: moved.at[p], ms, mr)
        gm.start()
        acc = small[at(me)]
        for i, _ in others:
            landed(got.at[i], sr.at[i])
            acc = acc + got[i]
        total[...] = acc
        copies.drain()
        gm.finish()
        keep.wait()

    return comm_call(
        body,
        (
            jax.ShapeDtypeStruct(small.shape[1:], F32),
            jax.ShapeDtypeStruct(cols.shape, BF),
        ),
        [VM, ANY],
        [VM, ANY],
        [pltpu.VMEM(small.shape, F32), DMA((n,)), DMA((n,)), DMA((7,)), DMA((8,)), DMA],
        15,
    )(small, cols)


def dot(a, b, dims):
    return lax.dot_general(a, b, (dims, ((), ())), preferred_element_type=F32)


def mm(a, b):
    return dot(a, b, ((1,), (0,)))


def mm_nt(a, b):
    return dot(a, b, ((1,), (1,)))


def mm_tn(a, b):
    return dot(a, b, ((0,), (0,)))


class Layout:
    def __init__(self, mesh_shape):
        self.A, self.B, self.H, self.L, self.C = mesh_shape
        self.team = self.B * self.L * self.C
        self.n = self.team * self.A * self.H

    def spread(self, v, whole):
        w = v.shape[-1] // self.n
        lead = v.shape[:-1]
        if w % whole:
            return v.reshape(*lead, self.team, -1)
        k = len(lead)
        v = v.reshape(*lead, self.A, self.B, self.H, self.L, self.C, w)
        v = v.transpose(*range(k), k + 1, k + 3, k + 4, k, k + 2, k + 5)
        return v.reshape(*lead, self.team, -1)

    def unspread(self, v, whole):
        lead = v.shape[:-2]
        w = v.shape[-1] * self.team // self.n
        if w % whole:
            return v.reshape(*lead, -1)
        k = len(lead)
        v = v.reshape(*lead, self.B, self.L, self.C, self.A, self.H, w)
        v = v.transpose(*range(k), k + 3, k, k + 4, k + 1, k + 2, k + 5)
        return v.reshape(*lead, -1)

    def rows_in(self, g):
        m = g.shape[-1]
        g = g.reshape(self.A, self.H, self.B, self.L, self.C, -1, m)
        return g.transpose(0, 2, 1, 3, 4, 5, 6).reshape(-1, m)

    def rows_out(self, g):
        m = g.shape[-1]
        g = g.reshape(self.A, self.B, self.H, self.L, self.C, -1, m)
        return g.transpose(0, 2, 1, 3, 4, 5, 6).reshape(self.A * self.H, self.team, -1, m)


def normed(v):
    mean = jnp.mean(v, axis=-1, keepdims=True)
    cent = v - mean
    rstd = lax.rsqrt(jnp.mean(cent * cent, axis=-1, keepdims=True) + EPS)
    return cent * rstd, rstd


def norm_back(e, xhat, rstd):
    m1 = jnp.mean(e, axis=-1, keepdims=True)
    m2 = jnp.mean(e * xhat, axis=-1, keepdims=True)
    return (e - m1 - xhat * m2) * rstd


def with_before(rows, halo, segs):
    v = rows.reshape(segs, -1, rows.shape[-1])
    return jnp.concatenate([halo, v[:, :-1]], axis=1).reshape(rows.shape)


def with_after(rows, segs):
    v = rows.reshape(segs, -1, rows.shape[-1])
    return (
        jnp.concatenate([v[:, 1:], jnp.zeros_like(v[:, :1])], axis=1).reshape(rows.shape),
        v[:, :1],
    )


EX = lax.Precision.HIGHEST


def ein(spec, a, b):
    return jnp.einsum(spec, a, b, precision=EX, preferred_element_type=F32)


class Wkv:
    def __init__(self, r, k, v, lam, u):
        c = r.shape[2]
        self.c = c
        i = jnp.arange(c, dtype=F32)[:, None, None]
        self.i = i
        self.down = jnp.exp(-lam[None] * i)
        self.up = jnp.exp(lam[None] * (i + 1.0))
        self.tail = jnp.exp(-lam[None] * (c - 1.0 - i))
        self.span = jnp.exp(-lam * c)
        self.r, self.k, self.v, self.u = r, k, v, u
        self.rd, self.kg, self.kt = r * self.down, k * self.up, k * self.tail
        self.low = jnp.arange(c)[:, None] > jnp.arange(c)[None, :]
        self.add = ein("znsgc,znsgv->zngcv", self.kt, v)

    def closing(self):
        s = 0.0
        for n in range(self.r.shape[1]):
            s = self.span[..., None] * s + self.add[:, n]
        return s

    def forward(self, s):
        states = []
        for n in range(self.r.shape[1]):
            states.append(s)
            s = self.span[..., None] * s + self.add[:, n]
        self.states = jnp.stack(states, 1)
        att = jnp.where(self.low, ein("zntgc,znsgc->zngts", self.rd, self.kg), 0.0)
        self.att = att
        self.diag = jnp.sum(self.r * self.u * self.k, axis=-1, keepdims=True)
        y = ein("zngts,znsgv->zntgv", att, self.v) + self.diag * self.v
        y = y + ein("zntgc,zngcv->zntgv", self.rd, self.states)
        return y, s

    def back_add(self, dy):
        return ein("zntgc,zntgv->zngcv", self.rd, dy)

    def back_closing(self, adds):
        g = 0.0
        for n in reversed(range(self.r.shape[1])):
            g = self.span[..., None] * g + adds[:, n]
        return g

    def backward(self, dy, adds, g):
        ends = []
        for n in reversed(range(self.r.shape[1])):
            ends.append(g)
            g = self.span[..., None] * g + adds[:, n]
        ends = jnp.stack(ends[::-1], 1)
        datt = jnp.where(self.low, ein("zntgv,znsgv->zngts", dy, self.v), 0.0)
        ddiag = jnp.sum(dy * self.v, axis=-1, keepdims=True)
        d_rd = ein("zngts,znsgc->zntgc", datt, self.kg) + ein("zntgv,zngcv->zntgc", dy, self.states)
        d_kg = ein("zngts,zntgc->znsgc", datt, self.rd)
        d_kt = ein("znsgv,zngcv->znsgc", self.v, ends)
        d_v = ein("zngts,zntgv->znsgv", self.att, dy) + self.diag * dy
        d_v = d_v + ein("znsgc,zngcv->znsgv", self.kt, ends)
        d_r = d_rd * self.down + ddiag * self.u * self.k
        d_k = d_kg * self.up + d_kt * self.tail + ddiag * self.u * self.r
        d_u = jnp.sum(ddiag * self.r * self.k, axis=(0, 1, 2))
        i = self.i
        d_l = jnp.sum(
            (i + 1.0) * self.kg * d_kg
            - i * self.rd * d_rd
            - (self.c - 1.0 - i) * self.kt * d_kt,
            axis=(0, 1, 2),
        )
        d_l = d_l - self.c * self.span * jnp.sum(self.states * ends, axis=(0, 1, 4))
        return d_r, d_k, d_v, d_u, d_l


def chain(first, add, span, n, ahead):
    place = lax.axis_index("h")
    state = jnp.where(place == (0 if ahead else n - 1), first, 0.0)
    for i in range(n - 1):
        pairs = [(j, j + 1) for j in range(n - 1)] if ahead else [(j + 1, j) for j in range(n - 1)]
        arrived = lax.ppermute(span * state + add, "h", pairs)
        state = jnp.where(place == (i + 1 if ahead else n - 2 - i), arrived, state)
    return state


def swap(v, axis):
    return lax.ppermute(v, axis, [(0, 1), (1, 0)])


def shifted(v, dh, H):
    return lax.ppermute(v, "h", [(i, (i + dh) % H) for i in range(H)])


def in_order(near, far, lay):
    a, h = lax.axis_index("a"), lax.axis_index("h")
    out = []
    for i in range(lay.A):
        for j in range(lay.H):
            pick = lambda group: lax.select_n(lax.rem(h - j + lay.H, lay.H), *group)
            if lay.H == 2:
                pick = lambda group: jnp.where(h == j, group[0], group[1])
            elif lay.H > 2:
                pick = lambda group: lax.dynamic_index_in_dim(
                    jnp.stack(group), lax.rem(h - j + lay.H, lay.H), 0, False
                )
            out.append(jnp.where(a == i, pick(near), pick(far)))
    return jnp.stack(out)


def teams_gather(v, lay):
    near = [v] + [shifted(v, dh, lay.H) for dh in range(1, lay.H)]
    far = [swap(n, "a") for n in near]
    return in_order(near, far, lay)


def teams_sum(g, lay):
    a, h = lax.axis_index("a"), lax.axis_index("h")
    g = g.reshape(lay.A, lay.H, *g.shape[1:])
    keep = lax.dynamic_index_in_dim(g, a, 0, False)
    got = swap(lax.dynamic_index_in_dim(g, 1 - a, 0, False), "a")
    part = (keep.astype(F32) + got.astype(F32)).astype(BF)
    total = lax.dynamic_index_in_dim(part, h, 0, False).astype(F32)
    for dh in range(1, lay.H):
        sent = lax.dynamic_index_in_dim(part, lax.rem(h + dh, lay.H), 0, False)
        total = total + shifted(sent, dh, lay.H).astype(F32)
    return total.astype(BF)


def swap_blocks(v, rank):
    got = [lax.dynamic_index_in_dim(v, rank, 0, False)]
    for m in range(1, 8):
        sent = lax.dynamic_index_in_dim(v, rank ^ m, 0, False)
        got.append(lax.ppermute(sent, TEAM, [(i, i ^ m) for i in range(8)]))
    got = jnp.stack(got)
    return jnp.stack([lax.dynamic_index_in_dim(got, rank ^ p, 0, False) for p in range(8)])


def per_device(lay, *args):
    (x_in, up_in, start_in) = args[:3]
    vec = args[3:13]
    w_r, w_k, w_v, w_g, w_o = args[13:18]
    vec2 = args[18:22]
    w_ck, w_cv, w_cr = args[22:]
    a_at, b_at, h_at = (lax.axis_index(n) for n in ("a", "b", "h"))
    rank = (b_at * lay.L + lax.axis_index("l")) * lay.C + lax.axis_index("c")
    H = lay.H
    segs = lay.B
    D = x_in.shape[-1]
    x_own = x_in[0]
    rows = x_own.shape[0]
    T = rows * lay.team
    dcol = D // lay.team
    heads = dcol // HEAD
    half = lay.L * lay.C
    w_row = D // lay.n
    hid = w_ck.shape[1] // lay.team

    stacked = jnp.stack([*vec, *vec2])
    nv = stacked.shape[0]
    stacked = jnp.pad(stacked, ((0, 16 - nv), (0, 128 - w_row)))
    spread4 = jnp.concatenate(
        [lay.spread(w, HEAD) for w in (w_r, w_k, w_v, w_g)], axis=-1
    ).transpose(1, 0, 2)
    ffn = jnp.concatenate([lay.spread(w_ck, 1), lay.spread(w_cr, D)], axis=-1).transpose(1, 0, 2)
    va, xg, halo_x, upc, W4, ffn_got = opening(H, stacked, x_own, up_in[0], spread4, ffn)
    every = va.reshape(lay.n, 16, 128)[:, :nv, :w_row].transpose(1, 0, 2).reshape(nv, D).astype(F32)
    g1, b1, s_r, s_k, s_v, s_g, lam, bonus, gn_g, gn_b, g2, b2, s_ck, s_cr = every
    W4 = W4.reshape(D, 4 * dcol)
    W_r, W_k, W_v, W_g = (W4[:, i * dcol : (i + 1) * dcol] for i in range(4))
    w_o, w_cv, ffn_got, xg = lax.optimization_barrier((w_o, w_cv, ffn_got, xg))
    if w_row % HEAD:
        W_o = lax.all_gather(w_o, ALL, axis=0, tiled=True)
        W_o = lax.dynamic_slice_in_dim(W_o, rank * dcol, dcol, 0)
    else:
        W_o = teams_gather(w_o, lay).reshape(dcol, D)
    ffn_all = lay.rows_in(teams_gather(ffn_got, lay))
    W_ck, W_cr = ffn_all[:, :hid], ffn_all[:, hid:]
    W_cv = teams_gather(w_cv, lay).reshape(hid, D)

    def mine(v):
        return lax.dynamic_index_in_dim(lay.spread(v, HEAD), rank, 0, False)

    lam_m, u_m, gs_m, gb_m = (mine(v) for v in (lam, bonus, gn_g, gn_b))

    def halo_rows(halo):
        return jnp.where(h_at > 0, halo[:, -1:].astype(F32), 0.0)

    xf = xg.reshape(T, D).astype(F32)
    n1 = normed(xf)[0] * g1 + b1
    halo_1 = jnp.where(h_at > 0, normed(halo_rows(halo_x))[0] * g1 + b1, 0.0)
    before = with_before(n1, halo_1, segs)
    diff1 = n1 - before
    m_r, m_k, m_v, m_g = ((before + s * diff1).astype(BF) for s in (s_r, s_k, s_v, s_g))
    r = mm(m_r, W_r).astype(BF)
    k = mm(m_k, W_k).astype(BF)
    v = mm(m_v, W_v).astype(BF)
    gate = mm(m_g, W_g)
    shape = (segs, T // segs // CHUNK, CHUNK, heads, HEAD)
    lam_h, u_h = lam_m.reshape(heads, HEAD), u_m.reshape(heads, HEAD)
    wkv = Wkv(*(t.astype(F32).reshape(shape) for t in (r, k, v)), lam_h, u_h)
    span_all = jnp.exp(-lam_h * (T // segs))[..., None]
    nh = start_in.shape[1]
    head_ids = jnp.arange(nh * HEAD, dtype=jnp.int32)

    def heads_of(p):
        ids = lax.dynamic_index_in_dim(lay.spread(head_ids, HEAD), p, 0, False)
        return ids[::HEAD] // HEAD

    my_heads = heads_of(rank)
    own_start = jnp.take(start_in[0], my_heads, axis=0)
    got_start = swap(jnp.take(start_in[0], heads_of(rank ^ 4), axis=0), "b")
    start = jnp.where(b_at == 0, jnp.stack([own_start, got_start]), jnp.stack([got_start, own_start]))
    s_in = chain(start, wkv.closing(), span_all, lay.H, True)
    mixer, s_out = wkv.forward(s_in)
    mix = mixer.reshape(T, heads, HEAD)
    cent = mix - jnp.mean(mix, axis=-1, keepdims=True)
    g_rstd = lax.rsqrt(jnp.mean(cent * cent, axis=-1, keepdims=True) + GROUP_EPS)
    g_hat = (cent * g_rstd).reshape(T, dcol)
    n_mix = g_hat * gs_m + gb_m
    sig = jax.nn.sigmoid(gate)
    silu = gate * sig
    gated = (n_mix * silu).astype(BF)
    part = mm(gated, W_o).astype(BF).reshape(8, rows, D)
    middle = x_own.astype(F32) + sum_rows(H, part, None, 1)

    placed = jnp.zeros((segs, nh, HEAD, HEAD), BF)
    s_fin = jnp.where(h_at == lay.H - 1, s_out, 0.0).astype(BF)
    placed = placed.at[:, my_heads].set(s_fin)
    final = lax.psum_scatter(placed, "b", scatter_dimension=0, tiled=True)
    final = lax.psum_scatter(final, SEQ, scatter_dimension=1, tiled=True).astype(F32)

    hat2, rstd2 = normed(middle)
    n2_own = (hat2 * g2 + b2).astype(BF)
    n2, halo_2 = gather_rows(H, n2_own, 2, True)
    n2 = n2.reshape(T, D).astype(F32)
    before2 = with_before(n2, halo_rows(halo_2), segs)
    diff2 = n2 - before2
    m_ck, m_cr = ((before2 + s * diff2).astype(BF) for s in (s_ck, s_cr))
    relu = jax.nn.relu(mm(m_ck, W_ck))
    act = (relu * relu).astype(BF)
    val = sum_columns(mm(act, W_cv).astype(BF), 3)
    sigma = jax.nn.sigmoid(mm(m_cr, W_cr))
    upc = upc.reshape(T, dcol).astype(F32)
    add = (sigma * val).astype(BF).reshape(lay.team, rows, dcol)

    d_value = (sigma * upc).astype(BF)
    d_pregate = (upc * val * sigma * (1.0 - sigma)).astype(BF)
    d_val = gather_columns(d_value, 4)
    g_cv = mm_tn(act, d_val)
    d_pre = (mm_nt(d_val, W_cv) * 2.0 * relu).astype(BF)
    g_ck = mm_tn(m_ck, d_pre)
    g_cr = mm_tn(m_cr, d_pregate)
    d_mck = mm_nt(d_pre, W_ck)
    d_mcr = mm_nt(d_pregate, W_cr)
    g_s_ck = jnp.sum(d_mck * diff2, axis=0)
    g_s_cr = jnp.sum(d_mcr * diff2, axis=0)
    nxt, first = with_after((1.0 - s_ck) * d_mck + (1.0 - s_cr) * d_mcr, segs)
    dn2_part = (s_ck * d_mck + s_cr * d_mcr + nxt).astype(BF)

    def edge_rows(first):
        return jnp.pad(first.astype(BF), ((0, 0), (0, 15), (0, 0)))

    dn2 = sum_rows(H, dn2_part.reshape(8, rows, D), edge_rows(first), 5)
    g_g2 = jnp.sum(dn2 * hat2, axis=0)
    g_b2 = jnp.sum(dn2, axis=0)
    d_mid = up_in[0].astype(F32) + norm_back(dn2 * g2, hat2, rstd2)

    d_br, moved = gather_rows(H, d_mid.astype(BF), 6, False, add)
    layer_output = (middle + moved.transpose(1, 0, 2).reshape(rows, D).astype(F32)).astype(BF)
    d_br = d_br.reshape(T, D)
    g_o = mm_tn(gated, d_br)
    d_gated = mm_nt(d_br, W_o)
    dn = d_gated * silu
    g_gs = jnp.sum(dn * g_hat, axis=0)
    g_gb = jnp.sum(dn, axis=0)
    d_gate = (d_gated * n_mix * sig * (1.0 + gate * (1.0 - sig))).astype(BF)
    d_mix = norm_back(
        (dn * gs_m).reshape(T, heads, HEAD), g_hat.reshape(T, heads, HEAD), g_rstd
    ).reshape(shape)
    adds = wkv.back_add(d_mix)
    g_in = chain(0.0, wkv.back_closing(adds), span_all, lay.H, False)
    d_r, d_k, d_v, d_u, d_l = wkv.backward(d_mix, adds, g_in)
    d_r, d_k, d_v = (t.reshape(T, dcol).astype(BF) for t in (d_r, d_k, d_v))
    g_r, g_k, g_v, g_w = (
        mm_tn(m, d) for m, d in ((m_r, d_r), (m_k, d_k), (m_v, d_v), (m_g, d_gate))
    )
    d_m = [mm_nt(d, w) for d, w in ((d_r, W_r), (d_k, W_k), (d_v, W_v), (d_gate, W_g))]
    shares = (s_r, s_k, s_v, s_g)
    g_shares = [jnp.sum(d * diff1, axis=0) for d in d_m]
    nxt, first = with_after(sum((1.0 - s) * d for s, d in zip(shares, d_m)), segs)
    dn1_part = (sum(s * d for s, d in zip(shares, d_m)) + nxt).astype(BF)
    dn1 = sum_rows(H, dn1_part.reshape(8, rows, D), edge_rows(first), 7)
    hat1, rstd1 = normed(x_own.astype(F32))
    g_g1 = jnp.sum(dn1 * hat1, axis=0)
    g_b1 = jnp.sum(dn1, axis=0)
    input_grad = d_mid + norm_back(dn1 * g1, hat1, rstd1)

    g_cv = teams_sum(g_cv.astype(BF).reshape(lay.A * H, -1, D), lay).astype(F32)
    if w_row % HEAD:
        g_o = jnp.zeros((D, D), BF).at[rank * dcol + jnp.arange(dcol)].set(g_o.astype(BF))
        g_o = lax.psum_scatter(g_o, ALL, scatter_dimension=0, tiled=True).astype(F32)
    else:
        g_o = teams_sum(g_o.astype(BF).reshape(lay.A * H, -1, D), lay).astype(F32)

    def shares_out(pieces):
        whole = jnp.concatenate([g.astype(BF) for g in pieces], axis=1)
        return teams_sum(lay.rows_out(whole), lay)

    g_ffn = swap_blocks(shares_out([g_ck, g_cr]), rank)
    g_4 = shares_out([g_r, g_k, g_v, g_w])

    def in_place(v):
        spread = jnp.where(jnp.arange(lay.team)[:, None] == rank, v.reshape(1, -1), 0.0)
        return lay.unspread(spread, HEAD)

    small = jnp.stack(
        [g_g1, g_b1, *g_shares, in_place(d_l), in_place(d_u), in_place(g_gs), in_place(g_gb)]
        + [g_g2, g_b2, g_s_ck, g_s_cr]
    )
    small = small.reshape(nv, lay.n, w_row).transpose(1, 0, 2)
    small = jnp.pad(small, ((0, 0), (0, 16 - nv), (0, 128 - w_row)))
    small, g_4 = closing(H, small, g_4)
    small = small[:nv, :w_row]

    def columns(got, lo, hi, unit):
        return lay.unspread(got[:, :, lo:hi].transpose(1, 0, 2), unit).astype(F32)

    g_r, g_k, g_v, g_w = (columns(g_4, i * dcol, (i + 1) * dcol, HEAD) for i in range(4))
    g_ck, g_cr = columns(g_ffn, 0, hid, 1), columns(g_ffn, hid, hid + dcol, D)
    return (
        layer_output[None],
        input_grad[None],
        final,
        *(small[i] for i in range(10)),
        g_r,
        g_k,
        g_v,
        g_w,
        g_o,
        *(small[i] for i in range(10, 14)),
        g_ck,
        g_cv,
        g_cr,
    )


def solution(mesh):
    n_seg, n_seq = mesh.devices.shape
    shape = (n_seg // 2, 2, n_seq // 4, 2, 2)
    view = Mesh(mesh.devices.reshape(shape), ALL)
    lay = Layout(shape)
    seg = ("a", "b")
    vec, mat = P(ALL), P(ALL, None)
    tok = P(seg, SEQ, None)

    def step(*args):
        return per_device(lay, *args)

    return jax.shard_map(
        step,
        mesh=view,
        in_specs=(tok, tok, P(seg, None, None, None), *[vec] * 10, *[mat] * 5, *[vec] * 4, *[mat] * 3),
        out_specs=(tok, tok, P(seg, SEQ, None, None), *[vec] * 10, *[mat] * 5, *[vec] * 4, *[mat] * 3),
        check_vma=False,
    )
```

```python
import jax
import jax.numpy as jnp
from jax import lax
from jax.experimental import pallas as pl
from jax.experimental.pallas import tpu as pltpu
from jax.sharding import Mesh, PartitionSpec as P

TEAM = ("b", "l", "c")
TEAMS = ("a", "h")
SEQ = ("h", "l", "c")
ALL = ("a", "b", "h", "l", "c")
HEAD = 64
CHUNK = 128
EPS = 1e-05
GROUP_EPS = 0.00064
BF = jnp.bfloat16
F32 = jnp.float32


MESH = pl.DeviceIdType.MESH
DMA = pltpu.SemaphoreType.DMA
VMEM_BYTES = 60 << 20


def coords():
    return {name: lax.axis_index(name) for name in ALL}


def rank_of(b, l, c):
    return (b * 2 + l) * 2 + c


def remote(src, dst, sent, landed, to):
    return pltpu.make_async_remote_copy(
        src_ref=src,
        dst_ref=dst,
        send_sem=sent,
        recv_sem=landed,
        device_id=to,
        device_id_type=MESH,
    )


def mates(me):
    for m in range(1, 8):
        yield m, {"b": me["b"] ^ (m >> 2), "l": me["l"] ^ ((m >> 1) & 1), "c": me["c"] ^ (m & 1)}


def greet(me, H, column, across):
    sem = pltpu.get_barrier_semaphore()
    count = 0
    for dh in range(H if column else 1):
        h = lax.rem(me["h"] + dh, H)
        for m in range(8):
            if dh == 0 and m == 0:
                continue
            to = {
                "b": me["b"] ^ (m >> 2),
                "h": h if column else me["h"],
                "l": me["l"] ^ ((m >> 1) & 1),
                "c": me["c"] ^ (m & 1),
            }
            pl.semaphore_signal(sem, inc=1, device_id=to, device_id_type=MESH)
            count += 1
    if across:
        pl.semaphore_signal(sem, inc=1, device_id={"a": 1 - me["a"]}, device_id_type=MESH)
        count += 1
    pl.semaphore_wait(sem, count)


class Copies:
    def __init__(self, sems):
        self.sems, self.k, self.open = sems, 0, []

    def go(self, src, dst, landed, to):
        copy = remote(src, dst, self.sems.at[self.k], landed, to)
        self.k += 1
        copy.start()
        self.open.append(copy)

    def drain(self):
        for copy in self.open:
            copy.wait_send()


def landed(ref, sem):
    remote(ref, ref, sem, sem, {"c": 1 - lax.axis_index("c")}).wait_recv()


def upper(ref, half):
    n = ref.shape[0] // 2
    return ref.at[pl.ds(half * n, n)]


class TeamGather:
    def __init__(self, me, own, view, send, recv, via=("xz", "zx")):
        self.me, self.own, self.view, self.recv, self.via = me, own, view, recv, via
        self.copies = Copies(send)
        self.tx, self.tz, self.ts = {"b": 1 - me["b"]}, {"l": 1 - me["l"]}, {"c": 1 - me["c"]}

    def put(self, src, p, half, to):
        self.copies.go(src, upper(self.view(p), half), self.recv.at[p, half], to)

    def start(self):
        mine = rank_of(self.me["b"], self.me["l"], self.me["c"])
        order = [(half, self.tx if self.via[half] == "xz" else self.tz) for half in range(2)]
        order += [(half, self.tz if self.via[half] == "xz" else self.tx) for half in range(2)]
        order += [(0, self.ts), (1, self.ts)]
        for half, to in order:
            self.put(upper(self.own, half), mine, half, to)

    def finish(self):
        b, l, c = self.me["b"], self.me["l"], self.me["c"]
        px, pz, pd = rank_of(1 - b, l, c), rank_of(b, 1 - l, c), rank_of(1 - b, 1 - l, c)
        order = [
            (px, half, self.tz) if self.via[half] == "xz" else (pz, half, self.tx)
            for half in range(2)
        ]
        order += [
            (pz, half, None) if self.via[half] == "xz" else (px, half, None) for half in range(2)
        ]
        for p, half, on in order + [(pd, 0, None), (pd, 1, None)]:
            block = upper(self.view(p), half)
            landed(block, self.recv.at[p, half])
            if on is not None:
                self.put(block, p, half, on)
            self.put(block, p, half, self.ts)
        for q in range(4):
            p = q * 2 + 1 - c
            for half in range(2):
                landed(upper(self.view(p), half), self.recv.at[p, half])
        self.copies.drain()


class TeamSum:
    def __init__(self, me, part, near, acc, mid, far, send, recv, via=("xz", "zx")):
        self.me, self.part, self.near, self.acc, self.mid, self.far = me, part, near, acc, mid, far
        self.recv, self.via = recv, via
        self.copies = Copies(send)

    def start(self):
        b, l, c = self.me["b"], self.me["l"], self.me["c"]
        self.spots = [(b, l), (1 - b, l), (b, 1 - l), (1 - b, 1 - l)]
        for i in (3, 1, 2, 0):
            bb, ll = self.spots[i]
            self.copies.go(
                self.part(rank_of(bb, ll, 1 - c)), self.near.at[i], self.recv.at[i], {"c": 1 - c}
            )

    def tiles(self, rows, body):
        step = max(16, 65536 // self.near.shape[2])

        @pl.loop(0, rows // step)
        def _(t):
            body(pl.ds(pl.multiple_of(t * step, step), step))

    def pair(self, i, write):
        bb, ll = self.spots[i]
        landed(self.near.at[i], self.recv.at[i])
        mine = self.part(rank_of(bb, ll, self.me["c"]))
        self.tiles(
            self.near.shape[1], lambda at: write(at, mine[at].astype(F32) + self.near[i, at].astype(F32))
        )

    def finish(self, write):
        b, l = self.me["b"], self.me["l"]
        tx, tz = {"b": 1 - b}, {"l": 1 - l}
        acc, mid, far, recv, go = self.acc, self.mid, self.far, self.recv, self.copies.go
        n = mid.shape[1]
        hops = [
            (tx, 0, tz, 1) if self.via[half] == "xz" else (tz, 1, tx, 0) for half in range(2)
        ]
        for i in (3, 1, 2):

            def put(at, v):
                acc[i - 1, at] = v.astype(BF)

            self.pair(i, put)
            for half, (one, direct, _, _) in enumerate(hops):
                if i == 3:
                    go(upper(acc.at[2], half), mid.at[half], recv.at[4 + half], one)
                elif i - 1 == direct:
                    go(
                        upper(acc.at[direct], half),
                        upper(far.at[direct], half),
                        recv.at[6 + half],
                        one,
                    )
        for half, (_, _, two, other) in enumerate(hops):
            landed(mid.at[half], recv.at[4 + half])
            into, came = upper(acc.at[other], half), mid.at[half]

            def add(at):
                into[at] = (into[at].astype(F32) + came[at].astype(F32)).astype(BF)

            self.tiles(n, add)
            go(into, upper(far.at[other], half), recv.at[8 + half], two)
        for half, (_, direct, _, other) in enumerate(hops):
            landed(upper(far.at[direct], half), recv.at[6 + half])
            landed(upper(far.at[other], half), recv.at[8 + half])

        def last(at, v):
            write(at, v + far[0, at].astype(F32) + far[1, at].astype(F32))

        self.pair(0, last)
        self.copies.drain()

    @staticmethod
    def scratch(R, C):
        return [
            pltpu.VMEM((4, R, C), BF),
            pltpu.VMEM((3, R, C), BF),
            pltpu.VMEM((2, R // 2, C), BF),
            pltpu.VMEM((2, R, C), BF),
            DMA((10,)),
            DMA((10,)),
        ]


class TeamsGather:
    def __init__(self, me, H, source, out, send, near, far, team=None):
        self.me, self.H, self.source, self.out = me, H, source, out
        self.near, self.far, self.team = near, far, team
        self.copies = Copies(send)

    @staticmethod
    def sems(H):
        return [DMA((9 + 4 * (H - 1),)), DMA((8,)), DMA((2 * H, 2))]

    def groups(self):
        b = self.me["b"]
        return ((0, b), (1, 1 - b))

    def start(self):
        me = self.me
        a, b, h, l, c = (me[n] for n in ALL)
        for m, to in mates(me):
            p = rank_of(to["b"], to["l"], to["c"])
            mine = rank_of(b, l, c)
            self.copies.go(self.source(p), self.out.at[a, b, h, l * 2 + c], self.near.at[mine], to)

    def spread(self, local=None):
        me = self.me
        a, b, h, l, c = (me[n] for n in ALL)
        if local is not None:
            local.wait()
        for g, bb in self.groups():
            block = self.out.at[a, bb, h]
            src = block
            if self.team is not None:
                src = self.team.at[pl.ds(bb * 4, 4)]
            else:
                for m in range(1 - g, 4):
                    ll, cc = l ^ (m >> 1), c ^ (m & 1)
                    landed(self.out.at[a, bb, h, ll * 2 + cc], self.near.at[rank_of(bb, ll, cc)])
            for dh in range(1, self.H):
                to = lax.rem(h + dh, self.H)
                self.copies.go(src, block, self.far.at[dh, g], {"h": to})
            self.copies.go(src, block, self.far.at[0, g], {"a": 1 - a})

    def forward(self, only=(0, 1)):
        a, h, H = self.me["a"], self.me["h"], self.H
        for g, bb in self.groups():
            if g not in only:
                continue
            for dh in range(1, H):
                block = self.out.at[a, bb, lax.rem(h - dh + H, H)]
                landed(block, self.far.at[dh, g])
                self.copies.go(block, block, self.far.at[H - 1 + dh, g], {"a": 1 - a})

    def finish(self):
        a, h, H = self.me["a"], self.me["h"], self.H
        for g, bb in self.groups():
            landed(self.out.at[1 - a, bb, h], self.far.at[0, g])
            for dh in range(1, H):
                block = self.out.at[1 - a, bb, lax.rem(h - dh + H, H)]
                landed(block, self.far.at[H - 1 + dh, g])
        self.copies.drain()


class Halo:
    def __init__(self, me, H, own, out, send, recv):
        self.me, self.H, self.own, self.out, self.send, self.recv = me, H, own, out, send, recv
        self.last = (me["l"] == 1) & (me["c"] == 1) & (me["h"] < H - 1)

    def each(self):
        me = self.me
        n = self.own.shape[0]
        for p in range(8):
            to = {
                "b": p >> 2,
                "h": jnp.minimum(me["h"] + 1, self.H - 1),
                "l": (p >> 1) & 1,
                "c": p & 1,
            }
            src = self.own.at[pl.ds(n - 16, 16)]
            yield remote(src, self.out.at[me["b"]], self.send.at[p], self.recv.at[me["b"]], to)

    def start(self):
        if self.H == 1:
            return

        @pl.when(self.last)
        def _():
            for copy in self.each():
                copy.start()

    def finish(self):
        if self.H == 1:
            return

        @pl.when(self.me["h"] > 0)
        def _():
            for b in range(2):
                landed(self.out.at[b], self.recv.at[b])

        @pl.when(self.last)
        def _():
            for copy in self.each():
                copy.wait_send()


class Edge:
    def __init__(self, me, H, first, got, send, recv):
        self.me, self.H, self.first, self.got, self.send, self.recv = me, H, first, got, send, recv

    def each(self):
        me = self.me
        mine = rank_of(me["b"], me["l"], me["c"])
        for b in range(2):
            to = {"b": b, "h": jnp.maximum(me["h"] - 1, 0), "l": 1, "c": 1}
            yield remote(self.first.at[b], self.got.at[mine], self.send.at[b], self.recv.at[mine], to)

    def start(self):
        if self.H == 1:
            return

        @pl.when(self.me["h"] > 0)
        def _():
            for copy in self.each():
                copy.start()

    def finish(self, out):
        if self.H == 1:
            return
        me = self.me

        @pl.when((me["l"] == 1) & (me["c"] == 1) & (me["h"] < self.H - 1))
        def _():
            for p in range(8):
                landed(self.got.at[p], self.recv.at[p])
            total = self.got[0, 0:1].astype(F32)
            for p in range(1, 8):
                total = total + self.got[p, 0:1].astype(F32)
            n = out.shape[0]
            out[n - 1 : n] = out[n - 1 : n] + total

        @pl.when(me["h"] > 0)
        def _():
            for copy in self.each():
                copy.wait_send()


class Exchange:
    def __init__(self, me, source, out, send, recv):
        self.me, self.source, self.out, self.recv = me, source, out, recv
        self.copies = Copies(send)

    def start(self):
        mine = rank_of(self.me["b"], self.me["l"], self.me["c"])
        for m, to in mates(self.me):
            p = rank_of(to["b"], to["l"], to["c"])
            self.copies.go(self.source(p), self.out(mine), self.recv.at[mine], to)

    def finish(self):
        for m, to in mates(self.me):
            p = rank_of(to["b"], to["l"], to["c"])
            landed(self.out(p), self.recv.at[p])
        self.copies.drain()


ANY = pl.BlockSpec(memory_space=pl.ANY)
VM = pl.BlockSpec(memory_space=pltpu.VMEM)


def comm_call(body, outs, in_specs, out_specs, scratch, cid):
    return pl.pallas_call(
        body,
        out_shape=outs,
        in_specs=in_specs,
        out_specs=out_specs,
        scratch_shapes=scratch,
        compiler_params=pltpu.CompilerParams(
            collective_id=cid, has_side_effects=True, vmem_limit_bytes=VMEM_BYTES
        ),
    )


def dot_nn(a, b):
    return jnp.dot(a, b, preferred_element_type=F32)


def dot_nt(a, b):
    return lax.dot_general(a, b, (((1,), (1,)), ((), ())), preferred_element_type=F32)


def dot_tn(a, b):
    return lax.dot_general(a, b, (((0,), (0,)), ((), ())), preferred_element_type=F32)


MIX = 32


def rows_at(i, n):
    return pl.ds(pl.multiple_of(i * n, n), n)


class RowsGather:
    def __init__(self, me, H, own, out, send, recv, at=None):
        self.me, self.H, self.own, self.out, self.recv, self.at = me, H, own, out, recv, at
        self.copies = Copies(send)

    @staticmethod
    def sems(H):
        return [DMA((2 * H - 1,)), DMA((2 * H,))]

    def block(self, a, h):
        return self.out.at[a, h] if self.at is None else self.out.at[a, h, self.at]

    def start(self):
        a, h = self.me["a"], self.me["h"]
        block = self.block(a, h)
        for dh in range(1, self.H):
            to = lax.rem(h + dh, self.H)
            self.copies.go(self.own, block, self.recv.at[dh], {"h": to})
        self.copies.go(self.own, block, self.recv.at[0], {"a": 1 - a})

    def forward(self):
        a, h, H = self.me["a"], self.me["h"], self.H
        for dh in range(1, H):
            block = self.block(a, lax.rem(h - dh + H, H))
            landed(block, self.recv.at[dh])
            self.copies.go(block, block, self.recv.at[H - 1 + dh], {"a": 1 - a})

    def finish(self):
        a, h, H = self.me["a"], self.me["h"], self.H
        landed(self.block(1 - a, h), self.recv.at[0])
        for dh in range(1, H):
            landed(self.block(1 - a, lax.rem(h - dh + H, H)), self.recv.at[H - 1 + dh])
        self.copies.drain()


def join_lanes(pieces, width):
    per = 128 // width
    out = []
    for g in range(0, len(pieces), per):
        acc = pieces[g]
        for k in range(1, per):
            acc = acc + pltpu.roll(pieces[g + k], width * k, axis=1)
        out.append(acc)
    return jnp.concatenate(out, axis=1) if len(out) > 1 else out[0]


def norm_rows(v):
    mean = jnp.mean(v, axis=-1, keepdims=True)
    cent = v - mean
    rstd = lax.rsqrt(jnp.mean(cent * cent, axis=-1, keepdims=True) + EPS)
    return cent * rstd, rstd


def mix_rows(read, first, carry, shares, write, tiles, rows):
    per = tiles // 2

    @pl.loop(0, tiles)
    def _(p):
        n = read(p)
        prev = jnp.where(lax.rem(p, per) == 0, first(p // per), carry[...])
        row = lax.broadcasted_iota(jnp.int32, n.shape, 0)
        before = jnp.where(row == 0, prev, pltpu.roll(n, 1, axis=0))
        carry[...] = n[rows - 1 : rows]
        diff = n - before
        for i, s in enumerate(shares):
            write(i, p, (before + s * diff).astype(BF))
        write(None, p, diff.astype(BF))


def opening(lay, vecs, x, up, w, later, w_o, w_cv, early):
    H, A = lay.H, lay.A
    grid = (A, 2, H, 4)
    rows, D = x.shape
    T = 8 * rows
    m = D // 8
    w_row = D // lay.n
    kk = D // (2 * A)
    bring_o = lay.strided
    wo_shape = (A, H, w_o.shape[0], D) if bring_o else w_o.shape

    def body(*refs):
        vecs, x, up, w, later, w_o, w_cv = refs[:7]
        full, mine_v, mixed, diff, rkv, gate, upc, w_out, team, wo, wcv = refs[7:18]
        va, xg, halo, hn, carry, mx, df, wa = refs[18:26]
        vs, vn, vf, xs, xr, hs, hr, us, ur, ws, wn, wf, qs, qr, os_, or_, es, er, ls = refs[26:]
        me = coords()
        a, b, h, l, c = (me[n] for n in ALL)
        mine = rank_of(b, l, c)

        def cols(ref, p):
            return ref.at[:, pl.ds(pl.multiple_of(p * m, m), m)]

        local = [
            pltpu.make_async_copy(w.at[mine], wa.at[a, b, h, l * 2 + c], ls.at[0]),
            pltpu.make_async_copy(vecs, va.at[a, b, h, l * 2 + c], ls.at[1]),
            pltpu.make_async_copy(x, xg.at[rows_at(mine, rows)], ls.at[2]),
            pltpu.make_async_copy(cols(up, mine), upc.at[mine], ls.at[3]),
            pltpu.make_async_copy(later.at[mine], team.at[mine], ls.at[4]),
            pltpu.make_async_copy(w_o, wo.at[a, h] if bring_o else wo, ls.at[5]),
        ]
        if early:
            first = w_cv.at[pl.ds(0, early)]
            local.append(pltpu.make_async_copy(first, wcv.at[a, h], ls.at[6]))
        for copy in local:
            copy.start()
        greet(me, H, True, True)
        gw = TeamsGather(me, H, lambda p: w.at[p], wa, ws, wn, wf)
        gv = TeamsGather(me, H, lambda p: vecs, va, vs, vn, vf)
        gx = TeamGather(me, x, lambda p: xg.at[rows_at(p, rows)], xs, xr, ("zx", "zx"))
        gh = Halo(me, H, x, halo, hs, hr)
        gu = Exchange(me, lambda p: cols(up, p), lambda p: upc.at[p], us, ur)
        gq = Exchange(me, lambda p: later.at[p], lambda p: team.at[p], qs, qr)
        if bring_o:
            go = RowsGather(me, H, w_o, wo, os_, or_)
        gv.start()
        gw.start()
        gv.spread(local[1])
        gv.forward()
        gw.spread(local[0])
        gx.start()
        gv.finish()
        local[2].wait()
        gx.finish()
        gh.start()
        gw.forward((0,))
        gu.start()
        if early:
            ge = RowsGather(me, H, first, wcv, es, er)
            ge.start()
        gh.finish()

        def piece(*at):
            return va[at].astype(F32)

        flat = [
            piece(i, j, k, q) for i in range(A) for j in range(2) for k in range(H) for q in range(4)
        ]
        full[...] = join_lanes(flat, w_row)
        if lay.strided:
            own = [piece(i, b, k, l * 2 + c) for i in range(A) for k in range(H)]
            mine_v[...] = join_lanes(own, w_row)
        else:
            mine_v[...] = full[:, pl.ds(pl.multiple_of(mine * m, m), m)]
        gain, bias = full[0:1], full[1:2]
        for s in range(2):
            row = (norm_rows(halo[s].astype(F32))[0] * gain + bias)[15:16]
            hn[s] = jnp.where(h > 0, row, jnp.zeros_like(row))

        def write(i, p, v):
            if i is None:
                df[rows_at(p, MIX)] = v
            else:
                mx[i, rows_at(p, MIX)] = v

        mix_rows(
            lambda p: norm_rows(xg[rows_at(p, MIX)].astype(F32))[0] * gain + bias,
            lambda s: hn[s],
            carry,
            [full[2 + i : 3 + i] for i in range(4)],
            write,
            T // MIX,
            MIX,
        )
        keep = [
            pltpu.make_async_copy(mx, mixed, ls.at[7]),
            pltpu.make_async_copy(df, diff, ls.at[8]),
        ]
        for copy in keep:
            copy.start()
        gw.forward((1,))
        gq.start()
        if bring_o:
            go.start()
        if early:
            ge.forward()
        gw.finish()
        keep.append(pltpu.make_async_copy(wa, w_out, ls.at[9]))
        keep[-1].start()
        for j in range(4):

            @pl.loop(0, 4)
            def _(t):
                at = rows_at(t, T // 4)
                acc = jnp.zeros((T // 4, m), F32)
                for i in range(A):
                    for k in range(2):
                        lo = (i * 2 + k) * kk
                        wt = wa[i, k, :, :, :, j * m : (j + 1) * m].reshape(kk, m)
                        acc = acc + dot_nn(mx[j, at, lo : lo + kk], wt)
                if j < 3:
                    rkv[j, at] = acc.astype(BF)
                else:
                    gate[at] = acc

        gu.finish()
        gq.finish()
        if bring_o:
            go.forward()
            go.finish()
        if early:
            ge.finish()
        for copy in local[3:] + keep:
            copy.wait()

    gsems = TeamsGather.sems(H)
    return comm_call(
        body,
        (
            jax.ShapeDtypeStruct((16, D), F32),
            jax.ShapeDtypeStruct((16, m), F32),
            jax.ShapeDtypeStruct((4, T, D), BF),
            jax.ShapeDtypeStruct((T, D), BF),
            jax.ShapeDtypeStruct((3, T, m), BF),
            jax.ShapeDtypeStruct((T, m), F32),
            jax.ShapeDtypeStruct((8, rows, m), BF),
            jax.ShapeDtypeStruct((*grid, *w.shape[1:]), BF),
            jax.ShapeDtypeStruct(later.shape, BF),
            jax.ShapeDtypeStruct(wo_shape, BF),
            jax.ShapeDtypeStruct((A, H, max(early, 16), D), BF),
        ),
        [ANY] * 7,
        (VM, VM, ANY, ANY, VM, VM, ANY, ANY, ANY, ANY, ANY),
        [
            pltpu.VMEM((*grid, *vecs.shape), BF),
            pltpu.VMEM((T, D), BF),
            pltpu.VMEM((2, 16, D), BF),
            pltpu.VMEM((2, 1, D), F32),
            pltpu.VMEM((1, D), F32),
            pltpu.VMEM((4, T, D), BF),
            pltpu.VMEM((T, D), BF),
            pltpu.VMEM((*grid, *w.shape[1:]), BF),
            *gsems,
            DMA((14,)),
            DMA((8, 2)),
            DMA((8,)),
            DMA((2,)),
            DMA((7,)),
            DMA((8,)),
            *gsems,
            DMA((7,)),
            DMA((8,)),
            *RowsGather.sems(H),
            *RowsGather.sems(H),
            DMA((10,)),
        ],
        0,
    )(vecs, x, up, w, later, w_o, w_cv)


def block_ones(m):
    row = lax.broadcasted_iota(jnp.int32, (m, m), 0) // HEAD
    col = lax.broadcasted_iota(jnp.int32, (m, m), 1) // HEAD
    return jnp.where(row == col, 1.0, 0.0).astype(F32)


def dot_exact(a, b):
    return jnp.dot(a, b, preferred_element_type=F32, precision=lax.Precision.HIGHEST)


class Decay:
    def __init__(self, lam):
        m = lam.shape[1]
        i = lax.broadcasted_iota(jnp.int32, (CHUNK, m), 0).astype(F32)
        self.i = i
        self.down = jnp.exp(-lam * i)
        self.up = jnp.exp(lam * (i + 1.0))
        self.tail = jnp.exp(-lam * (CHUNK - 1.0 - i))
        self.span = jnp.exp(-lam * CHUNK)


def stacked_heads(v):
    m = v.shape[1]
    lane = lax.broadcasted_iota(jnp.int32, v.shape, 1) // HEAD
    zero = jnp.zeros_like(v)
    return jnp.concatenate([jnp.where(lane == g, v, zero) for g in range(m // HEAD)], axis=0)


def own_heads(v):
    m = v.shape[1]
    lane = lax.broadcasted_iota(jnp.int32, (CHUNK, m), 1) // HEAD
    out = v[:CHUNK]
    for g in range(1, m // HEAD):
        out = jnp.where(lane == g, v[g * CHUNK : (g + 1) * CHUNK], out)
    return out


def triangle(heads, low):
    shape = (heads * CHUNK, CHUNK)
    row = lax.rem(lax.broadcasted_iota(jnp.int32, shape, 0), CHUNK)
    col = lax.broadcasted_iota(jnp.int32, shape, 1)
    return row > col if low else row < col


def squeeze(s0, s1):
    def fold(s):
        out = s[:, :128]
        for g in range(1, s.shape[1] // 128):
            out = out + s[:, g * 128 : (g + 1) * 128]
        return out + pltpu.roll(out, HEAD, axis=1)

    lane = lax.broadcasted_iota(jnp.int32, (s0.shape[0], 128), 1)
    return jnp.where(lane < HEAD, fold(s0), fold(s1))


def widen(p, second, ones):
    lane = lax.broadcasted_iota(jnp.int32, p.shape, 1)
    keep = (lane >= HEAD) if second else (lane < HEAD)
    both = jnp.where(keep, p, pltpu.roll(p, HEAD, axis=1))
    return jnp.concatenate([both] * (ones.shape[1] // 128), axis=1) * ones


class Chain:
    def __init__(self, me, H, ahead, out_box, in_box, send, recv):
        h = me["h"]
        self.h, self.H = h, H
        nxt = jnp.minimum(h + 1, H - 1) if ahead else jnp.maximum(h - 1, 0)
        self.has_next = (h < H - 1) if ahead else (h > 0)
        self.has_prev = (h > 0) if ahead else (h < H - 1)
        self.out_box, self.in_box = out_box, in_box
        self.copy = remote(out_box, in_box, send, recv, {"h": nxt})

    def run(self, state, closing, span_all, ones):
        if self.H == 1:
            return

        @pl.when(self.has_prev)
        def _():
            self.copy.wait_recv()
            p = self.in_box[...]
            for s in range(2):
                state[s] = widen(p, s == 1, ones)

        @pl.when(self.has_next)
        def _():
            self.out_box[...] = squeeze(*(span_all * state[s] + closing[s] for s in range(2)))
            self.copy.start()

    def finish(self):
        if self.H == 1:
            return

        @pl.when(self.has_next)
        def _():
            self.copy.wait_send()


def time_mix(lay, rkv, gate, mv, full, start, x, wo, w_cv, wcv_first, early, team):
    H, A = lay.H, lay.A
    rows, D = x.shape
    T = 8 * rows
    m = D // 8
    heads = m // HEAD
    per = T // 2 // CHUNK
    grid = (A, 2, H, 4)
    rest = w_cv.shape[0] - early

    def body(*refs):
        rkv, gate, mv, full, start, x, wo, w_cv, wcv_first, team = refs[:10]
        gated, ghat, grstd, states, fin, middle, n2, halo, wcv, wf = refs[10:20]
        (adds, st, cl, obox, ibox, own, part) = refs[20:27]
        near, acc, mid, far, ss, sr = refs[27:33]
        cs, cr, vs, vr, ws, wn, wfar, gs, gr, hs, hr, ls = refs[33:]
        me = coords()
        a, b, h, l, c = (me[n] for n in ALL)
        mine = rank_of(b, l, c)
        tail = pl.ds(early, rest)
        local = [
            pltpu.make_async_copy(team.at[pl.ds(0, 4)], wf.at[a, 0, h], ls.at[0]),
            pltpu.make_async_copy(team.at[pl.ds(4, 4)], wf.at[a, 1, h], ls.at[1]),
            pltpu.make_async_copy(w_cv.at[tail], wcv.at[a, h, tail], ls.at[2]),
        ]
        if early:
            head = wcv.at[:, :, pl.ds(0, early)]
            local.append(pltpu.make_async_copy(wcv_first, head, ls.at[3]))
        for copy in local:
            copy.start()
        greet(me, H, True, True)
        gw = TeamsGather(me, H, None, wf, ws, wn, wfar, team)
        gv = RowsGather(me, H, w_cv.at[tail], wcv, vs, vr, tail)
        ones = block_ones(m)
        dec = Decay(mv[6:7])
        u = mv[7:8]
        span_all = jnp.exp(-mv[6:7] * (T // 2))

        def tile(i, s, n):
            return rkv[i, rows_at(s * per + n, CHUNK)].astype(F32)

        cl[...] = jnp.zeros_like(cl)

        @pl.loop(0, per)
        def _(n):
            for s in range(2):
                kt = (tile(1, s, n) * dec.tail).astype(BF)
                v = rkv[2, rows_at(s * per + n, CHUNK)]
                add = dot_tn(v, kt) * ones
                adds[s, n] = add
                cl[s] = dec.span * cl[s] + add

        for s in range(2):
            st[s] = jnp.where(h > 0, jnp.zeros_like(start[s]), start[s])
        chain = Chain(me, H, True, obox, ibox, cs, cr)
        chain.run(st, cl, span_all, ones)
        gw.spread()
        low = triangle(heads, True)

        @pl.loop(0, per)
        def _(n):
            for s in range(2):
                at = rows_at(s * per + n, CHUNK)
                r, k, v = (tile(i, s, n) for i in range(3))
                vb = rkv[2, at]
                rd = (r * dec.down).astype(BF)
                kg = (k * dec.up).astype(BF)
                state = st[s]
                states[s, n] = state
                att = jnp.where(low, dot_nt(stacked_heads(rd), kg), 0.0).astype(BF)
                y = own_heads(dot_nn(att, vb)) + dot_nt(rd, state.astype(BF))
                y = y + dot_exact(r * u * k, ones) * v
                st[s] = dec.span * state + adds[s, n]
                mean = dot_exact(y, ones) * (1.0 / HEAD)
                cent = y - mean
                rstd = lax.rsqrt(dot_exact(cent * cent, ones) * (1.0 / HEAD) + GROUP_EPS)
                hat = cent * rstd
                ghat[at] = hat
                grstd[at] = rstd
                g = gate[at]
                silu = g / (1.0 + jnp.exp(-g))
                gated[at] = ((hat * mv[8:9] + mv[9:10]) * silu).astype(BF)

        for s in range(2):
            fin[s] = st[s]
        chain.finish()

        @pl.loop(0, 8)
        def _(p):
            g = gated[rows_at(p, rows)]
            w = wo[...].reshape(m, D)
            for q in range(4):
                lo = q * (D // 4)
                part[p, :, lo : lo + D // 4] = dot_nn(g, w[:, lo : lo + D // 4]).astype(BF)

        sums = TeamSum(me, lambda p: part.at[p], near, acc, mid, far, ss, sr, ("xz", "xz"))
        sums.start()

        def put(at, v):
            v = x[at].astype(F32) + v
            middle[at] = v
            own[at] = (norm_rows(v)[0] * full[10:11] + full[11:12]).astype(BF)

        sums.finish(put)
        keep = pltpu.make_async_copy(own, n2.at[mine], ls.at[4])
        keep.start()
        gx = TeamGather(me, own, lambda p: n2.at[p], gs, gr, ("zx", "zx"))
        gx.start()
        gh = Halo(me, H, own, halo, hs, hr)
        gh.start()
        gv.start()
        gw.forward((0,))
        gx.finish()
        gh.finish()
        keep.wait()
        gw.forward((1,))
        gv.forward()
        gw.finish()
        gv.finish()
        for copy in local:
            copy.wait()

    return comm_call(
        body,
        (
            jax.ShapeDtypeStruct((T, m), BF),
            jax.ShapeDtypeStruct((T, m), F32),
            jax.ShapeDtypeStruct((T, m), F32),
            jax.ShapeDtypeStruct((2, per, m, m), F32),
            jax.ShapeDtypeStruct((2, m, m), F32),
            jax.ShapeDtypeStruct((rows, D), F32),
            jax.ShapeDtypeStruct((8, rows, D), BF),
            jax.ShapeDtypeStruct((2, 16, D), BF),
            jax.ShapeDtypeStruct((A, H, *w_cv.shape), BF),
            jax.ShapeDtypeStruct((*grid, *team.shape[1:]), BF),
        ),
        [VM, VM, VM, VM, VM, VM, VM, ANY, ANY, ANY],
        (VM, VM, VM, VM, VM, VM, ANY, ANY, ANY, ANY),
        [
            pltpu.VMEM((2, per, m, m), F32),
            pltpu.VMEM((2, m, m), F32),
            pltpu.VMEM((2, m, m), F32),
            pltpu.VMEM((m, 128), F32),
            pltpu.VMEM((m, 128), F32),
            pltpu.VMEM((rows, D), BF),
            pltpu.VMEM((8, rows, D), BF),
            *TeamSum.scratch(rows, D),
            DMA,
            DMA,
            *RowsGather.sems(H),
            *TeamsGather.sems(H),
            DMA((14,)),
            DMA((8, 2)),
            DMA((8,)),
            DMA((2,)),
            DMA((5,)),
        ],
        1,
    )(rkv, gate, mv, full, start, x, wo, w_cv, wcv_first, team)


def time_mix_back(lay, d_br, wo, gated, ghat, grstd, gate, rkv, states, mv, items):
    H, A = lay.H, lay.A
    T, m = gate.shape
    D = d_br.shape[-1]
    heads = m // HEAD
    per = T // 2 // CHUNK

    bg = Background(items, H)
    nb = len(items)

    def body(*refs):
        d_br, wo, gated, ghat, grstd, gate, rkv, states, mv = refs[:9]
        srcs, refs = refs[9 : 9 + nb], refs[9 + nb :]
        g_o, d_all, sums = refs[:3]
        dsts, refs = refs[3 : 3 + nb], refs[3 + nb :]
        dy, adds, cl, st, obox, ibox, cs, cr = refs[:8]
        me = coords()
        h = me["h"]
        greet(me, H, True, True)
        ones = block_ones(m)
        dec = Decay(mv[6:7])
        u = mv[7:8]
        span_all = jnp.exp(-mv[6:7] * (T // 2))
        lowT = triangle(heads, False)
        low = triangle(heads, True)
        sums[...] = jnp.zeros_like(sums)

        @pl.loop(0, 2 * per)
        def _(t):
            at = rows_at(t, CHUNK)
            d_gated = dot_nt(d_br[t], wo[...].reshape(m, D))
            g = gate[at]
            sig = 1.0 / (1.0 + jnp.exp(-g))
            hat, rstd = ghat[at], grstd[at]
            dn = d_gated * (g * sig)
            sums[2:3] += jnp.sum(dn * hat, axis=0, keepdims=True)
            sums[3:4] += jnp.sum(dn, axis=0, keepdims=True)
            n = hat * mv[8:9] + mv[9:10]
            d_all[at, 3 * m :] = (d_gated * n * sig * (1.0 + g * (1.0 - sig))).astype(BF)
            e = dn * mv[8:9]
            m1 = dot_exact(e, ones) * (1.0 / HEAD)
            m2 = dot_exact(e * hat, ones) * (1.0 / HEAD)
            dy[at] = (e - m1 - hat * m2) * rstd

        cl[...] = jnp.zeros_like(cl)

        @pl.loop(0, per)
        def _(q):
            n = per - 1 - q
            for s in range(2):
                at = rows_at(s * per + n, CHUNK)
                rd = (rkv[0, at].astype(F32) * dec.down).astype(BF)
                add = dot_tn(dy[at].astype(BF), rd) * ones
                adds[s, n] = add
                cl[s] = dec.span * cl[s] + add

        st[...] = jnp.zeros_like(st)
        chain = Chain(me, H, False, obox, ibox, cs, cr)
        chain.run(st, cl, span_all, ones)
        bg.start(me, srcs, dsts, refs[8:])

        @pl.loop(0, per)
        def _(q):
            n = per - 1 - q
            for s in range(2):
                at = rows_at(s * per + n, CHUNK)
                r, k, v = (rkv[i, at].astype(F32) for i in range(3))
                vb = rkv[2, at]
                rd, kg, kt = r * dec.down, k * dec.up, k * dec.tail
                rdb, kgb, ktb = rd.astype(BF), kg.astype(BF), kt.astype(BF)
                dyt = dy[at]
                dyb = dyt.astype(BF)
                state, end = states[s, n], st[s]
                endb = end.astype(BF)
                datt = jnp.where(low, dot_nt(stacked_heads(dyb), vb), 0.0).astype(BF)
                dattT = jnp.where(lowT, dot_nt(stacked_heads(vb), dyb), 0.0).astype(BF)
                attT = jnp.where(lowT, dot_nt(stacked_heads(kgb), rdb), 0.0).astype(BF)
                ddiag = dot_exact(dyt * v, ones)
                diag = dot_exact(r * u * k, ones)
                d_rd = own_heads(dot_nn(datt, kgb)) + dot_nn(dyb, state.astype(BF))
                d_kg = own_heads(dot_nn(dattT, rdb))
                d_kt = dot_nn(vb, endb)
                d_v = own_heads(dot_nn(attT, dyb)) + diag * dyt + dot_nt(ktb, endb)
                d_r = d_rd * dec.down + ddiag * u * k
                d_k = d_kg * dec.up + d_kt * dec.tail + ddiag * u * r
                d_all[at, :m] = d_r.astype(BF)
                d_all[at, m : 2 * m] = d_k.astype(BF)
                d_all[at, 2 * m : 3 * m] = d_v.astype(BF)
                sums[1:2] += jnp.sum(ddiag * r * k, axis=0, keepdims=True)
                d_l = jnp.sum(
                    (dec.i + 1.0) * kg * d_kg
                    - dec.i * rd * d_rd
                    - (CHUNK - 1.0 - dec.i) * kt * d_kt,
                    axis=0,
                    keepdims=True,
                )
                d_l = d_l - CHUNK * dec.span * jnp.sum(state * end, axis=0, keepdims=True)
                sums[0:1] += d_l
                st[s] = dec.span * end + adds[s, n]

        nw = D // 4
        for q in range(4):
            w = jnp.concatenate([d_br[p, :, q * nw : (q + 1) * nw] for p in range(8)], axis=0)
            g = dot_tn(gated[...], w).astype(BF)
            g_o[:, :, :, q * nw : (q + 1) * nw] = g.reshape(*g_o.shape[:3], nw)
        chain.finish()
        bg.finish()

    out = comm_call(
        body,
        (
            jax.ShapeDtypeStruct(wo.shape, BF),
            jax.ShapeDtypeStruct((T, 4 * m), BF),
            jax.ShapeDtypeStruct((8, m), F32),
            *bg.outs(),
        ),
        [VM] * 9 + [ANY] * nb,
        (VM, VM, VM, *[ANY] * nb),
        [
            pltpu.VMEM((T, m), F32),
            pltpu.VMEM((2, per, m, m), F32),
            pltpu.VMEM((2, m, m), F32),
            pltpu.VMEM((2, m, m), F32),
            pltpu.VMEM((m, 128), F32),
            pltpu.VMEM((m, 128), F32),
            DMA,
            DMA,
            *bg.sems(),
        ],
        5,
    )(d_br, wo, gated, ghat, grstd, gate, rkv, states, mv, *bg.arrays())
    return out[0], out[1], out[2], out[3:]


class Background:
    def __init__(self, items, H):
        self.items, self.H = items, H

    def arrays(self):
        return [v for v, _ in self.items]

    def outs(self):
        shapes = []
        for v, kind in self.items:
            lead = {"h": (max(self.H - 1, 1),), "a": (), "t": (8,)}[kind]
            shapes.append(jax.ShapeDtypeStruct((*lead, *v.shape[1:]), BF))
        return shapes

    def sems(self):
        out = []
        for _, kind in self.items:
            n = {"h": max(self.H - 1, 1), "a": 1, "t": 8}[kind]
            out += [DMA((n,)), DMA((n,))] + ([DMA] if kind == "t" else [])
        return out

    def start(self, me, srcs, dsts, sems):
        self.open = []
        sems = list(sems)
        h, H = me["h"], self.H
        mine = rank_of(me["b"], me["l"], me["c"])
        for (_, kind), src, dst in zip(self.items, srcs, dsts):
            ss, sr = sems.pop(0), sems.pop(0)
            copies = Copies(ss)
            if kind == "h":
                for dh in range(1, H):
                    to = lax.rem(h + dh, H)
                    copies.go(src.at[to], dst.at[dh - 1], sr.at[dh - 1], {"h": to})
                    self.open.append((dst.at[dh - 1], sr.at[dh - 1]))
            elif kind == "a":
                copies.go(src.at[1 - me["a"]], dst, sr.at[0], {"a": 1 - me["a"]})
                self.open.append((dst, sr.at[0]))
            else:
                keep = pltpu.make_async_copy(src.at[mine], dst.at[mine], sems.pop(0))
                keep.start()
                self.open.append(keep)
                for m, to in mates(me):
                    p = rank_of(to["b"], to["l"], to["c"])
                    copies.go(src.at[p], dst.at[mine], sr.at[mine], to)
                    self.open.append((dst.at[p], sr.at[p]))
            self.open.append(copies)

    def finish(self):
        for item in self.open:
            if isinstance(item, tuple):
                landed(*item)
            elif isinstance(item, Copies):
                item.drain()
            else:
                item.wait()


def back_rows(T, tile, chunk, shares, diff, part, first, sums):
    per = T // 2 // tile

    def step(q, carry):
        t = 2 * per - 1 - q
        ds = chunk(t)
        dif = diff(t)
        late = jnp.zeros_like(ds[0])
        here = jnp.zeros_like(ds[0])
        for i, (d, s) in enumerate(zip(ds, shares)):
            sums[i][...] = sums[i][...] + jnp.sum(d * dif, axis=0, keepdims=True)
            late = late + (1.0 - s) * d
            here = here + s * d
        carry = jnp.where(lax.rem(t, per) == per - 1, jnp.zeros_like(carry), carry)
        row = lax.broadcasted_iota(jnp.int32, late.shape, 0)
        part(t, here + jnp.where(row == tile - 1, carry, pltpu.roll(late, tile - 1, axis=0)))

        @pl.when(lax.rem(t, per) == 0)
        def _():
            first(t // per, late[:16].astype(BF))

        return late[:1]

    zero = jnp.zeros((1, diff(0).shape[1]), F32)
    lax.fori_loop(0, 2 * per, step, zero)


def channel_mix(lay, n2, halo, full, wcv, wf, upc, middle, up):
    H, A = lay.H, lay.A
    rows, D = middle.shape
    T = 8 * rows
    F, m = wcv.shape[0], D // 8
    nk, kk, _ = wf.shape
    w_cv = F // (A * H)
    tile = T // 4
    dq = D // 4

    def body(n2, halo, full, wcv, wf, upc, middle, up, *rest):
        d_mid, d_br, moved, s_cv, got_cv, g_f, got_f, sums = rest[:8]
        (big, m2, df, carry, relu, act, sg, d_pg, d_val, dval, gcv, cvbuf, stage) = rest[8:21]
        (dn2, own, add, first, edge) = rest[21:26]
        cn, ca, cm, cf, c_s, c_r = rest[26:32]
        rn, ra, rm, rf, r_s, r_r = rest[32:38]
        ds, dr, bs, br, es, er, ms, mr, vs, vr, fs, fr, ls = rest[38:]
        d_pre = act
        me = coords()
        a, b, h, l, c = (me[n] for n in ALL)
        mine = rank_of(b, l, c)
        loads = [
            pltpu.make_async_copy(n2.at[p], big.at[pl.ds(p * rows, rows)], ls.at[p]) for p in range(8)
        ]
        for copy in loads:
            copy.start()
        greet(me, H, True, True)
        for copy in loads:
            copy.wait()

        def write(i, p, v):
            if i is None:
                df[rows_at(p, MIX)] = v
            else:
                m2[i, rows_at(p, MIX)] = v

        def before(s):
            row = halo[s].astype(F32)[15:16]
            return jnp.where(h > 0, row, jnp.zeros_like(row))

        s_ck, s_cr = full[12:13], full[13:14]
        mix_rows(
            lambda p: big[rows_at(p, MIX)].astype(F32),
            before,
            carry,
            [s_ck, s_cr],
            write,
            T // MIX,
            MIX,
        )

        @pl.loop(0, 4)
        def _(t):
            at = rows_at(t, tile)
            acc = jnp.zeros((tile, F), F32)
            for i in range(nk):
                acc = acc + dot_nn(m2[0, at, i * kk : (i + 1) * kk], wf[i, :, :F])
            pos = jnp.maximum(acc, 0.0)
            relu[at] = pos.astype(BF)
            act[at] = (pos * pos).astype(BF)

        @pl.loop(0, 4)
        def _(t):
            at = rows_at(t, tile)
            for q in range(4):
                lo = q * dq
                big[at, lo : lo + dq] = dot_nn(act[at], wcv[:, lo : lo + dq]).astype(BF)

        def cols(ref):
            return lambda p: ref.at[:, pl.ds(pl.multiple_of(p * m, m), m)]

        total = TeamSum(me, cols(big), cn, ca, cm, cf, c_s, c_r)
        total.start()

        @pl.loop(0, 4)
        def _(t):
            at = rows_at(t, tile)
            acc = jnp.zeros((tile, m), F32)
            for i in range(nk):
                acc = acc + dot_nn(m2[1, at, i * kk : (i + 1) * kk], wf[i, :, F:])
            sg[at] = 1.0 / (1.0 + jnp.exp(-acc))

        def gate_back(at, val):
            sig = sg[at]
            upv = upc[at].astype(F32)
            d_val[at] = (sig * upv).astype(BF)
            d_pg[at] = (upv * val * sig * (1.0 - sig)).astype(BF)
            add[at] = (sig * val).astype(BF)

        total.finish(gate_back)
        keep_val = pltpu.make_async_copy(d_val, cols(dval)(mine), ls.at[8])
        keep_val.start()
        gv = TeamGather(me, d_val, cols(dval), ds, dr)
        gv.start()
        gv.finish()
        keep_val.wait()

        @pl.loop(0, 8)
        def _(q):
            at = pl.ds(pl.multiple_of(q * m, m), m)
            g = dot_tn(act[...], dval[:, at])
            for i in range(A):
                for j in range(H):
                    lo = (i * H + j) * w_cv
                    gcv[i, j, :, at] = g[lo : lo + w_cv].astype(BF)

        cv = Copies(vs)
        cv.go(gcv.at[1 - a], cvbuf, vr.at[0], {"a": 1 - a})

        @pl.loop(0, 4)
        def _(t):
            at = rows_at(t, tile)
            d_pre[at] = (dot_nt(dval[at], wcv[...]) * 2.0 * relu[at].astype(F32)).astype(BF)

        ff = Copies(fs)
        sums[...] = jnp.zeros_like(sums)

        def chunk_of(i):
            lo = i * kk

            def chunk(t):
                at = rows_at(t, tile)
                return (dot_nt(d_pre[at], wf[i, :, :F]), dot_nt(d_pg[at], wf[i, :, F:]))

            def put(t, v):
                big[rows_at(t, tile), lo : lo + kk] = v.astype(BF)

            def put_first(s, v):
                first[s, :, lo : lo + kk] = v

            back_rows(
                T,
                tile,
                chunk,
                (s_ck[:, lo : lo + kk], s_cr[:, lo : lo + kk]),
                lambda t: df[rows_at(t, tile), lo : lo + kk].astype(F32),
                put,
                put_first,
                [sums.at[k : k + 1, lo : lo + kk] for k in range(2)],
            )

        def grads(i):
            lo = i * kk
            for k in range(2):
                at = slice(lo + k * kk // 2, lo + (k + 1) * kk // 2)
                to = slice(k * kk // 2, (k + 1) * kk // 2)
                stage[to, :F] = dot_tn(m2[0, :, at], d_pre[...]).astype(BF)
                stage[to, F:] = dot_tn(m2[1, :, at], d_pg[...]).astype(BF)
            copy = pltpu.make_async_copy(stage, g_f.at[i // 2, i % 2], ls.at[9])
            copy.start()
            return copy

        for i in range(nk):
            copy = grads(i)
            chunk_of(i)
            copy.wait()
        ff.go(g_f.at[1 - a], got_f, fr.at[0], {"a": 1 - a})
        total = TeamSum(me, lambda p: big.at[pl.ds(pl.multiple_of(p * rows, rows), rows)], rn, ra, rm, rf, r_s, r_r)
        total.start()
        e = Edge(me, H, first, edge, es, er)
        e.start()

        def put_dn(at, v):
            dn2[at] = v

        total.finish(put_dn)
        e.finish(dn2)

        @pl.loop(0, rows // MIX)
        def _(t):
            at = rows_at(t, MIX)
            d = dn2[at]
            hat, rstd = norm_rows(middle[at])
            sums[2:3] = sums[2:3] + jnp.sum(d * hat, axis=0, keepdims=True)
            sums[3:4] = sums[3:4] + jnp.sum(d, axis=0, keepdims=True)
            dm = up[at].astype(F32) + norm_back(d * full[10:11], hat, rstd)
            d_mid[at] = dm
            own[at] = dm.astype(BF)

        keep = [
            pltpu.make_async_copy(own, d_br.at[mine], ls.at[10]),
            pltpu.make_async_copy(add.at[rows_at(mine, rows)], moved.at[mine], ls.at[11]),
        ]
        for copy in keep:
            copy.start()
        gx = TeamGather(me, own, lambda p: d_br.at[p], bs, br)
        gx.start()
        landed(cvbuf, vr.at[0])

        @pl.loop(0, H)
        def _(j):
            gcv[a, j] = (gcv[a, j].astype(F32) + cvbuf[j].astype(F32)).astype(BF)

        for dh in range(1, H):
            to = lax.rem(h + dh, H)
            cv.go(gcv.at[a, to], got_cv.at[dh - 1], vr.at[dh], {"h": to})
        keep.append(pltpu.make_async_copy(gcv.at[a, h], s_cv, ls.at[12]))
        keep[-1].start()
        gx.finish()
        gm = Exchange(me, lambda p: add.at[rows_at(p, rows)], lambda p: moved.at[p], ms, mr)
        gm.start()
        gm.finish()
        landed(got_f, fr.at[0])
        ff.drain()
        for dh in range(1, H):
            landed(got_cv.at[dh - 1], vr.at[dh])
        cv.drain()
        for copy in keep:
            copy.wait()

    return comm_call(
        body,
        (
            jax.ShapeDtypeStruct((rows, D), F32),
            jax.ShapeDtypeStruct((8, rows, D), BF),
            jax.ShapeDtypeStruct((8, rows, m), BF),
            jax.ShapeDtypeStruct((w_cv, D), BF),
            jax.ShapeDtypeStruct((max(H - 1, 1), w_cv, D), BF),
            jax.ShapeDtypeStruct((A, nk // A, kk, F + m), BF),
            jax.ShapeDtypeStruct((nk // A, kk, F + m), BF),
            jax.ShapeDtypeStruct((8, D), F32),
        ),
        [ANY, VM, VM, VM, VM, VM, VM, VM],
        (VM, ANY, ANY, ANY, ANY, ANY, ANY, VM),
        [
            pltpu.VMEM((T, D), BF),
            pltpu.VMEM((2, T, D), BF),
            pltpu.VMEM((T, D), BF),
            pltpu.VMEM((1, D), F32),
            pltpu.VMEM((T, F), BF),
            pltpu.VMEM((T, F), BF),
            pltpu.VMEM((T, m), F32),
            pltpu.VMEM((T, m), BF),
            pltpu.VMEM((T, m), BF),
            pltpu.VMEM((T, D), BF),
            pltpu.VMEM((A, H, w_cv, D), BF),
            pltpu.VMEM((H, w_cv, D), BF),
            pltpu.VMEM((kk, F + m), BF),
            pltpu.VMEM((rows, D), F32),
            pltpu.VMEM((rows, D), BF),
            pltpu.VMEM((T, m), BF),
            pltpu.VMEM((2, 16, D), BF),
            pltpu.VMEM((8, 16, D), BF),
            *TeamSum.scratch(T, m),
            *TeamSum.scratch(rows, D),
            DMA((14,)),
            DMA((8, 2)),
            DMA((14,)),
            DMA((8, 2)),
            DMA((2,)),
            DMA((8,)),
            DMA((7,)),
            DMA((8,)),
            DMA((H,)),
            DMA((H,)),
            DMA((1,)),
            DMA((1,)),
            DMA((13,)),
        ],
        2,
    )(n2, halo, full, wcv, wf, upc, middle, up)


def time_in_back(lay, d_all, mixed, diff, w4, full, x, d_mid, items):
    H, A = lay.H, lay.A
    rows, D = x.shape
    T = 8 * rows
    m = D // 8
    nk, kk, _ = w4.shape
    tile = T // 4
    hk = kk // H
    bg = Background(items, H)
    nb = len(items)

    def body(*refs):
        refs = list(refs)
        d_all, mixed, diff, w4, full, x, d_mid = refs[:7]
        srcs, refs = refs[7 : 7 + nb], refs[7 + nb :]
        in_grad, g_out, sums = refs[:3]
        dsts, refs = refs[3 : 3 + nb], refs[3 + nb :]
        part, g4, got, late, dn1, first, edge = refs[:7]
        rn, ra, rm, rf, r_s, r_r = refs[7:13]
        es, er, gs, gr = refs[13:17]
        me = coords()
        a, h = me["a"], me["h"]
        greet(me, H, True, True)
        bg.start(me, srcs, dsts, refs[17:])
        sums[...] = jnp.zeros_like(sums)
        cg = Copies(gs)

        for step in range(A):
            i = lax.rem(a + 1 + step, A)
            for k in range(2):
                lo = pl.ds(pl.multiple_of((i * 2 + k) * kk, kk), kk)
                for j in range(4):
                    g = dot_tn(mixed[j, :, lo], d_all[:, j * m : (j + 1) * m])
                    g4[i * 2 + k, :, j * m : (j + 1) * m] = g.astype(BF)
                if step < A - 1:
                    cg.go(g4.at[i * 2 + k], got.at[k], gr.at[k], {"a": 1 - a})

        def chunk_of(i):
            lo = i * kk

            def chunk(t):
                at = rows_at(t, tile)
                return tuple(
                    dot_nt(d_all[at, j * m : (j + 1) * m], w4[i, :, j * m : (j + 1) * m])
                    for j in range(4)
                )

            def put(t, v):
                part[rows_at(t, tile), lo : lo + kk] = v.astype(BF)

            def put_first(s, v):
                first[s, :, lo : lo + kk] = v

            back_rows(
                T,
                tile,
                chunk,
                tuple(full[2 + j : 3 + j, lo : lo + kk] for j in range(4)),
                lambda t: diff[rows_at(t, tile), lo : lo + kk].astype(F32),
                put,
                put_first,
                [sums.at[j : j + 1, lo : lo + kk] for j in range(4)],
            )

        for i in range(nk):
            chunk_of(i)
        total = TeamSum(me, lambda p: part.at[pl.ds(pl.multiple_of(p * rows, rows), rows)], rn, ra, rm, rf, r_s, r_r)
        total.start()
        e = Edge(me, H, first, edge, es, er)
        e.start()
        for k in range(2):
            landed(got.at[k], gr.at[k])
            g4[a * 2 + k] = (g4[a * 2 + k].astype(F32) + got[k].astype(F32)).astype(BF)
            for dh in range(1, H):
                to = lax.rem(h + dh, H)
                n = (dh - 1) * 2 + k
                cg.go(
                    g4.at[a * 2 + k, pl.ds(pl.multiple_of(to * hk, hk), hk)],
                    late.at[dh - 1, k],
                    gr.at[2 + n],
                    {"h": to},
                )

        def put_dn(at, v):
            dn1[at] = v

        total.finish(put_dn)
        e.finish(dn1)

        @pl.loop(0, rows // MIX)
        def _(t):
            at = rows_at(t, MIX)
            d = dn1[at]
            hat, rstd = norm_rows(x[at].astype(F32))
            sums[4:5] = sums[4:5] + jnp.sum(d * hat, axis=0, keepdims=True)
            sums[5:6] = sums[5:6] + jnp.sum(d, axis=0, keepdims=True)
            in_grad[at] = d_mid[at] + norm_back(d * full[0:1], hat, rstd)

        for k in range(2):
            g = g4[a * 2 + k, pl.ds(pl.multiple_of(h * hk, hk), hk)].astype(F32)
            for dh in range(1, H):
                landed(late.at[dh - 1, k], gr.at[2 + (dh - 1) * 2 + k])
                g = g + late[dh - 1, k].astype(F32)
            g_out[k] = g.astype(BF)
        cg.drain()
        bg.finish()

    out = comm_call(
        body,
        (
            jax.ShapeDtypeStruct((rows, D), F32),
            jax.ShapeDtypeStruct((2, hk, 4 * m), BF),
            jax.ShapeDtypeStruct((8, D), F32),
            *bg.outs(),
        ),
        [VM] * 7 + [ANY] * nb,
        (VM, VM, VM, *[ANY] * nb),
        [
            pltpu.VMEM((T, D), BF),
            pltpu.VMEM((nk, kk, 4 * m), BF),
            pltpu.VMEM((2, kk, 4 * m), BF),
            pltpu.VMEM((max(H - 1, 1), 2, hk, 4 * m), BF),
            pltpu.VMEM((rows, D), F32),
            pltpu.VMEM((2, 16, D), BF),
            pltpu.VMEM((8, 16, D), BF),
            *TeamSum.scratch(rows, D),
            DMA((2,)),
            DMA((8,)),
            DMA((2 + 2 * max(H - 1, 1),)),
            DMA((2 + 2 * max(H - 1, 1),)),
            *bg.sems(),
        ],
        6,
    )(d_all, mixed, diff, w4, full, x, d_mid, *bg.arrays())
    return out[0], out[1], out[2], out[3:]


def closing(lay, small, items):
    H, A, n = lay.H, lay.A, lay.n
    bg = Background(items, H)
    nb = len(items)

    def body(*refs):
        small, srcs, refs = refs[0], refs[1 : 1 + nb], refs[1 + nb :]
        total, dsts, refs = refs[0], refs[1 : 1 + nb], refs[1 + nb :]
        got, ss, sr = refs[:3]
        me = coords()
        a, b, h, l, c = (me[k] for k in ALL)
        sem = pltpu.get_barrier_semaphore()
        others = []
        for i in range(1, n):
            k = i
            dc, k = k % 2, k // 2
            dl, k = k % 2, k // 2
            dh, k = k % H, k // H
            db, da = k % 2, k // 2
            to = {
                "a": lax.rem(a + da, A),
                "b": b ^ db,
                "h": lax.rem(h + dh, H),
                "l": l ^ dl,
                "c": c ^ dc,
            }
            others.append((i, to))
            pl.semaphore_signal(sem, inc=1, device_id=to, device_id_type=MESH)
        pl.semaphore_wait(sem, n - 1)
        bg.start(me, srcs, dsts, refs[3:])
        copies = Copies(ss)

        def at(d):
            return (((d["a"] * 2 + d["b"]) * H + d["h"]) * 2 + d["l"]) * 2 + d["c"]

        for i, to in others:
            copies.go(small.at[at(to)], got.at[i], sr.at[i], to)
        acc = small[at(me)]
        for i, _ in others:
            landed(got.at[i], sr.at[i])
            acc = acc + got[i]
        total[...] = acc
        copies.drain()
        bg.finish()

    out = comm_call(
        body,
        (jax.ShapeDtypeStruct(small.shape[1:], F32), *bg.outs()),
        [VM] + [ANY] * nb,
        (VM, *[ANY] * nb),
        [pltpu.VMEM(small.shape, F32), DMA((n,)), DMA((n,)), *bg.sems()],
        7,
    )(small, *bg.arrays())
    return out[0], out[1:]


def dot(a, b, dims):
    return lax.dot_general(a, b, (dims, ((), ())), preferred_element_type=F32)


def mm(a, b):
    return dot(a, b, ((1,), (0,)))


def mm_nt(a, b):
    return dot(a, b, ((1,), (1,)))


def mm_tn(a, b):
    return dot(a, b, ((0,), (0,)))


class Layout:
    def __init__(self, mesh_shape):
        self.A, self.B, self.H, self.L, self.C = mesh_shape
        self.team = self.B * self.L * self.C
        self.n = self.team * self.A * self.H

    def of(self, D):
        self.strided = (D // self.n) % HEAD == 0
        return self

    def spread(self, v, whole):
        w = v.shape[-1] // self.n
        lead = v.shape[:-1]
        if w % whole:
            return v.reshape(*lead, self.team, -1)
        k = len(lead)
        v = v.reshape(*lead, self.A, self.B, self.H, self.L, self.C, w)
        v = v.transpose(*range(k), k + 1, k + 3, k + 4, k, k + 2, k + 5)
        return v.reshape(*lead, self.team, -1)

    def unspread(self, v, whole):
        lead = v.shape[:-2]
        w = v.shape[-1] * self.team // self.n
        if w % whole:
            return v.reshape(*lead, -1)
        k = len(lead)
        v = v.reshape(*lead, self.B, self.L, self.C, self.A, self.H, w)
        v = v.transpose(*range(k), k + 3, k, k + 4, k + 1, k + 2, k + 5)
        return v.reshape(*lead, -1)

    def rows_in(self, g):
        m = g.shape[-1]
        g = g.reshape(self.A, self.H, self.B, self.L, self.C, -1, m)
        return g.transpose(0, 2, 1, 3, 4, 5, 6).reshape(-1, m)

    def rows_out(self, g):
        m = g.shape[-1]
        g = g.reshape(self.A, self.B, self.H, self.L, self.C, -1, m)
        return g.transpose(0, 2, 1, 3, 4, 5, 6).reshape(self.A * self.H, self.team, -1, m)


def normed(v):
    mean = jnp.mean(v, axis=-1, keepdims=True)
    cent = v - mean
    rstd = lax.rsqrt(jnp.mean(cent * cent, axis=-1, keepdims=True) + EPS)
    return cent * rstd, rstd


def norm_back(e, xhat, rstd):
    m1 = jnp.mean(e, axis=-1, keepdims=True)
    m2 = jnp.mean(e * xhat, axis=-1, keepdims=True)
    return (e - m1 - xhat * m2) * rstd


def with_before(rows, halo, segs):
    v = rows.reshape(segs, -1, rows.shape[-1])
    return jnp.concatenate([halo, v[:, :-1]], axis=1).reshape(rows.shape)


def with_after(rows, segs):
    v = rows.reshape(segs, -1, rows.shape[-1])
    return (
        jnp.concatenate([v[:, 1:], jnp.zeros_like(v[:, :1])], axis=1).reshape(rows.shape),
        v[:, :1],
    )


def swap(v, axis):
    return lax.ppermute(v, axis, [(0, 1), (1, 0)])


def per_device(lay, *args):
    (x_in, up_in, start_in) = args[:3]
    vec = args[3:13]
    w_r, w_k, w_v, w_g, w_o = args[13:18]
    vec2 = args[18:22]
    w_ck, w_cv, w_cr = args[22:]
    a_at, b_at, h_at = (lax.axis_index(n) for n in ("a", "b", "h"))
    rank = (b_at * lay.L + lax.axis_index("l")) * lay.C + lax.axis_index("c")
    H = lay.H
    segs = lay.B
    D = x_in.shape[-1]
    x_own = x_in[0]
    rows = x_own.shape[0]
    T = rows * lay.team
    dcol = D // lay.team
    heads = dcol // HEAD
    half = lay.L * lay.C
    w_row = D // lay.n
    lay.of(D)
    hid = w_ck.shape[1] // lay.team

    stacked = jnp.stack([*vec, *vec2])
    nv = stacked.shape[0]
    stacked = jnp.pad(stacked, ((0, 16 - nv), (0, 128 - w_row)))
    spread4 = jnp.concatenate(
        [lay.spread(w, HEAD) for w in (w_r, w_k, w_v, w_g)], axis=-1
    ).transpose(1, 0, 2)
    ffn = jnp.concatenate([lay.spread(w_ck, 1), lay.spread(w_cr, D)], axis=-1).transpose(1, 0, 2)
    o_own = w_o
    if not lay.strided:
        o_own = lax.all_gather(w_o, ALL, axis=0, tiled=True)
        o_own = lax.dynamic_slice_in_dim(o_own, rank * dcol, dcol, 0)
        o_own = o_own.reshape(lay.A, H, -1, D)
    early = w_cv.shape[0] // 3 // 16 * 16 if w_cv.shape[0] % 16 == 0 else 0
    every, my_vecs, mixed, diff1, rkv, gate, upc, W4, team, W_o, cv_first = opening(
        lay, stacked, x_own, up_in[0], spread4, ffn, o_own, w_cv, early
    )
    nh = start_in.shape[1]
    head_ids = jnp.arange(nh * HEAD, dtype=jnp.int32)

    def heads_of(p):
        ids = lax.dynamic_index_in_dim(lay.spread(head_ids, HEAD), p, 0, False)
        return ids[::HEAD] // HEAD

    my_heads = heads_of(rank)
    own_start = jnp.take(start_in[0], my_heads, axis=0)
    got_start = swap(jnp.take(start_in[0], heads_of(rank ^ 4), axis=0), "b")
    start = jnp.where(b_at == 0, jnp.stack([own_start, got_start]), jnp.stack([got_start, own_start]))
    eye = jnp.eye(heads, dtype=F32)
    start = jnp.einsum("sgcv,gj->sgvjc", start, eye).reshape(segs, dcol, dcol)
    gated, ghat, grstd, states, fin, middle, n2, halo_2, W_cv, ffn_all = time_mix(
        lay, rkv, gate, my_vecs, every, start, x_own, W_o, w_cv, cv_first, early, team
    )
    W_cv = W_cv.reshape(hid, D)
    s_out = jnp.einsum("sgvgc->sgcv", fin.reshape(segs, heads, HEAD, heads, HEAD))

    placed = jnp.zeros((segs, nh, HEAD, HEAD), BF)
    s_fin = jnp.where(h_at == lay.H - 1, s_out, 0.0).astype(BF)
    placed = placed.at[:, my_heads].set(s_fin)
    final = lax.psum_scatter(placed, "b", scatter_dimension=0, tiled=True)
    final = lax.psum_scatter(final, SEQ, scatter_dimension=1, tiled=True).astype(F32)

    wf = ffn_all.reshape(2 * lay.A, D // (2 * lay.A), -1)
    d_mid, d_br, moved, s_cv, got_cv, g_f, got_f, cm_sums = channel_mix(
        lay, n2, halo_2, every, W_cv, wf, upc.reshape(T, dcol), middle, up_in[0]
    )
    layer_output = (middle + moved.transpose(1, 0, 2).reshape(rows, D).astype(F32)).astype(BF)
    g_cv = s_cv.astype(F32) + jnp.sum(got_cv.astype(F32), axis=0)

    def own_half(g, got):
        part = lax.dynamic_index_in_dim(g, a_at, 0, False).astype(F32) + got.astype(F32)
        part = part.astype(BF).reshape(part.shape[0], H, -1, part.shape[-1])
        return part.transpose(1, 0, 2, 3)

    def total(part, got):
        own = lax.dynamic_index_in_dim(part, h_at, 0, False).astype(F32)
        return own + jnp.sum(got.astype(F32), axis=0)

    s_f = own_half(g_f, got_f)
    g_o, d_all, tm_sums, (got_f2,) = time_mix_back(
        lay, d_br, W_o, gated, ghat, grstd, gate, rkv, states, my_vecs, [(s_f, "h")]
    )
    d_l, d_u, g_gs, g_gb = tm_sums[:4]
    t_f = total(s_f, got_f2).astype(BF).reshape(lay.team, -1, hid + dcol)
    w4 = W4.reshape(2 * lay.A, D // (2 * lay.A), -1)
    items = [(t_f, "t")] + ([(g_o, "a")] if lay.strided else [])
    input_grad, g_4, ti_sums, (moved_f, *got_o) = time_in_back(
        lay, d_all, mixed, diff1, w4, every, x_own, d_mid, items
    )
    if lay.strided:
        s_o = lax.dynamic_index_in_dim(g_o, a_at, 0, False).astype(F32) + got_o[0].astype(F32)
        s_o = s_o.astype(BF)
    else:
        g_o = jnp.zeros((D, D), BF).at[rank * dcol + jnp.arange(dcol)].set(g_o.reshape(dcol, D))
        g_o = lax.psum_scatter(g_o, ALL, scatter_dimension=0, tiled=True).astype(F32)

    def in_place(v):
        spread = jnp.where(jnp.arange(lay.team)[:, None] == rank, v.reshape(1, -1), 0.0)
        return lay.unspread(spread, HEAD)

    small = jnp.stack(
        [*ti_sums[4:6], *ti_sums[:4], in_place(d_l), in_place(d_u), in_place(g_gs), in_place(g_gb)]
        + [*cm_sums[2:4], *cm_sums[:2]]
    )
    small = small.reshape(nv, lay.n, w_row).transpose(1, 0, 2)
    small = jnp.pad(small, ((0, 0), (0, 16 - nv), (0, 128 - w_row)))
    items = [(g_4.reshape(lay.team, -1, 4 * dcol), "t")] + ([(s_o, "h")] if lay.strided else [])
    small, (g_4, *got_o) = closing(lay, small, items)
    if lay.strided:
        g_o = total(s_o, got_o[0])
    small = small[:nv, :w_row]

    def columns(got, lo, hi, unit):
        return lay.unspread(got[:, :, lo:hi].transpose(1, 0, 2), unit).astype(F32)

    g_r, g_k, g_v, g_w = (columns(g_4, i * dcol, (i + 1) * dcol, HEAD) for i in range(4))
    g_ck, g_cr = columns(moved_f, 0, hid, 1), columns(moved_f, hid, hid + dcol, D)
    return (
        layer_output[None],
        input_grad[None],
        final,
        *(small[i] for i in range(10)),
        g_r,
        g_k,
        g_v,
        g_w,
        g_o,
        *(small[i] for i in range(10, 14)),
        g_ck,
        g_cv,
        g_cr,
    )


def solution(mesh):
    n_seg, n_seq = mesh.devices.shape
    shape = (n_seg // 2, 2, n_seq // 4, 2, 2)
    view = Mesh(mesh.devices.reshape(shape), ALL)
    lay = Layout(shape)
    seg = ("a", "b")
    vec, mat = P(ALL), P(ALL, None)
    tok = P(seg, SEQ, None)

    def step(*args):
        return per_device(lay, *args)

    return jax.shard_map(
        step,
        mesh=view,
        in_specs=(tok, tok, P(seg, None, None, None), *[vec] * 10, *[mat] * 5, *[vec] * 4, *[mat] * 3),
        out_specs=(tok, tok, P(seg, SEQ, None, None), *[vec] * 10, *[mat] * 5, *[vec] * 4, *[mat] * 3),
        check_vma=False,
    )
```

```python
import jax
import jax.numpy as jnp
from jax import lax
from jax.experimental import pallas as pl
from jax.experimental.pallas import tpu as pltpu
from jax.sharding import Mesh, PartitionSpec as P

TEAM = ("b", "l", "c")
TEAMS = ("a", "h")
SEQ = ("h", "l", "c")
ALL = ("a", "b", "h", "l", "c")
HEAD = 64
CHUNK = 128
EPS = 1e-05
GROUP_EPS = 0.00064
BF = jnp.bfloat16
F32 = jnp.float32


MESH = pl.DeviceIdType.MESH
DMA = pltpu.SemaphoreType.DMA
VMEM_BYTES = 62 << 20


def coords():
    return {name: lax.axis_index(name) for name in ALL}


def rank_of(b, l, c):
    return (b * 2 + l) * 2 + c


def remote(src, dst, sent, landed, to):
    return pltpu.make_async_remote_copy(
        src_ref=src,
        dst_ref=dst,
        send_sem=sent,
        recv_sem=landed,
        device_id=to,
        device_id_type=MESH,
    )


def mates(me):
    for m in range(1, 8):
        yield m, {"b": me["b"] ^ (m >> 2), "l": me["l"] ^ ((m >> 1) & 1), "c": me["c"] ^ (m & 1)}


def greet(me, H, column, across):
    sem = pltpu.get_barrier_semaphore()
    count = 0
    for dh in range(H if column else 1):
        h = lax.rem(me["h"] + dh, H)
        for m in range(8):
            if dh == 0 and m == 0:
                continue
            to = {
                "b": me["b"] ^ (m >> 2),
                "h": h if column else me["h"],
                "l": me["l"] ^ ((m >> 1) & 1),
                "c": me["c"] ^ (m & 1),
            }
            pl.semaphore_signal(sem, inc=1, device_id=to, device_id_type=MESH)
            count += 1
    if across:
        pl.semaphore_signal(sem, inc=1, device_id={"a": 1 - me["a"]}, device_id_type=MESH)
        count += 1
    pl.semaphore_wait(sem, count)


class Copies:
    def __init__(self, sems):
        self.sems, self.k, self.open = sems, 0, []

    def go(self, src, dst, landed, to):
        copy = remote(src, dst, self.sems.at[self.k], landed, to)
        self.k += 1
        copy.start()
        self.open.append(copy)

    def drain(self):
        for copy in self.open:
            copy.wait_send()


def landed(ref, sem):
    remote(ref, ref, sem, sem, {"c": 1 - lax.axis_index("c")}).wait_recv()


def upper(ref, half):
    n = ref.shape[0] // 2
    return ref.at[pl.ds(half * n, n)]


class TeamGather:
    def __init__(self, me, own, view, send, recv, via=("xz", "zx")):
        self.me, self.own, self.view, self.recv, self.via = me, own, view, recv, via
        self.copies = Copies(send)
        self.tx, self.tz, self.ts = {"b": 1 - me["b"]}, {"l": 1 - me["l"]}, {"c": 1 - me["c"]}

    def put(self, src, p, half, to):
        self.copies.go(src, upper(self.view(p), half), self.recv.at[p, half], to)

    def start(self):
        mine = rank_of(self.me["b"], self.me["l"], self.me["c"])
        order = [(half, self.tx if self.via[half] == "xz" else self.tz) for half in range(2)]
        order += [(half, self.tz if self.via[half] == "xz" else self.tx) for half in range(2)]
        order += [(0, self.ts), (1, self.ts)]
        for half, to in order:
            self.put(upper(self.own, half), mine, half, to)

    def finish(self):
        b, l, c = self.me["b"], self.me["l"], self.me["c"]
        px, pz, pd = rank_of(1 - b, l, c), rank_of(b, 1 - l, c), rank_of(1 - b, 1 - l, c)
        order = [
            (px, half, self.tz) if self.via[half] == "xz" else (pz, half, self.tx)
            for half in range(2)
        ]
        order += [
            (pz, half, None) if self.via[half] == "xz" else (px, half, None) for half in range(2)
        ]
        for p, half, on in order + [(pd, 0, None), (pd, 1, None)]:
            block = upper(self.view(p), half)
            landed(block, self.recv.at[p, half])
            if on is not None:
                self.put(block, p, half, on)
            self.put(block, p, half, self.ts)
        for q in range(4):
            p = q * 2 + 1 - c
            for half in range(2):
                landed(upper(self.view(p), half), self.recv.at[p, half])
        self.copies.drain()


class TeamSum:
    def __init__(self, me, part, near, acc, mid, far, send, recv, via=("xz", "zx")):
        self.me, self.part, self.near, self.acc, self.mid, self.far = me, part, near, acc, mid, far
        self.recv, self.via = recv, via
        self.copies = Copies(send)

    def start(self):
        b, l, c = self.me["b"], self.me["l"], self.me["c"]
        self.spots = [(b, l), (1 - b, l), (b, 1 - l), (1 - b, 1 - l)]
        for i in (3, 1, 2, 0):
            bb, ll = self.spots[i]
            self.copies.go(
                self.part(rank_of(bb, ll, 1 - c)), self.near.at[i], self.recv.at[i], {"c": 1 - c}
            )

    def tiles(self, rows, body):
        step = max(16, 65536 // self.near.shape[2])

        @pl.loop(0, rows // step)
        def _(t):
            body(pl.ds(pl.multiple_of(t * step, step), step))

    def pair(self, i, write):
        bb, ll = self.spots[i]
        landed(self.near.at[i], self.recv.at[i])
        mine = self.part(rank_of(bb, ll, self.me["c"]))
        self.tiles(
            self.near.shape[1], lambda at: write(at, mine[at].astype(F32) + self.near[i, at].astype(F32))
        )

    def finish(self, write, then=lambda: None):
        b, l = self.me["b"], self.me["l"]
        tx, tz = {"b": 1 - b}, {"l": 1 - l}
        acc, mid, far, recv, go = self.acc, self.mid, self.far, self.recv, self.copies.go
        n = mid.shape[1]
        hops = [
            (tx, 0, tz, 1) if self.via[half] == "xz" else (tz, 1, tx, 0) for half in range(2)
        ]
        for i in (3, 1, 2):

            def put(at, v):
                acc[i - 1, at] = v.astype(BF)

            self.pair(i, put)
            if i == 3:
                for half, (one, _, _, _) in enumerate(hops):
                    go(upper(acc.at[2], half), mid.at[half], recv.at[4 + half], one)
        for half, (one, direct, two, other) in enumerate(hops):
            landed(mid.at[half], recv.at[4 + half])
            into, came = upper(acc.at[other], half), mid.at[half]

            def add(at):
                into[at] = (into[at].astype(F32) + came[at].astype(F32)).astype(BF)

            self.tiles(n, add)
            go(into, upper(far.at[other], half), recv.at[8 + half], two)
            go(upper(acc.at[direct], half), upper(far.at[direct], half), recv.at[6 + half], one)
        then()
        for half, (_, direct, _, other) in enumerate(hops):
            landed(upper(far.at[direct], half), recv.at[6 + half])
            landed(upper(far.at[other], half), recv.at[8 + half])

        def last(at, v):
            write(at, v + far[0, at].astype(F32) + far[1, at].astype(F32))

        self.pair(0, last)
        self.copies.drain()

    @staticmethod
    def scratch(R, C):
        return [
            pltpu.VMEM((4, R, C), BF),
            pltpu.VMEM((3, R, C), BF),
            pltpu.VMEM((2, R // 2, C), BF),
            pltpu.VMEM((2, R, C), BF),
            DMA((10,)),
            DMA((10,)),
        ]


class TeamsGather:
    def __init__(self, me, H, source, out, send, near, far, team=None, count=2):
        self.me, self.H, self.source, self.out = me, H, source, out
        self.near, self.far, self.team, self.count = near, far, team, count
        self.copies = Copies(send)

    @staticmethod
    def sems(H, count=2):
        return [DMA((7 + count * (2 * H - 1),)), DMA((8,)), DMA((2 * H, count))]

    def groups(self, only=None):
        b, n = self.me["b"], 8 // self.count
        for g in range(self.count):
            if only is None or g in only:
                at = g * n
                yield g, (b if at < 4 else 1 - b), at % 4, n

    def block(self, a, bb, h, lo, n):
        return self.out.at[a, bb, h, pl.ds(lo, n)]

    def start(self):
        me = self.me
        a, b, h, l, c = (me[n] for n in ALL)
        for m, to in mates(me):
            p = rank_of(to["b"], to["l"], to["c"])
            mine = rank_of(b, l, c)
            self.copies.go(self.source(p), self.out.at[a, b, h, l * 2 + c], self.near.at[mine], to)

    def spread(self, local=None, only=None):
        me = self.me
        a, b, h, l, c = (me[n] for n in ALL)
        if local is not None:
            local.wait()
        for g, bb, lo, n in self.groups(only):
            block = self.block(a, bb, h, lo, n)
            src = block
            if self.team is not None:
                src = self.team.at[pl.ds(bb * 4 + lo, n)]
            else:
                for m in range(1 - g, 4):
                    ll, cc = l ^ (m >> 1), c ^ (m & 1)
                    landed(self.out.at[a, bb, h, ll * 2 + cc], self.near.at[rank_of(bb, ll, cc)])
            for dh in range(1, self.H):
                to = lax.rem(h + dh, self.H)
                self.copies.go(src, block, self.far.at[dh, g], {"h": to})
            self.copies.go(src, block, self.far.at[0, g], {"a": 1 - a})

    def forward(self, only=None):
        a, h, H = self.me["a"], self.me["h"], self.H
        for g, bb, lo, n in self.groups(only):
            for dh in range(1, H):
                block = self.block(a, bb, lax.rem(h - dh + H, H), lo, n)
                landed(block, self.far.at[dh, g])
                self.copies.go(block, block, self.far.at[H - 1 + dh, g], {"a": 1 - a})

    def finish(self):
        a, h, H = self.me["a"], self.me["h"], self.H
        for g, bb, lo, n in self.groups():
            landed(self.block(1 - a, bb, h, lo, n), self.far.at[0, g])
            for dh in range(1, H):
                block = self.block(1 - a, bb, lax.rem(h - dh + H, H), lo, n)
                landed(block, self.far.at[H - 1 + dh, g])
        self.copies.drain()


class Halo:
    def __init__(self, me, H, own, out, send, recv):
        self.me, self.H, self.own, self.out, self.send, self.recv = me, H, own, out, send, recv
        self.last = (me["l"] == 1) & (me["c"] == 1) & (me["h"] < H - 1)

    def each(self):
        me = self.me
        n = self.own.shape[0]
        for p in range(8):
            to = {
                "b": p >> 2,
                "h": jnp.minimum(me["h"] + 1, self.H - 1),
                "l": (p >> 1) & 1,
                "c": p & 1,
            }
            src = self.own.at[pl.ds(n - 16, 16)]
            yield remote(src, self.out.at[me["b"]], self.send.at[p], self.recv.at[me["b"]], to)

    def start(self):
        if self.H == 1:
            return

        @pl.when(self.last)
        def _():
            for copy in self.each():
                copy.start()

    def finish(self):
        if self.H == 1:
            return

        @pl.when(self.me["h"] > 0)
        def _():
            for b in range(2):
                landed(self.out.at[b], self.recv.at[b])

        @pl.when(self.last)
        def _():
            for copy in self.each():
                copy.wait_send()


class Edge:
    def __init__(self, me, H, first, got, send, recv):
        self.me, self.H, self.first, self.got, self.send, self.recv = me, H, first, got, send, recv

    def each(self):
        me = self.me
        mine = rank_of(me["b"], me["l"], me["c"])
        for b in range(2):
            to = {"b": b, "h": jnp.maximum(me["h"] - 1, 0), "l": 1, "c": 1}
            yield remote(self.first.at[b], self.got.at[mine], self.send.at[b], self.recv.at[mine], to)

    def start(self):
        if self.H == 1:
            return

        @pl.when(self.me["h"] > 0)
        def _():
            for copy in self.each():
                copy.start()

    def finish(self, out):
        if self.H == 1:
            return
        me = self.me

        @pl.when((me["l"] == 1) & (me["c"] == 1) & (me["h"] < self.H - 1))
        def _():
            for p in range(8):
                landed(self.got.at[p], self.recv.at[p])
            total = self.got[0, 0:1].astype(F32)
            for p in range(1, 8):
                total = total + self.got[p, 0:1].astype(F32)
            n = out.shape[0]
            out[n - 1 : n] = out[n - 1 : n] + total

        @pl.when(me["h"] > 0)
        def _():
            for copy in self.each():
                copy.wait_send()


class Exchange:
    def __init__(self, me, source, out, send, recv):
        self.me, self.source, self.out, self.recv = me, source, out, recv
        self.copies = Copies(send)

    def start(self):
        mine = rank_of(self.me["b"], self.me["l"], self.me["c"])
        for m, to in mates(self.me):
            p = rank_of(to["b"], to["l"], to["c"])
            self.copies.go(self.source(p), self.out(mine), self.recv.at[mine], to)

    def finish(self):
        for m, to in mates(self.me):
            p = rank_of(to["b"], to["l"], to["c"])
            landed(self.out(p), self.recv.at[p])
        self.copies.drain()


ANY = pl.BlockSpec(memory_space=pl.ANY)
VM = pl.BlockSpec(memory_space=pltpu.VMEM)


def comm_call(body, outs, in_specs, out_specs, scratch, cid):
    return pl.pallas_call(
        body,
        out_shape=outs,
        in_specs=in_specs,
        out_specs=out_specs,
        scratch_shapes=scratch,
        compiler_params=pltpu.CompilerParams(
            collective_id=cid, has_side_effects=True, vmem_limit_bytes=VMEM_BYTES
        ),
    )


def dot_nn(a, b):
    return jnp.dot(a, b, preferred_element_type=F32)


def dot_nt(a, b):
    return lax.dot_general(a, b, (((1,), (1,)), ((), ())), preferred_element_type=F32)


def dot_tn(a, b):
    return lax.dot_general(a, b, (((0,), (0,)), ((), ())), preferred_element_type=F32)


MIX = 32


def rows_at(i, n):
    return pl.ds(pl.multiple_of(i * n, n), n)


class RowsGather:
    def __init__(self, me, H, own, out, send, recv, at=None):
        self.me, self.H, self.own, self.out, self.recv, self.at = me, H, own, out, recv, at
        self.copies = Copies(send)

    @staticmethod
    def sems(H):
        return [DMA((2 * H - 1,)), DMA((2 * H,))]

    def block(self, a, h):
        return self.out.at[a, h] if self.at is None else self.out.at[a, h, self.at]

    def start(self):
        a, h = self.me["a"], self.me["h"]
        block = self.block(a, h)
        for dh in range(1, self.H):
            to = lax.rem(h + dh, self.H)
            self.copies.go(self.own, block, self.recv.at[dh], {"h": to})
        self.copies.go(self.own, block, self.recv.at[0], {"a": 1 - a})

    def forward(self):
        a, h, H = self.me["a"], self.me["h"], self.H
        for dh in range(1, H):
            block = self.block(a, lax.rem(h - dh + H, H))
            landed(block, self.recv.at[dh])
            self.copies.go(block, block, self.recv.at[H - 1 + dh], {"a": 1 - a})

    def finish(self):
        a, h, H = self.me["a"], self.me["h"], self.H
        landed(self.block(1 - a, h), self.recv.at[0])
        for dh in range(1, H):
            landed(self.block(1 - a, lax.rem(h - dh + H, H)), self.recv.at[H - 1 + dh])
        self.copies.drain()


def join_lanes(pieces, width):
    per = 128 // width
    out = []
    for g in range(0, len(pieces), per):
        acc = pieces[g]
        for k in range(1, per):
            acc = acc + pltpu.roll(pieces[g + k], width * k, axis=1)
        out.append(acc)
    return jnp.concatenate(out, axis=1) if len(out) > 1 else out[0]


def norm_rows(v):
    mean = jnp.mean(v, axis=-1, keepdims=True)
    cent = v - mean
    rstd = lax.rsqrt(jnp.mean(cent * cent, axis=-1, keepdims=True) + EPS)
    return cent * rstd, rstd


def mix_rows(read, first, carry, shares, write, tiles, rows):
    per = tiles // 2

    @pl.loop(0, tiles)
    def _(p):
        n = read(p)
        prev = jnp.where(lax.rem(p, per) == 0, first(p // per), carry[...])
        row = lax.broadcasted_iota(jnp.int32, n.shape, 0)
        before = jnp.where(row == 0, prev, pltpu.roll(n, 1, axis=0))
        carry[...] = n[rows - 1 : rows]
        diff = n - before
        for i, s in enumerate(shares):
            write(i, p, (before + s * diff).astype(BF))
        write(None, p, diff.astype(BF))


def block_ones(m):
    row = lax.broadcasted_iota(jnp.int32, (m, m), 0) // HEAD
    col = lax.broadcasted_iota(jnp.int32, (m, m), 1) // HEAD
    return jnp.where(row == col, 1.0, 0.0).astype(F32)


def dot_exact(a, b):
    return jnp.dot(a, b, preferred_element_type=F32, precision=lax.Precision.HIGHEST)


class Decay:
    def __init__(self, lam):
        m = lam.shape[1]
        i = lax.broadcasted_iota(jnp.int32, (CHUNK, m), 0).astype(F32)
        self.i = i
        self.down = jnp.exp(-lam * i)
        self.up = jnp.exp(lam * (i + 1.0))
        self.tail = jnp.exp(-lam * (CHUNK - 1.0 - i))
        self.span = jnp.exp(-lam * CHUNK)


def stacked_heads(v):
    m = v.shape[1]
    lane = lax.broadcasted_iota(jnp.int32, v.shape, 1) // HEAD
    zero = jnp.zeros_like(v)
    return jnp.concatenate([jnp.where(lane == g, v, zero) for g in range(m // HEAD)], axis=0)


def own_heads(v):
    m = v.shape[1]
    lane = lax.broadcasted_iota(jnp.int32, (CHUNK, m), 1) // HEAD
    out = v[:CHUNK]
    for g in range(1, m // HEAD):
        out = jnp.where(lane == g, v[g * CHUNK : (g + 1) * CHUNK], out)
    return out


def triangle(heads, low):
    shape = (heads * CHUNK, CHUNK)
    row = lax.rem(lax.broadcasted_iota(jnp.int32, shape, 0), CHUNK)
    col = lax.broadcasted_iota(jnp.int32, shape, 1)
    return row > col if low else row < col


def squeeze(s0, s1):
    def fold(s):
        out = s[:, :128]
        for g in range(1, s.shape[1] // 128):
            out = out + s[:, g * 128 : (g + 1) * 128]
        return out + pltpu.roll(out, HEAD, axis=1)

    lane = lax.broadcasted_iota(jnp.int32, (s0.shape[0], 128), 1)
    return jnp.where(lane < HEAD, fold(s0), fold(s1))


def widen(p, second, ones):
    lane = lax.broadcasted_iota(jnp.int32, p.shape, 1)
    keep = (lane >= HEAD) if second else (lane < HEAD)
    both = jnp.where(keep, p, pltpu.roll(p, HEAD, axis=1))
    return jnp.concatenate([both] * (ones.shape[1] // 128), axis=1) * ones


class Chain:
    def __init__(self, me, H, ahead, out_box, in_box, send, recv):
        h = me["h"]
        self.h, self.H = h, H
        nxt = jnp.minimum(h + 1, H - 1) if ahead else jnp.maximum(h - 1, 0)
        self.has_next = (h < H - 1) if ahead else (h > 0)
        self.has_prev = (h > 0) if ahead else (h < H - 1)
        self.out_box, self.in_box = out_box, in_box
        self.copy = remote(out_box, in_box, send, recv, {"h": nxt})

    def run(self, state, closing, span_all, ones):
        if self.H == 1:
            return

        @pl.when(self.has_prev)
        def _():
            self.copy.wait_recv()
            p = self.in_box[...].astype(F32)
            for s in range(2):
                state[s] = widen(p, s == 1, ones)

        @pl.when(self.has_next)
        def _():
            out = squeeze(*(span_all * state[s] + closing[s] for s in range(2)))
            self.out_box[...] = out.astype(BF)
            self.copy.start()

    def finish(self):
        if self.H == 1:
            return

        @pl.when(self.has_next)
        def _():
            self.copy.wait_send()


def window(read, width, s):
    if s < 0:
        return pltpu.roll(read(0, 128).astype(F32), -s, axis=1)
    t, off = s // 128 * 128, s % 128
    if off == 0:
        return read(t, t + 128).astype(F32)
    if t + 256 <= width:
        return pltpu.roll(read(t, t + 256).astype(F32), 256 - off, axis=1)[:, :128]
    return pltpu.roll(read(t, t + 128).astype(F32), 128 - off, axis=1)


def lay_lanes(width, parts, put):
    for lo in range(0, width, 128):
        out = None
        for read, wide, src, dst, n in parts:
            d0, d1 = max(dst - lo, 0), min(dst + n - lo, 128)
            if d0 >= d1:
                continue
            v = window(read, wide, src + lo - dst)
            if out is not None:
                lane = lax.broadcasted_iota(jnp.int32, v.shape, 1)
                v = jnp.where((lane >= d0) & (lane < d1), v, out)
            out = v
        put(lo, out)


def rank_columns(lay, n, whole, p):
    w, m = n // lay.n, n // 8
    if w % whole:
        return [(p * m, 0, m)]
    b, l, c = p >> 2, (p >> 1) & 1, p & 1
    teams = [(i, j) for i in range(lay.A) for j in range(lay.H)]
    return [
        (((((i * 2 + b) * lay.H + j) * 2 + l) * 2 + c) * w, k * w, w) for k, (i, j) in enumerate(teams)
    ]


def front(lay, vecs, x, up, w4, w_ck, w_cr, w_o, w_cv, start):
    H, A = lay.H, lay.A
    grid = (A, 2, H, 4)
    rows, D = x.shape
    T = 8 * rows
    m = D // 8
    w_row = D // lay.n
    kk = D // (2 * A)
    heads = m // HEAD
    per = T // 2 // CHUNK
    bring_o = lay.strided
    wo_shape = (A, H, m // (A * H), D)
    cv_rows = w_cv.shape[0]
    F = w_ck.shape[1]
    nf = F // 8 + m
    k_row = w_ck.shape[0]
    early = cv_rows // 2 // 16 * 16 if cv_rows % 16 == 0 else 0

    def body(*refs):
        vecs, x, up, w_r, w_k, w_v, w_g, w_ck, w_cr, w_o, w_cv, start = refs[:12]
        refs = refs[4:]
        full, mine_v, mixed, diff, rkv, gate, upc, w_out = refs[8:16]
        wo, gated, ghat, grstd, states, fin, middle, n2, halo2, wcv, wf = refs[16:27]
        va, xg, halo, hn, carry, mx, df, wa, wos, team = refs[27:37]
        adds, st, cl, obox, ibox, own = refs[37:43]
        near, acc, mid, far, ss, sr = refs[43:49]
        vs, vn, vf, xs, xr, hs, hr, us, ur, ws, wn, wf_, qs, qr, os_, or_ = refs[49:65]
        es, er, cs, cr, ts, tr, fs, fn, ff, gs, gr, ks, kr, ls = refs[65:79]
        w, later, sbuf, zbuf, bs, br = refs[79:]
        part = xg
        me = coords()
        a, b, h, l, c = (me[n] for n in ALL)
        mine = rank_of(b, l, c)

        def cols(ref, p):
            return ref.at[:, pl.ds(pl.multiple_of(p * m, m), m)]

        for p in range(8):
            for j, ref in enumerate((w_r, w_k, w_v, w_g)):
                read = lambda lo, hi, ref=ref: ref[:, lo:hi]
                parts = [(read, D, *at) for at in rank_columns(lay, D, HEAD, p)]

                def put_w(lo, v, p=p, j=j):
                    w[p, :, j * m + lo : j * m + lo + 128] = v.astype(BF)

                lay_lanes(m, parts, put_w)

        local = [
            pltpu.make_async_copy(w.at[mine], wa.at[a, b, h, l * 2 + c], ls.at[0]),
            pltpu.make_async_copy(x, xg.at[rows_at(mine, rows)], ls.at[2]),
            pltpu.make_async_copy(cols(up, mine), upc.at[mine], ls.at[3]),
            pltpu.make_async_copy(vecs, va.at[a, b, h, l * 2 + c], ls.at[4]),
            pltpu.make_async_copy(w_o, wos.at[a, h] if bring_o else wos, ls.at[5]),
            pltpu.make_async_copy(w_cv, wcv.at[a, h], ls.at[6]),
        ]
        for copy in local:
            copy.start()
        greet(me, H, True, True)
        gw = TeamsGather(me, H, lambda p: w.at[p], wa, ws, wn, wf_)
        gv = TeamsGather(me, H, lambda p: vecs, va, vs, vn, vf)
        gx = TeamGather(me, x, lambda p: xg.at[rows_at(p, rows)], xs, xr, ("zx", "zx"))
        gh = Halo(me, H, x, halo, hs, hr)
        gu = Exchange(me, lambda p: cols(up, p), lambda p: upc.at[p], us, ur)
        gq = Exchange(me, lambda p: later.at[p], lambda p: team.at[p], qs, qr)
        gf = TeamsGather(me, H, None, wf, fs, fn, ff, team, 4)
        if bring_o:
            go = RowsGather(me, H, w_o, wos, os_, or_)
        top, rest = pl.ds(0, early), pl.ds(early, cv_rows - early)
        if early:
            ge = RowsGather(me, H, w_cv.at[top], wcv, es, er, top)
        gc = RowsGather(me, H, w_cv.at[rest], wcv, ts, tr, rest)
        def head(bb, k):
            if lay.strided:
                return (((k // H * 2 + bb) * H + k % H) * 2 + l) * 2 + c
            return rank_of(bb, l, c) * heads + k

        near_states = [
            pltpu.make_async_copy(start.at[head(b, k)], sbuf.at[b, k], ls.at[14 + k]) for k in range(heads)
        ]
        far_states = [
            remote(start.at[head(1 - b, k)], sbuf.at[b, k], bs.at[k], br.at[k], {"b": 1 - b})
            for k in range(heads)
        ]
        gv.start()
        gh.start()
        gw.start()
        for copy in near_states + far_states:
            copy.start()
        gx.start()
        gv.spread(local[3])
        gv.forward()
        gw.spread(local[0])
        gv.finish()
        for p in range(8):
            parts = [(lambda lo, hi: w_ck[:, lo:hi], F, *at) for at in rank_columns(lay, F, 1, p)]

            def put_ck(lo, v, p=p):
                later[p, :, lo : lo + 128] = v.astype(BF)

            lay_lanes(F // 8, parts, put_ck)
            later[p, :, F // 8 :] = w_cr[:, p * m : (p + 1) * m]
        mine_team = pltpu.make_async_copy(later.at[mine], team.at[mine], ls.at[1])
        mine_team.start()
        local[1].wait()
        gx.finish()
        gq.start()
        gu.start()
        gw.forward((0,))
        gh.finish()

        def piece(*at):
            return va[at].astype(F32)

        flat = [
            piece(i, j, k, q) for i in range(A) for j in range(2) for k in range(H) for q in range(4)
        ]
        full[...] = join_lanes(flat, w_row)
        if lay.strided:
            held = [piece(i, b, k, l * 2 + c) for i in range(A) for k in range(H)]
            mine_v[...] = join_lanes(held, w_row)
        else:
            mine_v[...] = full[:, pl.ds(pl.multiple_of(mine * m, m), m)]
        gain, bias = full[0:1], full[1:2]
        for s in range(2):
            row = (norm_rows(halo[s].astype(F32))[0] * gain + bias)[15:16]
            hn[s] = jnp.where(h > 0, row, jnp.zeros_like(row))

        def write(i, p, v):
            if i is None:
                df[rows_at(p, MIX)] = v
            else:
                mx[i, rows_at(p, MIX)] = v

        mix_rows(
            lambda p: norm_rows(xg[rows_at(p, MIX)].astype(F32))[0] * gain + bias,
            lambda s: hn[s],
            carry,
            [full[2 + i : 3 + i] for i in range(4)],
            write,
            T // MIX,
            MIX,
        )
        keep = [
            pltpu.make_async_copy(mx, mixed, ls.at[7]),
            pltpu.make_async_copy(df, diff, ls.at[8]),
        ]
        for copy in keep:
            copy.start()
        gw.forward((1,))
        if bring_o:
            go.start()
        mine_team.wait()
        gq.finish()
        keep += [
            pltpu.make_async_copy(team.at[pl.ds(0, 4)], wf.at[a, 0, h], ls.at[11]),
            pltpu.make_async_copy(team.at[pl.ds(4, 4)], wf.at[a, 1, h], ls.at[12]),
        ]
        for copy in keep[2:]:
            copy.start()
        gf.spread(None, (0,))
        gw.finish()
        keep.append(pltpu.make_async_copy(wa, w_out, ls.at[9]))
        keep[-1].start()
        for j in range(4):

            @pl.loop(0, 4)
            def _(t):
                at = rows_at(t, T // 4)
                acc = jnp.zeros((T // 4, m), F32)
                for i in range(A):
                    for k in range(2):
                        lo = (i * 2 + k) * kk
                        wt = wa[i, k, :, :, :, j * m : (j + 1) * m].reshape(kk, m)
                        acc = acc + dot_nn(mx[j, at, lo : lo + kk], wt)
                if j < 3:
                    rkv[j, at] = acc.astype(BF)
                else:
                    gate[at] = acc

        ones = block_ones(m)
        dec = Decay(mine_v[6:7])
        u = mine_v[7:8]
        span_all = jnp.exp(-mine_v[6:7] * (T // 2))

        def tile(i, s, n):
            return rkv[i, rows_at(s * per + n, CHUNK)].astype(F32)

        cl[...] = jnp.zeros_like(cl)

        @pl.loop(0, per)
        def _(n):
            for s in range(2):
                kt = (tile(1, s, n) * dec.tail).astype(BF)
                v = rkv[2, rows_at(s * per + n, CHUNK)]
                add = dot_tn(v, kt) * ones
                adds[s, n] = add
                cl[s] = dec.span * cl[s] + add

        for copy in near_states:
            copy.wait()
        for copy in far_states:
            copy.wait_send()
        for k in range(heads):
            landed(sbuf.at[1 - b, k], br.at[k])
        odd = lax.rem(lax.broadcasted_iota(jnp.int32, (m, 128), 0) // HEAD, 2) == 1
        zbuf[...] = jnp.zeros_like(zbuf)
        for s in range(2):
            for k in range(heads):
                zbuf[k * HEAD : (k + 1) * HEAD, :HEAD] = sbuf[s, k]
            z = zbuf[...]
            z = jnp.where(odd, pltpu.roll(z, HEAD, axis=1), z)
            z = (jnp.concatenate([z] * (m // 128), axis=1) * ones).T
            st[s] = jnp.where(h > 0, jnp.zeros_like(z), z)
        chain = Chain(me, H, True, obox, ibox, cs, cr)
        chain.run(st, cl, span_all, ones)
        gf.spread(None, (1, 2))
        local[4].wait()
        if bring_o:
            go.forward()
        low = triangle(heads, True)

        @pl.loop(0, per)
        def _(n):
            for s in range(2):
                at = rows_at(s * per + n, CHUNK)
                r, k, v = (tile(i, s, n) for i in range(3))
                vb = rkv[2, at]
                rd = (r * dec.down).astype(BF)
                kg = (k * dec.up).astype(BF)
                state = st[s]
                states[s, n] = state
                att = jnp.where(low, dot_nt(stacked_heads(rd), kg), 0.0).astype(BF)
                y = own_heads(dot_nn(att, vb)) + dot_nt(rd, state.astype(BF))
                y = y + dot_exact(r * u * k, ones) * v
                st[s] = dec.span * state + adds[s, n]
                mean = dot_exact(y, ones) * (1.0 / HEAD)
                cent = y - mean
                rstd = lax.rsqrt(dot_exact(cent * cent, ones) * (1.0 / HEAD) + GROUP_EPS)
                hat = cent * rstd
                ghat[at] = hat
                grstd[at] = rstd
                g = gate[at]
                silu = g / (1.0 + jnp.exp(-g))
                gated[at] = ((hat * mine_v[8:9] + mine_v[9:10]) * silu).astype(BF)

        fin[...] = squeeze(st[0], st[1])
        chain.finish()
        if bring_o:
            go.finish()
        keep.append(pltpu.make_async_copy(wos, wo, ls.at[13]))
        keep[-1].start()

        @pl.loop(0, 8)
        def _(p):
            g = gated[rows_at(p, rows)]
            w = wos[...].reshape(m, D)
            for q in range(4):
                lo = q * (D // 4)
                part[rows_at(p, rows), lo : lo + D // 4] = dot_nn(g, w[:, lo : lo + D // 4]).astype(BF)

        sums = TeamSum(me, lambda p: part.at[rows_at(p, rows)], near, acc, mid, far, ss, sr, ("xz", "xz"))
        sums.start()

        def put(at, v):
            v = x[at].astype(F32) + v
            middle[at] = v
            own[at] = (norm_rows(v)[0] * full[10:11] + full[11:12]).astype(BF)

        sums.finish(put)
        keep.append(pltpu.make_async_copy(own, n2.at[mine], ls.at[10]))
        keep[-1].start()
        gn = TeamGather(me, own, lambda p: n2.at[p], gs, gr, ("zx", "zx"))
        gn.start()
        gk = Halo(me, H, own, halo2, ks, kr)
        gk.start()
        gf.spread(None, (3,))
        if early:
            ge.start()
        gc.start()
        gf.forward((0, 1, 2))
        gn.finish()
        gk.finish()
        gf.forward((3,))
        if early:
            ge.forward()
        gc.forward()
        gu.finish()
        gf.finish()
        if early:
            ge.finish()
        gc.finish()
        for copy in local[2:3] + local[5:] + keep:
            copy.wait()

    gsems = TeamsGather.sems(H)
    team_sems = [DMA((14,)), DMA((8, 2))]
    halo_sems = [DMA((8,)), DMA((2,))]
    move_sems = [DMA((7,)), DMA((8,))]
    return comm_call(
        body,
        (
            jax.ShapeDtypeStruct((16, D), F32),
            jax.ShapeDtypeStruct((16, m), F32),
            jax.ShapeDtypeStruct((4, T, D), BF),
            jax.ShapeDtypeStruct((T, D), BF),
            jax.ShapeDtypeStruct((3, T, m), BF),
            jax.ShapeDtypeStruct((T, m), F32),
            jax.ShapeDtypeStruct((8, rows, m), BF),
            jax.ShapeDtypeStruct((*grid, k_row, 4 * m), BF),
            jax.ShapeDtypeStruct(wo_shape, BF),
            jax.ShapeDtypeStruct((T, m), BF),
            jax.ShapeDtypeStruct((T, m), F32),
            jax.ShapeDtypeStruct((T, m), F32),
            jax.ShapeDtypeStruct((2, per, m, m), F32),
            jax.ShapeDtypeStruct((m, 128), F32),
            jax.ShapeDtypeStruct((rows, D), F32),
            jax.ShapeDtypeStruct((8, rows, D), BF),
            jax.ShapeDtypeStruct((2, 16, D), BF),
            jax.ShapeDtypeStruct((A, H, *w_cv.shape), BF),
            jax.ShapeDtypeStruct((*grid, k_row, nf), BF),
        ),
        [VM] * 11 + [ANY],
        (VM, VM, ANY, ANY, VM, VM, ANY, ANY, ANY, VM, VM, VM, VM, VM, VM, ANY, ANY, ANY, ANY),
        [
            pltpu.VMEM((*grid, *vecs.shape), BF),
            pltpu.VMEM((T, D), BF),
            pltpu.VMEM((2, 16, D), BF),
            pltpu.VMEM((2, 1, D), F32),
            pltpu.VMEM((1, D), F32),
            pltpu.VMEM((4, T, D), BF),
            pltpu.VMEM((T, D), BF),
            pltpu.VMEM((*grid, k_row, 4 * m), BF),
            pltpu.VMEM(wo_shape, BF),
            pltpu.VMEM((8, k_row, nf), BF),
            pltpu.VMEM((2, per, m, m), F32),
            pltpu.VMEM((2, m, m), F32),
            pltpu.VMEM((2, m, m), F32),
            pltpu.VMEM((m, 128), BF),
            pltpu.VMEM((m, 128), BF),
            pltpu.VMEM((rows, D), BF),
            *TeamSum.scratch(rows, D),
            *gsems,
            *team_sems,
            *halo_sems,
            *move_sems,
            *gsems,
            *move_sems,
            *RowsGather.sems(H),
            *RowsGather.sems(H),
            DMA,
            DMA,
            *RowsGather.sems(H),
            *TeamsGather.sems(H, 4),
            *team_sems,
            *halo_sems,
            DMA((14 + heads,)),
            pltpu.VMEM((8, k_row, 4 * m), BF),
            pltpu.VMEM((8, k_row, nf), BF),
            pltpu.VMEM((2, heads, HEAD, HEAD), F32),
            pltpu.VMEM((m, 128), F32),
            DMA((heads,)),
            DMA((heads,)),
        ],
        0,
    )(vecs, x, up, *w4, w_ck, w_cr, w_o, w_cv, start)


class Background:
    def __init__(self, items, H):
        self.items, self.H = items, H

    def arrays(self):
        return [v for v, _ in self.items]

    def outs(self):
        shapes = []
        for v, kind in self.items:
            lead = {"h": (max(self.H - 1, 1),), "a": (), "t": (8,)}[kind]
            shapes.append(jax.ShapeDtypeStruct((*lead, *v.shape[1:]), BF))
        return shapes

    def sems(self):
        out = []
        for _, kind in self.items:
            n = {"h": max(self.H - 1, 1), "a": 1, "t": 8}[kind]
            out += [DMA((n,)), DMA((n,))] + ([DMA] if kind == "t" else [])
        return out

    def start(self, me, srcs, dsts, sems):
        self.open = []
        sems = list(sems)
        h, H = me["h"], self.H
        mine = rank_of(me["b"], me["l"], me["c"])
        for (_, kind), src, dst in zip(self.items, srcs, dsts):
            ss, sr = sems.pop(0), sems.pop(0)
            copies = Copies(ss)
            if kind == "h":
                for dh in range(1, H):
                    to = lax.rem(h + dh, H)
                    copies.go(src.at[to], dst.at[dh - 1], sr.at[dh - 1], {"h": to})
                    self.open.append((dst.at[dh - 1], sr.at[dh - 1]))
            elif kind == "a":
                copies.go(src.at[1 - me["a"]], dst, sr.at[0], {"a": 1 - me["a"]})
                self.open.append((dst, sr.at[0]))
            else:
                keep = pltpu.make_async_copy(src.at[mine], dst.at[mine], sems.pop(0))
                keep.start()
                self.open.append(keep)
                for m, to in mates(me):
                    p = rank_of(to["b"], to["l"], to["c"])
                    copies.go(src.at[p], dst.at[mine], sr.at[mine], to)
                    self.open.append((dst.at[p], sr.at[p]))
            self.open.append(copies)

    def finish(self):
        for item in self.open:
            if isinstance(item, tuple):
                landed(*item)
            elif isinstance(item, Copies):
                item.drain()
            else:
                item.wait()


def back_rows(T, tile, chunk, shares, diff, part, first, sums):
    per = T // 2 // tile

    def step(q, carry):
        t = 2 * per - 1 - q
        ds = chunk(t)
        dif = diff(t)
        late = jnp.zeros_like(ds[0])
        here = jnp.zeros_like(ds[0])
        for i, (d, s) in enumerate(zip(ds, shares)):
            sums[i][...] = sums[i][...] + jnp.sum(d * dif, axis=0, keepdims=True)
            late = late + (1.0 - s) * d
            here = here + s * d
        carry = jnp.where(lax.rem(t, per) == per - 1, jnp.zeros_like(carry), carry)
        row = lax.broadcasted_iota(jnp.int32, late.shape, 0)
        part(t, here + jnp.where(row == tile - 1, carry, pltpu.roll(late, tile - 1, axis=0)))

        @pl.when(lax.rem(t, per) == 0)
        def _():
            first(t // per, late[:16].astype(BF))

        return late[:1]

    zero = jnp.zeros((1, diff(0).shape[1]), F32)
    lax.fori_loop(0, 2 * per, step, zero)


def channel_mix(lay, n2, halo, full, wcv, wf, upc, middle, up, items):
    H, A = lay.H, lay.A
    rows, D = middle.shape
    T = 8 * rows
    F, m = wcv.shape[0], D // 8
    nk, kk, _ = wf.shape
    w_cv = F // (A * H)
    tile = T // 4
    dq = D // 4
    bg = Background(items, H)
    nb = len(items)

    def body(n2, halo, full, wcv, wf, upc, middle, up, *rest):
        srcs, rest = rest[:nb], rest[nb:]
        d_mid, d_br, moved, s_cv, got_cv, g_f, got_f, sums = rest[:8]
        dsts, rest = rest[8 : 8 + nb], rest[:8] + rest[8 + nb :]
        (big, m2, df, carry, relu, act, sg, d_pg, d_val, dval, gcv, cvbuf, stage) = rest[8:21]
        (dn2, own, add, first, edge) = rest[21:26]
        cn, ca, cm, cf, c_s, c_r = rest[26:32]
        rn, ra, rm, rf, r_s, r_r = rest[32:38]
        ds, dr, bs, br, es, er, ms, mr, vs, vr, fs, fr, ls = rest[38:51]
        d_pre = act
        me = coords()
        a, b, h, l, c = (me[n] for n in ALL)
        mine = rank_of(b, l, c)
        loads = [
            pltpu.make_async_copy(n2.at[p], big.at[pl.ds(p * rows, rows)], ls.at[p]) for p in range(8)
        ]
        for copy in loads:
            copy.start()
        greet(me, H, True, True)
        for copy in loads:
            copy.wait()

        def write(i, p, v):
            if i is None:
                df[rows_at(p, MIX)] = v
            else:
                m2[i, rows_at(p, MIX)] = v

        def before(s):
            row = halo[s].astype(F32)[15:16]
            return jnp.where(h > 0, row, jnp.zeros_like(row))

        s_ck, s_cr = full[12:13], full[13:14]
        mix_rows(
            lambda p: big[rows_at(p, MIX)].astype(F32),
            before,
            carry,
            [s_ck, s_cr],
            write,
            T // MIX,
            MIX,
        )

        @pl.loop(0, 4)
        def _(t):
            at = rows_at(t, tile)
            acc = jnp.zeros((tile, F), F32)
            for i in range(nk):
                acc = acc + dot_nn(m2[0, at, i * kk : (i + 1) * kk], wf[i, :, :F])
            pos = jnp.maximum(acc, 0.0)
            relu[at] = pos.astype(BF)
            act[at] = (pos * pos).astype(BF)

        @pl.loop(0, 4)
        def _(t):
            at = rows_at(t, tile)
            for q in range(4):
                lo = q * dq
                big[at, lo : lo + dq] = dot_nn(act[at], wcv[:, lo : lo + dq]).astype(BF)

        def cols(ref):
            return lambda p: ref.at[:, pl.ds(pl.multiple_of(p * m, m), m)]

        total = TeamSum(me, cols(big), cn, ca, cm, cf, c_s, c_r)
        total.start()

        @pl.loop(0, 4)
        def _(t):
            at = rows_at(t, tile)
            acc = jnp.zeros((tile, m), F32)
            for i in range(nk):
                acc = acc + dot_nn(m2[1, at, i * kk : (i + 1) * kk], wf[i, :, F:])
            sg[at] = 1.0 / (1.0 + jnp.exp(-acc))

        def gate_back(at, val):
            sig = sg[at]
            upv = upc[at].astype(F32)
            d_val[at] = (sig * upv).astype(BF)
            d_pg[at] = (upv * val * sig * (1.0 - sig)).astype(BF)
            add[at] = (sig * val).astype(BF)

        total.finish(gate_back)
        keep_val = pltpu.make_async_copy(d_val, cols(dval)(mine), ls.at[8])
        keep_val.start()
        gv = TeamGather(me, d_val, cols(dval), ds, dr)
        gv.start()
        gv.finish()
        keep_val.wait()

        @pl.loop(0, 8)
        def _(q):
            at = pl.ds(pl.multiple_of(q * m, m), m)
            g = dot_tn(act[...], dval[:, at])
            for i in range(A):
                for j in range(H):
                    lo = (i * H + j) * w_cv
                    gcv[i, j, :, at] = g[lo : lo + w_cv].astype(BF)

        cv = Copies(vs)
        cv.go(gcv.at[1 - a], cvbuf, vr.at[0], {"a": 1 - a})

        @pl.loop(0, 4)
        def _(t):
            at = rows_at(t, tile)
            d_pre[at] = (dot_nt(dval[at], wcv[...]) * 2.0 * relu[at].astype(F32)).astype(BF)

        ff = Copies(fs)
        sums[...] = jnp.zeros_like(sums)

        def chunk_of(i):
            lo = i * kk

            def chunk(t):
                at = rows_at(t, tile)
                return (dot_nt(d_pre[at], wf[i, :, :F]), dot_nt(d_pg[at], wf[i, :, F:]))

            def put(t, v):
                big[rows_at(t, tile), lo : lo + kk] = v.astype(BF)

            def put_first(s, v):
                first[s, :, lo : lo + kk] = v

            back_rows(
                T,
                tile,
                chunk,
                (s_ck[:, lo : lo + kk], s_cr[:, lo : lo + kk]),
                lambda t: df[rows_at(t, tile), lo : lo + kk].astype(F32),
                put,
                put_first,
                [sums.at[k : k + 1, lo : lo + kk] for k in range(2)],
            )

        def grads(i):
            lo = i * kk
            for k in range(2):
                at = slice(lo + k * kk // 2, lo + (k + 1) * kk // 2)
                to = slice(k * kk // 2, (k + 1) * kk // 2)
                stage[to, :F] = dot_tn(m2[0, :, at], d_pre[...]).astype(BF)
                stage[to, F:] = dot_tn(m2[1, :, at], d_pg[...]).astype(BF)
            copy = pltpu.make_async_copy(stage, g_f.at[i // 2, i % 2], ls.at[9])
            copy.start()
            return copy

        for i in range(nk):
            copy = grads(i)
            chunk_of(i)
            copy.wait()
        ff.go(g_f.at[1 - a], got_f, fr.at[0], {"a": 1 - a})
        total = TeamSum(me, lambda p: big.at[rows_at(p, rows)], rn, ra, rm, rf, r_s, r_r)
        total.start()
        e = Edge(me, H, first, edge, es, er)
        e.start()

        def put_dn(at, v):
            dn2[at] = v

        halves = 2 if w_cv % 32 == 0 else 1

        def pass_on(g):
            at = pl.ds(g * (w_cv // halves), w_cv // halves)
            for dh in range(1, H):
                to = lax.rem(h + dh, H)
                cv.go(
                    gcv.at[a, to, at],
                    got_cv.at[dh - 1, at],
                    vr.at[1 + (dh - 1) * 2 + g],
                    {"h": to},
                )

        def value_sums():
            landed(cvbuf, vr.at[0])

            @pl.loop(0, H)
            def _(j):
                gcv[a, j] = (gcv[a, j].astype(F32) + cvbuf[j].astype(F32)).astype(BF)

            pass_on(0)

        total.finish(put_dn, value_sums)
        e.finish(dn2)

        @pl.loop(0, rows // MIX)
        def _(t):
            at = rows_at(t, MIX)
            d = dn2[at]
            hat, rstd = norm_rows(middle[at])
            sums[2:3] = sums[2:3] + jnp.sum(d * hat, axis=0, keepdims=True)
            sums[3:4] = sums[3:4] + jnp.sum(d, axis=0, keepdims=True)
            dm = up[at].astype(F32) + norm_back(d * full[10:11], hat, rstd)
            d_mid[at] = dm
            own[at] = dm.astype(BF)

        keep = [
            pltpu.make_async_copy(own, d_br.at[mine], ls.at[10]),
            pltpu.make_async_copy(add.at[rows_at(mine, rows)], moved.at[mine], ls.at[11]),
        ]
        for copy in keep:
            copy.start()
        gx = TeamGather(me, own, lambda p: d_br.at[p], bs, br, ("zx", "zx"))
        gx.start()
        if halves == 2:
            pass_on(1)
        keep.append(pltpu.make_async_copy(gcv.at[a, h], s_cv, ls.at[12]))
        keep[-1].start()
        gx.finish()
        gm = Exchange(me, lambda p: add.at[rows_at(p, rows)], lambda p: moved.at[p], ms, mr)
        gm.start()
        bg.start(me, srcs, dsts, rest[51:])
        gm.finish()
        bg.finish()
        landed(got_f, fr.at[0])
        ff.drain()
        for dh in range(1, H):
            for g in range(halves):
                at = pl.ds(g * (w_cv // halves), w_cv // halves)
                landed(got_cv.at[dh - 1, at], vr.at[1 + (dh - 1) * 2 + g])
        cv.drain()
        for copy in keep:
            copy.wait()

    return comm_call(
        body,
        (
            jax.ShapeDtypeStruct((rows, D), F32),
            jax.ShapeDtypeStruct((8, rows, D), BF),
            jax.ShapeDtypeStruct((8, rows, m), BF),
            jax.ShapeDtypeStruct((w_cv, D), BF),
            jax.ShapeDtypeStruct((max(H - 1, 1), w_cv, D), BF),
            jax.ShapeDtypeStruct((A, nk // A, kk, F + m), BF),
            jax.ShapeDtypeStruct((nk // A, kk, F + m), BF),
            jax.ShapeDtypeStruct((8, D), F32),
            *bg.outs(),
        ),
        [ANY, VM, VM, VM, VM, VM, VM, VM] + [ANY] * nb,
        (VM, ANY, ANY, ANY, ANY, ANY, ANY, VM, *[ANY] * nb),
        [
            pltpu.VMEM((T, D), BF),
            pltpu.VMEM((2, T, D), BF),
            pltpu.VMEM((T, D), BF),
            pltpu.VMEM((1, D), F32),
            pltpu.VMEM((T, F), BF),
            pltpu.VMEM((T, F), BF),
            pltpu.VMEM((T, m), F32),
            pltpu.VMEM((T, m), BF),
            pltpu.VMEM((T, m), BF),
            pltpu.VMEM((T, D), BF),
            pltpu.VMEM((A, H, w_cv, D), BF),
            pltpu.VMEM((H, w_cv, D), BF),
            pltpu.VMEM((kk, F + m), BF),
            pltpu.VMEM((rows, D), F32),
            pltpu.VMEM((rows, D), BF),
            pltpu.VMEM((T, m), BF),
            pltpu.VMEM((2, 16, D), BF),
            pltpu.VMEM((8, 16, D), BF),
            *TeamSum.scratch(T, m),
            *TeamSum.scratch(rows, D),
            DMA((14,)),
            DMA((8, 2)),
            DMA((14,)),
            DMA((8, 2)),
            DMA((2,)),
            DMA((8,)),
            DMA((7,)),
            DMA((8,)),
            DMA((2 * H,)),
            DMA((2 * H,)),
            DMA((1,)),
            DMA((1,)),
            DMA((13,)),
            *bg.sems(),
        ],
        2,
    )(n2, halo, full, wcv, wf, upc, middle, up, *bg.arrays())


def time_back(lay, d_br, wo, gated, ghat, grstd, gate, rkv, states, mv, full, mixed, diff, w4, x, d_mid, cm_sums, s_f, fin):
    H, A, n_dev = lay.H, lay.A, lay.n
    T, m = gate.shape
    rows, D = x.shape
    heads = m // HEAD
    per = T // 2 // CHUNK
    nk, kk, _ = w4.shape
    tile = T // 4
    hk = kk // H
    w_row = D // n_dev
    nf = s_f.shape[-1]
    H1 = max(H - 1, 1)
    strided = lay.strided
    hop = fin is not None
    F = (nf - m) * 8
    k_row = hk // 4

    def body(*refs):
        d_br, wo, gated, ghat, grstd, gate, rkv, states, mv, full, mixed, diff, w4, x, d_mid, cm_sums, s_f = refs[:17]
        if hop:
            fin, refs = refs[17], refs[:17] + refs[18:]
        in_grad, o_out, total_out, fin_out, ck_out, cr_out, *four = refs[17:27]
        refs = refs[5:]
        (big, dy, adds, cl, st, obox, ibox, d_all, tsum, sums) = refs[22:32]
        (mbuf, g4, got, late, t4, first, edge) = refs[32:39]
        dn1 = in_grad
        (g_o, o_got, o_late, f_own, f_got, t_f, small, s_got) = refs[39:47]
        rn, ra, rm, rf, r_s, r_r = refs[47:53]
        cs, cr, es, er, gs, gr, os_, or_, fs, fr, xs, xr, ys, yr, ss, sr, ls, f_out, g_out, hs, hr = refs[53:]
        me = coords()
        a, b, h, l, c = (me[k] for k in ALL)
        mine = rank_of(b, l, c)
        loads = [
            pltpu.make_async_copy(d_br.at[p], big.at[pl.ds(p * rows, rows)], ls.at[p]) for p in range(8)
        ]
        loads.append(pltpu.make_async_copy(s_f.at[h], f_own, ls.at[8]))
        for copy in loads:
            copy.start()

        sem = pltpu.get_barrier_semaphore()
        others = []
        for i in range(1, n_dev):
            k = i
            dc, k = k % 2, k // 2
            dl, k = k % 2, k // 2
            dh, k = k % H, k // H
            db, da = k % 2, k // 2
            to = {
                "a": lax.rem(a + da, A),
                "b": b ^ db,
                "h": lax.rem(h + dh, H),
                "l": l ^ dl,
                "c": c ^ dc,
            }
            others.append((i, to))
            pl.semaphore_signal(sem, inc=1, device_id=to, device_id_type=MESH)
        pl.semaphore_wait(sem, n_dev - 1)
        for copy in loads[:8]:
            copy.wait()

        ones = block_ones(m)
        dec = Decay(mv[6:7])
        u = mv[7:8]
        span_all = jnp.exp(-mv[6:7] * (T // 2))
        low_t = triangle(heads, False)
        low = triangle(heads, True)
        tsum[...] = jnp.zeros_like(tsum)

        @pl.loop(0, 2 * per)
        def _(t):
            at = rows_at(t, CHUNK)
            d_gated = dot_nt(big[at], wo[...].reshape(m, D))
            g = gate[at]
            sig = 1.0 / (1.0 + jnp.exp(-g))
            hat, rstd = ghat[at], grstd[at]
            dn = d_gated * (g * sig)
            tsum[2:3] += jnp.sum(dn * hat, axis=0, keepdims=True)
            tsum[3:4] += jnp.sum(dn, axis=0, keepdims=True)
            nm = hat * mv[8:9] + mv[9:10]
            d_all[at, 3 * m :] = (d_gated * nm * sig * (1.0 + g * (1.0 - sig))).astype(BF)
            e = dn * mv[8:9]
            m1 = dot_exact(e, ones) * (1.0 / HEAD)
            m2 = dot_exact(e * hat, ones) * (1.0 / HEAD)
            dy[at] = (e - m1 - hat * m2) * rstd

        cl[...] = jnp.zeros_like(cl)

        @pl.loop(0, per)
        def _(q):
            n = per - 1 - q
            for s in range(2):
                at = rows_at(s * per + n, CHUNK)
                rd = (rkv[0, at].astype(F32) * dec.down).astype(BF)
                add = dot_tn(dy[at].astype(BF), rd) * ones
                adds[s, n] = add
                cl[s] = dec.span * cl[s] + add

        st[...] = jnp.zeros_like(st)
        chain = Chain(me, H, False, obox, ibox, cs, cr)
        chain.run(st, cl, span_all, ones)
        cf = Copies(fs)
        for dh in range(1, H):
            to = lax.rem(h + dh, H)
            cf.go(s_f.at[to], f_got.at[dh - 1], fr.at[dh - 1], {"h": to})

        if hop:
            mine_fin = fin.at[pl.ds(l * 4, 4)]
            last = h == H - 1
            to_first = remote(mine_fin.at[:, pl.ds(0, HEAD)], fin_out, hs, hr, {"h": 0})
            kept = pltpu.make_async_copy(mine_fin.at[:, pl.ds(HEAD, HEAD)], fin_out, hs)

            @pl.when(last)
            def _():
                to_first.start()

        nw = D // 8

        @pl.loop(0, 8)
        def _(q):
            at = pl.ds(pl.multiple_of(q * nw, nw), nw)
            g = dot_tn(gated[...], big[:, at]).astype(BF)
            g_o[:, :, :, at] = g.reshape(*g_o.shape[:3], nw)

        co = Copies(os_)
        if strided:
            co.go(g_o.at[1 - a], o_got, or_.at[0], {"a": 1 - a})

        @pl.loop(0, per)
        def _(q):
            n = per - 1 - q
            for s in range(2):
                at = rows_at(s * per + n, CHUNK)
                r, k, v = (rkv[i, at].astype(F32) for i in range(3))
                vb = rkv[2, at]
                rd, kg, kt = r * dec.down, k * dec.up, k * dec.tail
                rdb, kgb, ktb = rd.astype(BF), kg.astype(BF), kt.astype(BF)
                dyt = dy[at]
                dyb = dyt.astype(BF)
                state, end = states[s, n], st[s]
                endb = end.astype(BF)
                datt = jnp.where(low, dot_nt(stacked_heads(dyb), vb), 0.0).astype(BF)
                datt_t = jnp.where(low_t, dot_nt(stacked_heads(vb), dyb), 0.0).astype(BF)
                att_t = jnp.where(low_t, dot_nt(stacked_heads(kgb), rdb), 0.0).astype(BF)
                ddiag = dot_exact(dyt * v, ones)
                diag = dot_exact(r * u * k, ones)
                d_rd = own_heads(dot_nn(datt, kgb)) + dot_nn(dyb, state.astype(BF))
                d_kg = own_heads(dot_nn(datt_t, rdb))
                d_kt = dot_nn(vb, endb)
                d_v = own_heads(dot_nn(att_t, dyb)) + diag * dyt + dot_nt(ktb, endb)
                d_r = d_rd * dec.down + ddiag * u * k
                d_k = d_kg * dec.up + d_kt * dec.tail + ddiag * u * r
                d_all[at, :m] = d_r.astype(BF)
                d_all[at, m : 2 * m] = d_k.astype(BF)
                d_all[at, 2 * m : 3 * m] = d_v.astype(BF)
                tsum[1:2] += jnp.sum(ddiag * r * k, axis=0, keepdims=True)
                d_l = jnp.sum(
                    (dec.i + 1.0) * kg * d_kg
                    - dec.i * rd * d_rd
                    - (CHUNK - 1.0 - dec.i) * kt * d_kt,
                    axis=0,
                    keepdims=True,
                )
                d_l = d_l - CHUNK * dec.span * jnp.sum(state * end, axis=0, keepdims=True)
                tsum[0:1] += d_l
                st[s] = dec.span * end + adds[s, n]

        chain.finish()

        cg = Copies(gs)
        units = [(step, k, jj) for step in range(A) for k in range(2) for jj in range(2)]

        def unit(v):
            step, k, jj = units[v]
            i = lax.rem(a + 1 + step, A)
            lo = pl.ds(pl.multiple_of((i * 2 + k) * kk, kk), kk)
            src = mixed.at[pl.ds(jj * 2, 2), :, lo]
            return pltpu.make_async_copy(src, mbuf.at[v % 2], ls.at[9 + v % 2])

        unit(0).start()
        for v, (step, k, jj) in enumerate(units):
            if v + 1 < len(units):
                unit(v + 1).start()
            unit(v).wait()
            i = lax.rem(a + 1 + step, A)
            for q in range(2):
                j = jj * 2 + q
                g = dot_tn(mbuf[v % 2, q], d_all[:, j * m : (j + 1) * m])
                g4[i * 2 + k, :, j * m : (j + 1) * m] = g.astype(BF)
            if step < A - 1 and jj == 1:
                cg.go(g4.at[i * 2 + k], got.at[k], gr.at[k], {"a": 1 - a})

        difs = [
            pltpu.make_async_copy(diff.at[:, pl.ds(i * kk, kk)], mbuf.at[i // 2, i % 2], ls.at[13 + i])
            for i in range(nk)
        ]
        for copy in difs:
            copy.start()
        sums[...] = jnp.zeros_like(sums)

        def chunk_of(i):
            lo = i * kk

            def chunk(t):
                at = rows_at(t, tile)
                return tuple(
                    dot_nt(d_all[at, j * m : (j + 1) * m], w4[i, :, j * m : (j + 1) * m])
                    for j in range(4)
                )

            def put(t, v):
                big[rows_at(t, tile), lo : lo + kk] = v.astype(BF)

            def put_first(s, v):
                first[s, :, lo : lo + kk] = v

            back_rows(
                T,
                tile,
                chunk,
                tuple(full[2 + j : 3 + j, lo : lo + kk] for j in range(4)),
                lambda t: mbuf[i // 2, i % 2, rows_at(t, tile)].astype(F32),
                put,
                put_first,
                [sums.at[j : j + 1, lo : lo + kk] for j in range(4)],
            )

        for i in range(nk):
            difs[i].wait()
            chunk_of(i)
        total = TeamSum(
            me, lambda p: big.at[rows_at(p, rows)], rn, ra, rm, rf, r_s, r_r, ("xz", "xz")
        )
        total.start()
        e = Edge(me, H, first, edge, es, er)
        e.start()

        def pass_on():
            if strided:
                landed(o_got, or_.at[0])

                @pl.loop(0, H)
                def _(j):
                    g_o[a, j] = (g_o[a, j].astype(F32) + o_got[j].astype(F32)).astype(BF)

                for dh in range(1, H):
                    to = lax.rem(h + dh, H)
                    co.go(g_o.at[a, to], o_late.at[dh - 1], or_.at[dh], {"h": to})
            for k in range(2):
                landed(got.at[k], gr.at[k])

                @pl.loop(0, kk // 64)
                def _(q):
                    at = rows_at(q, 64)
                    g4[a * 2 + k, at] = (g4[a * 2 + k, at].astype(F32) + got[k, at].astype(F32)).astype(BF)

                for dh in range(1, H):
                    to = lax.rem(h + dh, H)
                    v = (dh - 1) * 2 + k
                    cg.go(
                        g4.at[a * 2 + k, rows_at(to, hk)], late.at[dh - 1, k], gr.at[2 + v], {"h": to}
                    )

        def put_dn(at, v):
            dn1[at] = v

        total.finish(put_dn, pass_on)
        e.finish(dn1)

        @pl.loop(0, rows // MIX)
        def _(t):
            at = rows_at(t, MIX)
            d = dn1[at]
            hat, rstd = norm_rows(x[at].astype(F32))
            sums[4:5] = sums[4:5] + jnp.sum(d * hat, axis=0, keepdims=True)
            sums[5:6] = sums[5:6] + jnp.sum(d, axis=0, keepdims=True)
            in_grad[at] = d_mid[at] + norm_back(d * full[0:1], hat, rstd)

        small[...] = jnp.zeros_like(small)
        per_lane = 128 // w_row
        for f in range(n_dev):
            g = pl.ds(f // per_lane * 128, 128)
            block = jnp.concatenate([sums[:, g], cm_sums[:, g]], axis=0)
            shift = (128 - w_row * (f % per_lane)) % 128
            small[f] = pltpu.roll(block, shift, axis=1) if shift else block

        if strided:
            for i in range(A):
                for j in range(H):
                    f = (((i * 2 + b) * H + j) * 2 + l) * 2 + c
                    v = (i * H + j) * w_row
                    block = tsum[:, v // 128 * 128 : v // 128 * 128 + 128]
                    shift = (128 - v % 128) % 128
                    block = pltpu.roll(block, shift, axis=1) if shift else block
                    small[f, 12:16] = block[:4]
        else:
            span = n_dev // 8
            for i in range(span):
                v = i * w_row
                block = tsum[:, v // 128 * 128 : v // 128 * 128 + 128]
                shift = (128 - v % 128) % 128
                block = pltpu.roll(block, shift, axis=1) if shift else block
                small[mine * span + i, 12:16] = block[:4]
        cv = Copies(ss)

        def flat(d):
            return (((d["a"] * 2 + d["b"]) * H + d["h"]) * 2 + d["l"]) * 2 + d["c"]

        for i, to in others:
            cv.go(small.at[flat(to)], s_got.at[i], sr.at[i], to)

        loads[8].wait()
        for dh in range(1, H):
            landed(f_got.at[dh - 1], fr.at[dh - 1])
        for k in range(2):
            for q in range(4):
                at = pl.ds(q * (hk // 4), hk // 4)
                v = f_own[k, at].astype(F32)
                for dh in range(1, H):
                    v = v + f_got[dh - 1, k, at].astype(F32)
                t_f[k * 4 + q] = v.astype(BF)
        keep = [pltpu.make_async_copy(t_f.at[mine], f_out.at[mine], ls.at[11])]
        keep[0].start()
        gf = Exchange(me, lambda p: t_f.at[p], lambda p: f_out.at[p], xs, xr)
        gf.start()
        for k in range(2):
            for dh in range(1, H):
                landed(late.at[dh - 1, k], gr.at[2 + (dh - 1) * 2 + k])
            for q in range(4):
                at = pl.ds(pl.multiple_of(h * hk + q * (hk // 4), hk // 4), hk // 4)
                v = g4[a * 2 + k, at].astype(F32)
                for dh in range(1, H):
                    v = v + late[dh - 1, k, pl.ds(q * (hk // 4), hk // 4)].astype(F32)
                t4[k * 4 + q] = v.astype(BF)
        keep.append(pltpu.make_async_copy(t4.at[mine], g_out.at[mine], ls.at[12]))
        keep[1].start()
        gg = Exchange(me, lambda p: t4.at[p], lambda p: g_out.at[p], ys, yr)
        gg.start()
        if strided:
            v = g_o[a, h].astype(F32)
            for dh in range(1, H):
                landed(o_late.at[dh - 1], or_.at[dh])
                v = v + o_late[dh - 1].astype(F32)
            o_out[...] = v
        else:
            o_out[...] = g_o[...]
        acc = small[flat(me)]
        for i, _ in others:
            landed(s_got.at[i], sr.at[i])
            acc = acc + s_got[i]
        total_out[...] = acc
        if hop:

            @pl.when(last)
            def _():
                to_first.wait_send()
                kept.start()
                kept.wait()

            @pl.when(h == 0)
            def _():
                to_first.wait_recv()

        gf.finish()
        for copy in keep:
            copy.wait()

        def from_ranks(ref, lo, n, whole):
            parts = []
            for p in range(8):
                read = lambda i, j, p=p: ref[p, :, lo + i : lo + j]
                for src, dst, many in rank_columns(lay, n, whole, p):
                    parts.append((read, n // 8, dst, src, many))
            return parts

        def into(ref):
            def put(lo, v):
                ref[:, lo : lo + 128] = v

            return put

        lay_lanes(F, from_ranks(f_out, 0, F, 1), into(ck_out))
        for p in range(8):
            cr_out[:, p * m : (p + 1) * m] = f_out[p, :, F // 8 :].astype(F32)
        gg.finish()
        for j, ref in enumerate(four):
            lay_lanes(D, from_ranks(g_out, j * m, D, HEAD), into(ref))
        for copies in (cf, co, cg, cv):
            copies.drain()

    o_shape = wo.shape[2:] if strided else wo.shape
    return comm_call(
        body,
        (
            jax.ShapeDtypeStruct((rows, D), F32),
            jax.ShapeDtypeStruct(o_shape, F32 if strided else BF),
            jax.ShapeDtypeStruct((16, 128), F32),
            jax.ShapeDtypeStruct((4, HEAD, 128), BF),
            jax.ShapeDtypeStruct((k_row, F), F32),
            *[jax.ShapeDtypeStruct((k_row, D), F32)] * 5,
        ),
        [ANY] + [VM] * 9 + [ANY] * 2 + [VM] * 4 + [ANY] * (2 if hop else 1),
        (VM, VM, VM, ANY, *[VM] * 6),
        [
            pltpu.VMEM((T, D), BF),
            pltpu.VMEM((T, m), F32),
            pltpu.VMEM((2, per, m, m), F32),
            pltpu.VMEM((2, m, m), F32),
            pltpu.VMEM((2, m, m), F32),
            pltpu.VMEM((m, 128), BF),
            pltpu.VMEM((m, 128), BF),
            pltpu.VMEM((T, 4 * m), BF),
            pltpu.VMEM((8, m), F32),
            pltpu.VMEM((8, D), F32),
            pltpu.VMEM((2, 2, T, kk), BF),
            pltpu.VMEM((nk, kk, 4 * m), BF),
            pltpu.VMEM((2, kk, 4 * m), BF),
            pltpu.VMEM((H1, 2, hk, 4 * m), BF),
            pltpu.VMEM((8, hk // 4, 4 * m), BF),
            pltpu.VMEM((2, 16, D), BF),
            pltpu.VMEM((8, 16, D), BF),
            pltpu.VMEM(wo.shape, BF),
            pltpu.VMEM(wo.shape[1:], BF),
            pltpu.VMEM((H1, *wo.shape[2:]), BF),
            pltpu.VMEM(s_f.shape[1:], BF),
            pltpu.VMEM((H1, *s_f.shape[1:]), BF),
            pltpu.VMEM((8, hk // 4, nf), BF),
            pltpu.VMEM((n_dev, 16, 128), F32),
            pltpu.VMEM((n_dev, 16, 128), F32),
            *TeamSum.scratch(rows, D),
            DMA,
            DMA,
            DMA((2,)),
            DMA((8,)),
            DMA((2 + 2 * H1,)),
            DMA((2 + 2 * H1,)),
            DMA((H,)),
            DMA((H,)),
            DMA((H1,)),
            DMA((H1,)),
            DMA((7,)),
            DMA((8,)),
            DMA((7,)),
            DMA((8,)),
            DMA((n_dev,)),
            DMA((n_dev,)),
            DMA((13 + nk,)),
            pltpu.VMEM((8, k_row, nf), BF),
            pltpu.VMEM((8, k_row, 4 * m), BF),
            DMA,
            DMA,
        ],
        3,
    )(d_br, wo, gated, ghat, grstd, gate, rkv, states, mv, full, mixed, diff, w4, x, d_mid, cm_sums, s_f, *([fin] if hop else []))


def dot(a, b, dims):
    return lax.dot_general(a, b, (dims, ((), ())), preferred_element_type=F32)


def mm(a, b):
    return dot(a, b, ((1,), (0,)))


def mm_nt(a, b):
    return dot(a, b, ((1,), (1,)))


def mm_tn(a, b):
    return dot(a, b, ((0,), (0,)))


class Layout:
    def __init__(self, mesh_shape):
        self.A, self.B, self.H, self.L, self.C = mesh_shape
        self.team = self.B * self.L * self.C
        self.n = self.team * self.A * self.H

    def of(self, D):
        self.strided = (D // self.n) % HEAD == 0
        return self

    def spread(self, v, whole):
        w = v.shape[-1] // self.n
        lead = v.shape[:-1]
        if w % whole:
            return v.reshape(*lead, self.team, -1)
        k = len(lead)
        v = v.reshape(*lead, self.A, self.B, self.H, self.L, self.C, w)
        v = v.transpose(*range(k), k + 1, k + 3, k + 4, k, k + 2, k + 5)
        return v.reshape(*lead, self.team, -1)

    def unspread(self, v, whole):
        lead = v.shape[:-2]
        w = v.shape[-1] * self.team // self.n
        if w % whole:
            return v.reshape(*lead, -1)
        k = len(lead)
        v = v.reshape(*lead, self.B, self.L, self.C, self.A, self.H, w)
        v = v.transpose(*range(k), k + 3, k, k + 4, k + 1, k + 2, k + 5)
        return v.reshape(*lead, -1)

    def rows_in(self, g):
        m = g.shape[-1]
        g = g.reshape(self.A, self.H, self.B, self.L, self.C, -1, m)
        return g.transpose(0, 2, 1, 3, 4, 5, 6).reshape(-1, m)

    def rows_out(self, g):
        m = g.shape[-1]
        g = g.reshape(self.A, self.B, self.H, self.L, self.C, -1, m)
        return g.transpose(0, 2, 1, 3, 4, 5, 6).reshape(self.A * self.H, self.team, -1, m)


def normed(v):
    mean = jnp.mean(v, axis=-1, keepdims=True)
    cent = v - mean
    rstd = lax.rsqrt(jnp.mean(cent * cent, axis=-1, keepdims=True) + EPS)
    return cent * rstd, rstd


def norm_back(e, xhat, rstd):
    m1 = jnp.mean(e, axis=-1, keepdims=True)
    m2 = jnp.mean(e * xhat, axis=-1, keepdims=True)
    return (e - m1 - xhat * m2) * rstd


def with_before(rows, halo, segs):
    v = rows.reshape(segs, -1, rows.shape[-1])
    return jnp.concatenate([halo, v[:, :-1]], axis=1).reshape(rows.shape)


def with_after(rows, segs):
    v = rows.reshape(segs, -1, rows.shape[-1])
    return (
        jnp.concatenate([v[:, 1:], jnp.zeros_like(v[:, :1])], axis=1).reshape(rows.shape),
        v[:, :1],
    )


def swap(v, axis):
    return lax.ppermute(v, axis, [(0, 1), (1, 0)])


def per_device(lay, *args):
    (x_in, up_in, start_in) = args[:3]
    vec = args[3:13]
    w_r, w_k, w_v, w_g, w_o = args[13:18]
    vec2 = args[18:22]
    w_ck, w_cv, w_cr = args[22:]
    a_at, b_at, h_at = (lax.axis_index(n) for n in ("a", "b", "h"))
    rank = (b_at * lay.L + lax.axis_index("l")) * lay.C + lax.axis_index("c")
    H = lay.H
    segs = lay.B
    D = x_in.shape[-1]
    x_own = x_in[0]
    rows = x_own.shape[0]
    T = rows * lay.team
    dcol = D // lay.team
    heads = dcol // HEAD
    half = lay.L * lay.C
    w_row = D // lay.n
    lay.of(D)
    hid = w_ck.shape[1] // lay.team

    stacked = jnp.stack([*vec, *vec2])
    nv = stacked.shape[0]
    stacked = jnp.pad(stacked, ((0, 16 - nv), (0, 128 - w_row)))
    o_own = w_o
    if not lay.strided:
        o_own = lax.all_gather(w_o, ALL, axis=0, tiled=True)
        o_own = lax.dynamic_slice_in_dim(o_own, rank * dcol, dcol, 0)
        o_own = o_own.reshape(lay.A, H, -1, D)
    (
        every, my_vecs, mixed, diff1, rkv, gate, upc, W4, W_o, gated, ghat, grstd, states, fin, middle, n2, halo_2,
        W_cv, ffn_all,
    ) = front(lay, stacked, x_own, up_in[0], (w_r, w_k, w_v, w_g), w_ck, w_cr, o_own, w_cv, start_in[0])
    W_cv = W_cv.reshape(hid, D)
    direct = lay.strided and H == 2 and lay.A == 2
    items = []
    if direct:
        blocks = fin.astype(BF).reshape(lay.A, H, HEAD, 128).transpose(1, 0, 2, 3)
        blocks = jnp.broadcast_to(blocks.reshape(H, lay.A * HEAD, 128), (4, H, lay.A * HEAD, 128))
        items = [(blocks.reshape(8, lay.A * HEAD, 128), "t")]
    else:
        nh = start_in.shape[1]
        head_ids = lay.spread(jnp.arange(nh * HEAD, dtype=jnp.int32), HEAD)
        my_heads = lax.dynamic_index_in_dim(head_ids, rank, 0, False)[::HEAD] // HEAD
        s_out = fin.reshape(heads, HEAD, 2, HEAD).transpose(2, 0, 3, 1)
        placed = jnp.zeros((segs, nh, HEAD, HEAD), BF)
        s_fin = jnp.where(h_at == lay.H - 1, s_out, 0.0).astype(BF)
        placed = placed.at[:, my_heads].set(s_fin)
        final = lax.psum_scatter(placed, "b", scatter_dimension=0, tiled=True)
        final = lax.psum_scatter(final, SEQ, scatter_dimension=1, tiled=True).astype(F32)

    wf = ffn_all.reshape(2 * lay.A, D // (2 * lay.A), -1)
    d_mid, d_br, moved, s_cv, got_cv, g_f, got_f, cm_sums, *got_fin = channel_mix(
        lay, n2, halo_2, every, W_cv, wf, upc.reshape(T, dcol), middle, up_in[0], items
    )
    layer_output = (middle + moved.transpose(1, 0, 2).reshape(rows, D).astype(F32)).astype(BF)
    g_cv = s_cv.astype(F32) + jnp.sum(got_cv.astype(F32), axis=0)

    def own_half(g, got):
        part = lax.dynamic_index_in_dim(g, a_at, 0, False).astype(F32) + got.astype(F32)
        part = part.astype(BF).reshape(part.shape[0], H, -1, part.shape[-1])
        return part.transpose(1, 0, 2, 3)

    s_f = own_half(g_f, got_f)
    w4 = W4.reshape(2 * lay.A, D // (2 * lay.A), -1)
    input_grad, g_o, small, fin, g_ck, g_cr, g_r, g_k, g_v, g_w = time_back(
        lay, d_br, W_o, gated, ghat, grstd, gate, rkv, states, my_vecs, every, mixed, diff1, w4, x_own, d_mid,
        cm_sums, s_f, got_fin[0] if direct else None,
    )
    if direct:
        fin = jnp.where(b_at == 0, fin[:, :, :HEAD], fin[:, :, HEAD:])
        final = fin.transpose(0, 2, 1)[None].astype(F32)
    if not lay.strided:
        g_o = jnp.zeros((D, D), BF).at[rank * dcol + jnp.arange(dcol)].set(g_o.reshape(dcol, D))
        g_o = lax.psum_scatter(g_o, ALL, scatter_dimension=0, tiled=True).astype(F32)
    small = small[:, :w_row]
    order = (4, 5, 0, 1, 2, 3, 12, 13, 14, 15, 10, 11, 8, 9)
    small = [small[i] for i in order]

    return (
        layer_output[None],
        input_grad[None],
        final,
        *small[:10],
        g_r,
        g_k,
        g_v,
        g_w,
        g_o,
        *small[10:],
        g_ck,
        g_cv,
        g_cr,
    )


def solution(mesh):
    n_seg, n_seq = mesh.devices.shape
    shape = (n_seg // 2, 2, n_seq // 4, 2, 2)
    view = Mesh(mesh.devices.reshape(shape), ALL)
    lay = Layout(shape)
    seg = ("a", "b")
    vec, mat = P(ALL), P(ALL, None)
    tok = P(seg, SEQ, None)

    def step(*args):
        return per_device(lay, *args)

    return jax.shard_map(
        step,
        mesh=view,
        in_specs=(tok, tok, P(seg, None, None, None), *[vec] * 10, *[mat] * 5, *[vec] * 4, *[mat] * 3),
        out_specs=(tok, tok, P(seg, SEQ, None, None), *[vec] * 10, *[mat] * 5, *[vec] * 4, *[mat] * 3),
        check_vma=False,
    )
```

```python
import jax
import jax.numpy as jnp
from jax import lax
from jax.experimental import pallas as pl
from jax.experimental.pallas import tpu as pltpu
from jax.sharding import Mesh, PartitionSpec as P

TEAM = ("b", "l", "c")
TEAMS = ("a", "h")
SEQ = ("h", "l", "c")
ALL = ("a", "b", "h", "l", "c")
HEAD = 64
CHUNK = 128
EPS = 1e-05
GROUP_EPS = 0.00064
BF = jnp.bfloat16
F32 = jnp.float32


MESH = pl.DeviceIdType.MESH
DMA = pltpu.SemaphoreType.DMA
VMEM_BYTES = 62 << 20


def coords():
    return {name: lax.axis_index(name) for name in ALL}


def rank_of(b, l, c):
    return (b * 2 + l) * 2 + c


def remote(src, dst, sent, landed, to):
    return pltpu.make_async_remote_copy(
        src_ref=src,
        dst_ref=dst,
        send_sem=sent,
        recv_sem=landed,
        device_id=to,
        device_id_type=MESH,
    )


def mates(me):
    for m in range(1, 8):
        yield m, {"b": me["b"] ^ (m >> 2), "l": me["l"] ^ ((m >> 1) & 1), "c": me["c"] ^ (m & 1)}


def greet(me, H, column, across):
    sem = pltpu.get_barrier_semaphore()
    count = 0
    for dh in range(H if column else 1):
        h = lax.rem(me["h"] + dh, H)
        for m in range(8):
            if dh == 0 and m == 0:
                continue
            to = {
                "b": me["b"] ^ (m >> 2),
                "h": h if column else me["h"],
                "l": me["l"] ^ ((m >> 1) & 1),
                "c": me["c"] ^ (m & 1),
            }
            pl.semaphore_signal(sem, inc=1, device_id=to, device_id_type=MESH)
            count += 1
    if across:
        pl.semaphore_signal(sem, inc=1, device_id={"a": 1 - me["a"]}, device_id_type=MESH)
        count += 1
    pl.semaphore_wait(sem, count)


class Copies:
    def __init__(self, sems):
        self.sems, self.k, self.open = sems, 0, []

    def go(self, src, dst, landed, to, when=None):
        copy = remote(src, dst, self.sems.at[self.k], landed, to)
        self.k += 1
        if when is None:
            copy.start()
        else:
            pl.when(when)(copy.start)
        self.open.append(copy)
        return copy

    def drain(self):
        for copy in self.open:
            copy.wait_send()


def inner(me, H):
    return me["h"] != me["l"] if H == 2 else me["h"] < 0


def landed(ref, sem):
    remote(ref, ref, sem, sem, {"c": 1 - lax.axis_index("c")}).wait_recv()


def upper(ref, half):
    n = ref.shape[0] // 2
    return ref.at[pl.ds(half * n, n)]


class TeamGather:
    def __init__(self, me, own, view, send, recv, via=("xz", "zx")):
        self.me, self.own, self.view, self.recv, self.via = me, own, view, recv, via
        self.copies = Copies(send)
        self.tx, self.tz, self.ts = {"b": 1 - me["b"]}, {"l": 1 - me["l"]}, {"c": 1 - me["c"]}

    def put(self, src, p, half, to):
        self.copies.go(src, upper(self.view(p), half), self.recv.at[p, half], to)

    def start(self):
        mine = rank_of(self.me["b"], self.me["l"], self.me["c"])
        order = [(half, self.tx if self.via[half] == "xz" else self.tz) for half in range(2)]
        order += [(half, self.tz if self.via[half] == "xz" else self.tx) for half in range(2)]
        order += [(0, self.ts), (1, self.ts)]
        for half, to in order:
            self.put(upper(self.own, half), mine, half, to)

    def finish(self):
        b, l, c = self.me["b"], self.me["l"], self.me["c"]
        px, pz, pd = rank_of(1 - b, l, c), rank_of(b, 1 - l, c), rank_of(1 - b, 1 - l, c)
        order = [
            (px, half, self.tz) if self.via[half] == "xz" else (pz, half, self.tx)
            for half in range(2)
        ]
        order += [
            (pz, half, None) if self.via[half] == "xz" else (px, half, None) for half in range(2)
        ]
        for p, half, on in order + [(pd, 0, None), (pd, 1, None)]:
            block = upper(self.view(p), half)
            landed(block, self.recv.at[p, half])
            if on is not None:
                self.put(block, p, half, on)
            self.put(block, p, half, self.ts)
        for q in range(4):
            p = q * 2 + 1 - c
            for half in range(2):
                landed(upper(self.view(p), half), self.recv.at[p, half])
        self.copies.drain()


class TeamSum:
    def __init__(self, me, part, near, acc, mid, far, send, recv, via=("xz", "zx")):
        self.me, self.part, self.near, self.acc, self.mid, self.far = me, part, near, acc, mid, far
        self.recv, self.via = recv, via
        self.copies = Copies(send)

    def start(self):
        b, l, c = self.me["b"], self.me["l"], self.me["c"]
        self.spots = [(b, l), (1 - b, l), (b, 1 - l), (1 - b, 1 - l)]
        for i in (3, 1, 2, 0):
            bb, ll = self.spots[i]
            self.copies.go(
                self.part(rank_of(bb, ll, 1 - c)), self.near.at[i], self.recv.at[i], {"c": 1 - c}
            )

    def tiles(self, rows, body):
        step = max(16, 65536 // self.near.shape[2])

        @pl.loop(0, rows // step)
        def _(t):
            body(pl.ds(pl.multiple_of(t * step, step), step))

    def pair(self, i, write):
        bb, ll = self.spots[i]
        landed(self.near.at[i], self.recv.at[i])
        mine = self.part(rank_of(bb, ll, self.me["c"]))
        self.tiles(
            self.near.shape[1], lambda at: write(at, mine[at].astype(F32) + self.near[i, at].astype(F32))
        )

    def finish(self, write, then=lambda: None, between=lambda: None):
        b, l = self.me["b"], self.me["l"]
        tx, tz = {"b": 1 - b}, {"l": 1 - l}
        acc, mid, far, recv, go = self.acc, self.mid, self.far, self.recv, self.copies.go
        n = mid.shape[1]
        hops = [
            (tx, 0, tz, 1) if self.via[half] == "xz" else (tz, 1, tx, 0) for half in range(2)
        ]
        for i in (3, 1, 2):

            def put(at, v):
                acc[i - 1, at] = v.astype(BF)

            self.pair(i, put)
            if i == 3:
                for half, (one, _, _, _) in enumerate(hops):
                    go(upper(acc.at[2], half), mid.at[half], recv.at[4 + half], one)
        between()
        for half, (one, direct, two, other) in enumerate(hops):
            landed(mid.at[half], recv.at[4 + half])
            into, came = upper(acc.at[other], half), mid.at[half]

            def add(at):
                into[at] = (into[at].astype(F32) + came[at].astype(F32)).astype(BF)

            self.tiles(n, add)
            go(into, upper(far.at[other], half), recv.at[8 + half], two)
            go(upper(acc.at[direct], half), upper(far.at[direct], half), recv.at[6 + half], one)
        then()
        for half, (_, direct, _, other) in enumerate(hops):
            landed(upper(far.at[direct], half), recv.at[6 + half])
            landed(upper(far.at[other], half), recv.at[8 + half])

        def last(at, v):
            write(at, v + far[0, at].astype(F32) + far[1, at].astype(F32))

        self.pair(0, last)
        self.copies.drain()

    @staticmethod
    def scratch(R, C):
        return [
            pltpu.VMEM((4, R, C), BF),
            pltpu.VMEM((3, R, C), BF),
            pltpu.VMEM((2, R // 2, C), BF),
            pltpu.VMEM((2, R, C), BF),
            DMA((10,)),
            DMA((10,)),
        ]


class TeamsGather:
    def __init__(self, me, H, source, out, send, near, far, team=None, count=2):
        self.me, self.H, self.source, self.out = me, H, source, out
        self.near, self.far, self.team, self.count = near, far, team, count
        self.held = []
        self.copies = Copies(send)

    @staticmethod
    def sems(H, count=2):
        return [DMA((7 + count * (2 * H - 1),)), DMA((8,)), DMA((2 * H, count))]

    def groups(self, only=None):
        b, n = self.me["b"], 8 // self.count
        for g in range(self.count):
            if only is None or g in only:
                at = g * n
                yield g, (b if at < 4 else 1 - b), at % 4, n

    def block(self, a, bb, h, lo, n):
        return self.out.at[a, bb, h, pl.ds(lo, n)]

    def start(self):
        me = self.me
        a, b, h, l, c = (me[n] for n in ALL)
        for m, to in mates(me):
            p = rank_of(to["b"], to["l"], to["c"])
            mine = rank_of(b, l, c)
            self.copies.go(self.source(p), self.out.at[a, b, h, l * 2 + c], self.near.at[mine], to)

    def spread(self, local=None, only=None):
        me = self.me
        a, b, h, l, c = (me[n] for n in ALL)
        if local is not None:
            local.wait()
        for g, bb, lo, n in self.groups(only):
            block = self.block(a, bb, h, lo, n)
            src = block
            if self.team is not None:
                src = self.team.at[pl.ds(bb * 4 + lo, n)]
            else:
                for m in range(1 - g, 4):
                    ll, cc = l ^ (m >> 1), c ^ (m & 1)
                    landed(self.out.at[a, bb, h, ll * 2 + cc], self.near.at[rank_of(bb, ll, cc)])
            for dh in range(1, self.H):
                to = lax.rem(h + dh, self.H)
                when = jnp.logical_not(inner(me, self.H))
                copy = self.copies.go(src, block, self.far.at[dh, g], {"h": to}, when)
                self.held.append((g, copy))
            self.copies.go(src, block, self.far.at[0, g], {"a": 1 - a})

    def release(self, only=None):
        for g, copy in self.held:
            if only is None or g in only:
                pl.when(inner(self.me, self.H))(copy.start)

    def forward(self, only=None):
        a, h, H = self.me["a"], self.me["h"], self.H
        for g, bb, lo, n in self.groups(only):
            for dh in range(1, H):
                block = self.block(a, bb, lax.rem(h - dh + H, H), lo, n)
                landed(block, self.far.at[dh, g])
                self.copies.go(block, block, self.far.at[H - 1 + dh, g], {"a": 1 - a})

    def finish(self):
        a, h, H = self.me["a"], self.me["h"], self.H
        for g, bb, lo, n in self.groups():
            landed(self.block(1 - a, bb, h, lo, n), self.far.at[0, g])
            for dh in range(1, H):
                block = self.block(1 - a, bb, lax.rem(h - dh + H, H), lo, n)
                landed(block, self.far.at[H - 1 + dh, g])
        self.copies.drain()


class Halo:
    def __init__(self, me, H, own, out, send, recv):
        self.me, self.H, self.own, self.out, self.send, self.recv = me, H, own, out, send, recv
        self.last = (me["l"] == 1) & (me["c"] == 1) & (me["h"] < H - 1)

    def each(self):
        me = self.me
        n = self.own.shape[0]
        for p in range(8):
            to = {
                "b": p >> 2,
                "h": jnp.minimum(me["h"] + 1, self.H - 1),
                "l": (p >> 1) & 1,
                "c": p & 1,
            }
            src = self.own.at[pl.ds(n - 16, 16)]
            yield remote(src, self.out.at[me["b"]], self.send.at[p], self.recv.at[me["b"]], to)

    def start(self):
        if self.H == 1:
            return

        @pl.when(self.last)
        def _():
            for copy in self.each():
                copy.start()

    def finish(self):
        if self.H == 1:
            return

        @pl.when(self.me["h"] > 0)
        def _():
            for b in range(2):
                landed(self.out.at[b], self.recv.at[b])

        @pl.when(self.last)
        def _():
            for copy in self.each():
                copy.wait_send()


class Edge:
    def __init__(self, me, H, first, got, send, recv):
        self.me, self.H, self.first, self.got, self.send, self.recv = me, H, first, got, send, recv

    def each(self):
        me = self.me
        mine = rank_of(me["b"], me["l"], me["c"])
        for b in range(2):
            to = {"b": b, "h": jnp.maximum(me["h"] - 1, 0), "l": 1, "c": 1}
            yield remote(self.first.at[b], self.got.at[mine], self.send.at[b], self.recv.at[mine], to)

    def start(self):
        if self.H == 1:
            return

        @pl.when(self.me["h"] > 0)
        def _():
            for copy in self.each():
                copy.start()

    def finish(self, out):
        if self.H == 1:
            return
        me = self.me

        @pl.when((me["l"] == 1) & (me["c"] == 1) & (me["h"] < self.H - 1))
        def _():
            for p in range(8):
                landed(self.got.at[p], self.recv.at[p])
            total = self.got[0, 0:1].astype(F32)
            for p in range(1, 8):
                total = total + self.got[p, 0:1].astype(F32)
            n = out.shape[0]
            out[n - 1 : n] = out[n - 1 : n] + total

        @pl.when(me["h"] > 0)
        def _():
            for copy in self.each():
                copy.wait_send()


class Exchange:
    def __init__(self, me, source, out, send, recv):
        self.me, self.source, self.out, self.recv = me, source, out, recv
        self.copies = Copies(send)

    def start(self):
        mine = rank_of(self.me["b"], self.me["l"], self.me["c"])
        for m, to in mates(self.me):
            p = rank_of(to["b"], to["l"], to["c"])
            self.copies.go(self.source(p), self.out(mine), self.recv.at[mine], to)

    def finish(self):
        for m, to in mates(self.me):
            p = rank_of(to["b"], to["l"], to["c"])
            landed(self.out(p), self.recv.at[p])
        self.copies.drain()


ANY = pl.BlockSpec(memory_space=pl.ANY)
VM = pl.BlockSpec(memory_space=pltpu.VMEM)


def comm_call(body, outs, in_specs, out_specs, scratch, cid):
    return pl.pallas_call(
        body,
        out_shape=outs,
        in_specs=in_specs,
        out_specs=out_specs,
        scratch_shapes=scratch,
        compiler_params=pltpu.CompilerParams(
            collective_id=cid, has_side_effects=True, vmem_limit_bytes=VMEM_BYTES
        ),
    )


def dot_nn(a, b):
    return jnp.dot(a, b, preferred_element_type=F32)


def dot_nt(a, b):
    return lax.dot_general(a, b, (((1,), (1,)), ((), ())), preferred_element_type=F32)


def dot_tn(a, b):
    return lax.dot_general(a, b, (((0,), (0,)), ((), ())), preferred_element_type=F32)


MIX = 32


def rows_at(i, n):
    return pl.ds(pl.multiple_of(i * n, n), n)


class RowsGather:
    def __init__(self, me, H, own, out, send, recv, at=None, inner_first=False):
        self.me, self.H, self.own, self.out, self.recv, self.at = me, H, own, out, recv, at
        self.first = inner(me, H)
        if not inner_first:
            self.first = jnp.logical_not(self.first)
        self.copies = Copies(send)

    @staticmethod
    def sems(H):
        return [DMA((2 * H - 1,)), DMA((2 * H,))]

    def block(self, a, h):
        return self.out.at[a, h] if self.at is None else self.out.at[a, h, self.at]

    def start(self):
        a, h = self.me["a"], self.me["h"]
        block = self.block(a, h)
        self.held = []
        for dh in range(1, self.H):
            to = lax.rem(h + dh, self.H)
            self.held.append(self.copies.go(self.own, block, self.recv.at[dh], {"h": to}, self.first))
        self.copies.go(self.own, block, self.recv.at[0], {"a": 1 - a})

    def release(self):
        for copy in self.held:
            pl.when(jnp.logical_not(self.first))(copy.start)

    def forward(self):
        a, h, H = self.me["a"], self.me["h"], self.H
        for dh in range(1, H):
            block = self.block(a, lax.rem(h - dh + H, H))
            landed(block, self.recv.at[dh])
            self.copies.go(block, block, self.recv.at[H - 1 + dh], {"a": 1 - a})

    def finish(self):
        a, h, H = self.me["a"], self.me["h"], self.H
        landed(self.block(1 - a, h), self.recv.at[0])
        for dh in range(1, H):
            landed(self.block(1 - a, lax.rem(h - dh + H, H)), self.recv.at[H - 1 + dh])
        self.copies.drain()


def join_lanes(pieces, width):
    per = 128 // width
    out = []
    for g in range(0, len(pieces), per):
        acc = pieces[g]
        for k in range(1, per):
            acc = acc + pltpu.roll(pieces[g + k], width * k, axis=1)
        out.append(acc)
    return jnp.concatenate(out, axis=1) if len(out) > 1 else out[0]


def norm_rows(v):
    mean = jnp.mean(v, axis=-1, keepdims=True)
    cent = v - mean
    rstd = lax.rsqrt(jnp.mean(cent * cent, axis=-1, keepdims=True) + EPS)
    return cent * rstd, rstd


def mix_rows(read, first, carry, shares, write, tiles, rows):
    per = tiles // 2

    @pl.loop(0, tiles)
    def _(p):
        n = read(p)
        prev = jnp.where(lax.rem(p, per) == 0, first(p // per), carry[...])
        row = lax.broadcasted_iota(jnp.int32, n.shape, 0)
        before = jnp.where(row == 0, prev, pltpu.roll(n, 1, axis=0))
        carry[...] = n[rows - 1 : rows]
        diff = n - before
        for i, s in enumerate(shares):
            write(i, p, (before + s * diff).astype(BF))
        write(None, p, diff.astype(BF))


def block_ones(m):
    row = lax.broadcasted_iota(jnp.int32, (m, m), 0) // HEAD
    col = lax.broadcasted_iota(jnp.int32, (m, m), 1) // HEAD
    return jnp.where(row == col, 1.0, 0.0).astype(F32)


def dot_exact(a, b):
    return jnp.dot(a, b, preferred_element_type=F32, precision=lax.Precision.HIGHEST)


class Decay:
    def __init__(self, lam):
        m = lam.shape[1]
        i = lax.broadcasted_iota(jnp.int32, (CHUNK, m), 0).astype(F32)
        self.i = i
        self.down = jnp.exp(-lam * i)
        self.up = jnp.exp(lam * (i + 1.0))
        self.tail = jnp.exp(-lam * (CHUNK - 1.0 - i))
        self.span = jnp.exp(-lam * CHUNK)


def stacked_heads(v):
    m = v.shape[1]
    lane = lax.broadcasted_iota(jnp.int32, v.shape, 1) // HEAD
    zero = jnp.zeros_like(v)
    return jnp.concatenate([jnp.where(lane == g, v, zero) for g in range(m // HEAD)], axis=0)


def own_heads(v):
    m = v.shape[1]
    lane = lax.broadcasted_iota(jnp.int32, (CHUNK, m), 1) // HEAD
    out = v[:CHUNK]
    for g in range(1, m // HEAD):
        out = jnp.where(lane == g, v[g * CHUNK : (g + 1) * CHUNK], out)
    return out


def triangle(heads, low):
    shape = (heads * CHUNK, CHUNK)
    row = lax.rem(lax.broadcasted_iota(jnp.int32, shape, 0), CHUNK)
    col = lax.broadcasted_iota(jnp.int32, shape, 1)
    return row > col if low else row < col


def squeeze(s0, s1):
    def fold(s):
        out = s[:, :128]
        for g in range(1, s.shape[1] // 128):
            out = out + s[:, g * 128 : (g + 1) * 128]
        return out + pltpu.roll(out, HEAD, axis=1)

    lane = lax.broadcasted_iota(jnp.int32, (s0.shape[0], 128), 1)
    return jnp.where(lane < HEAD, fold(s0), fold(s1))


def widen(p, second, ones):
    lane = lax.broadcasted_iota(jnp.int32, p.shape, 1)
    keep = (lane >= HEAD) if second else (lane < HEAD)
    both = jnp.where(keep, p, pltpu.roll(p, HEAD, axis=1))
    return jnp.concatenate([both] * (ones.shape[1] // 128), axis=1) * ones


class Chain:
    def __init__(self, me, H, ahead, out_box, in_box, send, recv):
        h = me["h"]
        self.h, self.H = h, H
        nxt = jnp.minimum(h + 1, H - 1) if ahead else jnp.maximum(h - 1, 0)
        self.has_next = (h < H - 1) if ahead else (h > 0)
        self.has_prev = (h > 0) if ahead else (h < H - 1)
        self.out_box, self.in_box = out_box, in_box
        self.copy = remote(out_box, in_box, send, recv, {"h": nxt})

    def run(self, state, closing, span_all, ones):
        if self.H == 1:
            return

        @pl.when(self.has_prev)
        def _():
            self.copy.wait_recv()
            p = self.in_box[...].astype(F32)
            for s in range(2):
                state[s] = widen(p, s == 1, ones)

        @pl.when(self.has_next)
        def _():
            out = squeeze(*(span_all * state[s] + closing[s] for s in range(2)))
            self.out_box[...] = out.astype(BF)
            self.copy.start()

    def finish(self):
        if self.H == 1:
            return

        @pl.when(self.has_next)
        def _():
            self.copy.wait_send()


def window(read, width, s):
    if s < 0:
        return pltpu.roll(read(0, 128).astype(F32), -s, axis=1)
    t, off = s // 128 * 128, s % 128
    if off == 0:
        return read(t, t + 128).astype(F32)
    if t + 256 <= width:
        return pltpu.roll(read(t, t + 256).astype(F32), 256 - off, axis=1)[:, :128]
    return pltpu.roll(read(t, t + 128).astype(F32), 128 - off, axis=1)


def lay_lanes(width, parts, put):
    for lo in range(0, width, 128):
        out = None
        for read, wide, src, dst, n in parts:
            d0, d1 = max(dst - lo, 0), min(dst + n - lo, 128)
            if d0 >= d1:
                continue
            v = window(read, wide, src + lo - dst)
            if out is not None:
                lane = lax.broadcasted_iota(jnp.int32, v.shape, 1)
                v = jnp.where((lane >= d0) & (lane < d1), v, out)
            out = v
        put(lo, out)


def rank_columns(lay, n, whole, p):
    w, m = n // lay.n, n // 8
    if w % whole:
        return [(p * m, 0, m)]
    b, l, c = p >> 2, (p >> 1) & 1, p & 1
    teams = [(i, j) for i in range(lay.A) for j in range(lay.H)]
    return [
        (((((i * 2 + b) * lay.H + j) * 2 + l) * 2 + c) * w, k * w, w) for k, (i, j) in enumerate(teams)
    ]


def front(lay, vecs, x, up, w4, w_ck, w_cr, w_o, w_cv, start):
    H, A = lay.H, lay.A
    grid = (A, 2, H, 4)
    rows, D = x.shape
    T = 8 * rows
    m = D // 8
    w_row = D // lay.n
    kk = D // (2 * A)
    heads = m // HEAD
    per = T // 2 // CHUNK
    bring_o = lay.strided
    wo_shape = (A, H, m // (A * H), D)
    cv_rows = w_cv.shape[0]
    F = w_ck.shape[1]
    nf = F // 8 + m
    k_row = w_ck.shape[0]
    early = cv_rows // 2 // 16 * 16 if cv_rows % 16 == 0 else 0

    def body(*refs):
        vecs, x, up, w_r, w_k, w_v, w_g, w_ck, w_cr, w_o, w_cv, start = refs[:12]
        refs = refs[4:]
        full, mine_v, mixed, diff, rkv, gate, upc, w_out = refs[8:16]
        wo, gated, ghat, grstd, states, fin, middle, n2, halo2, wcv, wf = refs[16:27]
        va, xg, halo, hn, carry, mx, df, wa, wos, team = refs[27:37]
        adds, st, cl, obox, ibox, own = refs[37:43]
        near, acc, mid, far, ss, sr = refs[43:49]
        vs, vn, vf, xs, xr, hs, hr, us, ur, ws, wn, wf_, qs, qr, os_, or_ = refs[49:65]
        es, er, cs, cr, ts, tr, fs, fn, ff, gs, gr, ks, kr, ls = refs[65:79]
        w, later, sbuf, zbuf, bs, br = refs[79:]
        part = xg
        me = coords()
        a, b, h, l, c = (me[n] for n in ALL)
        mine = rank_of(b, l, c)

        def cols(ref, p):
            return ref.at[:, pl.ds(pl.multiple_of(p * m, m), m)]

        for p in range(8):
            for j, ref in enumerate((w_r, w_k, w_v, w_g)):
                read = lambda lo, hi, ref=ref: ref[:, lo:hi]
                parts = [(read, D, *at) for at in rank_columns(lay, D, HEAD, p)]

                def put_w(lo, v, p=p, j=j):
                    w[p, :, j * m + lo : j * m + lo + 128] = v.astype(BF)

                lay_lanes(m, parts, put_w)

        local = [
            pltpu.make_async_copy(w.at[mine], wa.at[a, b, h, l * 2 + c], ls.at[0]),
            pltpu.make_async_copy(x, xg.at[rows_at(mine, rows)], ls.at[2]),
            pltpu.make_async_copy(cols(up, mine), upc.at[mine], ls.at[3]),
            pltpu.make_async_copy(vecs, va.at[a, b, h, l * 2 + c], ls.at[4]),
            pltpu.make_async_copy(w_o, wos.at[a, h] if bring_o else wos, ls.at[5]),
            pltpu.make_async_copy(w_cv, wcv.at[a, h], ls.at[6]),
        ]
        for copy in local:
            copy.start()
        greet(me, H, True, True)
        gw = TeamsGather(me, H, lambda p: w.at[p], wa, ws, wn, wf_)
        gv = TeamsGather(me, H, lambda p: vecs, va, vs, vn, vf)
        gx = TeamGather(me, x, lambda p: xg.at[rows_at(p, rows)], xs, xr, ("zx", "zx"))
        gh = Halo(me, H, x, halo, hs, hr)
        gu = Exchange(me, lambda p: cols(up, p), lambda p: upc.at[p], us, ur)
        gq = Exchange(me, lambda p: later.at[p], lambda p: team.at[p], qs, qr)
        gf = TeamsGather(me, H, None, wf, fs, fn, ff, team, 4)
        if bring_o:
            go = RowsGather(me, H, w_o, wos, os_, or_)
        top, rest = pl.ds(0, early), pl.ds(early, cv_rows - early)
        if early:
            ge = RowsGather(me, H, w_cv.at[top], wcv, es, er, top, True)
        gc = RowsGather(me, H, w_cv.at[rest], wcv, ts, tr, rest, True)
        def head(bb, k):
            if lay.strided:
                return (((k // H * 2 + bb) * H + k % H) * 2 + l) * 2 + c
            return rank_of(bb, l, c) * heads + k

        near_states = [
            pltpu.make_async_copy(start.at[head(b, k)], sbuf.at[b, k], ls.at[14 + k]) for k in range(heads)
        ]
        far_states = [
            remote(start.at[head(1 - b, k)], sbuf.at[b, k], bs.at[k], br.at[k], {"b": 1 - b})
            for k in range(heads)
        ]
        gv.start()
        gh.start()
        gw.start()
        for copy in near_states + far_states:
            copy.start()
        if early:
            ge.start()
        gc.start()
        gx.start()
        gv.spread(local[3])
        gv.release()
        gv.forward()
        gw.spread(local[0])
        gv.finish()
        local[1].wait()
        gx.finish()
        gw.release()
        gu.start()
        for p in range(8):
            parts = [(lambda lo, hi: w_ck[:, lo:hi], F, *at) for at in rank_columns(lay, F, 1, p)]

            def put_ck(lo, v, p=p):
                later[p, :, lo : lo + 128] = v.astype(BF)

            lay_lanes(F // 8, parts, put_ck)
            later[p, :, F // 8 :] = w_cr[:, p * m : (p + 1) * m]
        mine_team = pltpu.make_async_copy(later.at[mine], team.at[mine], ls.at[1])
        mine_team.start()
        gq.start()
        gw.forward((0,))
        gh.finish()

        def piece(*at):
            return va[at].astype(F32)

        flat = [
            piece(i, j, k, q) for i in range(A) for j in range(2) for k in range(H) for q in range(4)
        ]
        full[...] = join_lanes(flat, w_row)
        if lay.strided:
            held = [piece(i, b, k, l * 2 + c) for i in range(A) for k in range(H)]
            mine_v[...] = join_lanes(held, w_row)
        else:
            mine_v[...] = full[:, pl.ds(pl.multiple_of(mine * m, m), m)]
        gain, bias = full[0:1], full[1:2]
        for s in range(2):
            row = (norm_rows(halo[s].astype(F32))[0] * gain + bias)[15:16]
            hn[s] = jnp.where(h > 0, row, jnp.zeros_like(row))

        def write(i, p, v):
            if i is None:
                df[rows_at(p, MIX)] = v
            else:
                mx[i, rows_at(p, MIX)] = v

        mix_rows(
            lambda p: norm_rows(xg[rows_at(p, MIX)].astype(F32))[0] * gain + bias,
            lambda s: hn[s],
            carry,
            [full[2 + i : 3 + i] for i in range(4)],
            write,
            T // MIX,
            MIX,
        )
        keep = [
            pltpu.make_async_copy(mx, mixed, ls.at[7]),
            pltpu.make_async_copy(df, diff, ls.at[8]),
        ]
        for copy in keep:
            copy.start()
        gw.forward((1,))
        if bring_o:
            go.start()
            go.release()
        mine_team.wait()
        gq.finish()
        keep += [
            pltpu.make_async_copy(team.at[pl.ds(0, 4)], wf.at[a, 0, h], ls.at[11]),
            pltpu.make_async_copy(team.at[pl.ds(4, 4)], wf.at[a, 1, h], ls.at[12]),
        ]
        for copy in keep[2:]:
            copy.start()
        gf.spread(None, (0, 1, 2))
        gf.release((0,))
        gw.finish()
        keep.append(pltpu.make_async_copy(wa, w_out, ls.at[9]))
        keep[-1].start()
        for j in range(4):

            @pl.loop(0, 4)
            def _(t):
                at = rows_at(t, T // 4)
                acc = jnp.zeros((T // 4, m), F32)
                for i in range(A):
                    for k in range(2):
                        lo = (i * 2 + k) * kk
                        wt = wa[i, k, :, :, :, j * m : (j + 1) * m].reshape(kk, m)
                        acc = acc + dot_nn(mx[j, at, lo : lo + kk], wt)
                if j < 3:
                    rkv[j, at] = acc.astype(BF)
                else:
                    gate[at] = acc

        ones = block_ones(m)
        dec = Decay(mine_v[6:7])
        u = mine_v[7:8]
        span_all = jnp.exp(-mine_v[6:7] * (T // 2))

        def tile(i, s, n):
            return rkv[i, rows_at(s * per + n, CHUNK)].astype(F32)

        cl[...] = jnp.zeros_like(cl)

        @pl.loop(0, per)
        def _(n):
            for s in range(2):
                kt = (tile(1, s, n) * dec.tail).astype(BF)
                v = rkv[2, rows_at(s * per + n, CHUNK)]
                add = dot_tn(v, kt) * ones
                adds[s, n] = add
                cl[s] = dec.span * cl[s] + add

        for copy in near_states:
            copy.wait()
        for copy in far_states:
            copy.wait_send()
        for k in range(heads):
            landed(sbuf.at[1 - b, k], br.at[k])
        odd = lax.rem(lax.broadcasted_iota(jnp.int32, (m, 128), 0) // HEAD, 2) == 1
        zbuf[...] = jnp.zeros_like(zbuf)
        for s in range(2):
            for k in range(heads):
                zbuf[k * HEAD : (k + 1) * HEAD, :HEAD] = sbuf[s, k]
            z = zbuf[...]
            z = jnp.where(odd, pltpu.roll(z, HEAD, axis=1), z)
            z = (jnp.concatenate([z] * (m // 128), axis=1) * ones).T
            st[s] = jnp.where(h > 0, jnp.zeros_like(z), z)
        chain = Chain(me, H, True, obox, ibox, cs, cr)
        chain.run(st, cl, span_all, ones)
        gf.release((1, 2))
        local[4].wait()
        if bring_o:
            go.forward()
        low = triangle(heads, True)

        @pl.loop(0, per)
        def _(n):
            for s in range(2):
                at = rows_at(s * per + n, CHUNK)
                r, k, v = (tile(i, s, n) for i in range(3))
                vb = rkv[2, at]
                rd = (r * dec.down).astype(BF)
                kg = (k * dec.up).astype(BF)
                state = st[s]
                states[s, n] = state
                att = jnp.where(low, dot_nt(stacked_heads(rd), kg), 0.0).astype(BF)
                y = own_heads(dot_nn(att, vb)) + dot_nt(rd, state.astype(BF))
                y = y + dot_exact(r * u * k, ones) * v
                st[s] = dec.span * state + adds[s, n]
                mean = dot_exact(y, ones) * (1.0 / HEAD)
                cent = y - mean
                rstd = lax.rsqrt(dot_exact(cent * cent, ones) * (1.0 / HEAD) + GROUP_EPS)
                hat = cent * rstd
                ghat[at] = hat
                grstd[at] = rstd
                g = gate[at]
                silu = g / (1.0 + jnp.exp(-g))
                gated[at] = ((hat * mine_v[8:9] + mine_v[9:10]) * silu).astype(BF)

        fin[...] = squeeze(st[0], st[1])
        chain.finish()
        if bring_o:
            go.finish()
        keep.append(pltpu.make_async_copy(wos, wo, ls.at[13]))
        keep[-1].start()

        @pl.loop(0, 8)
        def _(p):
            g = gated[rows_at(p, rows)]
            w = wos[...].reshape(m, D)
            for q in range(4):
                lo = q * (D // 4)
                part[rows_at(p, rows), lo : lo + D // 4] = dot_nn(g, w[:, lo : lo + D // 4]).astype(BF)

        sums = TeamSum(me, lambda p: part.at[rows_at(p, rows)], near, acc, mid, far, ss, sr, ("xz", "xz"))
        sums.start()

        def put(at, v):
            v = x[at].astype(F32) + v
            middle[at] = v
            own[at] = (norm_rows(v)[0] * full[10:11] + full[11:12]).astype(BF)

        def more():
            gf.spread(None, (3,))
            if early:
                ge.release()
            gc.release()

        sums.finish(put, more)
        keep.append(pltpu.make_async_copy(own, n2.at[mine], ls.at[10]))
        keep[-1].start()
        gn = TeamGather(me, own, lambda p: n2.at[p], gs, gr, ("zx", "zx"))
        gn.start()
        gk = Halo(me, H, own, halo2, ks, kr)
        gk.start()
        gf.release((3,))
        gf.forward((0, 1, 2))
        gn.finish()
        gk.finish()
        gf.forward((3,))
        if early:
            ge.forward()
        gc.forward()
        gu.finish()
        gf.finish()
        if early:
            ge.finish()
        gc.finish()
        for copy in local[2:3] + local[5:] + keep:
            copy.wait()

    gsems = TeamsGather.sems(H)
    team_sems = [DMA((14,)), DMA((8, 2))]
    halo_sems = [DMA((8,)), DMA((2,))]
    move_sems = [DMA((7,)), DMA((8,))]
    return comm_call(
        body,
        (
            jax.ShapeDtypeStruct((16, D), F32),
            jax.ShapeDtypeStruct((16, m), F32),
            jax.ShapeDtypeStruct((4, T, D), BF),
            jax.ShapeDtypeStruct((T, D), BF),
            jax.ShapeDtypeStruct((3, T, m), BF),
            jax.ShapeDtypeStruct((T, m), F32),
            jax.ShapeDtypeStruct((8, rows, m), BF),
            jax.ShapeDtypeStruct((*grid, k_row, 4 * m), BF),
            jax.ShapeDtypeStruct(wo_shape, BF),
            jax.ShapeDtypeStruct((T, m), BF),
            jax.ShapeDtypeStruct((T, m), F32),
            jax.ShapeDtypeStruct((T, m), F32),
            jax.ShapeDtypeStruct((2, per, m, m), F32),
            jax.ShapeDtypeStruct((m, 128), F32),
            jax.ShapeDtypeStruct((rows, D), F32),
            jax.ShapeDtypeStruct((8, rows, D), BF),
            jax.ShapeDtypeStruct((2, 16, D), BF),
            jax.ShapeDtypeStruct((A, H, *w_cv.shape), BF),
            jax.ShapeDtypeStruct((*grid, k_row, nf), BF),
        ),
        [VM] * 11 + [ANY],
        (VM, VM, ANY, ANY, VM, VM, ANY, ANY, ANY, VM, VM, VM, VM, VM, VM, ANY, ANY, ANY, ANY),
        [
            pltpu.VMEM((*grid, *vecs.shape), BF),
            pltpu.VMEM((T, D), BF),
            pltpu.VMEM((2, 16, D), BF),
            pltpu.VMEM((2, 1, D), F32),
            pltpu.VMEM((1, D), F32),
            pltpu.VMEM((4, T, D), BF),
            pltpu.VMEM((T, D), BF),
            pltpu.VMEM((*grid, k_row, 4 * m), BF),
            pltpu.VMEM(wo_shape, BF),
            pltpu.VMEM((8, k_row, nf), BF),
            pltpu.VMEM((2, per, m, m), F32),
            pltpu.VMEM((2, m, m), F32),
            pltpu.VMEM((2, m, m), F32),
            pltpu.VMEM((m, 128), BF),
            pltpu.VMEM((m, 128), BF),
            pltpu.VMEM((rows, D), BF),
            *TeamSum.scratch(rows, D),
            *gsems,
            *team_sems,
            *halo_sems,
            *move_sems,
            *gsems,
            *move_sems,
            *RowsGather.sems(H),
            *RowsGather.sems(H),
            DMA,
            DMA,
            *RowsGather.sems(H),
            *TeamsGather.sems(H, 4),
            *team_sems,
            *halo_sems,
            DMA((14 + heads,)),
            pltpu.VMEM((8, k_row, 4 * m), BF),
            pltpu.VMEM((8, k_row, nf), BF),
            pltpu.VMEM((2, heads, HEAD, HEAD), F32),
            pltpu.VMEM((m, 128), F32),
            DMA((heads,)),
            DMA((heads,)),
        ],
        0,
    )(vecs, x, up, *w4, w_ck, w_cr, w_o, w_cv, start)


class Background:
    def __init__(self, items, H):
        self.items, self.H = items, H

    def arrays(self):
        return [v for v, _ in self.items]

    def outs(self):
        shapes = []
        for v, kind in self.items:
            lead = {"h": (max(self.H - 1, 1),), "a": (), "t": (8,)}[kind]
            shapes.append(jax.ShapeDtypeStruct((*lead, *v.shape[1:]), BF))
        return shapes

    def sems(self):
        out = []
        for _, kind in self.items:
            n = {"h": max(self.H - 1, 1), "a": 1, "t": 8}[kind]
            out += [DMA((n,)), DMA((n,))] + ([DMA] if kind == "t" else [])
        return out

    def start(self, me, srcs, dsts, sems):
        self.open = []
        sems = list(sems)
        h, H = me["h"], self.H
        mine = rank_of(me["b"], me["l"], me["c"])
        for (_, kind), src, dst in zip(self.items, srcs, dsts):
            ss, sr = sems.pop(0), sems.pop(0)
            copies = Copies(ss)
            if kind == "h":
                for dh in range(1, H):
                    to = lax.rem(h + dh, H)
                    copies.go(src.at[to], dst.at[dh - 1], sr.at[dh - 1], {"h": to})
                    self.open.append((dst.at[dh - 1], sr.at[dh - 1]))
            elif kind == "a":
                copies.go(src.at[1 - me["a"]], dst, sr.at[0], {"a": 1 - me["a"]})
                self.open.append((dst, sr.at[0]))
            else:
                keep = pltpu.make_async_copy(src.at[mine], dst.at[mine], sems.pop(0))
                keep.start()
                self.open.append(keep)
                for m, to in mates(me):
                    p = rank_of(to["b"], to["l"], to["c"])
                    copies.go(src.at[p], dst.at[mine], sr.at[mine], to)
                    self.open.append((dst.at[p], sr.at[p]))
            self.open.append(copies)

    def finish(self):
        for item in self.open:
            if isinstance(item, tuple):
                landed(*item)
            elif isinstance(item, Copies):
                item.drain()
            else:
                item.wait()


def back_rows(T, tile, chunk, shares, diff, part, first, sums):
    per = T // 2 // tile

    def step(q, carry):
        t = 2 * per - 1 - q
        ds = chunk(t)
        dif = diff(t)
        late = jnp.zeros_like(ds[0])
        here = jnp.zeros_like(ds[0])
        for i, (d, s) in enumerate(zip(ds, shares)):
            sums[i][...] = sums[i][...] + jnp.sum(d * dif, axis=0, keepdims=True)
            late = late + (1.0 - s) * d
            here = here + s * d
        carry = jnp.where(lax.rem(t, per) == per - 1, jnp.zeros_like(carry), carry)
        row = lax.broadcasted_iota(jnp.int32, late.shape, 0)
        part(t, here + jnp.where(row == tile - 1, carry, pltpu.roll(late, tile - 1, axis=0)))

        @pl.when(lax.rem(t, per) == 0)
        def _():
            first(t // per, late[:16].astype(BF))

        return late[:1]

    zero = jnp.zeros((1, diff(0).shape[1]), F32)
    lax.fori_loop(0, 2 * per, step, zero)


def channel_mix(lay, n2, halo, full, wcv, wf, upc, middle, up, items):
    H, A = lay.H, lay.A
    rows, D = middle.shape
    T = 8 * rows
    F, m = wcv.shape[0], D // 8
    nk, kk, _ = wf.shape
    w_cv = F // (A * H)
    tile = T // 4
    dq = D // 4
    bg = Background(items, H)
    nb = len(items)

    def body(n2, halo, full, wcv_in, wf_in, upc, middle, up, *rest):
        srcs, rest = rest[:nb], rest[nb:]
        d_mid, d_br, moved, s_cv, got_cv, g_f, got_f, sums = rest[:8]
        dsts, rest = rest[8 : 8 + nb], rest[:8] + rest[8 + nb :]
        (big, m2, df, carry, relu, act, sg, d_pg, d_val, dval, gcv, cvbuf, stage) = rest[8:21]
        (dn2, own, add, first, edge) = rest[21:26]
        cn, ca, cm, cf, c_s, c_r = rest[26:32]
        rn, ra, rm, rf, r_s, r_r = rest[32:38]
        ds, dr, bs, br, es, er, ms, mr, vs, vr, fs, fr, ls = rest[38:51]
        wf, wcv = rest[51 + len(bg.sems()) :]
        d_pre = act
        me = coords()
        a, b, h, l, c = (me[n] for n in ALL)
        mine = rank_of(b, l, c)
        loads = [
            pltpu.make_async_copy(n2.at[p], big.at[pl.ds(p * rows, rows)], ls.at[p]) for p in range(8)
        ]
        loads.append(pltpu.make_async_copy(wf_in, wf, ls.at[14]))
        loads.append(pltpu.make_async_copy(wcv_in, wcv, ls.at[15]))
        for copy in loads:
            copy.start()
        greet(me, H, True, True)
        for copy in loads[:8]:
            copy.wait()

        def write(i, p, v):
            if i is None:
                df[rows_at(p, MIX)] = v
            else:
                m2[i, rows_at(p, MIX)] = v

        def before(s):
            row = halo[s].astype(F32)[15:16]
            return jnp.where(h > 0, row, jnp.zeros_like(row))

        s_ck, s_cr = full[12:13], full[13:14]
        mix_rows(
            lambda p: big[rows_at(p, MIX)].astype(F32),
            before,
            carry,
            [s_ck, s_cr],
            write,
            T // MIX,
            MIX,
        )

        loads[8].wait()

        @pl.loop(0, 4)
        def _(t):
            at = rows_at(t, tile)
            acc = jnp.zeros((tile, F), F32)
            for i in range(nk):
                acc = acc + dot_nn(m2[0, at, i * kk : (i + 1) * kk], wf[i, :, :F])
            pos = jnp.maximum(acc, 0.0)
            relu[at] = pos.astype(BF)
            act[at] = (pos * pos).astype(BF)

        loads[9].wait()

        @pl.loop(0, 4)
        def _(t):
            at = rows_at(t, tile)
            for q in range(4):
                lo = q * dq
                big[at, lo : lo + dq] = dot_nn(act[at], wcv[:, lo : lo + dq]).astype(BF)

        def cols(ref):
            return lambda p: ref.at[:, pl.ds(pl.multiple_of(p * m, m), m)]

        total = TeamSum(me, cols(big), cn, ca, cm, cf, c_s, c_r)
        total.start()

        @pl.loop(0, 4)
        def _(t):
            at = rows_at(t, tile)
            acc = jnp.zeros((tile, m), F32)
            for i in range(nk):
                acc = acc + dot_nn(m2[1, at, i * kk : (i + 1) * kk], wf[i, :, F:])
            sg[at] = 1.0 / (1.0 + jnp.exp(-acc))

        def gate_back(at, val):
            sig = sg[at]
            upv = upc[at].astype(F32)
            d_val[at] = (sig * upv).astype(BF)
            d_pg[at] = (upv * val * sig * (1.0 - sig)).astype(BF)
            add[at] = (sig * val).astype(BF)

        total.finish(gate_back)
        keep_val = pltpu.make_async_copy(d_val, cols(dval)(mine), ls.at[8])
        keep_val.start()
        gv = TeamGather(me, d_val, cols(dval), ds, dr)
        gv.start()
        gv.finish()
        keep_val.wait()
        keep_add = pltpu.make_async_copy(add.at[rows_at(mine, rows)], moved.at[mine], ls.at[11])
        keep_add.start()
        gm = Exchange(me, lambda p: add.at[rows_at(p, rows)], lambda p: moved.at[p], ms, mr)
        gm.start()
        bg.start(me, srcs, dsts, rest[51:-2])

        @pl.loop(0, 8)
        def _(q):
            at = pl.ds(pl.multiple_of(q * m, m), m)
            g = dot_tn(act[...], dval[:, at])
            for i in range(A):
                for j in range(H):
                    lo = (i * H + j) * w_cv
                    gcv[i, j, :, at] = g[lo : lo + w_cv].astype(BF)

        cv = Copies(vs)
        cv.go(gcv.at[1 - a], cvbuf, vr.at[0], {"a": 1 - a})

        @pl.loop(0, 4)
        def _(t):
            at = rows_at(t, tile)
            d_pre[at] = (dot_nt(dval[at], wcv[...]) * 2.0 * relu[at].astype(F32)).astype(BF)

        ff = Copies(fs)
        sums[...] = jnp.zeros_like(sums)

        def chunk_of(i):
            lo = i * kk

            def chunk(t):
                at = rows_at(t, tile)
                return (dot_nt(d_pre[at], wf[i, :, :F]), dot_nt(d_pg[at], wf[i, :, F:]))

            def put(t, v):
                big[rows_at(t, tile), lo : lo + kk] = v.astype(BF)

            def put_first(s, v):
                first[s, :, lo : lo + kk] = v

            back_rows(
                T,
                tile,
                chunk,
                (s_ck[:, lo : lo + kk], s_cr[:, lo : lo + kk]),
                lambda t: df[rows_at(t, tile), lo : lo + kk].astype(F32),
                put,
                put_first,
                [sums.at[k : k + 1, lo : lo + kk] for k in range(2)],
            )

        def grads(step, k):
            i = lax.rem(a + 1 + step, A)
            for q in range(2):
                at = pl.ds(pl.multiple_of((i * 2 + k) * kk + q * (kk // 2), kk // 2), kk // 2)
                to = slice(q * kk // 2, (q + 1) * kk // 2)
                stage[k, to, :F] = dot_tn(m2[0, :, at], d_pre[...]).astype(BF)
                stage[k, to, F:] = dot_tn(m2[1, :, at], d_pg[...]).astype(BF)
            copy = pltpu.make_async_copy(stage.at[k], g_f.at[i, k], ls.at[9 if k == 0 else 13])
            copy.start()
            return copy

        for i in range(nk):
            chunk_of(i)
        total = TeamSum(me, lambda p: big.at[rows_at(p, rows)], rn, ra, rm, rf, r_s, r_r)
        total.start()
        e = Edge(me, H, first, edge, es, er)
        e.start()

        def put_dn(at, v):
            dn2[at] = v

        halves = 2 if w_cv % 32 == 0 else 1

        held = []

        def pass_on(g):
            at = pl.ds(g * (w_cv // halves), w_cv // halves)
            for dh in range(1, H):
                to = lax.rem(h + dh, H)
                when = None if g == 0 else jnp.logical_not(inner(me, H))
                held.append(
                    cv.go(
                        gcv.at[a, to, at],
                        got_cv.at[dh - 1, at],
                        vr.at[1 + (dh - 1) * 2 + g],
                        {"h": to},
                        when,
                    )
                )

        def value_sums():
            landed(cvbuf, vr.at[0])

            @pl.loop(0, H)
            def _(j):
                gcv[a, j] = (gcv[a, j].astype(F32) + cvbuf[j].astype(F32)).astype(BF)

            pass_on(0)
            for copy in staged:
                copy.wait()
            ff.go(g_f.at[1 - a, 0], got_f, fr.at[0], {"a": 1 - a})
            staged[:] = [grads(1, 0), grads(1, 1)]

        staged = []
        total.finish(put_dn, value_sums, lambda: staged.extend([grads(0, 0), grads(0, 1)]))
        for copy in staged:
            copy.wait()
        e.finish(dn2)

        @pl.loop(0, rows // MIX)
        def _(t):
            at = rows_at(t, MIX)
            d = dn2[at]
            hat, rstd = norm_rows(middle[at])
            sums[2:3] = sums[2:3] + jnp.sum(d * hat, axis=0, keepdims=True)
            sums[3:4] = sums[3:4] + jnp.sum(d, axis=0, keepdims=True)
            dm = up[at].astype(F32) + norm_back(d * full[10:11], hat, rstd)
            d_mid[at] = dm
            own[at] = dm.astype(BF)

        keep = [
            pltpu.make_async_copy(own, d_br.at[mine], ls.at[10]),
            keep_add,
        ]
        keep[0].start()
        gx = TeamGather(me, own, lambda p: d_br.at[p], bs, br, ("zx", "zx"))
        gx.start()
        if halves == 2:
            pass_on(1)
            for copy in held[len(held) // 2 :]:
                pl.when(inner(me, H))(copy.start)
        keep.append(pltpu.make_async_copy(gcv.at[a, h], s_cv, ls.at[12]))
        keep[-1].start()
        gx.finish()
        gm.finish()
        bg.finish()
        landed(got_f, fr.at[0])
        ff.drain()
        for dh in range(1, H):
            for g in range(halves):
                at = pl.ds(g * (w_cv // halves), w_cv // halves)
                landed(got_cv.at[dh - 1, at], vr.at[1 + (dh - 1) * 2 + g])
        cv.drain()
        for copy in keep:
            copy.wait()

    return comm_call(
        body,
        (
            jax.ShapeDtypeStruct((rows, D), F32),
            jax.ShapeDtypeStruct((8, rows, D), BF),
            jax.ShapeDtypeStruct((8, rows, m), BF),
            jax.ShapeDtypeStruct((w_cv, D), BF),
            jax.ShapeDtypeStruct((max(H - 1, 1), w_cv, D), BF),
            jax.ShapeDtypeStruct((A, nk // A, kk, F + m), BF),
            jax.ShapeDtypeStruct((kk, F + m), BF),
            jax.ShapeDtypeStruct((8, D), F32),
            *bg.outs(),
        ),
        [ANY, VM, VM, ANY, ANY, VM, VM, VM] + [ANY] * nb,
        (VM, ANY, ANY, ANY, ANY, ANY, ANY, VM, *[ANY] * nb),
        [
            pltpu.VMEM((T, D), BF),
            pltpu.VMEM((2, T, D), BF),
            pltpu.VMEM((T, D), BF),
            pltpu.VMEM((1, D), F32),
            pltpu.VMEM((T, F), BF),
            pltpu.VMEM((T, F), BF),
            pltpu.VMEM((T, m), F32),
            pltpu.VMEM((T, m), BF),
            pltpu.VMEM((T, m), BF),
            pltpu.VMEM((T, D), BF),
            pltpu.VMEM((A, H, w_cv, D), BF),
            pltpu.VMEM((H, w_cv, D), BF),
            pltpu.VMEM((2, kk, F + m), BF),
            pltpu.VMEM((rows, D), F32),
            pltpu.VMEM((rows, D), BF),
            pltpu.VMEM((T, m), BF),
            pltpu.VMEM((2, 16, D), BF),
            pltpu.VMEM((8, 16, D), BF),
            *TeamSum.scratch(T, m),
            *TeamSum.scratch(rows, D),
            DMA((14,)),
            DMA((8, 2)),
            DMA((14,)),
            DMA((8, 2)),
            DMA((2,)),
            DMA((8,)),
            DMA((7,)),
            DMA((8,)),
            DMA((2 * H,)),
            DMA((2 * H,)),
            DMA((1,)),
            DMA((1,)),
            DMA((16,)),
            *bg.sems(),
            pltpu.VMEM(wf.shape, BF),
            pltpu.VMEM(wcv.shape, BF),
        ],
        2,
    )(n2, halo, full, wcv, wf, upc, middle, up, *bg.arrays())


def time_back(lay, d_br, wo, gated, ghat, grstd, gate, rkv, states, mv, full, mixed, diff, w4, x, d_mid, cm_sums, s_f, g_f, fin):
    H, A, n_dev = lay.H, lay.A, lay.n
    T, m = gate.shape
    rows, D = x.shape
    heads = m // HEAD
    per = T // 2 // CHUNK
    nk, kk, _ = w4.shape
    tile = T // 4
    hk = kk // H
    w_row = D // n_dev
    nf = s_f.shape[-1]
    H1 = max(H - 1, 1)
    strided = lay.strided
    hop = fin is not None
    F = (nf - m) * 8
    k_row = hk // 4

    def body(*refs):
        d_br, wo, gated, ghat, grstd, gate, rkv, states, mv, full, mixed, diff, w4_in, x, d_mid, cm_sums, s_f = refs[:17]
        g_f, refs = refs[17], refs[:17] + refs[18:]
        if hop:
            fin, refs = refs[17], refs[:17] + refs[18:]
        in_grad, o_out, total_out, fin_out, ck_out, cr_out, *four = refs[17:27]
        refs = refs[5:]
        (big, dy, adds, cl, st, obox, ibox, d_all, tsum, sums) = refs[22:32]
        (mbuf, g4, got, late, t4, first, edge) = refs[32:39]
        dn1 = in_grad
        (g_o, o_got, o_late, f_own, f_got, t_f, small, s_got) = refs[39:47]
        rn, ra, rm, rf, r_s, r_r = refs[47:53]
        cs, cr, es, er, gs, gr, os_, or_, fs, fr, xs, xr, ys, yr, ss, sr, ls, f_out, g_out, hs, hr, f1, f1_got, f1s, f1r, w4 = refs[53:]
        me = coords()
        a, b, h, l, c = (me[k] for k in ALL)
        mine = rank_of(b, l, c)
        loads = [
            pltpu.make_async_copy(d_br.at[p], big.at[pl.ds(p * rows, rows)], ls.at[p]) for p in range(8)
        ]
        loads.append(pltpu.make_async_copy(s_f.at[h], f_own, ls.at[8]))
        loads.append(pltpu.make_async_copy(g_f.at[a, 1], f1, ls.at[13 + nk]))
        loads.append(pltpu.make_async_copy(w4_in, w4, ls.at[14 + nk]))
        for copy in loads:
            copy.start()

        sem = pltpu.get_barrier_semaphore()
        others = []
        for i in range(1, n_dev):
            k = i
            dc, k = k % 2, k // 2
            dl, k = k % 2, k // 2
            dh, k = k % H, k // H
            db, da = k % 2, k // 2
            to = {
                "a": lax.rem(a + da, A),
                "b": b ^ db,
                "h": lax.rem(h + dh, H),
                "l": l ^ dl,
                "c": c ^ dc,
            }
            others.append((i, to))
            pl.semaphore_signal(sem, inc=1, device_id=to, device_id_type=MESH)
        pl.semaphore_wait(sem, n_dev - 1)
        c1 = Copies(f1s)
        c1.go(g_f.at[1 - a, 1], f1_got, f1r, {"a": 1 - a})
        for copy in loads[:8]:
            copy.wait()

        ones = block_ones(m)
        dec = Decay(mv[6:7])
        u = mv[7:8]
        span_all = jnp.exp(-mv[6:7] * (T // 2))
        low_t = triangle(heads, False)
        low = triangle(heads, True)
        tsum[...] = jnp.zeros_like(tsum)

        @pl.loop(0, 2 * per)
        def _(t):
            at = rows_at(t, CHUNK)
            d_gated = dot_nt(big[at], wo[...].reshape(m, D))
            g = gate[at]
            sig = 1.0 / (1.0 + jnp.exp(-g))
            hat, rstd = ghat[at], grstd[at]
            dn = d_gated * (g * sig)
            tsum[2:3] += jnp.sum(dn * hat, axis=0, keepdims=True)
            tsum[3:4] += jnp.sum(dn, axis=0, keepdims=True)
            nm = hat * mv[8:9] + mv[9:10]
            d_all[at, 3 * m :] = (d_gated * nm * sig * (1.0 + g * (1.0 - sig))).astype(BF)
            e = dn * mv[8:9]
            m1 = dot_exact(e, ones) * (1.0 / HEAD)
            m2 = dot_exact(e * hat, ones) * (1.0 / HEAD)
            dy[at] = (e - m1 - hat * m2) * rstd

        cl[...] = jnp.zeros_like(cl)

        @pl.loop(0, per)
        def _(q):
            n = per - 1 - q
            for s in range(2):
                at = rows_at(s * per + n, CHUNK)
                rd = (rkv[0, at].astype(F32) * dec.down).astype(BF)
                add = dot_tn(dy[at].astype(BF), rd) * ones
                adds[s, n] = add
                cl[s] = dec.span * cl[s] + add

        st[...] = jnp.zeros_like(st)
        chain = Chain(me, H, False, obox, ibox, cs, cr)
        chain.run(st, cl, span_all, ones)
        cf = Copies(fs)
        held = []
        for dh in range(1, H):
            to = lax.rem(h + dh, H)
            when = jnp.logical_not(inner(me, H))
            held.append(cf.go(s_f.at[to], f_got.at[dh - 1, 0], fr.at[2 * dh - 2], {"h": to}, when))

        if hop:
            mine_fin = fin.at[pl.ds(l * 4, 4)]
            last = h == H - 1
            to_first = remote(mine_fin.at[:, pl.ds(0, HEAD)], fin_out, hs, hr, {"h": 0})
            kept = pltpu.make_async_copy(mine_fin.at[:, pl.ds(HEAD, HEAD)], fin_out, hs)

            @pl.when(last)
            def _():
                to_first.start()

        nw = D // 8

        @pl.loop(0, 8)
        def _(q):
            at = pl.ds(pl.multiple_of(q * nw, nw), nw)
            g = dot_tn(gated[...], big[:, at]).astype(BF)
            g_o[:, :, :, at] = g.reshape(*g_o.shape[:3], nw)

        co = Copies(os_)
        if strided:
            co.go(g_o.at[1 - a], o_got, or_.at[0], {"a": 1 - a})

        @pl.loop(0, per)
        def _(q):
            n = per - 1 - q
            for s in range(2):
                at = rows_at(s * per + n, CHUNK)
                r, k, v = (rkv[i, at].astype(F32) for i in range(3))
                vb = rkv[2, at]
                rd, kg, kt = r * dec.down, k * dec.up, k * dec.tail
                rdb, kgb, ktb = rd.astype(BF), kg.astype(BF), kt.astype(BF)
                dyt = dy[at]
                dyb = dyt.astype(BF)
                state, end = states[s, n], st[s]
                endb = end.astype(BF)
                datt = jnp.where(low, dot_nt(stacked_heads(dyb), vb), 0.0).astype(BF)
                datt_t = jnp.where(low_t, dot_nt(stacked_heads(vb), dyb), 0.0).astype(BF)
                att_t = jnp.where(low_t, dot_nt(stacked_heads(kgb), rdb), 0.0).astype(BF)
                ddiag = dot_exact(dyt * v, ones)
                diag = dot_exact(r * u * k, ones)
                d_rd = own_heads(dot_nn(datt, kgb)) + dot_nn(dyb, state.astype(BF))
                d_kg = own_heads(dot_nn(datt_t, rdb))
                d_kt = dot_nn(vb, endb)
                d_v = own_heads(dot_nn(att_t, dyb)) + diag * dyt + dot_nt(ktb, endb)
                d_r = d_rd * dec.down + ddiag * u * k
                d_k = d_kg * dec.up + d_kt * dec.tail + ddiag * u * r
                d_all[at, :m] = d_r.astype(BF)
                d_all[at, m : 2 * m] = d_k.astype(BF)
                d_all[at, 2 * m : 3 * m] = d_v.astype(BF)
                tsum[1:2] += jnp.sum(ddiag * r * k, axis=0, keepdims=True)
                d_l = jnp.sum(
                    (dec.i + 1.0) * kg * d_kg
                    - dec.i * rd * d_rd
                    - (CHUNK - 1.0 - dec.i) * kt * d_kt,
                    axis=0,
                    keepdims=True,
                )
                d_l = d_l - CHUNK * dec.span * jnp.sum(state * end, axis=0, keepdims=True)
                tsum[0:1] += d_l
                st[s] = dec.span * end + adds[s, n]

        for copy in held:
            pl.when(inner(me, H))(copy.start)
        loads[9].wait()
        landed(f1_got, f1r)

        @pl.loop(0, kk // 64)
        def _(q):
            at = rows_at(q, 64)
            f1[at] = (f1[at].astype(F32) + f1_got[at].astype(F32)).astype(BF)

        for dh in range(1, H):
            to = lax.rem(h + dh, H)
            cf.go(f1.at[rows_at(to, hk)], f_got.at[dh - 1, 1], fr.at[2 * dh - 1], {"h": to})
        chain.finish()

        cg = Copies(gs)
        units = [(step, k, jj) for step in range(A) for k in range(2) for jj in range(2)]

        def unit(v):
            step, k, jj = units[v]
            i = lax.rem(a + 1 + step, A)
            lo = pl.ds(pl.multiple_of((i * 2 + k) * kk, kk), kk)
            src = mixed.at[pl.ds(jj * 2, 2), :, lo]
            return pltpu.make_async_copy(src, mbuf.at[v % 2], ls.at[9 + v % 2])

        unit(0).start()
        for v, (step, k, jj) in enumerate(units):
            if v + 1 < len(units):
                unit(v + 1).start()
            unit(v).wait()
            i = lax.rem(a + 1 + step, A)
            for q in range(2):
                j = jj * 2 + q
                g = dot_tn(mbuf[v % 2, q], d_all[:, j * m : (j + 1) * m])
                g4[i * 2 + k, :, j * m : (j + 1) * m] = g.astype(BF)
            if step < A - 1 and jj == 1:
                cg.go(g4.at[i * 2 + k], got.at[k], gr.at[k], {"a": 1 - a})

        difs = [
            pltpu.make_async_copy(diff.at[:, pl.ds(i * kk, kk)], mbuf.at[i // 2, i % 2], ls.at[13 + i])
            for i in range(nk)
        ]
        for copy in difs:
            copy.start()
        sums[...] = jnp.zeros_like(sums)

        def chunk_of(i):
            lo = i * kk

            def chunk(t):
                at = rows_at(t, tile)
                return tuple(
                    dot_nt(d_all[at, j * m : (j + 1) * m], w4[i, :, j * m : (j + 1) * m])
                    for j in range(4)
                )

            def put(t, v):
                big[rows_at(t, tile), lo : lo + kk] = v.astype(BF)

            def put_first(s, v):
                first[s, :, lo : lo + kk] = v

            back_rows(
                T,
                tile,
                chunk,
                tuple(full[2 + j : 3 + j, lo : lo + kk] for j in range(4)),
                lambda t: mbuf[i // 2, i % 2, rows_at(t, tile)].astype(F32),
                put,
                put_first,
                [sums.at[j : j + 1, lo : lo + kk] for j in range(4)],
            )

        loads[10].wait()
        for i in range(nk):
            difs[i].wait()
            chunk_of(i)
        total = TeamSum(
            me, lambda p: big.at[rows_at(p, rows)], rn, ra, rm, rf, r_s, r_r, ("xz", "xz")
        )
        total.start()
        e = Edge(me, H, first, edge, es, er)
        e.start()

        def pass_on():
            if strided:
                landed(o_got, or_.at[0])

                @pl.loop(0, H)
                def _(j):
                    g_o[a, j] = (g_o[a, j].astype(F32) + o_got[j].astype(F32)).astype(BF)

                for dh in range(1, H):
                    to = lax.rem(h + dh, H)
                    co.go(g_o.at[a, to], o_late.at[dh - 1], or_.at[dh], {"h": to})
            for k in range(2):
                landed(got.at[k], gr.at[k])

                @pl.loop(0, kk // 64)
                def _(q):
                    at = rows_at(q, 64)
                    g4[a * 2 + k, at] = (g4[a * 2 + k, at].astype(F32) + got[k, at].astype(F32)).astype(BF)

                for dh in range(1, H):
                    to = lax.rem(h + dh, H)
                    v = (dh - 1) * 2 + k
                    cg.go(
                        g4.at[a * 2 + k, rows_at(to, hk)], late.at[dh - 1, k], gr.at[2 + v], {"h": to}
                    )

            loads[8].wait()
            for dh in range(1, H):
                for k in range(2):
                    landed(f_got.at[dh - 1, k], fr.at[2 * dh - 2 + k])
            for k in range(2):
                for q in range(4):
                    at = pl.ds(q * (hk // 4), hk // 4)
                    if k == 0:
                        v = f_own[at].astype(F32)
                    else:
                        v = f1[pl.ds(pl.multiple_of(h * hk + q * (hk // 4), hk // 4), hk // 4)].astype(F32)
                    for dh in range(1, H):
                        v = v + f_got[dh - 1, k, at].astype(F32)
                    t_f[k * 4 + q] = v.astype(BF)
            keep_f.start()
            gf.start()

        keep_f = pltpu.make_async_copy(t_f.at[mine], f_out.at[mine], ls.at[11])
        gf = Exchange(me, lambda p: t_f.at[p], lambda p: f_out.at[p], xs, xr)

        def put_dn(at, v):
            dn1[at] = v

        total.finish(put_dn, pass_on)
        e.finish(dn1)

        @pl.loop(0, rows // MIX)
        def _(t):
            at = rows_at(t, MIX)
            d = dn1[at]
            hat, rstd = norm_rows(x[at].astype(F32))
            sums[4:5] = sums[4:5] + jnp.sum(d * hat, axis=0, keepdims=True)
            sums[5:6] = sums[5:6] + jnp.sum(d, axis=0, keepdims=True)
            in_grad[at] = d_mid[at] + norm_back(d * full[0:1], hat, rstd)

        small[...] = jnp.zeros_like(small)
        per_lane = 128 // w_row
        for f in range(n_dev):
            g = pl.ds(f // per_lane * 128, 128)
            block = jnp.concatenate([sums[:, g], cm_sums[:, g]], axis=0)
            shift = (128 - w_row * (f % per_lane)) % 128
            small[f] = pltpu.roll(block, shift, axis=1) if shift else block

        if strided:
            for i in range(A):
                for j in range(H):
                    f = (((i * 2 + b) * H + j) * 2 + l) * 2 + c
                    v = (i * H + j) * w_row
                    block = tsum[:, v // 128 * 128 : v // 128 * 128 + 128]
                    shift = (128 - v % 128) % 128
                    block = pltpu.roll(block, shift, axis=1) if shift else block
                    small[f, 12:16] = block[:4]
        else:
            span = n_dev // 8
            for i in range(span):
                v = i * w_row
                block = tsum[:, v // 128 * 128 : v // 128 * 128 + 128]
                shift = (128 - v % 128) % 128
                block = pltpu.roll(block, shift, axis=1) if shift else block
                small[mine * span + i, 12:16] = block[:4]
        cv = Copies(ss)

        def flat(d):
            return (((d["a"] * 2 + d["b"]) * H + d["h"]) * 2 + d["l"]) * 2 + d["c"]

        for i, to in others:
            cv.go(small.at[flat(to)], s_got.at[i], sr.at[i], to)

        for k in range(2):
            for dh in range(1, H):
                landed(late.at[dh - 1, k], gr.at[2 + (dh - 1) * 2 + k])
            for q in range(4):
                at = pl.ds(pl.multiple_of(h * hk + q * (hk // 4), hk // 4), hk // 4)
                v = g4[a * 2 + k, at].astype(F32)
                for dh in range(1, H):
                    v = v + late[dh - 1, k, pl.ds(q * (hk // 4), hk // 4)].astype(F32)
                t4[k * 4 + q] = v.astype(BF)
        keep = [keep_f, pltpu.make_async_copy(t4.at[mine], g_out.at[mine], ls.at[12])]
        keep[1].start()
        gg = Exchange(me, lambda p: t4.at[p], lambda p: g_out.at[p], ys, yr)
        gg.start()
        if strided:
            v = g_o[a, h].astype(F32)
            for dh in range(1, H):
                landed(o_late.at[dh - 1], or_.at[dh])
                v = v + o_late[dh - 1].astype(F32)
            o_out[...] = v
        else:
            o_out[...] = g_o[...]
        acc = small[flat(me)]
        for i, _ in others:
            landed(s_got.at[i], sr.at[i])
            acc = acc + s_got[i]
        total_out[...] = acc
        if hop:

            @pl.when(last)
            def _():
                to_first.wait_send()
                kept.start()
                kept.wait()

            @pl.when(h == 0)
            def _():
                to_first.wait_recv()

        gf.finish()
        for copy in keep:
            copy.wait()

        def from_ranks(ref, lo, n, whole):
            parts = []
            for p in range(8):
                read = lambda i, j, p=p: ref[p, :, lo + i : lo + j]
                for src, dst, many in rank_columns(lay, n, whole, p):
                    parts.append((read, n // 8, dst, src, many))
            return parts

        def into(ref):
            def put(lo, v):
                ref[:, lo : lo + 128] = v

            return put

        lay_lanes(F, from_ranks(f_out, 0, F, 1), into(ck_out))
        for p in range(8):
            cr_out[:, p * m : (p + 1) * m] = f_out[p, :, F // 8 :].astype(F32)
        gg.finish()
        for j, ref in enumerate(four):
            lay_lanes(D, from_ranks(g_out, j * m, D, HEAD), into(ref))
        for copies in (c1, cf, co, cg, cv):
            copies.drain()

    o_shape = wo.shape[2:] if strided else wo.shape
    return comm_call(
        body,
        (
            jax.ShapeDtypeStruct((rows, D), F32),
            jax.ShapeDtypeStruct(o_shape, F32 if strided else BF),
            jax.ShapeDtypeStruct((16, 128), F32),
            jax.ShapeDtypeStruct((4, HEAD, 128), BF),
            jax.ShapeDtypeStruct((k_row, F), F32),
            *[jax.ShapeDtypeStruct((k_row, D), F32)] * 5,
        ),
        [ANY] + [VM] * 9 + [ANY] * 3 + [VM] * 3 + [ANY] * (3 if hop else 2),
        (VM, VM, VM, ANY, *[VM] * 6),
        [
            pltpu.VMEM((T, D), BF),
            pltpu.VMEM((T, m), F32),
            pltpu.VMEM((2, per, m, m), F32),
            pltpu.VMEM((2, m, m), F32),
            pltpu.VMEM((2, m, m), F32),
            pltpu.VMEM((m, 128), BF),
            pltpu.VMEM((m, 128), BF),
            pltpu.VMEM((T, 4 * m), BF),
            pltpu.VMEM((8, m), F32),
            pltpu.VMEM((8, D), F32),
            pltpu.VMEM((2, 2, T, kk), BF),
            pltpu.VMEM((nk, kk, 4 * m), BF),
            pltpu.VMEM((2, kk, 4 * m), BF),
            pltpu.VMEM((H1, 2, hk, 4 * m), BF),
            pltpu.VMEM((8, hk // 4, 4 * m), BF),
            pltpu.VMEM((2, 16, D), BF),
            pltpu.VMEM((8, 16, D), BF),
            pltpu.VMEM(wo.shape, BF),
            pltpu.VMEM(wo.shape[1:], BF),
            pltpu.VMEM((H1, *wo.shape[2:]), BF),
            pltpu.VMEM(s_f.shape[1:], BF),
            pltpu.VMEM((H1, 2, *s_f.shape[1:]), BF),
            pltpu.VMEM((8, hk // 4, nf), BF),
            pltpu.VMEM((n_dev, 16, 128), F32),
            pltpu.VMEM((n_dev, 16, 128), F32),
            *TeamSum.scratch(rows, D),
            DMA,
            DMA,
            DMA((2,)),
            DMA((8,)),
            DMA((2 + 2 * H1,)),
            DMA((2 + 2 * H1,)),
            DMA((H,)),
            DMA((H,)),
            DMA((2 * H1,)),
            DMA((2 * H1,)),
            DMA((7,)),
            DMA((8,)),
            DMA((7,)),
            DMA((8,)),
            DMA((n_dev,)),
            DMA((n_dev,)),
            DMA((15 + nk,)),
            pltpu.VMEM((8, k_row, nf), BF),
            pltpu.VMEM((8, k_row, 4 * m), BF),
            DMA,
            DMA,
            pltpu.VMEM((kk, nf), BF),
            pltpu.VMEM((kk, nf), BF),
            DMA((1,)),
            DMA,
            pltpu.VMEM(w4.shape, BF),
        ],
        3,
    )(d_br, wo, gated, ghat, grstd, gate, rkv, states, mv, full, mixed, diff, w4, x, d_mid, cm_sums, s_f, g_f, *([fin] if hop else []))


def dot(a, b, dims):
    return lax.dot_general(a, b, (dims, ((), ())), preferred_element_type=F32)


def mm(a, b):
    return dot(a, b, ((1,), (0,)))


def mm_nt(a, b):
    return dot(a, b, ((1,), (1,)))


def mm_tn(a, b):
    return dot(a, b, ((0,), (0,)))


class Layout:
    def __init__(self, mesh_shape):
        self.A, self.B, self.H, self.L, self.C = mesh_shape
        self.team = self.B * self.L * self.C
        self.n = self.team * self.A * self.H

    def of(self, D):
        self.strided = (D // self.n) % HEAD == 0
        return self

    def spread(self, v, whole):
        w = v.shape[-1] // self.n
        lead = v.shape[:-1]
        if w % whole:
            return v.reshape(*lead, self.team, -1)
        k = len(lead)
        v = v.reshape(*lead, self.A, self.B, self.H, self.L, self.C, w)
        v = v.transpose(*range(k), k + 1, k + 3, k + 4, k, k + 2, k + 5)
        return v.reshape(*lead, self.team, -1)

    def unspread(self, v, whole):
        lead = v.shape[:-2]
        w = v.shape[-1] * self.team // self.n
        if w % whole:
            return v.reshape(*lead, -1)
        k = len(lead)
        v = v.reshape(*lead, self.B, self.L, self.C, self.A, self.H, w)
        v = v.transpose(*range(k), k + 3, k, k + 4, k + 1, k + 2, k + 5)
        return v.reshape(*lead, -1)

    def rows_in(self, g):
        m = g.shape[-1]
        g = g.reshape(self.A, self.H, self.B, self.L, self.C, -1, m)
        return g.transpose(0, 2, 1, 3, 4, 5, 6).reshape(-1, m)

    def rows_out(self, g):
        m = g.shape[-1]
        g = g.reshape(self.A, self.B, self.H, self.L, self.C, -1, m)
        return g.transpose(0, 2, 1, 3, 4, 5, 6).reshape(self.A * self.H, self.team, -1, m)


def normed(v):
    mean = jnp.mean(v, axis=-1, keepdims=True)
    cent = v - mean
    rstd = lax.rsqrt(jnp.mean(cent * cent, axis=-1, keepdims=True) + EPS)
    return cent * rstd, rstd


def norm_back(e, xhat, rstd):
    m1 = jnp.mean(e, axis=-1, keepdims=True)
    m2 = jnp.mean(e * xhat, axis=-1, keepdims=True)
    return (e - m1 - xhat * m2) * rstd


def with_before(rows, halo, segs):
    v = rows.reshape(segs, -1, rows.shape[-1])
    return jnp.concatenate([halo, v[:, :-1]], axis=1).reshape(rows.shape)


def with_after(rows, segs):
    v = rows.reshape(segs, -1, rows.shape[-1])
    return (
        jnp.concatenate([v[:, 1:], jnp.zeros_like(v[:, :1])], axis=1).reshape(rows.shape),
        v[:, :1],
    )


def swap(v, axis):
    return lax.ppermute(v, axis, [(0, 1), (1, 0)])


def per_device(lay, *args):
    (x_in, up_in, start_in) = args[:3]
    vec = args[3:13]
    w_r, w_k, w_v, w_g, w_o = args[13:18]
    vec2 = args[18:22]
    w_ck, w_cv, w_cr = args[22:]
    a_at, b_at, h_at = (lax.axis_index(n) for n in ("a", "b", "h"))
    rank = (b_at * lay.L + lax.axis_index("l")) * lay.C + lax.axis_index("c")
    H = lay.H
    segs = lay.B
    D = x_in.shape[-1]
    x_own = x_in[0]
    rows = x_own.shape[0]
    T = rows * lay.team
    dcol = D // lay.team
    heads = dcol // HEAD
    half = lay.L * lay.C
    w_row = D // lay.n
    lay.of(D)
    hid = w_ck.shape[1] // lay.team

    stacked = jnp.stack([*vec, *vec2])
    nv = stacked.shape[0]
    stacked = jnp.pad(stacked, ((0, 16 - nv), (0, 128 - w_row)))
    o_own = w_o
    if not lay.strided:
        o_own = lax.all_gather(w_o, ALL, axis=0, tiled=True)
        o_own = lax.dynamic_slice_in_dim(o_own, rank * dcol, dcol, 0)
        o_own = o_own.reshape(lay.A, H, -1, D)
    (
        every, my_vecs, mixed, diff1, rkv, gate, upc, W4, W_o, gated, ghat, grstd, states, fin, middle, n2, halo_2,
        W_cv, ffn_all,
    ) = front(lay, stacked, x_own, up_in[0], (w_r, w_k, w_v, w_g), w_ck, w_cr, o_own, w_cv, start_in[0])
    W_cv = W_cv.reshape(hid, D)
    direct = lay.strided and H == 2 and lay.A == 2
    items = []
    if direct:
        blocks = fin.astype(BF).reshape(lay.A, H, HEAD, 128).transpose(1, 0, 2, 3)
        blocks = jnp.broadcast_to(blocks.reshape(H, lay.A * HEAD, 128), (4, H, lay.A * HEAD, 128))
        items = [(blocks.reshape(8, lay.A * HEAD, 128), "t")]
    else:
        nh = start_in.shape[1]
        head_ids = lay.spread(jnp.arange(nh * HEAD, dtype=jnp.int32), HEAD)
        my_heads = lax.dynamic_index_in_dim(head_ids, rank, 0, False)[::HEAD] // HEAD
        s_out = fin.reshape(heads, HEAD, 2, HEAD).transpose(2, 0, 3, 1)
        placed = jnp.zeros((segs, nh, HEAD, HEAD), BF)
        s_fin = jnp.where(h_at == lay.H - 1, s_out, 0.0).astype(BF)
        placed = placed.at[:, my_heads].set(s_fin)
        final = lax.psum_scatter(placed, "b", scatter_dimension=0, tiled=True)
        final = lax.psum_scatter(final, SEQ, scatter_dimension=1, tiled=True).astype(F32)

    wf = ffn_all.reshape(2 * lay.A, D // (2 * lay.A), -1)
    d_mid, d_br, moved, s_cv, got_cv, g_f, got_f, cm_sums, *got_fin = channel_mix(
        lay, n2, halo_2, every, W_cv, wf, upc.reshape(T, dcol), middle, up_in[0], items
    )
    layer_output = (middle + moved.transpose(1, 0, 2).reshape(rows, D).astype(F32)).astype(BF)
    g_cv = s_cv.astype(F32) + jnp.sum(got_cv.astype(F32), axis=0)

    s_f = lax.dynamic_index_in_dim(g_f[:, 0], a_at, 0, False).astype(F32) + got_f.astype(F32)
    s_f = s_f.astype(BF).reshape(H, -1, s_f.shape[-1])
    w4 = W4.reshape(2 * lay.A, D // (2 * lay.A), -1)
    input_grad, g_o, small, fin, g_ck, g_cr, g_r, g_k, g_v, g_w = time_back(
        lay, d_br, W_o, gated, ghat, grstd, gate, rkv, states, my_vecs, every, mixed, diff1, w4, x_own, d_mid,
        cm_sums, s_f, g_f, got_fin[0] if direct else None,
    )
    if direct:
        fin = jnp.where(b_at == 0, fin[:, :, :HEAD], fin[:, :, HEAD:])
        final = fin.transpose(0, 2, 1)[None].astype(F32)
    if not lay.strided:
        g_o = jnp.zeros((D, D), BF).at[rank * dcol + jnp.arange(dcol)].set(g_o.reshape(dcol, D))
        g_o = lax.psum_scatter(g_o, ALL, scatter_dimension=0, tiled=True).astype(F32)
    small = small[:, :w_row]
    order = (4, 5, 0, 1, 2, 3, 12, 13, 14, 15, 10, 11, 8, 9)
    small = [small[i] for i in order]

    return (
        layer_output[None],
        input_grad[None],
        final,
        *small[:10],
        g_r,
        g_k,
        g_v,
        g_w,
        g_o,
        *small[10:],
        g_ck,
        g_cv,
        g_cr,
    )


def solution(mesh):
    n_seg, n_seq = mesh.devices.shape
    shape = (n_seg // 2, 2, n_seq // 4, 2, 2)
    view = Mesh(mesh.devices.reshape(shape), ALL)
    lay = Layout(shape)
    seg = ("a", "b")
    vec, mat = P(ALL), P(ALL, None)
    tok = P(seg, SEQ, None)

    def step(*args):
        return per_device(lay, *args)

    return jax.shard_map(
        step,
        mesh=view,
        in_specs=(tok, tok, P(seg, None, None, None), *[vec] * 10, *[mat] * 5, *[vec] * 4, *[mat] * 3),
        out_specs=(tok, tok, P(seg, SEQ, None, None), *[vec] * 10, *[mat] * 5, *[vec] * 4, *[mat] * 3),
        check_vma=False,
    )
```

```python
import jax
import jax.numpy as jnp
from jax import lax
from jax.experimental import pallas as pl
from jax.experimental.pallas import tpu as pltpu
from jax.sharding import Mesh, PartitionSpec as P

TEAM = ("b", "l", "c")
TEAMS = ("a", "h")
SEQ = ("h", "l", "c")
ALL = ("a", "b", "h", "l", "c")
HEAD = 64
CHUNK = 128
EPS = 1e-05
GROUP_EPS = 0.00064
BF = jnp.bfloat16
F32 = jnp.float32


MESH = pl.DeviceIdType.MESH
DMA = pltpu.SemaphoreType.DMA
VMEM_BYTES = 62 << 20


def coords():
    return {name: lax.axis_index(name) for name in ALL}


def rank_of(b, l, c):
    return (b * 2 + l) * 2 + c


def remote(src, dst, sent, landed, to):
    return pltpu.make_async_remote_copy(
        src_ref=src,
        dst_ref=dst,
        send_sem=sent,
        recv_sem=landed,
        device_id=to,
        device_id_type=MESH,
    )


def mates(me):
    for m in range(1, 8):
        yield m, {"b": me["b"] ^ (m >> 2), "l": me["l"] ^ ((m >> 1) & 1), "c": me["c"] ^ (m & 1)}


def greet(me, H, column, across):
    sem = pltpu.get_barrier_semaphore()
    count = 0
    for dh in range(H if column else 1):
        h = lax.rem(me["h"] + dh, H)
        for m in range(8):
            if dh == 0 and m == 0:
                continue
            to = {
                "b": me["b"] ^ (m >> 2),
                "h": h if column else me["h"],
                "l": me["l"] ^ ((m >> 1) & 1),
                "c": me["c"] ^ (m & 1),
            }
            pl.semaphore_signal(sem, inc=1, device_id=to, device_id_type=MESH)
            count += 1
    if across:
        pl.semaphore_signal(sem, inc=1, device_id={"a": 1 - me["a"]}, device_id_type=MESH)
        count += 1
    pl.semaphore_wait(sem, count)


class Copies:
    def __init__(self, sems):
        self.sems, self.k, self.open = sems, 0, []

    def plan(self, src, dst, landed, to):
        copy = remote(src, dst, self.sems.at[self.k], landed, to)
        self.k += 1
        self.open.append(copy)
        return copy

    def go(self, src, dst, landed, to, when=None):
        copy = self.plan(src, dst, landed, to)
        if when is None:
            copy.start()
        else:
            pl.when(when)(copy.start)
        return copy

    def drain(self):
        for copy in self.open:
            copy.wait_send()


def inner(me, H):
    return me["h"] != me["l"] if H == 2 else me["h"] < 0


def landed(ref, sem):
    remote(ref, ref, sem, sem, {"c": 1 - lax.axis_index("c")}).wait_recv()


def upper(ref, half):
    n = ref.shape[0] // 2
    return ref.at[pl.ds(half * n, n)]


class TeamGather:
    def __init__(self, me, own, view, send, recv, via=("xz", "zx")):
        self.me, self.own, self.view, self.recv, self.via = me, own, view, recv, via
        self.copies = Copies(send)
        self.tx, self.tz, self.ts = {"b": 1 - me["b"]}, {"l": 1 - me["l"]}, {"c": 1 - me["c"]}

    def put(self, src, p, half, to):
        self.copies.go(src, upper(self.view(p), half), self.recv.at[p, half], to)

    def start(self):
        mine = rank_of(self.me["b"], self.me["l"], self.me["c"])
        order = [(half, self.tx if self.via[half] == "xz" else self.tz) for half in range(2)]
        order += [(half, self.tz if self.via[half] == "xz" else self.tx) for half in range(2)]
        order += [(0, self.ts), (1, self.ts)]
        for half, to in order:
            self.put(upper(self.own, half), mine, half, to)

    def finish(self):
        b, l, c = self.me["b"], self.me["l"], self.me["c"]
        px, pz, pd = rank_of(1 - b, l, c), rank_of(b, 1 - l, c), rank_of(1 - b, 1 - l, c)
        order = [
            (px, half, self.tz) if self.via[half] == "xz" else (pz, half, self.tx)
            for half in range(2)
        ]
        order += [
            (pz, half, None) if self.via[half] == "xz" else (px, half, None) for half in range(2)
        ]
        for p, half, on in order + [(pd, 0, None), (pd, 1, None)]:
            block = upper(self.view(p), half)
            landed(block, self.recv.at[p, half])
            if on is not None:
                self.put(block, p, half, on)
            self.put(block, p, half, self.ts)
        for q in range(4):
            p = q * 2 + 1 - c
            for half in range(2):
                landed(upper(self.view(p), half), self.recv.at[p, half])
        self.copies.drain()


class TeamSum:
    def __init__(self, me, part, near, acc, mid, far, send, recv, via=("xz", "zx")):
        self.me, self.part, self.near, self.acc, self.mid, self.far = me, part, near, acc, mid, far
        self.recv, self.via = recv, via
        self.copies = Copies(send)

    def start(self):
        b, l, c = self.me["b"], self.me["l"], self.me["c"]
        self.spots = [(b, l), (1 - b, l), (b, 1 - l), (1 - b, 1 - l)]
        for i in (3, 1, 2, 0):
            bb, ll = self.spots[i]
            self.copies.go(
                self.part(rank_of(bb, ll, 1 - c)), self.near.at[i], self.recv.at[i], {"c": 1 - c}
            )

    def tiles(self, rows, body):
        step = max(16, 65536 // self.near.shape[2])

        @pl.loop(0, rows // step)
        def _(t):
            body(pl.ds(pl.multiple_of(t * step, step), step))

    def pair(self, i, write):
        bb, ll = self.spots[i]
        landed(self.near.at[i], self.recv.at[i])
        mine = self.part(rank_of(bb, ll, self.me["c"]))
        self.tiles(
            self.near.shape[1], lambda at: write(at, mine[at].astype(F32) + self.near[i, at].astype(F32))
        )

    def finish(self, write, then=lambda: None, between=lambda: None):
        b, l = self.me["b"], self.me["l"]
        tx, tz = {"b": 1 - b}, {"l": 1 - l}
        acc, mid, far, recv, go = self.acc, self.mid, self.far, self.recv, self.copies.go
        n = mid.shape[1]
        hops = [
            (tx, 0, tz, 1) if self.via[half] == "xz" else (tz, 1, tx, 0) for half in range(2)
        ]
        for i in (3, 1, 2):

            def put(at, v):
                acc[i - 1, at] = v.astype(BF)

            self.pair(i, put)
            if i == 3:
                for half, (one, _, _, _) in enumerate(hops):
                    go(upper(acc.at[2], half), mid.at[half], recv.at[4 + half], one)
        between()
        for half, (one, direct, two, other) in enumerate(hops):
            landed(mid.at[half], recv.at[4 + half])
            into, came = upper(acc.at[other], half), mid.at[half]

            def add(at):
                into[at] = (into[at].astype(F32) + came[at].astype(F32)).astype(BF)

            self.tiles(n, add)
            go(into, upper(far.at[other], half), recv.at[8 + half], two)
            go(upper(acc.at[direct], half), upper(far.at[direct], half), recv.at[6 + half], one)
        then()
        for half, (_, direct, _, other) in enumerate(hops):
            landed(upper(far.at[direct], half), recv.at[6 + half])
            landed(upper(far.at[other], half), recv.at[8 + half])

        def last(at, v):
            write(at, v + far[0, at].astype(F32) + far[1, at].astype(F32))

        self.pair(0, last)
        self.copies.drain()

    @staticmethod
    def scratch(R, C):
        return [
            pltpu.VMEM((4, R, C), BF),
            pltpu.VMEM((3, R, C), BF),
            pltpu.VMEM((2, R // 2, C), BF),
            pltpu.VMEM((2, R, C), BF),
            DMA((10,)),
            DMA((10,)),
        ]


class TeamsGather:
    def __init__(self, me, H, source, out, send, near, far, team=None, count=2):
        self.me, self.H, self.source, self.out = me, H, source, out
        self.near, self.far, self.team, self.count = near, far, team, count
        self.held = []
        self.copies = Copies(send)

    @staticmethod
    def sems(H, count=2):
        return [DMA((7 + count * (2 * H - 1),)), DMA((8,)), DMA((2 * H, count))]

    def groups(self, only=None):
        b, n = self.me["b"], 8 // self.count
        for g in range(self.count):
            if only is None or g in only:
                at = g * n
                yield g, (b if at < 4 else 1 - b), at % 4, n

    def block(self, a, bb, h, lo, n):
        return self.out.at[a, bb, h, pl.ds(lo, n)]

    def start(self):
        me = self.me
        a, b, h, l, c = (me[n] for n in ALL)
        for m, to in mates(me):
            p = rank_of(to["b"], to["l"], to["c"])
            mine = rank_of(b, l, c)
            self.copies.go(self.source(p), self.out.at[a, b, h, l * 2 + c], self.near.at[mine], to)

    def spread(self, local=None, only=None):
        me = self.me
        a, b, h, l, c = (me[n] for n in ALL)
        if local is not None:
            local.wait()
        for g, bb, lo, n in self.groups(only):
            block = self.block(a, bb, h, lo, n)
            src = block
            if self.team is not None:
                src = self.team.at[pl.ds(bb * 4 + lo, n)]
            else:
                for m in range(1 - g, 4):
                    ll, cc = l ^ (m >> 1), c ^ (m & 1)
                    landed(self.out.at[a, bb, h, ll * 2 + cc], self.near.at[rank_of(bb, ll, cc)])
            for dh in range(1, self.H):
                to = lax.rem(h + dh, self.H)
                when = jnp.logical_not(inner(me, self.H))
                copy = self.copies.go(src, block, self.far.at[dh, g], {"h": to}, when)
                self.held.append((g, copy))
            self.copies.go(src, block, self.far.at[0, g], {"a": 1 - a})

    def release(self, only=None):
        for g, copy in self.held:
            if only is None or g in only:
                pl.when(inner(self.me, self.H))(copy.start)

    def forward(self, only=None):
        a, h, H = self.me["a"], self.me["h"], self.H
        for g, bb, lo, n in self.groups(only):
            for dh in range(1, H):
                block = self.block(a, bb, lax.rem(h - dh + H, H), lo, n)
                landed(block, self.far.at[dh, g])
                self.copies.go(block, block, self.far.at[H - 1 + dh, g], {"a": 1 - a})

    def finish(self):
        a, h, H = self.me["a"], self.me["h"], self.H
        for g, bb, lo, n in self.groups():
            landed(self.block(1 - a, bb, h, lo, n), self.far.at[0, g])
            for dh in range(1, H):
                block = self.block(1 - a, bb, lax.rem(h - dh + H, H), lo, n)
                landed(block, self.far.at[H - 1 + dh, g])
        self.copies.drain()


class Halo:
    def __init__(self, me, H, own, out, send, recv):
        self.me, self.H, self.own, self.out, self.send, self.recv = me, H, own, out, send, recv
        self.last = (me["l"] == 1) & (me["c"] == 1) & (me["h"] < H - 1)

    def each(self):
        me = self.me
        n = self.own.shape[0]
        for p in range(8):
            to = {
                "b": p >> 2,
                "h": jnp.minimum(me["h"] + 1, self.H - 1),
                "l": (p >> 1) & 1,
                "c": p & 1,
            }
            src = self.own.at[pl.ds(n - 16, 16)]
            yield remote(src, self.out.at[me["b"]], self.send.at[p], self.recv.at[me["b"]], to)

    def start(self):
        if self.H == 1:
            return

        @pl.when(self.last)
        def _():
            for copy in self.each():
                copy.start()

    def finish(self):
        if self.H == 1:
            return

        @pl.when(self.me["h"] > 0)
        def _():
            for b in range(2):
                landed(self.out.at[b], self.recv.at[b])

        @pl.when(self.last)
        def _():
            for copy in self.each():
                copy.wait_send()


class Edge:
    def __init__(self, me, H, first, got, send, recv):
        self.me, self.H, self.first, self.got, self.send, self.recv = me, H, first, got, send, recv

    def each(self):
        me = self.me
        mine = rank_of(me["b"], me["l"], me["c"])
        for b in range(2):
            to = {"b": b, "h": jnp.maximum(me["h"] - 1, 0), "l": 1, "c": 1}
            yield remote(self.first.at[b], self.got.at[mine], self.send.at[b], self.recv.at[mine], to)

    def start(self):
        if self.H == 1:
            return

        @pl.when(self.me["h"] > 0)
        def _():
            for copy in self.each():
                copy.start()

    def finish(self, out):
        if self.H == 1:
            return
        me = self.me

        @pl.when((me["l"] == 1) & (me["c"] == 1) & (me["h"] < self.H - 1))
        def _():
            for p in range(8):
                landed(self.got.at[p], self.recv.at[p])
            total = self.got[0, 0:1].astype(F32)
            for p in range(1, 8):
                total = total + self.got[p, 0:1].astype(F32)
            n = out.shape[0]
            out[n - 1 : n] = out[n - 1 : n] + total

        @pl.when(me["h"] > 0)
        def _():
            for copy in self.each():
                copy.wait_send()


class Exchange:
    def __init__(self, me, source, out, send, recv):
        self.me, self.source, self.out, self.recv = me, source, out, recv
        self.copies = Copies(send)

    def start(self):
        mine = rank_of(self.me["b"], self.me["l"], self.me["c"])
        for m, to in mates(self.me):
            p = rank_of(to["b"], to["l"], to["c"])
            self.copies.go(self.source(p), self.out(mine), self.recv.at[mine], to)

    def finish(self):
        for m, to in mates(self.me):
            p = rank_of(to["b"], to["l"], to["c"])
            landed(self.out(p), self.recv.at[p])
        self.copies.drain()


ANY = pl.BlockSpec(memory_space=pl.ANY)
VM = pl.BlockSpec(memory_space=pltpu.VMEM)


def comm_call(body, outs, in_specs, out_specs, scratch, cid):
    return pl.pallas_call(
        body,
        out_shape=outs,
        in_specs=in_specs,
        out_specs=out_specs,
        scratch_shapes=scratch,
        compiler_params=pltpu.CompilerParams(
            collective_id=cid, has_side_effects=True, vmem_limit_bytes=VMEM_BYTES
        ),
    )


def dot_nn(a, b):
    return jnp.dot(a, b, preferred_element_type=F32)


def dot_nt(a, b):
    return lax.dot_general(a, b, (((1,), (1,)), ((), ())), preferred_element_type=F32)


def dot_tn(a, b):
    return lax.dot_general(a, b, (((0,), (0,)), ((), ())), preferred_element_type=F32)


MIX = 32


def rows_at(i, n):
    return pl.ds(pl.multiple_of(i * n, n), n)


class RowsGather:
    def __init__(self, me, H, own, out, send, recv, at=None, inner_first=False):
        self.me, self.H, self.own, self.out, self.recv, self.at = me, H, own, out, recv, at
        self.first = inner(me, H)
        if not inner_first:
            self.first = jnp.logical_not(self.first)
        self.copies = Copies(send)

    @staticmethod
    def sems(H):
        return [DMA((2 * H - 1,)), DMA((2 * H,))]

    def block(self, a, h):
        return self.out.at[a, h] if self.at is None else self.out.at[a, h, self.at]

    def start(self):
        a, h = self.me["a"], self.me["h"]
        block = self.block(a, h)
        self.held = []
        for dh in range(1, self.H):
            to = lax.rem(h + dh, self.H)
            self.held.append(self.copies.go(self.own, block, self.recv.at[dh], {"h": to}, self.first))
        self.copies.go(self.own, block, self.recv.at[0], {"a": 1 - a})

    def release(self):
        for copy in self.held:
            pl.when(jnp.logical_not(self.first))(copy.start)

    def forward(self, early=None):
        a, h, H = self.me["a"], self.me["h"], self.H
        if early:
            self.passed = []
        for dh in range(1, H):
            block = self.block(a, lax.rem(h - dh + H, H))
            if early is None:
                landed(block, self.recv.at[dh])
                self.copies.go(block, block, self.recv.at[H - 1 + dh], {"a": 1 - a})
                continue
            if early:
                on = self.copies.plan(block, block, self.recv.at[H - 1 + dh], {"a": 1 - a})
                self.passed.append(on)
            on = self.passed[dh - 1]
            now = jnp.logical_not(self.first) if H == 2 else self.first
            now = now if early else jnp.logical_not(now)

            @pl.when(now)
            def _():
                landed(block, self.recv.at[dh])
                on.start()

    def finish(self):
        a, h, H = self.me["a"], self.me["h"], self.H
        landed(self.block(1 - a, h), self.recv.at[0])
        for dh in range(1, H):
            landed(self.block(1 - a, lax.rem(h - dh + H, H)), self.recv.at[H - 1 + dh])
        self.copies.drain()


def join_lanes(pieces, width):
    per = 128 // width
    out = []
    for g in range(0, len(pieces), per):
        acc = pieces[g]
        for k in range(1, per):
            acc = acc + pltpu.roll(pieces[g + k], width * k, axis=1)
        out.append(acc)
    return jnp.concatenate(out, axis=1) if len(out) > 1 else out[0]


def norm_rows(v):
    mean = jnp.mean(v, axis=-1, keepdims=True)
    cent = v - mean
    rstd = lax.rsqrt(jnp.mean(cent * cent, axis=-1, keepdims=True) + EPS)
    return cent * rstd, rstd


def mix_rows(read, first, carry, shares, write, tiles, rows):
    per = tiles // 2

    @pl.loop(0, tiles)
    def _(p):
        n = read(p)
        prev = jnp.where(lax.rem(p, per) == 0, first(p // per), carry[...])
        row = lax.broadcasted_iota(jnp.int32, n.shape, 0)
        before = jnp.where(row == 0, prev, pltpu.roll(n, 1, axis=0))
        carry[...] = n[rows - 1 : rows]
        diff = n - before
        for i, s in enumerate(shares):
            write(i, p, (before + s * diff).astype(BF))
        write(None, p, diff.astype(BF))


def block_ones(m):
    row = lax.broadcasted_iota(jnp.int32, (m, m), 0) // HEAD
    col = lax.broadcasted_iota(jnp.int32, (m, m), 1) // HEAD
    return jnp.where(row == col, 1.0, 0.0).astype(F32)


def dot_exact(a, b):
    return jnp.dot(a, b, preferred_element_type=F32, precision=lax.Precision.HIGHEST)


class Decay:
    def __init__(self, lam):
        m = lam.shape[1]
        i = lax.broadcasted_iota(jnp.int32, (CHUNK, m), 0).astype(F32)
        self.i = i
        self.down = jnp.exp(-lam * i)
        self.up = jnp.exp(lam * (i + 1.0))
        self.tail = jnp.exp(-lam * (CHUNK - 1.0 - i))
        self.span = jnp.exp(-lam * CHUNK)


def stacked_heads(v):
    m = v.shape[1]
    lane = lax.broadcasted_iota(jnp.int32, v.shape, 1) // HEAD
    zero = jnp.zeros_like(v)
    return jnp.concatenate([jnp.where(lane == g, v, zero) for g in range(m // HEAD)], axis=0)


def own_heads(v):
    m = v.shape[1]
    lane = lax.broadcasted_iota(jnp.int32, (CHUNK, m), 1) // HEAD
    out = v[:CHUNK]
    for g in range(1, m // HEAD):
        out = jnp.where(lane == g, v[g * CHUNK : (g + 1) * CHUNK], out)
    return out


def triangle(heads, low):
    shape = (heads * CHUNK, CHUNK)
    row = lax.rem(lax.broadcasted_iota(jnp.int32, shape, 0), CHUNK)
    col = lax.broadcasted_iota(jnp.int32, shape, 1)
    return row > col if low else row < col


def squeeze(s0, s1):
    def fold(s):
        out = s[:, :128]
        for g in range(1, s.shape[1] // 128):
            out = out + s[:, g * 128 : (g + 1) * 128]
        return out + pltpu.roll(out, HEAD, axis=1)

    lane = lax.broadcasted_iota(jnp.int32, (s0.shape[0], 128), 1)
    return jnp.where(lane < HEAD, fold(s0), fold(s1))


def widen(p, second, ones):
    lane = lax.broadcasted_iota(jnp.int32, p.shape, 1)
    keep = (lane >= HEAD) if second else (lane < HEAD)
    both = jnp.where(keep, p, pltpu.roll(p, HEAD, axis=1))
    return jnp.concatenate([both] * (ones.shape[1] // 128), axis=1) * ones


class Chain:
    def __init__(self, me, H, ahead, out_box, in_box, send, recv):
        h = me["h"]
        self.h, self.H = h, H
        nxt = jnp.minimum(h + 1, H - 1) if ahead else jnp.maximum(h - 1, 0)
        self.has_next = (h < H - 1) if ahead else (h > 0)
        self.has_prev = (h > 0) if ahead else (h < H - 1)
        self.out_box, self.in_box = out_box, in_box
        self.copy = remote(out_box, in_box, send, recv, {"h": nxt})

    def run(self, state, closing, span_all, ones):
        if self.H == 1:
            return

        @pl.when(self.has_prev)
        def _():
            self.copy.wait_recv()
            p = self.in_box[...].astype(F32)
            for s in range(2):
                state[s] = widen(p, s == 1, ones)

        @pl.when(self.has_next)
        def _():
            out = squeeze(*(span_all * state[s] + closing[s] for s in range(2)))
            self.out_box[...] = out.astype(BF)
            self.copy.start()

    def finish(self):
        if self.H == 1:
            return

        @pl.when(self.has_next)
        def _():
            self.copy.wait_send()


def window(read, width, s):
    if s < 0:
        return pltpu.roll(read(0, 128).astype(F32), -s, axis=1)
    t, off = s // 128 * 128, s % 128
    if off == 0:
        return read(t, t + 128).astype(F32)
    if t + 256 <= width:
        return pltpu.roll(read(t, t + 256).astype(F32), 256 - off, axis=1)[:, :128]
    return pltpu.roll(read(t, t + 128).astype(F32), 128 - off, axis=1)


def lay_lanes(width, parts, put):
    for lo in range(0, width, 128):
        out = None
        for read, wide, src, dst, n in parts:
            d0, d1 = max(dst - lo, 0), min(dst + n - lo, 128)
            if d0 >= d1:
                continue
            v = window(read, wide, src + lo - dst)
            if out is not None:
                lane = lax.broadcasted_iota(jnp.int32, v.shape, 1)
                v = jnp.where((lane >= d0) & (lane < d1), v, out)
            out = v
        put(lo, out)


def rank_columns(lay, n, whole, p):
    w, m = n // lay.n, n // 8
    if w % whole:
        return [(p * m, 0, m)]
    b, l, c = p >> 2, (p >> 1) & 1, p & 1
    teams = [(i, j) for i in range(lay.A) for j in range(lay.H)]
    return [
        (((((i * 2 + b) * lay.H + j) * 2 + l) * 2 + c) * w, k * w, w) for k, (i, j) in enumerate(teams)
    ]


def front(lay, vecs, x, up, w4, w_ck, w_cr, w_o, w_cv, start):
    H, A = lay.H, lay.A
    grid = (A, 2, H, 4)
    rows, D = x.shape
    T = 8 * rows
    m = D // 8
    w_row = D // lay.n
    kk = D // (2 * A)
    heads = m // HEAD
    per = T // 2 // CHUNK
    bring_o = lay.strided
    wo_shape = (A, H, m // (A * H), D)
    cv_rows = w_cv.shape[0]
    F = w_ck.shape[1]
    nf = F // 8 + m
    k_row = w_ck.shape[0]
    early = cv_rows // 2 // 16 * 16 if cv_rows % 16 == 0 else 0

    def body(*refs):
        vecs, x, up, w_r, w_k, w_v, w_g, w_ck, w_cr, w_o, w_cv, start = refs[:12]
        refs = refs[4:]
        full, mine_v, mixed, diff, rkv, gate, upc, w_out = refs[8:16]
        wo, gated, ghat, grstd, states, fin, middle, n2, halo2, wcv, wf = refs[16:27]
        va, xg, halo, hn, carry, mx, df, wa, wos, team = refs[27:37]
        adds, st, cl, obox, ibox, own = refs[37:43]
        near, acc, mid, far, ss, sr = refs[43:49]
        vs, vn, vf, xs, xr, hs, hr, us, ur, ws, wn, wf_, qs, qr, os_, or_ = refs[49:65]
        es, er, cs, cr, ts, tr, fs, fn, ff, gs, gr, ks, kr, ls = refs[65:79]
        w, later, sbuf, zbuf, bs, br = refs[79:]
        part = xg
        me = coords()
        a, b, h, l, c = (me[n] for n in ALL)
        mine = rank_of(b, l, c)

        def cols(ref, p):
            return ref.at[:, pl.ds(pl.multiple_of(p * m, m), m)]

        for p in range(8):
            for j, ref in enumerate((w_r, w_k, w_v, w_g)):
                read = lambda lo, hi, ref=ref: ref[:, lo:hi]
                parts = [(read, D, *at) for at in rank_columns(lay, D, HEAD, p)]

                def put_w(lo, v, p=p, j=j):
                    w[p, :, j * m + lo : j * m + lo + 128] = v.astype(BF)

                lay_lanes(m, parts, put_w)

        local = [
            pltpu.make_async_copy(w.at[mine], wa.at[a, b, h, l * 2 + c], ls.at[0]),
            pltpu.make_async_copy(x, xg.at[rows_at(mine, rows)], ls.at[2]),
            pltpu.make_async_copy(cols(up, mine), upc.at[mine], ls.at[3]),
            pltpu.make_async_copy(vecs, va.at[a, b, h, l * 2 + c], ls.at[4]),
            pltpu.make_async_copy(w_o, wos.at[a, h] if bring_o else wos, ls.at[5]),
            pltpu.make_async_copy(w_cv, wcv.at[a, h], ls.at[6]),
        ]
        for copy in local:
            copy.start()
        greet(me, H, True, True)
        gw = TeamsGather(me, H, lambda p: w.at[p], wa, ws, wn, wf_)
        gv = TeamsGather(me, H, lambda p: vecs, va, vs, vn, vf)
        gx = TeamGather(me, x, lambda p: xg.at[rows_at(p, rows)], xs, xr, ("zx", "zx"))
        gh = Halo(me, H, x, halo, hs, hr)
        gu = Exchange(me, lambda p: cols(up, p), lambda p: upc.at[p], us, ur)
        gq = Exchange(me, lambda p: later.at[p], lambda p: team.at[p], qs, qr)
        gf = TeamsGather(me, H, None, wf, fs, fn, ff, team, 4)
        if bring_o:
            go = RowsGather(me, H, w_o, wos, os_, or_)
        top, rest = pl.ds(0, early), pl.ds(early, cv_rows - early)
        if early:
            ge = RowsGather(me, H, w_cv.at[top], wcv, es, er, top, True)
        gc = RowsGather(me, H, w_cv.at[rest], wcv, ts, tr, rest, True)
        def head(bb, k):
            if lay.strided:
                return (((k // H * 2 + bb) * H + k % H) * 2 + l) * 2 + c
            return rank_of(bb, l, c) * heads + k

        near_states = [
            pltpu.make_async_copy(start.at[head(b, k)], sbuf.at[b, k], ls.at[14 + k]) for k in range(heads)
        ]
        far_states = [
            remote(start.at[head(1 - b, k)], sbuf.at[b, k], bs.at[k], br.at[k], {"b": 1 - b})
            for k in range(heads)
        ]
        gv.start()
        gh.start()
        gw.start()
        for copy in near_states + far_states:
            copy.start()
        if early:
            ge.start()
        gc.start()
        gx.start()
        gv.spread(local[3])
        gv.release()
        gv.forward()
        gw.spread(local[0])
        gv.finish()
        local[1].wait()
        gx.finish()
        gw.release()
        gu.start()
        for p in range(8):
            parts = [(lambda lo, hi: w_ck[:, lo:hi], F, *at) for at in rank_columns(lay, F, 1, p)]

            def put_ck(lo, v, p=p):
                later[p, :, lo : lo + 128] = v.astype(BF)

            lay_lanes(F // 8, parts, put_ck)
            later[p, :, F // 8 :] = w_cr[:, p * m : (p + 1) * m]
        mine_team = pltpu.make_async_copy(later.at[mine], team.at[mine], ls.at[1])
        mine_team.start()
        gq.start()
        gw.forward((0,))
        gh.finish()

        def piece(*at):
            return va[at].astype(F32)

        flat = [
            piece(i, j, k, q) for i in range(A) for j in range(2) for k in range(H) for q in range(4)
        ]
        full[...] = join_lanes(flat, w_row)
        if lay.strided:
            held = [piece(i, b, k, l * 2 + c) for i in range(A) for k in range(H)]
            mine_v[...] = join_lanes(held, w_row)
        else:
            mine_v[...] = full[:, pl.ds(pl.multiple_of(mine * m, m), m)]
        gain, bias = full[0:1], full[1:2]
        for s in range(2):
            row = (norm_rows(halo[s].astype(F32))[0] * gain + bias)[15:16]
            hn[s] = jnp.where(h > 0, row, jnp.zeros_like(row))

        def write(i, p, v):
            if i is None:
                df[rows_at(p, MIX)] = v
            else:
                mx[i, rows_at(p, MIX)] = v

        mix_rows(
            lambda p: norm_rows(xg[rows_at(p, MIX)].astype(F32))[0] * gain + bias,
            lambda s: hn[s],
            carry,
            [full[2 + i : 3 + i] for i in range(4)],
            write,
            T // MIX,
            MIX,
        )
        keep = [
            pltpu.make_async_copy(mx, mixed, ls.at[7]),
            pltpu.make_async_copy(df, diff, ls.at[8]),
        ]
        for copy in keep:
            copy.start()
        gw.forward((1,))
        if bring_o:
            go.start()
            go.release()
        mine_team.wait()
        gq.finish()
        keep += [
            pltpu.make_async_copy(team.at[pl.ds(0, 4)], wf.at[a, 0, h], ls.at[11]),
            pltpu.make_async_copy(team.at[pl.ds(4, 4)], wf.at[a, 1, h], ls.at[12]),
        ]
        for copy in keep[2:]:
            copy.start()
        gf.spread(None, (0, 1, 2))
        gf.release((0,))
        gw.finish()
        keep.append(pltpu.make_async_copy(wa, w_out, ls.at[9]))
        keep[-1].start()
        for j in range(4):

            @pl.loop(0, 4)
            def _(t):
                at = rows_at(t, T // 4)
                acc = jnp.zeros((T // 4, m), F32)
                for i in range(A):
                    for k in range(2):
                        lo = (i * 2 + k) * kk
                        wt = wa[i, k, :, :, :, j * m : (j + 1) * m].reshape(kk, m)
                        acc = acc + dot_nn(mx[j, at, lo : lo + kk], wt)
                if j < 3:
                    rkv[j, at] = acc.astype(BF)
                else:
                    gate[at] = acc

        ones = block_ones(m)
        dec = Decay(mine_v[6:7])
        u = mine_v[7:8]
        span_all = jnp.exp(-mine_v[6:7] * (T // 2))

        def tile(i, s, n):
            return rkv[i, rows_at(s * per + n, CHUNK)].astype(F32)

        cl[...] = jnp.zeros_like(cl)

        @pl.loop(0, per)
        def _(n):
            for s in range(2):
                kt = (tile(1, s, n) * dec.tail).astype(BF)
                v = rkv[2, rows_at(s * per + n, CHUNK)]
                add = dot_tn(v, kt) * ones
                adds[s, n] = add
                cl[s] = dec.span * cl[s] + add

        for copy in near_states:
            copy.wait()
        for copy in far_states:
            copy.wait_send()
        for k in range(heads):
            landed(sbuf.at[1 - b, k], br.at[k])
        odd = lax.rem(lax.broadcasted_iota(jnp.int32, (m, 128), 0) // HEAD, 2) == 1
        zbuf[...] = jnp.zeros_like(zbuf)
        for s in range(2):
            for k in range(heads):
                zbuf[k * HEAD : (k + 1) * HEAD, :HEAD] = sbuf[s, k]
            z = zbuf[...]
            z = jnp.where(odd, pltpu.roll(z, HEAD, axis=1), z)
            z = (jnp.concatenate([z] * (m // 128), axis=1) * ones).T
            st[s] = jnp.where(h > 0, jnp.zeros_like(z), z)
        chain = Chain(me, H, True, obox, ibox, cs, cr)
        chain.run(st, cl, span_all, ones)
        gf.release((1, 2))
        if early:
            ge.release()
        local[4].wait()
        if bring_o:
            go.forward()
        gf.forward((0,))
        if early:
            ge.forward(True)
        gc.forward(True)
        low = triangle(heads, True)

        @pl.loop(0, per)
        def _(n):
            for s in range(2):
                at = rows_at(s * per + n, CHUNK)
                r, k, v = (tile(i, s, n) for i in range(3))
                vb = rkv[2, at]
                rd = (r * dec.down).astype(BF)
                kg = (k * dec.up).astype(BF)
                state = st[s]
                states[s, n] = state
                att = jnp.where(low, dot_nt(stacked_heads(rd), kg), 0.0).astype(BF)
                y = own_heads(dot_nn(att, vb)) + dot_nt(rd, state.astype(BF))
                y = y + dot_exact(r * u * k, ones) * v
                st[s] = dec.span * state + adds[s, n]
                mean = dot_exact(y, ones) * (1.0 / HEAD)
                cent = y - mean
                rstd = lax.rsqrt(dot_exact(cent * cent, ones) * (1.0 / HEAD) + GROUP_EPS)
                hat = cent * rstd
                ghat[at] = hat
                grstd[at] = rstd
                g = gate[at]
                silu = g / (1.0 + jnp.exp(-g))
                gated[at] = ((hat * mine_v[8:9] + mine_v[9:10]) * silu).astype(BF)

        fin[...] = squeeze(st[0], st[1])
        chain.finish()
        if bring_o:
            go.finish()
        keep.append(pltpu.make_async_copy(wos, wo, ls.at[13]))
        keep[-1].start()

        @pl.loop(0, 8)
        def _(p):
            g = gated[rows_at(p, rows)]
            w = wos[...].reshape(m, D)
            for q in range(4):
                lo = q * (D // 4)
                part[rows_at(p, rows), lo : lo + D // 4] = dot_nn(g, w[:, lo : lo + D // 4]).astype(BF)

        sums = TeamSum(me, lambda p: part.at[rows_at(p, rows)], near, acc, mid, far, ss, sr, ("xz", "xz"))
        sums.start()

        def put(at, v):
            v = x[at].astype(F32) + v
            middle[at] = v
            own[at] = (norm_rows(v)[0] * full[10:11] + full[11:12]).astype(BF)

        def more():
            gf.forward((1, 2))
            gf.spread(None, (3,))
            gc.release()

        sums.finish(put, more)
        keep.append(pltpu.make_async_copy(own, n2.at[mine], ls.at[10]))
        keep[-1].start()
        gn = TeamGather(me, own, lambda p: n2.at[p], gs, gr, ("zx", "zx"))
        gn.start()
        gk = Halo(me, H, own, halo2, ks, kr)
        gk.start()
        gf.release((3,))
        if early:
            ge.forward(False)
        gn.finish()
        gk.finish()
        gf.forward((3,))
        gc.forward(False)
        gu.finish()
        gf.finish()
        if early:
            ge.finish()
        gc.finish()
        for copy in local[2:3] + local[5:] + keep:
            copy.wait()

    gsems = TeamsGather.sems(H)
    team_sems = [DMA((14,)), DMA((8, 2))]
    halo_sems = [DMA((8,)), DMA((2,))]
    move_sems = [DMA((7,)), DMA((8,))]
    return comm_call(
        body,
        (
            jax.ShapeDtypeStruct((16, D), F32),
            jax.ShapeDtypeStruct((16, m), F32),
            jax.ShapeDtypeStruct((4, T, D), BF),
            jax.ShapeDtypeStruct((T, D), BF),
            jax.ShapeDtypeStruct((3, T, m), BF),
            jax.ShapeDtypeStruct((T, m), F32),
            jax.ShapeDtypeStruct((8, rows, m), BF),
            jax.ShapeDtypeStruct((*grid, k_row, 4 * m), BF),
            jax.ShapeDtypeStruct(wo_shape, BF),
            jax.ShapeDtypeStruct((T, m), BF),
            jax.ShapeDtypeStruct((T, m), F32),
            jax.ShapeDtypeStruct((T, m), F32),
            jax.ShapeDtypeStruct((2, per, m, m), F32),
            jax.ShapeDtypeStruct((m, 128), F32),
            jax.ShapeDtypeStruct((rows, D), F32),
            jax.ShapeDtypeStruct((8, rows, D), BF),
            jax.ShapeDtypeStruct((2, 16, D), BF),
            jax.ShapeDtypeStruct((A, H, *w_cv.shape), BF),
            jax.ShapeDtypeStruct((*grid, k_row, nf), BF),
        ),
        [VM] * 11 + [ANY],
        (VM, VM, ANY, ANY, VM, VM, ANY, ANY, ANY, VM, VM, VM, VM, VM, VM, ANY, ANY, ANY, ANY),
        [
            pltpu.VMEM((*grid, *vecs.shape), BF),
            pltpu.VMEM((T, D), BF),
            pltpu.VMEM((2, 16, D), BF),
            pltpu.VMEM((2, 1, D), F32),
            pltpu.VMEM((1, D), F32),
            pltpu.VMEM((4, T, D), BF),
            pltpu.VMEM((T, D), BF),
            pltpu.VMEM((*grid, k_row, 4 * m), BF),
            pltpu.VMEM(wo_shape, BF),
            pltpu.VMEM((8, k_row, nf), BF),
            pltpu.VMEM((2, per, m, m), F32),
            pltpu.VMEM((2, m, m), F32),
            pltpu.VMEM((2, m, m), F32),
            pltpu.VMEM((m, 128), BF),
            pltpu.VMEM((m, 128), BF),
            pltpu.VMEM((rows, D), BF),
            *TeamSum.scratch(rows, D),
            *gsems,
            *team_sems,
            *halo_sems,
            *move_sems,
            *gsems,
            *move_sems,
            *RowsGather.sems(H),
            *RowsGather.sems(H),
            DMA,
            DMA,
            *RowsGather.sems(H),
            *TeamsGather.sems(H, 4),
            *team_sems,
            *halo_sems,
            DMA((14 + heads,)),
            pltpu.VMEM((8, k_row, 4 * m), BF),
            pltpu.VMEM((8, k_row, nf), BF),
            pltpu.VMEM((2, heads, HEAD, HEAD), F32),
            pltpu.VMEM((m, 128), F32),
            DMA((heads,)),
            DMA((heads,)),
        ],
        0,
    )(vecs, x, up, *w4, w_ck, w_cr, w_o, w_cv, start)


class Background:
    def __init__(self, items, H):
        self.items, self.H = items, H

    def arrays(self):
        return [v for v, _ in self.items]

    def outs(self):
        shapes = []
        for v, kind in self.items:
            lead = {"h": (max(self.H - 1, 1),), "a": (), "t": (8,)}[kind]
            shapes.append(jax.ShapeDtypeStruct((*lead, *v.shape[1:]), BF))
        return shapes

    def sems(self):
        out = []
        for _, kind in self.items:
            n = {"h": max(self.H - 1, 1), "a": 1, "t": 8}[kind]
            out += [DMA((n,)), DMA((n,))] + ([DMA] if kind == "t" else [])
        return out

    def start(self, me, srcs, dsts, sems):
        self.open = []
        sems = list(sems)
        h, H = me["h"], self.H
        mine = rank_of(me["b"], me["l"], me["c"])
        for (_, kind), src, dst in zip(self.items, srcs, dsts):
            ss, sr = sems.pop(0), sems.pop(0)
            copies = Copies(ss)
            if kind == "h":
                for dh in range(1, H):
                    to = lax.rem(h + dh, H)
                    copies.go(src.at[to], dst.at[dh - 1], sr.at[dh - 1], {"h": to})
                    self.open.append((dst.at[dh - 1], sr.at[dh - 1]))
            elif kind == "a":
                copies.go(src.at[1 - me["a"]], dst, sr.at[0], {"a": 1 - me["a"]})
                self.open.append((dst, sr.at[0]))
            else:
                keep = pltpu.make_async_copy(src.at[mine], dst.at[mine], sems.pop(0))
                keep.start()
                self.open.append(keep)
                for m, to in mates(me):
                    p = rank_of(to["b"], to["l"], to["c"])
                    copies.go(src.at[p], dst.at[mine], sr.at[mine], to)
                    self.open.append((dst.at[p], sr.at[p]))
            self.open.append(copies)

    def finish(self):
        for item in self.open:
            if isinstance(item, tuple):
                landed(*item)
            elif isinstance(item, Copies):
                item.drain()
            else:
                item.wait()


def back_rows(T, tile, chunk, shares, diff, part, first, sums):
    per = T // 2 // tile

    def step(q, carry):
        t = 2 * per - 1 - q
        ds = chunk(t)
        dif = diff(t)
        late = jnp.zeros_like(ds[0])
        here = jnp.zeros_like(ds[0])
        for i, (d, s) in enumerate(zip(ds, shares)):
            sums[i][...] = sums[i][...] + jnp.sum(d * dif, axis=0, keepdims=True)
            late = late + (1.0 - s) * d
            here = here + s * d
        carry = jnp.where(lax.rem(t, per) == per - 1, jnp.zeros_like(carry), carry)
        row = lax.broadcasted_iota(jnp.int32, late.shape, 0)
        part(t, here + jnp.where(row == tile - 1, carry, pltpu.roll(late, tile - 1, axis=0)))

        @pl.when(lax.rem(t, per) == 0)
        def _():
            first(t // per, late[:16].astype(BF))

        return late[:1]

    zero = jnp.zeros((1, diff(0).shape[1]), F32)
    lax.fori_loop(0, 2 * per, step, zero)


def channel_mix(lay, n2, halo, full, wcv, wf, upc, middle, up, items):
    H, A = lay.H, lay.A
    rows, D = middle.shape
    T = 8 * rows
    F, m = wcv.shape[0], D // 8
    nk, kk, _ = wf.shape
    w_cv = F // (A * H)
    tile = T // 4
    dq = D // 4
    bg = Background(items, H)
    nb = len(items)

    def body(n2, halo, full, wcv_in, wf_in, upc, middle, up, *rest):
        srcs, rest = rest[:nb], rest[nb:]
        d_mid, d_br, moved, s_cv, got_cv, g_f, got_f, sums = rest[:8]
        dsts, rest = rest[8 : 8 + nb], rest[:8] + rest[8 + nb :]
        (big, m2, df, carry, relu, act, sg, d_pg, d_val, dval, gcv, cvbuf, stage) = rest[8:21]
        (dn2, own, add, first, edge) = rest[21:26]
        cn, ca, cm, cf, c_s, c_r = rest[26:32]
        rn, ra, rm, rf, r_s, r_r = rest[32:38]
        ds, dr, bs, br, es, er, ms, mr, vs, vr, fs, fr, ls = rest[38:51]
        wf, wcv = rest[51 + len(bg.sems()) :]
        d_pre = act
        me = coords()
        a, b, h, l, c = (me[n] for n in ALL)
        mine = rank_of(b, l, c)
        loads = [
            pltpu.make_async_copy(n2.at[p], big.at[pl.ds(p * rows, rows)], ls.at[p]) for p in range(8)
        ]
        loads.append(pltpu.make_async_copy(wf_in, wf, ls.at[14]))
        loads.append(pltpu.make_async_copy(wcv_in, wcv, ls.at[15]))
        for copy in loads:
            copy.start()
        greet(me, H, True, True)
        for copy in loads[:8]:
            copy.wait()

        def write(i, p, v):
            if i is None:
                df[rows_at(p, MIX)] = v
            else:
                m2[i, rows_at(p, MIX)] = v

        def before(s):
            row = halo[s].astype(F32)[15:16]
            return jnp.where(h > 0, row, jnp.zeros_like(row))

        s_ck, s_cr = full[12:13], full[13:14]
        mix_rows(
            lambda p: big[rows_at(p, MIX)].astype(F32),
            before,
            carry,
            [s_ck, s_cr],
            write,
            T // MIX,
            MIX,
        )

        loads[8].wait()

        @pl.loop(0, 4)
        def _(t):
            at = rows_at(t, tile)
            acc = jnp.zeros((tile, F), F32)
            for i in range(nk):
                acc = acc + dot_nn(m2[0, at, i * kk : (i + 1) * kk], wf[i, :, :F])
            pos = jnp.maximum(acc, 0.0)
            relu[at] = pos.astype(BF)
            act[at] = (pos * pos).astype(BF)

        loads[9].wait()

        @pl.loop(0, 4)
        def _(t):
            at = rows_at(t, tile)
            for q in range(4):
                lo = q * dq
                big[at, lo : lo + dq] = dot_nn(act[at], wcv[:, lo : lo + dq]).astype(BF)

        def cols(ref):
            return lambda p: ref.at[:, pl.ds(pl.multiple_of(p * m, m), m)]

        total = TeamSum(me, cols(big), cn, ca, cm, cf, c_s, c_r)
        total.start()

        @pl.loop(0, 4)
        def _(t):
            at = rows_at(t, tile)
            acc = jnp.zeros((tile, m), F32)
            for i in range(nk):
                acc = acc + dot_nn(m2[1, at, i * kk : (i + 1) * kk], wf[i, :, F:])
            sg[at] = 1.0 / (1.0 + jnp.exp(-acc))

        def gate_back(at, val):
            sig = sg[at]
            upv = upc[at].astype(F32)
            d_val[at] = (sig * upv).astype(BF)
            d_pg[at] = (upv * val * sig * (1.0 - sig)).astype(BF)
            add[at] = (sig * val).astype(BF)

        total.finish(gate_back)
        keep_val = pltpu.make_async_copy(d_val, cols(dval)(mine), ls.at[8])
        keep_val.start()
        gv = TeamGather(me, d_val, cols(dval), ds, dr)
        gv.start()
        gv.finish()
        keep_val.wait()
        keep_add = pltpu.make_async_copy(add.at[rows_at(mine, rows)], moved.at[mine], ls.at[11])
        keep_add.start()
        gm = Exchange(me, lambda p: add.at[rows_at(p, rows)], lambda p: moved.at[p], ms, mr)
        gm.start()
        bg.start(me, srcs, dsts, rest[51:-2])

        @pl.loop(0, 8)
        def _(q):
            at = pl.ds(pl.multiple_of(q * m, m), m)
            g = dot_tn(act[...], dval[:, at])
            for i in range(A):
                for j in range(H):
                    lo = (i * H + j) * w_cv
                    gcv[i, j, :, at] = g[lo : lo + w_cv].astype(BF)

        cv = Copies(vs)
        cv.go(gcv.at[1 - a], cvbuf, vr.at[0], {"a": 1 - a})

        @pl.loop(0, 4)
        def _(t):
            at = rows_at(t, tile)
            d_pre[at] = (dot_nt(dval[at], wcv[...]) * 2.0 * relu[at].astype(F32)).astype(BF)

        ff = Copies(fs)
        sums[...] = jnp.zeros_like(sums)

        def chunk_of(i):
            lo = i * kk

            def chunk(t):
                at = rows_at(t, tile)
                return (dot_nt(d_pre[at], wf[i, :, :F]), dot_nt(d_pg[at], wf[i, :, F:]))

            def put(t, v):
                big[rows_at(t, tile), lo : lo + kk] = v.astype(BF)

            def put_first(s, v):
                first[s, :, lo : lo + kk] = v

            back_rows(
                T,
                tile,
                chunk,
                (s_ck[:, lo : lo + kk], s_cr[:, lo : lo + kk]),
                lambda t: df[rows_at(t, tile), lo : lo + kk].astype(F32),
                put,
                put_first,
                [sums.at[k : k + 1, lo : lo + kk] for k in range(2)],
            )

        def grads(step, k):
            i = lax.rem(a + 1 + step, A)
            for q in range(2):
                at = pl.ds(pl.multiple_of((i * 2 + k) * kk + q * (kk // 2), kk // 2), kk // 2)
                to = slice(q * kk // 2, (q + 1) * kk // 2)
                stage[k, to, :F] = dot_tn(m2[0, :, at], d_pre[...]).astype(BF)
                stage[k, to, F:] = dot_tn(m2[1, :, at], d_pg[...]).astype(BF)
            copy = pltpu.make_async_copy(stage.at[k], g_f.at[i, k], ls.at[9 if k == 0 else 13])
            copy.start()
            return copy

        for i in range(nk):
            chunk_of(i)
        total = TeamSum(me, lambda p: big.at[rows_at(p, rows)], rn, ra, rm, rf, r_s, r_r)
        total.start()
        e = Edge(me, H, first, edge, es, er)
        e.start()

        def put_dn(at, v):
            dn2[at] = v

        halves = 2 if w_cv % 32 == 0 else 1

        held = []

        def pass_on(g):
            at = pl.ds(g * (w_cv // halves), w_cv // halves)
            for dh in range(1, H):
                to = lax.rem(h + dh, H)
                when = None if g == 0 else jnp.logical_not(inner(me, H))
                held.append(
                    cv.go(
                        gcv.at[a, to, at],
                        got_cv.at[dh - 1, at],
                        vr.at[1 + (dh - 1) * 2 + g],
                        {"h": to},
                        when,
                    )
                )

        def value_sums():
            landed(cvbuf, vr.at[0])

            @pl.loop(0, H)
            def _(j):
                gcv[a, j] = (gcv[a, j].astype(F32) + cvbuf[j].astype(F32)).astype(BF)

            pass_on(0)
            for copy in staged:
                copy.wait()
            ff.go(g_f.at[1 - a, 0], got_f, fr.at[0], {"a": 1 - a})
            staged[:] = [grads(1, 0), grads(1, 1)]

        staged = []
        total.finish(put_dn, value_sums, lambda: staged.extend([grads(0, 0), grads(0, 1)]))
        for copy in staged:
            copy.wait()
        e.finish(dn2)

        @pl.loop(0, rows // MIX)
        def _(t):
            at = rows_at(t, MIX)
            d = dn2[at]
            hat, rstd = norm_rows(middle[at])
            sums[2:3] = sums[2:3] + jnp.sum(d * hat, axis=0, keepdims=True)
            sums[3:4] = sums[3:4] + jnp.sum(d, axis=0, keepdims=True)
            dm = up[at].astype(F32) + norm_back(d * full[10:11], hat, rstd)
            d_mid[at] = dm
            own[at] = dm.astype(BF)

        keep = [
            pltpu.make_async_copy(own, d_br.at[mine], ls.at[10]),
            keep_add,
        ]
        keep[0].start()
        gx = TeamGather(me, own, lambda p: d_br.at[p], bs, br, ("zx", "zx"))
        gx.start()
        if halves == 2:
            pass_on(1)
            for copy in held[len(held) // 2 :]:
                pl.when(inner(me, H))(copy.start)
        keep.append(pltpu.make_async_copy(gcv.at[a, h], s_cv, ls.at[12]))
        keep[-1].start()
        gx.finish()
        gm.finish()
        bg.finish()
        landed(got_f, fr.at[0])
        ff.drain()
        for dh in range(1, H):
            for g in range(halves):
                at = pl.ds(g * (w_cv // halves), w_cv // halves)
                landed(got_cv.at[dh - 1, at], vr.at[1 + (dh - 1) * 2 + g])
        cv.drain()
        for copy in keep:
            copy.wait()

    return comm_call(
        body,
        (
            jax.ShapeDtypeStruct((rows, D), F32),
            jax.ShapeDtypeStruct((8, rows, D), BF),
            jax.ShapeDtypeStruct((8, rows, m), BF),
            jax.ShapeDtypeStruct((w_cv, D), BF),
            jax.ShapeDtypeStruct((max(H - 1, 1), w_cv, D), BF),
            jax.ShapeDtypeStruct((A, nk // A, kk, F + m), BF),
            jax.ShapeDtypeStruct((kk, F + m), BF),
            jax.ShapeDtypeStruct((8, D), F32),
            *bg.outs(),
        ),
        [ANY, VM, VM, ANY, ANY, VM, VM, VM] + [ANY] * nb,
        (VM, ANY, ANY, ANY, ANY, ANY, ANY, VM, *[ANY] * nb),
        [
            pltpu.VMEM((T, D), BF),
            pltpu.VMEM((2, T, D), BF),
            pltpu.VMEM((T, D), BF),
            pltpu.VMEM((1, D), F32),
            pltpu.VMEM((T, F), BF),
            pltpu.VMEM((T, F), BF),
            pltpu.VMEM((T, m), F32),
            pltpu.VMEM((T, m), BF),
            pltpu.VMEM((T, m), BF),
            pltpu.VMEM((T, D), BF),
            pltpu.VMEM((A, H, w_cv, D), BF),
            pltpu.VMEM((H, w_cv, D), BF),
            pltpu.VMEM((2, kk, F + m), BF),
            pltpu.VMEM((rows, D), F32),
            pltpu.VMEM((rows, D), BF),
            pltpu.VMEM((T, m), BF),
            pltpu.VMEM((2, 16, D), BF),
            pltpu.VMEM((8, 16, D), BF),
            *TeamSum.scratch(T, m),
            *TeamSum.scratch(rows, D),
            DMA((14,)),
            DMA((8, 2)),
            DMA((14,)),
            DMA((8, 2)),
            DMA((2,)),
            DMA((8,)),
            DMA((7,)),
            DMA((8,)),
            DMA((2 * H,)),
            DMA((2 * H,)),
            DMA((1,)),
            DMA((1,)),
            DMA((16,)),
            *bg.sems(),
            pltpu.VMEM(wf.shape, BF),
            pltpu.VMEM(wcv.shape, BF),
        ],
        2,
    )(n2, halo, full, wcv, wf, upc, middle, up, *bg.arrays())


def time_back(lay, d_br, wo, gated, ghat, grstd, gate, rkv, states, mv, full, mixed, diff, w4, x, d_mid, cm_sums, s_f, g_f, fin):
    H, A, n_dev = lay.H, lay.A, lay.n
    T, m = gate.shape
    rows, D = x.shape
    heads = m // HEAD
    per = T // 2 // CHUNK
    nk, kk, _ = w4.shape
    tile = T // 4
    hk = kk // H
    w_row = D // n_dev
    nf = s_f.shape[-1]
    H1 = max(H - 1, 1)
    strided = lay.strided
    hop = fin is not None
    F = (nf - m) * 8
    k_row = hk // 4

    def body(*refs):
        d_br, wo, gated, ghat, grstd, gate, rkv, states, mv, full, mixed, diff, w4_in, x, d_mid, cm_sums, s_f = refs[:17]
        g_f, refs = refs[17], refs[:17] + refs[18:]
        if hop:
            fin, refs = refs[17], refs[:17] + refs[18:]
        in_grad, o_out, total_out, fin_out, ck_out, cr_out, *four = refs[17:27]
        refs = refs[5:]
        (big, dy, adds, cl, st, obox, ibox, d_all, tsum, sums) = refs[22:32]
        (mbuf, g4, got, late, t4, first, edge) = refs[32:39]
        dn1 = in_grad
        (g_o, o_got, o_late, f_own, f_got, t_f, small, s_got) = refs[39:47]
        rn, ra, rm, rf, r_s, r_r = refs[47:53]
        cs, cr, es, er, gs, gr, os_, or_, fs, fr, xs, xr, ys, yr, ss, sr, ls, f_out, g_out, hs, hr, f1, f1_got, f1s, f1r, w4 = refs[53:]
        me = coords()
        a, b, h, l, c = (me[k] for k in ALL)
        mine = rank_of(b, l, c)
        loads = [
            pltpu.make_async_copy(d_br.at[p], big.at[pl.ds(p * rows, rows)], ls.at[p]) for p in range(8)
        ]
        loads.append(pltpu.make_async_copy(s_f.at[h], f_own, ls.at[8]))
        loads.append(pltpu.make_async_copy(g_f.at[a, 1], f1, ls.at[13 + nk]))
        loads.append(pltpu.make_async_copy(w4_in, w4, ls.at[14 + nk]))
        for copy in loads:
            copy.start()

        sem = pltpu.get_barrier_semaphore()
        others = []
        for i in range(1, n_dev):
            k = i
            dc, k = k % 2, k // 2
            dl, k = k % 2, k // 2
            dh, k = k % H, k // H
            db, da = k % 2, k // 2
            to = {
                "a": lax.rem(a + da, A),
                "b": b ^ db,
                "h": lax.rem(h + dh, H),
                "l": l ^ dl,
                "c": c ^ dc,
            }
            others.append((i, to))
            pl.semaphore_signal(sem, inc=1, device_id=to, device_id_type=MESH)
        pl.semaphore_wait(sem, n_dev - 1)
        c1 = Copies(f1s)
        c1.go(g_f.at[1 - a, 1], f1_got, f1r, {"a": 1 - a})
        for copy in loads[:8]:
            copy.wait()

        ones = block_ones(m)
        dec = Decay(mv[6:7])
        u = mv[7:8]
        span_all = jnp.exp(-mv[6:7] * (T // 2))
        low_t = triangle(heads, False)
        low = triangle(heads, True)
        tsum[...] = jnp.zeros_like(tsum)

        @pl.loop(0, 2 * per)
        def _(t):
            at = rows_at(t, CHUNK)
            d_gated = dot_nt(big[at], wo[...].reshape(m, D))
            g = gate[at]
            sig = 1.0 / (1.0 + jnp.exp(-g))
            hat, rstd = ghat[at], grstd[at]
            dn = d_gated * (g * sig)
            tsum[2:3] += jnp.sum(dn * hat, axis=0, keepdims=True)
            tsum[3:4] += jnp.sum(dn, axis=0, keepdims=True)
            nm = hat * mv[8:9] + mv[9:10]
            d_all[at, 3 * m :] = (d_gated * nm * sig * (1.0 + g * (1.0 - sig))).astype(BF)
            e = dn * mv[8:9]
            m1 = dot_exact(e, ones) * (1.0 / HEAD)
            m2 = dot_exact(e * hat, ones) * (1.0 / HEAD)
            dy[at] = (e - m1 - hat * m2) * rstd

        cl[...] = jnp.zeros_like(cl)

        @pl.loop(0, per)
        def _(q):
            n = per - 1 - q
            for s in range(2):
                at = rows_at(s * per + n, CHUNK)
                rd = (rkv[0, at].astype(F32) * dec.down).astype(BF)
                add = dot_tn(dy[at].astype(BF), rd) * ones
                adds[s, n] = add
                cl[s] = dec.span * cl[s] + add

        st[...] = jnp.zeros_like(st)
        chain = Chain(me, H, False, obox, ibox, cs, cr)
        chain.run(st, cl, span_all, ones)
        cf = Copies(fs)
        held = []
        for dh in range(1, H):
            to = lax.rem(h + dh, H)
            when = jnp.logical_not(inner(me, H))
            held.append(cf.go(s_f.at[to], f_got.at[dh - 1, 0], fr.at[2 * dh - 2], {"h": to}, when))

        if hop:
            mine_fin = fin.at[pl.ds(l * 4, 4)]
            last = h == H - 1
            to_first = remote(mine_fin.at[:, pl.ds(0, HEAD)], fin_out, hs, hr, {"h": 0})
            kept = pltpu.make_async_copy(mine_fin.at[:, pl.ds(HEAD, HEAD)], fin_out, hs)

            @pl.when(last)
            def _():
                to_first.start()

        nw = D // 8

        @pl.loop(0, 8)
        def _(q):
            at = pl.ds(pl.multiple_of(q * nw, nw), nw)
            g = dot_tn(gated[...], big[:, at]).astype(BF)
            g_o[:, :, :, at] = g.reshape(*g_o.shape[:3], nw)

        co = Copies(os_)
        if strided:
            co.go(g_o.at[1 - a], o_got, or_.at[0], {"a": 1 - a})

        @pl.loop(0, per)
        def _(q):
            n = per - 1 - q
            for s in range(2):
                at = rows_at(s * per + n, CHUNK)
                r, k, v = (rkv[i, at].astype(F32) for i in range(3))
                vb = rkv[2, at]
                rd, kg, kt = r * dec.down, k * dec.up, k * dec.tail
                rdb, kgb, ktb = rd.astype(BF), kg.astype(BF), kt.astype(BF)
                dyt = dy[at]
                dyb = dyt.astype(BF)
                state, end = states[s, n], st[s]
                endb = end.astype(BF)
                datt = jnp.where(low, dot_nt(stacked_heads(dyb), vb), 0.0).astype(BF)
                datt_t = jnp.where(low_t, dot_nt(stacked_heads(vb), dyb), 0.0).astype(BF)
                att_t = jnp.where(low_t, dot_nt(stacked_heads(kgb), rdb), 0.0).astype(BF)
                ddiag = dot_exact(dyt * v, ones)
                diag = dot_exact(r * u * k, ones)
                d_rd = own_heads(dot_nn(datt, kgb)) + dot_nn(dyb, state.astype(BF))
                d_kg = own_heads(dot_nn(datt_t, rdb))
                d_kt = dot_nn(vb, endb)
                d_v = own_heads(dot_nn(att_t, dyb)) + diag * dyt + dot_nt(ktb, endb)
                d_r = d_rd * dec.down + ddiag * u * k
                d_k = d_kg * dec.up + d_kt * dec.tail + ddiag * u * r
                d_all[at, :m] = d_r.astype(BF)
                d_all[at, m : 2 * m] = d_k.astype(BF)
                d_all[at, 2 * m : 3 * m] = d_v.astype(BF)
                tsum[1:2] += jnp.sum(ddiag * r * k, axis=0, keepdims=True)
                d_l = jnp.sum(
                    (dec.i + 1.0) * kg * d_kg
                    - dec.i * rd * d_rd
                    - (CHUNK - 1.0 - dec.i) * kt * d_kt,
                    axis=0,
                    keepdims=True,
                )
                d_l = d_l - CHUNK * dec.span * jnp.sum(state * end, axis=0, keepdims=True)
                tsum[0:1] += d_l
                st[s] = dec.span * end + adds[s, n]

        for copy in held:
            pl.when(inner(me, H))(copy.start)
        loads[9].wait()
        landed(f1_got, f1r)

        @pl.loop(0, kk // 64)
        def _(q):
            at = rows_at(q, 64)
            f1[at] = (f1[at].astype(F32) + f1_got[at].astype(F32)).astype(BF)

        for dh in range(1, H):
            to = lax.rem(h + dh, H)
            cf.go(f1.at[rows_at(to, hk)], f_got.at[dh - 1, 1], fr.at[2 * dh - 1], {"h": to})
        chain.finish()

        cg = Copies(gs)
        units = [(step, k, jj) for step in range(A) for k in range(2) for jj in range(2)]

        def unit(v):
            step, k, jj = units[v]
            i = lax.rem(a + 1 + step, A)
            lo = pl.ds(pl.multiple_of((i * 2 + k) * kk, kk), kk)
            src = mixed.at[pl.ds(jj * 2, 2), :, lo]
            return pltpu.make_async_copy(src, mbuf.at[v % 2], ls.at[9 + v % 2])

        unit(0).start()
        for v, (step, k, jj) in enumerate(units):
            if v + 1 < len(units):
                unit(v + 1).start()
            unit(v).wait()
            i = lax.rem(a + 1 + step, A)
            for q in range(2):
                j = jj * 2 + q
                g = dot_tn(mbuf[v % 2, q], d_all[:, j * m : (j + 1) * m])
                g4[i * 2 + k, :, j * m : (j + 1) * m] = g.astype(BF)
            if step < A - 1 and jj == 1:
                cg.go(g4.at[i * 2 + k], got.at[k], gr.at[k], {"a": 1 - a})

        difs = [
            pltpu.make_async_copy(diff.at[:, pl.ds(i * kk, kk)], mbuf.at[i // 2, i % 2], ls.at[13 + i])
            for i in range(nk)
        ]
        for copy in difs:
            copy.start()
        sums[...] = jnp.zeros_like(sums)

        def chunk_of(i):
            lo = i * kk

            def chunk(t):
                at = rows_at(t, tile)
                return tuple(
                    dot_nt(d_all[at, j * m : (j + 1) * m], w4[i, :, j * m : (j + 1) * m])
                    for j in range(4)
                )

            def put(t, v):
                big[rows_at(t, tile), lo : lo + kk] = v.astype(BF)

            def put_first(s, v):
                first[s, :, lo : lo + kk] = v

            back_rows(
                T,
                tile,
                chunk,
                tuple(full[2 + j : 3 + j, lo : lo + kk] for j in range(4)),
                lambda t: mbuf[i // 2, i % 2, rows_at(t, tile)].astype(F32),
                put,
                put_first,
                [sums.at[j : j + 1, lo : lo + kk] for j in range(4)],
            )

        loads[10].wait()
        for i in range(nk):
            difs[i].wait()
            chunk_of(i)
        total = TeamSum(
            me, lambda p: big.at[rows_at(p, rows)], rn, ra, rm, rf, r_s, r_r, ("xz", "xz")
        )
        total.start()
        e = Edge(me, H, first, edge, es, er)
        e.start()

        def pass_on():
            if strided:
                landed(o_got, or_.at[0])

                @pl.loop(0, H)
                def _(j):
                    g_o[a, j] = (g_o[a, j].astype(F32) + o_got[j].astype(F32)).astype(BF)

                for dh in range(1, H):
                    to = lax.rem(h + dh, H)
                    co.go(g_o.at[a, to], o_late.at[dh - 1], or_.at[dh], {"h": to})
            for k in range(2):
                landed(got.at[k], gr.at[k])

                @pl.loop(0, kk // 64)
                def _(q):
                    at = rows_at(q, 64)
                    g4[a * 2 + k, at] = (g4[a * 2 + k, at].astype(F32) + got[k, at].astype(F32)).astype(BF)

                for dh in range(1, H):
                    to = lax.rem(h + dh, H)
                    v = (dh - 1) * 2 + k
                    cg.go(
                        g4.at[a * 2 + k, rows_at(to, hk)], late.at[dh - 1, k], gr.at[2 + v], {"h": to}
                    )

            loads[8].wait()
            for dh in range(1, H):
                for k in range(2):
                    landed(f_got.at[dh - 1, k], fr.at[2 * dh - 2 + k])
            for k in range(2):
                for q in range(4):
                    at = pl.ds(q * (hk // 4), hk // 4)
                    if k == 0:
                        v = f_own[at].astype(F32)
                    else:
                        v = f1[pl.ds(pl.multiple_of(h * hk + q * (hk // 4), hk // 4), hk // 4)].astype(F32)
                    for dh in range(1, H):
                        v = v + f_got[dh - 1, k, at].astype(F32)
                    t_f[k * 4 + q] = v.astype(BF)
            keep_f.start()
            gf.start()

        keep_f = pltpu.make_async_copy(t_f.at[mine], f_out.at[mine], ls.at[11])
        gf = Exchange(me, lambda p: t_f.at[p], lambda p: f_out.at[p], xs, xr)

        def put_dn(at, v):
            dn1[at] = v

        total.finish(put_dn, pass_on)
        e.finish(dn1)

        @pl.loop(0, rows // MIX)
        def _(t):
            at = rows_at(t, MIX)
            d = dn1[at]
            hat, rstd = norm_rows(x[at].astype(F32))
            sums[4:5] = sums[4:5] + jnp.sum(d * hat, axis=0, keepdims=True)
            sums[5:6] = sums[5:6] + jnp.sum(d, axis=0, keepdims=True)
            in_grad[at] = d_mid[at] + norm_back(d * full[0:1], hat, rstd)

        small[...] = jnp.zeros_like(small)
        per_lane = 128 // w_row
        for f in range(n_dev):
            g = pl.ds(f // per_lane * 128, 128)
            block = jnp.concatenate([sums[:, g], cm_sums[:, g]], axis=0)
            shift = (128 - w_row * (f % per_lane)) % 128
            small[f] = pltpu.roll(block, shift, axis=1) if shift else block

        if strided:
            for i in range(A):
                for j in range(H):
                    f = (((i * 2 + b) * H + j) * 2 + l) * 2 + c
                    v = (i * H + j) * w_row
                    block = tsum[:, v // 128 * 128 : v // 128 * 128 + 128]
                    shift = (128 - v % 128) % 128
                    block = pltpu.roll(block, shift, axis=1) if shift else block
                    small[f, 12:16] = block[:4]
        else:
            span = n_dev // 8
            for i in range(span):
                v = i * w_row
                block = tsum[:, v // 128 * 128 : v // 128 * 128 + 128]
                shift = (128 - v % 128) % 128
                block = pltpu.roll(block, shift, axis=1) if shift else block
                small[mine * span + i, 12:16] = block[:4]
        cv = Copies(ss)

        def flat(d):
            return (((d["a"] * 2 + d["b"]) * H + d["h"]) * 2 + d["l"]) * 2 + d["c"]

        for i, to in others:
            cv.go(small.at[flat(to)], s_got.at[i], sr.at[i], to)

        for k in range(2):
            for dh in range(1, H):
                landed(late.at[dh - 1, k], gr.at[2 + (dh - 1) * 2 + k])
            for q in range(4):
                at = pl.ds(pl.multiple_of(h * hk + q * (hk // 4), hk // 4), hk // 4)
                v = g4[a * 2 + k, at].astype(F32)
                for dh in range(1, H):
                    v = v + late[dh - 1, k, pl.ds(q * (hk // 4), hk // 4)].astype(F32)
                t4[k * 4 + q] = v.astype(BF)
        keep = [keep_f, pltpu.make_async_copy(t4.at[mine], g_out.at[mine], ls.at[12])]
        keep[1].start()
        gg = Exchange(me, lambda p: t4.at[p], lambda p: g_out.at[p], ys, yr)
        gg.start()
        if strided:
            v = g_o[a, h].astype(F32)
            for dh in range(1, H):
                landed(o_late.at[dh - 1], or_.at[dh])
                v = v + o_late[dh - 1].astype(F32)
            o_out[...] = v
        else:
            o_out[...] = g_o[...]
        acc = small[flat(me)]
        for i, _ in others:
            landed(s_got.at[i], sr.at[i])
            acc = acc + s_got[i]
        total_out[...] = acc
        if hop:

            @pl.when(last)
            def _():
                to_first.wait_send()
                kept.start()
                kept.wait()

            @pl.when(h == 0)
            def _():
                to_first.wait_recv()

        gf.finish()
        for copy in keep:
            copy.wait()

        def from_ranks(ref, lo, n, whole):
            parts = []
            for p in range(8):
                read = lambda i, j, p=p: ref[p, :, lo + i : lo + j]
                for src, dst, many in rank_columns(lay, n, whole, p):
                    parts.append((read, n // 8, dst, src, many))
            return parts

        def into(ref):
            def put(lo, v):
                ref[:, lo : lo + 128] = v

            return put

        lay_lanes(F, from_ranks(f_out, 0, F, 1), into(ck_out))
        for p in range(8):
            cr_out[:, p * m : (p + 1) * m] = f_out[p, :, F // 8 :].astype(F32)
        gg.finish()
        for j, ref in enumerate(four):
            lay_lanes(D, from_ranks(g_out, j * m, D, HEAD), into(ref))
        for copies in (c1, cf, co, cg, cv):
            copies.drain()

    o_shape = wo.shape[2:] if strided else wo.shape
    return comm_call(
        body,
        (
            jax.ShapeDtypeStruct((rows, D), F32),
            jax.ShapeDtypeStruct(o_shape, F32 if strided else BF),
            jax.ShapeDtypeStruct((16, 128), F32),
            jax.ShapeDtypeStruct((4, HEAD, 128), BF),
            jax.ShapeDtypeStruct((k_row, F), F32),
            *[jax.ShapeDtypeStruct((k_row, D), F32)] * 5,
        ),
        [ANY] + [VM] * 9 + [ANY] * 3 + [VM] * 3 + [ANY] * (3 if hop else 2),
        (VM, VM, VM, ANY, *[VM] * 6),
        [
            pltpu.VMEM((T, D), BF),
            pltpu.VMEM((T, m), F32),
            pltpu.VMEM((2, per, m, m), F32),
            pltpu.VMEM((2, m, m), F32),
            pltpu.VMEM((2, m, m), F32),
            pltpu.VMEM((m, 128), BF),
            pltpu.VMEM((m, 128), BF),
            pltpu.VMEM((T, 4 * m), BF),
            pltpu.VMEM((8, m), F32),
            pltpu.VMEM((8, D), F32),
            pltpu.VMEM((2, 2, T, kk), BF),
            pltpu.VMEM((nk, kk, 4 * m), BF),
            pltpu.VMEM((2, kk, 4 * m), BF),
            pltpu.VMEM((H1, 2, hk, 4 * m), BF),
            pltpu.VMEM((8, hk // 4, 4 * m), BF),
            pltpu.VMEM((2, 16, D), BF),
            pltpu.VMEM((8, 16, D), BF),
            pltpu.VMEM(wo.shape, BF),
            pltpu.VMEM(wo.shape[1:], BF),
            pltpu.VMEM((H1, *wo.shape[2:]), BF),
            pltpu.VMEM(s_f.shape[1:], BF),
            pltpu.VMEM((H1, 2, *s_f.shape[1:]), BF),
            pltpu.VMEM((8, hk // 4, nf), BF),
            pltpu.VMEM((n_dev, 16, 128), F32),
            pltpu.VMEM((n_dev, 16, 128), F32),
            *TeamSum.scratch(rows, D),
            DMA,
            DMA,
            DMA((2,)),
            DMA((8,)),
            DMA((2 + 2 * H1,)),
            DMA((2 + 2 * H1,)),
            DMA((H,)),
            DMA((H,)),
            DMA((2 * H1,)),
            DMA((2 * H1,)),
            DMA((7,)),
            DMA((8,)),
            DMA((7,)),
            DMA((8,)),
            DMA((n_dev,)),
            DMA((n_dev,)),
            DMA((15 + nk,)),
            pltpu.VMEM((8, k_row, nf), BF),
            pltpu.VMEM((8, k_row, 4 * m), BF),
            DMA,
            DMA,
            pltpu.VMEM((kk, nf), BF),
            pltpu.VMEM((kk, nf), BF),
            DMA((1,)),
            DMA,
            pltpu.VMEM(w4.shape, BF),
        ],
        3,
    )(d_br, wo, gated, ghat, grstd, gate, rkv, states, mv, full, mixed, diff, w4, x, d_mid, cm_sums, s_f, g_f, *([fin] if hop else []))


def dot(a, b, dims):
    return lax.dot_general(a, b, (dims, ((), ())), preferred_element_type=F32)


def mm(a, b):
    return dot(a, b, ((1,), (0,)))


def mm_nt(a, b):
    return dot(a, b, ((1,), (1,)))


def mm_tn(a, b):
    return dot(a, b, ((0,), (0,)))


class Layout:
    def __init__(self, mesh_shape):
        self.A, self.B, self.H, self.L, self.C = mesh_shape
        self.team = self.B * self.L * self.C
        self.n = self.team * self.A * self.H

    def of(self, D):
        self.strided = (D // self.n) % HEAD == 0
        return self

    def spread(self, v, whole):
        w = v.shape[-1] // self.n
        lead = v.shape[:-1]
        if w % whole:
            return v.reshape(*lead, self.team, -1)
        k = len(lead)
        v = v.reshape(*lead, self.A, self.B, self.H, self.L, self.C, w)
        v = v.transpose(*range(k), k + 1, k + 3, k + 4, k, k + 2, k + 5)
        return v.reshape(*lead, self.team, -1)

    def unspread(self, v, whole):
        lead = v.shape[:-2]
        w = v.shape[-1] * self.team // self.n
        if w % whole:
            return v.reshape(*lead, -1)
        k = len(lead)
        v = v.reshape(*lead, self.B, self.L, self.C, self.A, self.H, w)
        v = v.transpose(*range(k), k + 3, k, k + 4, k + 1, k + 2, k + 5)
        return v.reshape(*lead, -1)

    def rows_in(self, g):
        m = g.shape[-1]
        g = g.reshape(self.A, self.H, self.B, self.L, self.C, -1, m)
        return g.transpose(0, 2, 1, 3, 4, 5, 6).reshape(-1, m)

    def rows_out(self, g):
        m = g.shape[-1]
        g = g.reshape(self.A, self.B, self.H, self.L, self.C, -1, m)
        return g.transpose(0, 2, 1, 3, 4, 5, 6).reshape(self.A * self.H, self.team, -1, m)


def normed(v):
    mean = jnp.mean(v, axis=-1, keepdims=True)
    cent = v - mean
    rstd = lax.rsqrt(jnp.mean(cent * cent, axis=-1, keepdims=True) + EPS)
    return cent * rstd, rstd


def norm_back(e, xhat, rstd):
    m1 = jnp.mean(e, axis=-1, keepdims=True)
    m2 = jnp.mean(e * xhat, axis=-1, keepdims=True)
    return (e - m1 - xhat * m2) * rstd


def with_before(rows, halo, segs):
    v = rows.reshape(segs, -1, rows.shape[-1])
    return jnp.concatenate([halo, v[:, :-1]], axis=1).reshape(rows.shape)


def with_after(rows, segs):
    v = rows.reshape(segs, -1, rows.shape[-1])
    return (
        jnp.concatenate([v[:, 1:], jnp.zeros_like(v[:, :1])], axis=1).reshape(rows.shape),
        v[:, :1],
    )


def swap(v, axis):
    return lax.ppermute(v, axis, [(0, 1), (1, 0)])


def per_device(lay, *args):
    (x_in, up_in, start_in) = args[:3]
    vec = args[3:13]
    w_r, w_k, w_v, w_g, w_o = args[13:18]
    vec2 = args[18:22]
    w_ck, w_cv, w_cr = args[22:]
    a_at, b_at, h_at = (lax.axis_index(n) for n in ("a", "b", "h"))
    rank = (b_at * lay.L + lax.axis_index("l")) * lay.C + lax.axis_index("c")
    H = lay.H
    segs = lay.B
    D = x_in.shape[-1]
    x_own = x_in[0]
    rows = x_own.shape[0]
    T = rows * lay.team
    dcol = D // lay.team
    heads = dcol // HEAD
    half = lay.L * lay.C
    w_row = D // lay.n
    lay.of(D)
    hid = w_ck.shape[1] // lay.team

    stacked = jnp.stack([*vec, *vec2])
    nv = stacked.shape[0]
    stacked = jnp.pad(stacked, ((0, 16 - nv), (0, 128 - w_row)))
    o_own = w_o
    if not lay.strided:
        o_own = lax.all_gather(w_o, ALL, axis=0, tiled=True)
        o_own = lax.dynamic_slice_in_dim(o_own, rank * dcol, dcol, 0)
        o_own = o_own.reshape(lay.A, H, -1, D)
    (
        every, my_vecs, mixed, diff1, rkv, gate, upc, W4, W_o, gated, ghat, grstd, states, fin, middle, n2, halo_2,
        W_cv, ffn_all,
    ) = front(lay, stacked, x_own, up_in[0], (w_r, w_k, w_v, w_g), w_ck, w_cr, o_own, w_cv, start_in[0])
    W_cv = W_cv.reshape(hid, D)
    direct = lay.strided and H == 2 and lay.A == 2
    items = []
    if direct:
        blocks = fin.astype(BF).reshape(lay.A, H, HEAD, 128).transpose(1, 0, 2, 3)
        blocks = jnp.broadcast_to(blocks.reshape(H, lay.A * HEAD, 128), (4, H, lay.A * HEAD, 128))
        items = [(blocks.reshape(8, lay.A * HEAD, 128), "t")]
    else:
        nh = start_in.shape[1]
        head_ids = lay.spread(jnp.arange(nh * HEAD, dtype=jnp.int32), HEAD)
        my_heads = lax.dynamic_index_in_dim(head_ids, rank, 0, False)[::HEAD] // HEAD
        s_out = fin.reshape(heads, HEAD, 2, HEAD).transpose(2, 0, 3, 1)
        placed = jnp.zeros((segs, nh, HEAD, HEAD), BF)
        s_fin = jnp.where(h_at == lay.H - 1, s_out, 0.0).astype(BF)
        placed = placed.at[:, my_heads].set(s_fin)
        final = lax.psum_scatter(placed, "b", scatter_dimension=0, tiled=True)
        final = lax.psum_scatter(final, SEQ, scatter_dimension=1, tiled=True).astype(F32)

    wf = ffn_all.reshape(2 * lay.A, D // (2 * lay.A), -1)
    d_mid, d_br, moved, s_cv, got_cv, g_f, got_f, cm_sums, *got_fin = channel_mix(
        lay, n2, halo_2, every, W_cv, wf, upc.reshape(T, dcol), middle, up_in[0], items
    )
    layer_output = (middle + moved.transpose(1, 0, 2).reshape(rows, D).astype(F32)).astype(BF)
    g_cv = s_cv.astype(F32) + jnp.sum(got_cv.astype(F32), axis=0)

    s_f = lax.dynamic_index_in_dim(g_f[:, 0], a_at, 0, False).astype(F32) + got_f.astype(F32)
    s_f = s_f.astype(BF).reshape(H, -1, s_f.shape[-1])
    w4 = W4.reshape(2 * lay.A, D // (2 * lay.A), -1)
    input_grad, g_o, small, fin, g_ck, g_cr, g_r, g_k, g_v, g_w = time_back(
        lay, d_br, W_o, gated, ghat, grstd, gate, rkv, states, my_vecs, every, mixed, diff1, w4, x_own, d_mid,
        cm_sums, s_f, g_f, got_fin[0] if direct else None,
    )
    if direct:
        fin = jnp.where(b_at == 0, fin[:, :, :HEAD], fin[:, :, HEAD:])
        final = fin.transpose(0, 2, 1)[None].astype(F32)
    if not lay.strided:
        g_o = jnp.zeros((D, D), BF).at[rank * dcol + jnp.arange(dcol)].set(g_o.reshape(dcol, D))
        g_o = lax.psum_scatter(g_o, ALL, scatter_dimension=0, tiled=True).astype(F32)
    small = small[:, :w_row]
    order = (4, 5, 0, 1, 2, 3, 12, 13, 14, 15, 10, 11, 8, 9)
    small = [small[i] for i in order]

    return (
        layer_output[None],
        input_grad[None],
        final,
        *small[:10],
        g_r,
        g_k,
        g_v,
        g_w,
        g_o,
        *small[10:],
        g_ck,
        g_cv,
        g_cr,
    )


def solution(mesh):
    n_seg, n_seq = mesh.devices.shape
    shape = (n_seg // 2, 2, n_seq // 4, 2, 2)
    view = Mesh(mesh.devices.reshape(shape), ALL)
    lay = Layout(shape)
    seg = ("a", "b")
    vec, mat = P(ALL), P(ALL, None)
    tok = P(seg, SEQ, None)

    def step(*args):
        return per_device(lay, *args)

    return jax.shard_map(
        step,
        mesh=view,
        in_specs=(tok, tok, P(seg, None, None, None), *[vec] * 10, *[mat] * 5, *[vec] * 4, *[mat] * 3),
        out_specs=(tok, tok, P(seg, SEQ, None, None), *[vec] * 10, *[mat] * 5, *[vec] * 4, *[mat] * 3),
        check_vma=False,
    )
```

```python
import jax
import jax.numpy as jnp
from jax import lax
from jax.experimental import pallas as pl
from jax.experimental.pallas import tpu as pltpu
from jax.sharding import Mesh, PartitionSpec as P

TEAM = ("b", "l", "c")
TEAMS = ("a", "h")
SEQ = ("h", "l", "c")
ALL = ("a", "b", "h", "l", "c")
HEAD = 64
CHUNK = 128
EPS = 1e-05
GROUP_EPS = 0.00064
BF = jnp.bfloat16
F32 = jnp.float32


MESH = pl.DeviceIdType.MESH
DMA = pltpu.SemaphoreType.DMA
VMEM_BYTES = 62 << 20


def coords():
    return {name: lax.axis_index(name) for name in ALL}


def rank_of(b, l, c):
    return (b * 2 + l) * 2 + c


def remote(src, dst, sent, landed, to):
    return pltpu.make_async_remote_copy(
        src_ref=src,
        dst_ref=dst,
        send_sem=sent,
        recv_sem=landed,
        device_id=to,
        device_id_type=MESH,
    )


def mates(me):
    for m in range(1, 8):
        yield m, {"b": me["b"] ^ (m >> 2), "l": me["l"] ^ ((m >> 1) & 1), "c": me["c"] ^ (m & 1)}


def greet(me, H, column, across):
    sem = pltpu.get_barrier_semaphore()
    count = 0
    for dh in range(H if column else 1):
        h = lax.rem(me["h"] + dh, H)
        for m in range(8):
            if dh == 0 and m == 0:
                continue
            to = {
                "b": me["b"] ^ (m >> 2),
                "h": h if column else me["h"],
                "l": me["l"] ^ ((m >> 1) & 1),
                "c": me["c"] ^ (m & 1),
            }
            pl.semaphore_signal(sem, inc=1, device_id=to, device_id_type=MESH)
            count += 1
    if across:
        pl.semaphore_signal(sem, inc=1, device_id={"a": 1 - me["a"]}, device_id_type=MESH)
        count += 1
    pl.semaphore_wait(sem, count)


class Copies:
    def __init__(self, sems):
        self.sems, self.k, self.open = sems, 0, []

    def plan(self, src, dst, landed, to):
        copy = remote(src, dst, self.sems.at[self.k], landed, to)
        self.k += 1
        self.open.append(copy)
        return copy

    def go(self, src, dst, landed, to, when=None):
        copy = self.plan(src, dst, landed, to)
        if when is None:
            copy.start()
        else:
            pl.when(when)(copy.start)
        return copy

    def drain(self):
        for copy in self.open:
            copy.wait_send()


def inner(me, H):
    return me["h"] != me["l"] if H == 2 else me["h"] < 0


def landed(ref, sem):
    remote(ref, ref, sem, sem, {"c": 1 - lax.axis_index("c")}).wait_recv()


def upper(ref, half):
    n = ref.shape[0] // 2
    return ref.at[pl.ds(half * n, n)]


class TeamGather:
    def __init__(self, me, own, view, send, recv, via=("xz", "zx")):
        self.me, self.own, self.view, self.recv, self.via = me, own, view, recv, via
        self.copies = Copies(send)
        self.tx, self.tz, self.ts = {"b": 1 - me["b"]}, {"l": 1 - me["l"]}, {"c": 1 - me["c"]}

    def put(self, src, p, half, to):
        self.copies.go(src, upper(self.view(p), half), self.recv.at[p, half], to)

    def start(self):
        mine = rank_of(self.me["b"], self.me["l"], self.me["c"])
        order = [(half, self.tx if self.via[half] == "xz" else self.tz) for half in range(2)]
        order += [(half, self.tz if self.via[half] == "xz" else self.tx) for half in range(2)]
        order += [(0, self.ts), (1, self.ts)]
        for half, to in order:
            self.put(upper(self.own, half), mine, half, to)

    def finish(self):
        b, l, c = self.me["b"], self.me["l"], self.me["c"]
        px, pz, pd = rank_of(1 - b, l, c), rank_of(b, 1 - l, c), rank_of(1 - b, 1 - l, c)
        order = [
            (px, half, self.tz) if self.via[half] == "xz" else (pz, half, self.tx)
            for half in range(2)
        ]
        order += [
            (pz, half, None) if self.via[half] == "xz" else (px, half, None) for half in range(2)
        ]
        for p, half, on in order + [(pd, 0, None), (pd, 1, None)]:
            block = upper(self.view(p), half)
            landed(block, self.recv.at[p, half])
            if on is not None:
                self.put(block, p, half, on)
            self.put(block, p, half, self.ts)
        for q in range(4):
            p = q * 2 + 1 - c
            for half in range(2):
                landed(upper(self.view(p), half), self.recv.at[p, half])
        self.copies.drain()


class TeamSum:
    def __init__(self, me, part, near, acc, mid, far, send, recv, via=("xz", "zx")):
        self.me, self.part, self.near, self.acc, self.mid, self.far = me, part, near, acc, mid, far
        self.recv, self.via = recv, via
        self.copies = Copies(send)

    def start(self):
        b, l, c = self.me["b"], self.me["l"], self.me["c"]
        self.spots = [(b, l), (1 - b, l), (b, 1 - l), (1 - b, 1 - l)]
        for i in (3, 1, 2, 0):
            bb, ll = self.spots[i]
            self.copies.go(
                self.part(rank_of(bb, ll, 1 - c)), self.near.at[i], self.recv.at[i], {"c": 1 - c}
            )

    def tiles(self, rows, body):
        step = max(16, 65536 // self.near.shape[2])

        @pl.loop(0, rows // step)
        def _(t):
            body(pl.ds(pl.multiple_of(t * step, step), step))

    def pair(self, i, write):
        bb, ll = self.spots[i]
        landed(self.near.at[i], self.recv.at[i])
        mine = self.part(rank_of(bb, ll, self.me["c"]))
        self.tiles(
            self.near.shape[1], lambda at: write(at, mine[at].astype(F32) + self.near[i, at].astype(F32))
        )

    def finish(self, write, then=lambda: None, between=lambda: None):
        b, l = self.me["b"], self.me["l"]
        tx, tz = {"b": 1 - b}, {"l": 1 - l}
        acc, mid, far, recv, go = self.acc, self.mid, self.far, self.recv, self.copies.go
        n = mid.shape[1]
        hops = [
            (tx, 0, tz, 1) if self.via[half] == "xz" else (tz, 1, tx, 0) for half in range(2)
        ]
        for i in (3, 1, 2):

            def put(at, v):
                acc[i - 1, at] = v.astype(BF)

            self.pair(i, put)
            if i == 3:
                for half, (one, _, _, _) in enumerate(hops):
                    go(upper(acc.at[2], half), mid.at[half], recv.at[4 + half], one)
        between()
        for half, (one, direct, two, other) in enumerate(hops):
            landed(mid.at[half], recv.at[4 + half])
            into, came = upper(acc.at[other], half), mid.at[half]

            def add(at):
                into[at] = (into[at].astype(F32) + came[at].astype(F32)).astype(BF)

            self.tiles(n, add)
            go(into, upper(far.at[other], half), recv.at[8 + half], two)
            go(upper(acc.at[direct], half), upper(far.at[direct], half), recv.at[6 + half], one)
        then()
        for half, (_, direct, _, other) in enumerate(hops):
            landed(upper(far.at[direct], half), recv.at[6 + half])
            landed(upper(far.at[other], half), recv.at[8 + half])

        def last(at, v):
            write(at, v + far[0, at].astype(F32) + far[1, at].astype(F32))

        self.pair(0, last)
        self.copies.drain()

    @staticmethod
    def scratch(R, C):
        return [
            pltpu.VMEM((4, R, C), BF),
            pltpu.VMEM((3, R, C), BF),
            pltpu.VMEM((2, R // 2, C), BF),
            pltpu.VMEM((2, R, C), BF),
            DMA((10,)),
            DMA((10,)),
        ]


class TeamsGather:
    def __init__(self, me, H, source, out, send, near, far, team=None, count=2):
        self.me, self.H, self.source, self.out = me, H, source, out
        self.near, self.far, self.team, self.count = near, far, team, count
        self.held = []
        self.copies = Copies(send)

    @staticmethod
    def sems(H, count=2):
        return [DMA((7 + count * (2 * H - 1),)), DMA((8,)), DMA((2 * H, count))]

    def groups(self, only=None):
        b, n = self.me["b"], 8 // self.count
        for g in range(self.count):
            if only is None or g in only:
                at = g * n
                yield g, (b if at < 4 else 1 - b), at % 4, n

    def block(self, a, bb, h, lo, n):
        return self.out.at[a, bb, h, pl.ds(lo, n)]

    def start(self):
        me = self.me
        a, b, h, l, c = (me[n] for n in ALL)
        for m, to in mates(me):
            p = rank_of(to["b"], to["l"], to["c"])
            mine = rank_of(b, l, c)
            self.copies.go(self.source(p), self.out.at[a, b, h, l * 2 + c], self.near.at[mine], to)

    def spread(self, local=None, only=None):
        me = self.me
        a, b, h, l, c = (me[n] for n in ALL)
        if local is not None:
            local.wait()
        for g, bb, lo, n in self.groups(only):
            block = self.block(a, bb, h, lo, n)
            src = block
            if self.team is not None:
                src = self.team.at[pl.ds(bb * 4 + lo, n)]
            else:
                for m in range(1 - g, 4):
                    ll, cc = l ^ (m >> 1), c ^ (m & 1)
                    landed(self.out.at[a, bb, h, ll * 2 + cc], self.near.at[rank_of(bb, ll, cc)])
            for dh in range(1, self.H):
                to = lax.rem(h + dh, self.H)
                when = jnp.logical_not(inner(me, self.H))
                copy = self.copies.go(src, block, self.far.at[dh, g], {"h": to}, when)
                self.held.append((g, copy))
            self.copies.go(src, block, self.far.at[0, g], {"a": 1 - a})

    def release(self, only=None):
        for g, copy in self.held:
            if only is None or g in only:
                pl.when(inner(self.me, self.H))(copy.start)

    def forward(self, only=None):
        a, h, H = self.me["a"], self.me["h"], self.H
        for g, bb, lo, n in self.groups(only):
            for dh in range(1, H):
                block = self.block(a, bb, lax.rem(h - dh + H, H), lo, n)
                landed(block, self.far.at[dh, g])
                self.copies.go(block, block, self.far.at[H - 1 + dh, g], {"a": 1 - a})

    def finish(self):
        a, h, H = self.me["a"], self.me["h"], self.H
        for g, bb, lo, n in self.groups():
            landed(self.block(1 - a, bb, h, lo, n), self.far.at[0, g])
            for dh in range(1, H):
                block = self.block(1 - a, bb, lax.rem(h - dh + H, H), lo, n)
                landed(block, self.far.at[H - 1 + dh, g])
        self.copies.drain()


class Halo:
    def __init__(self, me, H, own, out, send, recv):
        self.me, self.H, self.own, self.out, self.send, self.recv = me, H, own, out, send, recv
        self.last = (me["l"] == 1) & (me["c"] == 1) & (me["h"] < H - 1)

    def each(self):
        me = self.me
        n = self.own.shape[0]
        for p in range(8):
            to = {
                "b": p >> 2,
                "h": jnp.minimum(me["h"] + 1, self.H - 1),
                "l": (p >> 1) & 1,
                "c": p & 1,
            }
            src = self.own.at[pl.ds(n - 16, 16)]
            yield remote(src, self.out.at[me["b"]], self.send.at[p], self.recv.at[me["b"]], to)

    def start(self):
        if self.H == 1:
            return

        @pl.when(self.last)
        def _():
            for copy in self.each():
                copy.start()

    def finish(self):
        if self.H == 1:
            return

        @pl.when(self.me["h"] > 0)
        def _():
            for b in range(2):
                landed(self.out.at[b], self.recv.at[b])

        @pl.when(self.last)
        def _():
            for copy in self.each():
                copy.wait_send()


class Edge:
    def __init__(self, me, H, first, got, send, recv):
        self.me, self.H, self.first, self.got, self.send, self.recv = me, H, first, got, send, recv

    def each(self):
        me = self.me
        mine = rank_of(me["b"], me["l"], me["c"])
        for b in range(2):
            to = {"b": b, "h": jnp.maximum(me["h"] - 1, 0), "l": 1, "c": 1}
            yield remote(self.first.at[b], self.got.at[mine], self.send.at[b], self.recv.at[mine], to)

    def start(self):
        if self.H == 1:
            return

        @pl.when(self.me["h"] > 0)
        def _():
            for copy in self.each():
                copy.start()

    def finish(self, out):
        if self.H == 1:
            return
        me = self.me

        @pl.when((me["l"] == 1) & (me["c"] == 1) & (me["h"] < self.H - 1))
        def _():
            for p in range(8):
                landed(self.got.at[p], self.recv.at[p])
            total = self.got[0, 0:1].astype(F32)
            for p in range(1, 8):
                total = total + self.got[p, 0:1].astype(F32)
            n = out.shape[0]
            out[n - 1 : n] = out[n - 1 : n] + total

        @pl.when(me["h"] > 0)
        def _():
            for copy in self.each():
                copy.wait_send()


class Exchange:
    def __init__(self, me, source, out, send, recv):
        self.me, self.source, self.out, self.recv = me, source, out, recv
        self.copies = Copies(send)

    def start(self):
        mine = rank_of(self.me["b"], self.me["l"], self.me["c"])
        for m, to in mates(self.me):
            p = rank_of(to["b"], to["l"], to["c"])
            self.copies.go(self.source(p), self.out(mine), self.recv.at[mine], to)

    def finish(self):
        for m, to in mates(self.me):
            p = rank_of(to["b"], to["l"], to["c"])
            landed(self.out(p), self.recv.at[p])
        self.copies.drain()


ANY = pl.BlockSpec(memory_space=pl.ANY)
VM = pl.BlockSpec(memory_space=pltpu.VMEM)


def comm_call(body, outs, in_specs, out_specs, scratch, cid):
    return pl.pallas_call(
        body,
        out_shape=outs,
        in_specs=in_specs,
        out_specs=out_specs,
        scratch_shapes=scratch,
        compiler_params=pltpu.CompilerParams(
            collective_id=cid, has_side_effects=True, vmem_limit_bytes=VMEM_BYTES
        ),
    )


def dot_nn(a, b):
    return jnp.dot(a, b, preferred_element_type=F32)


def dot_nt(a, b):
    return lax.dot_general(a, b, (((1,), (1,)), ((), ())), preferred_element_type=F32)


def dot_tn(a, b):
    return lax.dot_general(a, b, (((0,), (0,)), ((), ())), preferred_element_type=F32)


MIX = 32


def rows_at(i, n):
    return pl.ds(pl.multiple_of(i * n, n), n)


class RowsGather:
    def __init__(self, me, H, own, out, send, recv, at=None, inner_first=False):
        self.me, self.H, self.own, self.out, self.recv, self.at = me, H, own, out, recv, at
        self.first = inner(me, H)
        if not inner_first:
            self.first = jnp.logical_not(self.first)
        self.copies = Copies(send)

    @staticmethod
    def sems(H):
        return [DMA((2 * H - 1,)), DMA((2 * H,))]

    def block(self, a, h):
        return self.out.at[a, h] if self.at is None else self.out.at[a, h, self.at]

    def start(self):
        a, h = self.me["a"], self.me["h"]
        block = self.block(a, h)
        self.held = []
        for dh in range(1, self.H):
            to = lax.rem(h + dh, self.H)
            self.held.append(self.copies.go(self.own, block, self.recv.at[dh], {"h": to}, self.first))
        self.copies.go(self.own, block, self.recv.at[0], {"a": 1 - a})

    def release(self):
        for copy in self.held:
            pl.when(jnp.logical_not(self.first))(copy.start)

    def forward(self, early=None):
        a, h, H = self.me["a"], self.me["h"], self.H
        if early:
            self.passed = []
        for dh in range(1, H):
            block = self.block(a, lax.rem(h - dh + H, H))
            if early is None:
                landed(block, self.recv.at[dh])
                self.copies.go(block, block, self.recv.at[H - 1 + dh], {"a": 1 - a})
                continue
            if early:
                on = self.copies.plan(block, block, self.recv.at[H - 1 + dh], {"a": 1 - a})
                self.passed.append(on)
            on = self.passed[dh - 1]
            now = jnp.logical_not(self.first) if H == 2 else self.first
            now = now if early else jnp.logical_not(now)

            @pl.when(now)
            def _():
                landed(block, self.recv.at[dh])
                on.start()

    def finish(self):
        a, h, H = self.me["a"], self.me["h"], self.H
        landed(self.block(1 - a, h), self.recv.at[0])
        for dh in range(1, H):
            landed(self.block(1 - a, lax.rem(h - dh + H, H)), self.recv.at[H - 1 + dh])
        self.copies.drain()


def join_lanes(pieces, width):
    per = 128 // width
    out = []
    for g in range(0, len(pieces), per):
        acc = pieces[g]
        for k in range(1, per):
            acc = acc + pltpu.roll(pieces[g + k], width * k, axis=1)
        out.append(acc)
    return jnp.concatenate(out, axis=1) if len(out) > 1 else out[0]


def norm_rows(v):
    mean = jnp.mean(v, axis=-1, keepdims=True)
    cent = v - mean
    rstd = lax.rsqrt(jnp.mean(cent * cent, axis=-1, keepdims=True) + EPS)
    return cent * rstd, rstd


def mix_rows(read, first, carry, shares, write, tiles, rows):
    per = tiles // 2

    @pl.loop(0, tiles)
    def _(p):
        n = read(p)
        prev = jnp.where(lax.rem(p, per) == 0, first(p // per), carry[...])
        row = lax.broadcasted_iota(jnp.int32, n.shape, 0)
        before = jnp.where(row == 0, prev, pltpu.roll(n, 1, axis=0))
        carry[...] = n[rows - 1 : rows]
        diff = n - before
        for i, s in enumerate(shares):
            write(i, p, (before + s * diff).astype(BF))
        write(None, p, diff.astype(BF))


def block_ones(m):
    row = lax.broadcasted_iota(jnp.int32, (m, m), 0) // HEAD
    col = lax.broadcasted_iota(jnp.int32, (m, m), 1) // HEAD
    return jnp.where(row == col, 1.0, 0.0).astype(F32)


def dot_exact(a, b):
    return jnp.dot(a, b, preferred_element_type=F32, precision=lax.Precision.HIGHEST)


class Decay:
    def __init__(self, lam):
        m = lam.shape[1]
        i = lax.broadcasted_iota(jnp.int32, (CHUNK, m), 0).astype(F32)
        self.i = i
        self.down = jnp.exp(-lam * i)
        self.up = jnp.exp(lam * (i + 1.0))
        self.tail = jnp.exp(-lam * (CHUNK - 1.0 - i))
        self.span = jnp.exp(-lam * CHUNK)


def stacked_heads(v):
    m = v.shape[1]
    lane = lax.broadcasted_iota(jnp.int32, v.shape, 1) // HEAD
    zero = jnp.zeros_like(v)
    return jnp.concatenate([jnp.where(lane == g, v, zero) for g in range(m // HEAD)], axis=0)


def own_heads(v):
    m = v.shape[1]
    lane = lax.broadcasted_iota(jnp.int32, (CHUNK, m), 1) // HEAD
    out = v[:CHUNK]
    for g in range(1, m // HEAD):
        out = jnp.where(lane == g, v[g * CHUNK : (g + 1) * CHUNK], out)
    return out


def triangle(heads, low):
    shape = (heads * CHUNK, CHUNK)
    row = lax.rem(lax.broadcasted_iota(jnp.int32, shape, 0), CHUNK)
    col = lax.broadcasted_iota(jnp.int32, shape, 1)
    return row > col if low else row < col


def squeeze(s0, s1):
    def fold(s):
        out = s[:, :128]
        for g in range(1, s.shape[1] // 128):
            out = out + s[:, g * 128 : (g + 1) * 128]
        return out + pltpu.roll(out, HEAD, axis=1)

    lane = lax.broadcasted_iota(jnp.int32, (s0.shape[0], 128), 1)
    return jnp.where(lane < HEAD, fold(s0), fold(s1))


def widen(p, second, ones):
    lane = lax.broadcasted_iota(jnp.int32, p.shape, 1)
    keep = (lane >= HEAD) if second else (lane < HEAD)
    both = jnp.where(keep, p, pltpu.roll(p, HEAD, axis=1))
    return jnp.concatenate([both] * (ones.shape[1] // 128), axis=1) * ones


class Chain:
    def __init__(self, me, H, ahead, out_box, in_box, send, recv):
        h = me["h"]
        self.h, self.H = h, H
        nxt = jnp.minimum(h + 1, H - 1) if ahead else jnp.maximum(h - 1, 0)
        self.has_next = (h < H - 1) if ahead else (h > 0)
        self.has_prev = (h > 0) if ahead else (h < H - 1)
        self.out_box, self.in_box = out_box, in_box
        self.copy = remote(out_box, in_box, send, recv, {"h": nxt})

    def run(self, state, closing, span_all, ones):
        if self.H == 1:
            return

        @pl.when(self.has_prev)
        def _():
            self.copy.wait_recv()
            p = self.in_box[...].astype(F32)
            for s in range(2):
                state[s] = widen(p, s == 1, ones)

        @pl.when(self.has_next)
        def _():
            out = squeeze(*(span_all * state[s] + closing[s] for s in range(2)))
            self.out_box[...] = out.astype(BF)
            self.copy.start()

    def finish(self):
        if self.H == 1:
            return

        @pl.when(self.has_next)
        def _():
            self.copy.wait_send()


def window(read, width, s):
    if s < 0:
        return pltpu.roll(read(0, 128).astype(F32), -s, axis=1)
    t, off = s // 128 * 128, s % 128
    if off == 0:
        return read(t, t + 128).astype(F32)
    if t + 256 <= width:
        return pltpu.roll(read(t, t + 256).astype(F32), 256 - off, axis=1)[:, :128]
    return pltpu.roll(read(t, t + 128).astype(F32), 128 - off, axis=1)


def lay_lanes(width, parts, put):
    for lo in range(0, width, 128):
        out = None
        for read, wide, src, dst, n in parts:
            d0, d1 = max(dst - lo, 0), min(dst + n - lo, 128)
            if d0 >= d1:
                continue
            v = window(read, wide, src + lo - dst)
            if out is not None:
                lane = lax.broadcasted_iota(jnp.int32, v.shape, 1)
                v = jnp.where((lane >= d0) & (lane < d1), v, out)
            out = v
        put(lo, out)


def rank_columns(lay, n, whole, p):
    w, m = n // lay.n, n // 8
    if w % whole:
        return [(p * m, 0, m)]
    b, l, c = p >> 2, (p >> 1) & 1, p & 1
    teams = [(i, j) for i in range(lay.A) for j in range(lay.H)]
    return [
        (((((i * 2 + b) * lay.H + j) * 2 + l) * 2 + c) * w, k * w, w) for k, (i, j) in enumerate(teams)
    ]


def front(lay, vecs, x, up, w4, w_ck, w_cr, w_o, w_cv, start):
    H, A = lay.H, lay.A
    grid = (A, 2, H, 4)
    rows, D = x.shape
    T = 8 * rows
    m = D // 8
    w_row = D // lay.n
    kk = D // (2 * A)
    heads = m // HEAD
    per = T // 2 // CHUNK
    bring_o = lay.strided
    wo_shape = (A, H, m // (A * H), D)
    cv_rows = w_cv.shape[0]
    F = w_ck.shape[1]
    nf = F // 8 + m
    k_row = w_ck.shape[0]
    early = cv_rows // 2 // 16 * 16 if cv_rows % 16 == 0 else 0

    def body(*refs):
        vecs, x, up, w_r, w_k, w_v, w_g, w_ck, w_cr, w_o, w_cv, start = refs[:12]
        refs = refs[4:]
        full, mine_v, mixed, diff, rkv, gate, upc, w_out = refs[8:16]
        wo, gated, ghat, grstd, states, fin, middle, n2, halo2, wcv, wf = refs[16:27]
        va, xg, halo, hn, carry, mx, df, wa, wos, team = refs[27:37]
        adds, st, cl, obox, ibox, own = refs[37:43]
        near, acc, mid, far, ss, sr = refs[43:49]
        vs, vn, vf, xs, xr, hs, hr, us, ur, ws, wn, wf_, qs, qr, os_, or_ = refs[49:65]
        es, er, cs, cr, ts, tr, fs, fn, ff, gs, gr, ks, kr, ls = refs[65:79]
        w, later, sbuf, zbuf, bs, br = refs[79:]
        part = xg
        me = coords()
        a, b, h, l, c = (me[n] for n in ALL)
        mine = rank_of(b, l, c)

        def cols(ref, p):
            return ref.at[:, pl.ds(pl.multiple_of(p * m, m), m)]

        for p in range(8):
            for j, ref in enumerate((w_r, w_k, w_v, w_g)):
                read = lambda lo, hi, ref=ref: ref[:, lo:hi]
                parts = [(read, D, *at) for at in rank_columns(lay, D, HEAD, p)]

                def put_w(lo, v, p=p, j=j):
                    w[p, :, j * m + lo : j * m + lo + 128] = v.astype(BF)

                lay_lanes(m, parts, put_w)

        local = [
            pltpu.make_async_copy(w.at[mine], wa.at[a, b, h, l * 2 + c], ls.at[0]),
            pltpu.make_async_copy(x, xg.at[rows_at(mine, rows)], ls.at[2]),
            pltpu.make_async_copy(cols(up, mine), upc.at[mine], ls.at[3]),
            pltpu.make_async_copy(vecs, va.at[a, b, h, l * 2 + c], ls.at[4]),
            pltpu.make_async_copy(w_o, wos.at[a, h] if bring_o else wos, ls.at[5]),
            pltpu.make_async_copy(w_cv, wcv.at[a, h], ls.at[6]),
        ]
        for copy in local:
            copy.start()
        greet(me, H, True, True)
        gw = TeamsGather(me, H, lambda p: w.at[p], wa, ws, wn, wf_)
        gv = TeamsGather(me, H, lambda p: vecs, va, vs, vn, vf)
        gx = TeamGather(me, x, lambda p: xg.at[rows_at(p, rows)], xs, xr, ("zx", "zx"))
        gh = Halo(me, H, x, halo, hs, hr)
        gu = Exchange(me, lambda p: cols(up, p), lambda p: upc.at[p], us, ur)
        gq = Exchange(me, lambda p: later.at[p], lambda p: team.at[p], qs, qr)
        gf = TeamsGather(me, H, None, wf, fs, fn, ff, team, 4)
        if bring_o:
            go = RowsGather(me, H, w_o, wos, os_, or_)
        top, rest = pl.ds(0, early), pl.ds(early, cv_rows - early)
        if early:
            ge = RowsGather(me, H, w_cv.at[top], wcv, es, er, top, True)
        gc = RowsGather(me, H, w_cv.at[rest], wcv, ts, tr, rest, True)
        def head(bb, k):
            if lay.strided:
                return (((k // H * 2 + bb) * H + k % H) * 2 + l) * 2 + c
            return rank_of(bb, l, c) * heads + k

        near_states = [
            pltpu.make_async_copy(start.at[head(b, k)], sbuf.at[b, k], ls.at[14 + k]) for k in range(heads)
        ]
        far_states = [
            remote(start.at[head(1 - b, k)], sbuf.at[b, k], bs.at[k], br.at[k], {"b": 1 - b})
            for k in range(heads)
        ]
        gv.start()
        gh.start()
        gw.start()
        for copy in near_states + far_states:
            copy.start()
        if early:
            ge.start()
        gc.start()
        gx.start()
        gv.spread(local[3])
        gv.release()
        gv.forward()
        gw.spread(local[0])
        gv.finish()
        local[1].wait()
        gx.finish()
        gw.release()
        gu.start()
        for p in range(8):
            parts = [(lambda lo, hi: w_ck[:, lo:hi], F, *at) for at in rank_columns(lay, F, 1, p)]

            def put_ck(lo, v, p=p):
                later[p, :, lo : lo + 128] = v.astype(BF)

            lay_lanes(F // 8, parts, put_ck)
            later[p, :, F // 8 :] = w_cr[:, p * m : (p + 1) * m]
        mine_team = pltpu.make_async_copy(later.at[mine], team.at[mine], ls.at[1])
        mine_team.start()
        gq.start()
        gw.forward((0,))
        gh.finish()

        def piece(*at):
            return va[at].astype(F32)

        flat = [
            piece(i, j, k, q) for i in range(A) for j in range(2) for k in range(H) for q in range(4)
        ]
        full[...] = join_lanes(flat, w_row)
        if lay.strided:
            held = [piece(i, b, k, l * 2 + c) for i in range(A) for k in range(H)]
            mine_v[...] = join_lanes(held, w_row)
        else:
            mine_v[...] = full[:, pl.ds(pl.multiple_of(mine * m, m), m)]
        gain, bias = full[0:1], full[1:2]
        for s in range(2):
            row = (norm_rows(halo[s].astype(F32))[0] * gain + bias)[15:16]
            hn[s] = jnp.where(h > 0, row, jnp.zeros_like(row))

        def write(i, p, v):
            if i is None:
                df[rows_at(p, MIX)] = v
            else:
                mx[i, rows_at(p, MIX)] = v

        mix_rows(
            lambda p: norm_rows(xg[rows_at(p, MIX)].astype(F32))[0] * gain + bias,
            lambda s: hn[s],
            carry,
            [full[2 + i : 3 + i] for i in range(4)],
            write,
            T // MIX,
            MIX,
        )
        keep = [
            pltpu.make_async_copy(mx, mixed, ls.at[7]),
            pltpu.make_async_copy(df, diff, ls.at[8]),
        ]
        for copy in keep:
            copy.start()
        gw.forward((1,))
        if bring_o:
            go.start()
            go.release()
        mine_team.wait()
        gq.finish()
        keep += [
            pltpu.make_async_copy(team.at[pl.ds(0, 4)], wf.at[a, 0, h], ls.at[11]),
            pltpu.make_async_copy(team.at[pl.ds(4, 4)], wf.at[a, 1, h], ls.at[12]),
        ]
        for copy in keep[2:]:
            copy.start()
        gf.spread(None, (0, 1, 2))
        gf.release((0,))
        gw.finish()
        keep.append(pltpu.make_async_copy(wa, w_out, ls.at[9]))
        keep[-1].start()
        for j in range(4):

            @pl.loop(0, 4)
            def _(t):
                at = rows_at(t, T // 4)
                acc = jnp.zeros((T // 4, m), F32)
                for i in range(A):
                    for k in range(2):
                        lo = (i * 2 + k) * kk
                        wt = wa[i, k, :, :, :, j * m : (j + 1) * m].reshape(kk, m)
                        acc = acc + dot_nn(mx[j, at, lo : lo + kk], wt)
                if j < 3:
                    rkv[j, at] = acc.astype(BF)
                else:
                    gate[at] = acc

        ones = block_ones(m)
        dec = Decay(mine_v[6:7])
        u = mine_v[7:8]
        span_all = jnp.exp(-mine_v[6:7] * (T // 2))

        def tile(i, s, n):
            return rkv[i, rows_at(s * per + n, CHUNK)].astype(F32)

        cl[...] = jnp.zeros_like(cl)

        @pl.loop(0, per)
        def _(n):
            for s in range(2):
                kt = (tile(1, s, n) * dec.tail).astype(BF)
                v = rkv[2, rows_at(s * per + n, CHUNK)]
                add = dot_tn(v, kt) * ones
                adds[s, n] = add
                cl[s] = dec.span * cl[s] + add

        for copy in near_states:
            copy.wait()
        for copy in far_states:
            copy.wait_send()
        for k in range(heads):
            landed(sbuf.at[1 - b, k], br.at[k])
        odd = lax.rem(lax.broadcasted_iota(jnp.int32, (m, 128), 0) // HEAD, 2) == 1
        zbuf[...] = jnp.zeros_like(zbuf)
        for s in range(2):
            for k in range(heads):
                zbuf[k * HEAD : (k + 1) * HEAD, :HEAD] = sbuf[s, k]
            z = zbuf[...]
            z = jnp.where(odd, pltpu.roll(z, HEAD, axis=1), z)
            z = (jnp.concatenate([z] * (m // 128), axis=1) * ones).T
            st[s] = jnp.where(h > 0, jnp.zeros_like(z), z)
        chain = Chain(me, H, True, obox, ibox, cs, cr)
        chain.run(st, cl, span_all, ones)
        gf.release((1, 2))
        if early:
            ge.release()
        gc.release()
        local[4].wait()
        if bring_o:
            go.forward()
        gf.forward((0,))
        if early:
            ge.forward(True)
        gc.forward(True)
        low = triangle(heads, True)

        @pl.loop(0, per)
        def _(n):
            for s in range(2):
                at = rows_at(s * per + n, CHUNK)
                r, k, v = (tile(i, s, n) for i in range(3))
                vb = rkv[2, at]
                rd = (r * dec.down).astype(BF)
                kg = (k * dec.up).astype(BF)
                state = st[s]
                states[s, n] = state
                att = jnp.where(low, dot_nt(stacked_heads(rd), kg), 0.0).astype(BF)
                y = own_heads(dot_nn(att, vb)) + dot_nt(rd, state.astype(BF))
                y = y + dot_exact(r * u * k, ones) * v
                st[s] = dec.span * state + adds[s, n]
                mean = dot_exact(y, ones) * (1.0 / HEAD)
                cent = y - mean
                rstd = lax.rsqrt(dot_exact(cent * cent, ones) * (1.0 / HEAD) + GROUP_EPS)
                hat = cent * rstd
                ghat[at] = hat
                grstd[at] = rstd
                g = gate[at]
                silu = g / (1.0 + jnp.exp(-g))
                gated[at] = ((hat * mine_v[8:9] + mine_v[9:10]) * silu).astype(BF)

        fin[...] = squeeze(st[0], st[1])
        chain.finish()
        if bring_o:
            go.finish()
        keep.append(pltpu.make_async_copy(wos, wo, ls.at[13]))
        keep[-1].start()

        @pl.loop(0, 8)
        def _(p):
            g = gated[rows_at(p, rows)]
            w = wos[...].reshape(m, D)
            for q in range(4):
                lo = q * (D // 4)
                part[rows_at(p, rows), lo : lo + D // 4] = dot_nn(g, w[:, lo : lo + D // 4]).astype(BF)

        sums = TeamSum(me, lambda p: part.at[rows_at(p, rows)], near, acc, mid, far, ss, sr, ("xz", "xz"))
        sums.start()

        def put(at, v):
            v = x[at].astype(F32) + v
            middle[at] = v
            own[at] = (norm_rows(v)[0] * full[10:11] + full[11:12]).astype(BF)

        def more():
            gf.forward((1, 2))
            gf.spread(None, (3,))

        sums.finish(put, more)
        keep.append(pltpu.make_async_copy(own, n2.at[mine], ls.at[10]))
        keep[-1].start()
        gn = TeamGather(me, own, lambda p: n2.at[p], gs, gr, ("zx", "zx"))
        gn.start()
        gk = Halo(me, H, own, halo2, ks, kr)
        gk.start()
        gf.release((3,))
        if early:
            ge.forward(False)
        gc.forward(False)
        gn.finish()
        gk.finish()
        gf.forward((3,))
        gu.finish()
        gf.finish()
        if early:
            ge.finish()
        gc.finish()
        for copy in local[2:3] + local[5:] + keep:
            copy.wait()

    gsems = TeamsGather.sems(H)
    team_sems = [DMA((14,)), DMA((8, 2))]
    halo_sems = [DMA((8,)), DMA((2,))]
    move_sems = [DMA((7,)), DMA((8,))]
    return comm_call(
        body,
        (
            jax.ShapeDtypeStruct((16, D), F32),
            jax.ShapeDtypeStruct((16, m), F32),
            jax.ShapeDtypeStruct((4, T, D), BF),
            jax.ShapeDtypeStruct((T, D), BF),
            jax.ShapeDtypeStruct((3, T, m), BF),
            jax.ShapeDtypeStruct((T, m), F32),
            jax.ShapeDtypeStruct((8, rows, m), BF),
            jax.ShapeDtypeStruct((*grid, k_row, 4 * m), BF),
            jax.ShapeDtypeStruct(wo_shape, BF),
            jax.ShapeDtypeStruct((T, m), BF),
            jax.ShapeDtypeStruct((T, m), F32),
            jax.ShapeDtypeStruct((T, m), F32),
            jax.ShapeDtypeStruct((2, per, m, m), F32),
            jax.ShapeDtypeStruct((m, 128), F32),
            jax.ShapeDtypeStruct((rows, D), F32),
            jax.ShapeDtypeStruct((8, rows, D), BF),
            jax.ShapeDtypeStruct((2, 16, D), BF),
            jax.ShapeDtypeStruct((A, H, *w_cv.shape), BF),
            jax.ShapeDtypeStruct((*grid, k_row, nf), BF),
        ),
        [VM] * 11 + [ANY],
        (VM, VM, ANY, ANY, VM, VM, ANY, ANY, ANY, VM, VM, VM, VM, VM, VM, ANY, ANY, ANY, ANY),
        [
            pltpu.VMEM((*grid, *vecs.shape), BF),
            pltpu.VMEM((T, D), BF),
            pltpu.VMEM((2, 16, D), BF),
            pltpu.VMEM((2, 1, D), F32),
            pltpu.VMEM((1, D), F32),
            pltpu.VMEM((4, T, D), BF),
            pltpu.VMEM((T, D), BF),
            pltpu.VMEM((*grid, k_row, 4 * m), BF),
            pltpu.VMEM(wo_shape, BF),
            pltpu.VMEM((8, k_row, nf), BF),
            pltpu.VMEM((2, per, m, m), F32),
            pltpu.VMEM((2, m, m), F32),
            pltpu.VMEM((2, m, m), F32),
            pltpu.VMEM((m, 128), BF),
            pltpu.VMEM((m, 128), BF),
            pltpu.VMEM((rows, D), BF),
            *TeamSum.scratch(rows, D),
            *gsems,
            *team_sems,
            *halo_sems,
            *move_sems,
            *gsems,
            *move_sems,
            *RowsGather.sems(H),
            *RowsGather.sems(H),
            DMA,
            DMA,
            *RowsGather.sems(H),
            *TeamsGather.sems(H, 4),
            *team_sems,
            *halo_sems,
            DMA((14 + heads,)),
            pltpu.VMEM((8, k_row, 4 * m), BF),
            pltpu.VMEM((8, k_row, nf), BF),
            pltpu.VMEM((2, heads, HEAD, HEAD), F32),
            pltpu.VMEM((m, 128), F32),
            DMA((heads,)),
            DMA((heads,)),
        ],
        0,
    )(vecs, x, up, *w4, w_ck, w_cr, w_o, w_cv, start)


class Background:
    def __init__(self, items, H):
        self.items, self.H = items, H

    def arrays(self):
        return [v for v, _ in self.items]

    def outs(self):
        shapes = []
        for v, kind in self.items:
            lead = {"h": (max(self.H - 1, 1),), "a": (), "t": (8,)}[kind]
            shapes.append(jax.ShapeDtypeStruct((*lead, *v.shape[1:]), BF))
        return shapes

    def sems(self):
        out = []
        for _, kind in self.items:
            n = {"h": max(self.H - 1, 1), "a": 1, "t": 8}[kind]
            out += [DMA((n,)), DMA((n,))] + ([DMA] if kind == "t" else [])
        return out

    def start(self, me, srcs, dsts, sems):
        self.open = []
        sems = list(sems)
        h, H = me["h"], self.H
        mine = rank_of(me["b"], me["l"], me["c"])
        for (_, kind), src, dst in zip(self.items, srcs, dsts):
            ss, sr = sems.pop(0), sems.pop(0)
            copies = Copies(ss)
            if kind == "h":
                for dh in range(1, H):
                    to = lax.rem(h + dh, H)
                    copies.go(src.at[to], dst.at[dh - 1], sr.at[dh - 1], {"h": to})
                    self.open.append((dst.at[dh - 1], sr.at[dh - 1]))
            elif kind == "a":
                copies.go(src.at[1 - me["a"]], dst, sr.at[0], {"a": 1 - me["a"]})
                self.open.append((dst, sr.at[0]))
            else:
                keep = pltpu.make_async_copy(src.at[mine], dst.at[mine], sems.pop(0))
                keep.start()
                self.open.append(keep)
                for m, to in mates(me):
                    p = rank_of(to["b"], to["l"], to["c"])
                    copies.go(src.at[p], dst.at[mine], sr.at[mine], to)
                    self.open.append((dst.at[p], sr.at[p]))
            self.open.append(copies)

    def finish(self):
        for item in self.open:
            if isinstance(item, tuple):
                landed(*item)
            elif isinstance(item, Copies):
                item.drain()
            else:
                item.wait()


def back_rows(T, tile, chunk, shares, diff, part, first, sums):
    per = T // 2 // tile

    def step(q, carry):
        t = 2 * per - 1 - q
        ds = chunk(t)
        dif = diff(t)
        late = jnp.zeros_like(ds[0])
        here = jnp.zeros_like(ds[0])
        for i, (d, s) in enumerate(zip(ds, shares)):
            sums[i][...] = sums[i][...] + jnp.sum(d * dif, axis=0, keepdims=True)
            late = late + (1.0 - s) * d
            here = here + s * d
        carry = jnp.where(lax.rem(t, per) == per - 1, jnp.zeros_like(carry), carry)
        row = lax.broadcasted_iota(jnp.int32, late.shape, 0)
        part(t, here + jnp.where(row == tile - 1, carry, pltpu.roll(late, tile - 1, axis=0)))

        @pl.when(lax.rem(t, per) == 0)
        def _():
            first(t // per, late[:16].astype(BF))

        return late[:1]

    zero = jnp.zeros((1, diff(0).shape[1]), F32)
    lax.fori_loop(0, 2 * per, step, zero)


def channel_mix(lay, n2, halo, full, wcv, wf, upc, middle, up, items):
    H, A = lay.H, lay.A
    rows, D = middle.shape
    T = 8 * rows
    F, m = wcv.shape[0], D // 8
    nk, kk, _ = wf.shape
    w_cv = F // (A * H)
    tile = T // 4
    dq = D // 4
    bg = Background(items, H)
    nb = len(items)

    def body(n2, halo, full, wcv_in, wf_in, upc, middle, up, *rest):
        srcs, rest = rest[:nb], rest[nb:]
        d_mid, d_br, moved, s_cv, got_cv, g_f, got_f, sums = rest[:8]
        dsts, rest = rest[8 : 8 + nb], rest[:8] + rest[8 + nb :]
        (big, m2, df, carry, relu, act, sg, d_pg, d_val, dval, gcv, cvbuf, stage) = rest[8:21]
        (dn2, own, add, first, edge) = rest[21:26]
        cn, ca, cm, cf, c_s, c_r = rest[26:32]
        rn, ra, rm, rf, r_s, r_r = rest[32:38]
        ds, dr, bs, br, es, er, ms, mr, vs, vr, fs, fr, ls = rest[38:51]
        wf, wcv = rest[51 + len(bg.sems()) :]
        d_pre = act
        me = coords()
        a, b, h, l, c = (me[n] for n in ALL)
        mine = rank_of(b, l, c)
        loads = [
            pltpu.make_async_copy(n2.at[p], big.at[pl.ds(p * rows, rows)], ls.at[p]) for p in range(8)
        ]
        loads.append(pltpu.make_async_copy(wf_in, wf, ls.at[14]))
        loads.append(pltpu.make_async_copy(wcv_in, wcv, ls.at[15]))
        for copy in loads:
            copy.start()
        greet(me, H, True, True)
        for copy in loads[:8]:
            copy.wait()

        def write(i, p, v):
            if i is None:
                df[rows_at(p, MIX)] = v
            else:
                m2[i, rows_at(p, MIX)] = v

        def before(s):
            row = halo[s].astype(F32)[15:16]
            return jnp.where(h > 0, row, jnp.zeros_like(row))

        s_ck, s_cr = full[12:13], full[13:14]
        mix_rows(
            lambda p: big[rows_at(p, MIX)].astype(F32),
            before,
            carry,
            [s_ck, s_cr],
            write,
            T // MIX,
            MIX,
        )

        loads[8].wait()

        @pl.loop(0, 4)
        def _(t):
            at = rows_at(t, tile)
            acc = jnp.zeros((tile, F), F32)
            for i in range(nk):
                acc = acc + dot_nn(m2[0, at, i * kk : (i + 1) * kk], wf[i, :, :F])
            pos = jnp.maximum(acc, 0.0)
            relu[at] = pos.astype(BF)
            act[at] = (pos * pos).astype(BF)

        loads[9].wait()

        @pl.loop(0, 4)
        def _(t):
            at = rows_at(t, tile)
            for q in range(4):
                lo = q * dq
                big[at, lo : lo + dq] = dot_nn(act[at], wcv[:, lo : lo + dq]).astype(BF)

        def cols(ref):
            return lambda p: ref.at[:, pl.ds(pl.multiple_of(p * m, m), m)]

        total = TeamSum(me, cols(big), cn, ca, cm, cf, c_s, c_r)
        total.start()

        @pl.loop(0, 4)
        def _(t):
            at = rows_at(t, tile)
            acc = jnp.zeros((tile, m), F32)
            for i in range(nk):
                acc = acc + dot_nn(m2[1, at, i * kk : (i + 1) * kk], wf[i, :, F:])
            sg[at] = 1.0 / (1.0 + jnp.exp(-acc))

        def gate_back(at, val):
            sig = sg[at]
            upv = upc[at].astype(F32)
            d_val[at] = (sig * upv).astype(BF)
            d_pg[at] = (upv * val * sig * (1.0 - sig)).astype(BF)
            add[at] = (sig * val).astype(BF)

        total.finish(gate_back)
        keep_val = pltpu.make_async_copy(d_val, cols(dval)(mine), ls.at[8])
        keep_val.start()
        gv = TeamGather(me, d_val, cols(dval), ds, dr)
        gv.start()
        gv.finish()
        keep_val.wait()
        keep_add = pltpu.make_async_copy(add.at[rows_at(mine, rows)], moved.at[mine], ls.at[11])
        keep_add.start()
        gm = Exchange(me, lambda p: add.at[rows_at(p, rows)], lambda p: moved.at[p], ms, mr)
        gm.start()
        bg.start(me, srcs, dsts, rest[51:-2])

        @pl.loop(0, 8)
        def _(q):
            at = pl.ds(pl.multiple_of(q * m, m), m)
            g = dot_tn(act[...], dval[:, at])
            for i in range(A):
                for j in range(H):
                    lo = (i * H + j) * w_cv
                    gcv[i, j, :, at] = g[lo : lo + w_cv].astype(BF)

        cv = Copies(vs)
        cv.go(gcv.at[1 - a], cvbuf, vr.at[0], {"a": 1 - a})

        @pl.loop(0, 4)
        def _(t):
            at = rows_at(t, tile)
            d_pre[at] = (dot_nt(dval[at], wcv[...]) * 2.0 * relu[at].astype(F32)).astype(BF)

        ff = Copies(fs)
        sums[...] = jnp.zeros_like(sums)

        def chunk_of(i):
            lo = i * kk

            def chunk(t):
                at = rows_at(t, tile)
                return (dot_nt(d_pre[at], wf[i, :, :F]), dot_nt(d_pg[at], wf[i, :, F:]))

            def put(t, v):
                big[rows_at(t, tile), lo : lo + kk] = v.astype(BF)

            def put_first(s, v):
                first[s, :, lo : lo + kk] = v

            back_rows(
                T,
                tile,
                chunk,
                (s_ck[:, lo : lo + kk], s_cr[:, lo : lo + kk]),
                lambda t: df[rows_at(t, tile), lo : lo + kk].astype(F32),
                put,
                put_first,
                [sums.at[k : k + 1, lo : lo + kk] for k in range(2)],
            )

        def grads(step, k):
            i = lax.rem(a + 1 + step, A)
            for q in range(2):
                at = pl.ds(pl.multiple_of((i * 2 + k) * kk + q * (kk // 2), kk // 2), kk // 2)
                to = slice(q * kk // 2, (q + 1) * kk // 2)
                stage[k, to, :F] = dot_tn(m2[0, :, at], d_pre[...]).astype(BF)
                stage[k, to, F:] = dot_tn(m2[1, :, at], d_pg[...]).astype(BF)
            copy = pltpu.make_async_copy(stage.at[k], g_f.at[i, k], ls.at[9 if k == 0 else 13])
            copy.start()
            return copy

        for i in range(nk):
            chunk_of(i)
        total = TeamSum(me, lambda p: big.at[rows_at(p, rows)], rn, ra, rm, rf, r_s, r_r)
        total.start()
        e = Edge(me, H, first, edge, es, er)
        e.start()

        def put_dn(at, v):
            dn2[at] = v

        halves = 2 if w_cv % 32 == 0 else 1

        held = []

        def pass_on(g):
            at = pl.ds(g * (w_cv // halves), w_cv // halves)
            for dh in range(1, H):
                to = lax.rem(h + dh, H)
                when = None if g == 0 else jnp.logical_not(inner(me, H))
                held.append(
                    cv.go(
                        gcv.at[a, to, at],
                        got_cv.at[dh - 1, at],
                        vr.at[1 + (dh - 1) * 2 + g],
                        {"h": to},
                        when,
                    )
                )

        def value_sums():
            landed(cvbuf, vr.at[0])

            @pl.loop(0, H)
            def _(j):
                gcv[a, j] = (gcv[a, j].astype(F32) + cvbuf[j].astype(F32)).astype(BF)

            pass_on(0)
            for copy in staged:
                copy.wait()
            ff.go(g_f.at[1 - a, 0], got_f, fr.at[0], {"a": 1 - a})
            staged[:] = [grads(1, 0), grads(1, 1)]

        staged = []
        total.finish(put_dn, value_sums, lambda: staged.extend([grads(0, 0), grads(0, 1)]))
        for copy in staged:
            copy.wait()
        e.finish(dn2)

        @pl.loop(0, rows // MIX)
        def _(t):
            at = rows_at(t, MIX)
            d = dn2[at]
            hat, rstd = norm_rows(middle[at])
            sums[2:3] = sums[2:3] + jnp.sum(d * hat, axis=0, keepdims=True)
            sums[3:4] = sums[3:4] + jnp.sum(d, axis=0, keepdims=True)
            dm = up[at].astype(F32) + norm_back(d * full[10:11], hat, rstd)
            d_mid[at] = dm
            own[at] = dm.astype(BF)

        keep = [
            pltpu.make_async_copy(own, d_br.at[mine], ls.at[10]),
            keep_add,
        ]
        keep[0].start()
        gx = TeamGather(me, own, lambda p: d_br.at[p], bs, br, ("zx", "zx"))
        gx.start()
        if halves == 2:
            pass_on(1)
            for copy in held[len(held) // 2 :]:
                pl.when(inner(me, H))(copy.start)
        keep.append(pltpu.make_async_copy(gcv.at[a, h], s_cv, ls.at[12]))
        keep[-1].start()
        gx.finish()
        gm.finish()
        bg.finish()
        landed(got_f, fr.at[0])
        ff.drain()
        for dh in range(1, H):
            for g in range(halves):
                at = pl.ds(g * (w_cv // halves), w_cv // halves)
                landed(got_cv.at[dh - 1, at], vr.at[1 + (dh - 1) * 2 + g])
        cv.drain()
        for copy in keep:
            copy.wait()

    return comm_call(
        body,
        (
            jax.ShapeDtypeStruct((rows, D), F32),
            jax.ShapeDtypeStruct((8, rows, D), BF),
            jax.ShapeDtypeStruct((8, rows, m), BF),
            jax.ShapeDtypeStruct((w_cv, D), BF),
            jax.ShapeDtypeStruct((max(H - 1, 1), w_cv, D), BF),
            jax.ShapeDtypeStruct((A, nk // A, kk, F + m), BF),
            jax.ShapeDtypeStruct((kk, F + m), BF),
            jax.ShapeDtypeStruct((8, D), F32),
            *bg.outs(),
        ),
        [ANY, VM, VM, ANY, ANY, VM, VM, VM] + [ANY] * nb,
        (VM, ANY, ANY, ANY, ANY, ANY, ANY, VM, *[ANY] * nb),
        [
            pltpu.VMEM((T, D), BF),
            pltpu.VMEM((2, T, D), BF),
            pltpu.VMEM((T, D), BF),
            pltpu.VMEM((1, D), F32),
            pltpu.VMEM((T, F), BF),
            pltpu.VMEM((T, F), BF),
            pltpu.VMEM((T, m), F32),
            pltpu.VMEM((T, m), BF),
            pltpu.VMEM((T, m), BF),
            pltpu.VMEM((T, D), BF),
            pltpu.VMEM((A, H, w_cv, D), BF),
            pltpu.VMEM((H, w_cv, D), BF),
            pltpu.VMEM((2, kk, F + m), BF),
            pltpu.VMEM((rows, D), F32),
            pltpu.VMEM((rows, D), BF),
            pltpu.VMEM((T, m), BF),
            pltpu.VMEM((2, 16, D), BF),
            pltpu.VMEM((8, 16, D), BF),
            *TeamSum.scratch(T, m),
            *TeamSum.scratch(rows, D),
            DMA((14,)),
            DMA((8, 2)),
            DMA((14,)),
            DMA((8, 2)),
            DMA((2,)),
            DMA((8,)),
            DMA((7,)),
            DMA((8,)),
            DMA((2 * H,)),
            DMA((2 * H,)),
            DMA((1,)),
            DMA((1,)),
            DMA((16,)),
            *bg.sems(),
            pltpu.VMEM(wf.shape, BF),
            pltpu.VMEM(wcv.shape, BF),
        ],
        2,
    )(n2, halo, full, wcv, wf, upc, middle, up, *bg.arrays())


def time_back(lay, d_br, wo, gated, ghat, grstd, gate, rkv, states, mv, full, mixed, diff, w4, x, d_mid, cm_sums, s_f, g_f, fin):
    H, A, n_dev = lay.H, lay.A, lay.n
    T, m = gate.shape
    rows, D = x.shape
    heads = m // HEAD
    per = T // 2 // CHUNK
    nk, kk, _ = w4.shape
    tile = T // 4
    hk = kk // H
    w_row = D // n_dev
    nf = s_f.shape[-1]
    H1 = max(H - 1, 1)
    strided = lay.strided
    hop = fin is not None
    F = (nf - m) * 8
    k_row = hk // 4

    def body(*refs):
        d_br, wo, gated, ghat, grstd, gate, rkv, states, mv, full, mixed, diff, w4_in, x, d_mid, cm_sums, s_f = refs[:17]
        g_f, refs = refs[17], refs[:17] + refs[18:]
        if hop:
            fin, refs = refs[17], refs[:17] + refs[18:]
        in_grad, o_out, total_out, fin_out, ck_out, cr_out, *four = refs[17:27]
        refs = refs[5:]
        (big, dy, adds, cl, st, obox, ibox, d_all, tsum, sums) = refs[22:32]
        (mbuf, g4, got, late, t4, first, edge) = refs[32:39]
        dn1 = in_grad
        (g_o, o_got, o_late, f_own, f_got, t_f, small, s_got) = refs[39:47]
        rn, ra, rm, rf, r_s, r_r = refs[47:53]
        cs, cr, es, er, gs, gr, os_, or_, fs, fr, xs, xr, ys, yr, ss, sr, ls, f_out, g_out, hs, hr, f1, f1_got, f1s, f1r, w4 = refs[53:]
        me = coords()
        a, b, h, l, c = (me[k] for k in ALL)
        mine = rank_of(b, l, c)
        loads = [
            pltpu.make_async_copy(d_br.at[p], big.at[pl.ds(p * rows, rows)], ls.at[p]) for p in range(8)
        ]
        loads.append(pltpu.make_async_copy(s_f.at[h], f_own, ls.at[8]))
        loads.append(pltpu.make_async_copy(g_f.at[a, 1], f1, ls.at[13 + nk]))
        loads.append(pltpu.make_async_copy(w4_in, w4, ls.at[14 + nk]))
        for copy in loads:
            copy.start()

        sem = pltpu.get_barrier_semaphore()
        others = []
        for i in range(1, n_dev):
            k = i
            dc, k = k % 2, k // 2
            dl, k = k % 2, k // 2
            dh, k = k % H, k // H
            db, da = k % 2, k // 2
            to = {
                "a": lax.rem(a + da, A),
                "b": b ^ db,
                "h": lax.rem(h + dh, H),
                "l": l ^ dl,
                "c": c ^ dc,
            }
            others.append((i, to))
            pl.semaphore_signal(sem, inc=1, device_id=to, device_id_type=MESH)
        pl.semaphore_wait(sem, n_dev - 1)
        c1 = Copies(f1s)
        c1.go(g_f.at[1 - a, 1], f1_got, f1r, {"a": 1 - a})
        for copy in loads[:8]:
            copy.wait()

        ones = block_ones(m)
        dec = Decay(mv[6:7])
        u = mv[7:8]
        span_all = jnp.exp(-mv[6:7] * (T // 2))
        low_t = triangle(heads, False)
        low = triangle(heads, True)
        tsum[...] = jnp.zeros_like(tsum)

        @pl.loop(0, 2 * per)
        def _(t):
            at = rows_at(t, CHUNK)
            d_gated = dot_nt(big[at], wo[...].reshape(m, D))
            g = gate[at]
            sig = 1.0 / (1.0 + jnp.exp(-g))
            hat, rstd = ghat[at], grstd[at]
            dn = d_gated * (g * sig)
            tsum[2:3] += jnp.sum(dn * hat, axis=0, keepdims=True)
            tsum[3:4] += jnp.sum(dn, axis=0, keepdims=True)
            nm = hat * mv[8:9] + mv[9:10]
            d_all[at, 3 * m :] = (d_gated * nm * sig * (1.0 + g * (1.0 - sig))).astype(BF)
            e = dn * mv[8:9]
            m1 = dot_exact(e, ones) * (1.0 / HEAD)
            m2 = dot_exact(e * hat, ones) * (1.0 / HEAD)
            dy[at] = (e - m1 - hat * m2) * rstd

        cl[...] = jnp.zeros_like(cl)

        @pl.loop(0, per)
        def _(q):
            n = per - 1 - q
            for s in range(2):
                at = rows_at(s * per + n, CHUNK)
                rd = (rkv[0, at].astype(F32) * dec.down).astype(BF)
                add = dot_tn(dy[at].astype(BF), rd) * ones
                adds[s, n] = add
                cl[s] = dec.span * cl[s] + add

        st[...] = jnp.zeros_like(st)
        chain = Chain(me, H, False, obox, ibox, cs, cr)
        chain.run(st, cl, span_all, ones)
        cf = Copies(fs)
        held = []
        for dh in range(1, H):
            to = lax.rem(h + dh, H)
            when = jnp.logical_not(inner(me, H))
            held.append(cf.go(s_f.at[to], f_got.at[dh - 1, 0], fr.at[2 * dh - 2], {"h": to}, when))

        if hop:
            mine_fin = fin.at[pl.ds(l * 4, 4)]
            last = h == H - 1
            to_first = remote(mine_fin.at[:, pl.ds(0, HEAD)], fin_out, hs, hr, {"h": 0})
            kept = pltpu.make_async_copy(mine_fin.at[:, pl.ds(HEAD, HEAD)], fin_out, hs)

            @pl.when(last)
            def _():
                to_first.start()

        nw = D // 8

        @pl.loop(0, 8)
        def _(q):
            at = pl.ds(pl.multiple_of(q * nw, nw), nw)
            g = dot_tn(gated[...], big[:, at]).astype(BF)
            g_o[:, :, :, at] = g.reshape(*g_o.shape[:3], nw)

        co = Copies(os_)
        if strided:
            co.go(g_o.at[1 - a], o_got, or_.at[0], {"a": 1 - a})

        @pl.loop(0, per)
        def _(q):
            n = per - 1 - q
            for s in range(2):
                at = rows_at(s * per + n, CHUNK)
                r, k, v = (rkv[i, at].astype(F32) for i in range(3))
                vb = rkv[2, at]
                rd, kg, kt = r * dec.down, k * dec.up, k * dec.tail
                rdb, kgb, ktb = rd.astype(BF), kg.astype(BF), kt.astype(BF)
                dyt = dy[at]
                dyb = dyt.astype(BF)
                state, end = states[s, n], st[s]
                endb = end.astype(BF)
                datt = jnp.where(low, dot_nt(stacked_heads(dyb), vb), 0.0).astype(BF)
                datt_t = jnp.where(low_t, dot_nt(stacked_heads(vb), dyb), 0.0).astype(BF)
                att_t = jnp.where(low_t, dot_nt(stacked_heads(kgb), rdb), 0.0).astype(BF)
                ddiag = dot_exact(dyt * v, ones)
                diag = dot_exact(r * u * k, ones)
                d_rd = own_heads(dot_nn(datt, kgb)) + dot_nn(dyb, state.astype(BF))
                d_kg = own_heads(dot_nn(datt_t, rdb))
                d_kt = dot_nn(vb, endb)
                d_v = own_heads(dot_nn(att_t, dyb)) + diag * dyt + dot_nt(ktb, endb)
                d_r = d_rd * dec.down + ddiag * u * k
                d_k = d_kg * dec.up + d_kt * dec.tail + ddiag * u * r
                d_all[at, :m] = d_r.astype(BF)
                d_all[at, m : 2 * m] = d_k.astype(BF)
                d_all[at, 2 * m : 3 * m] = d_v.astype(BF)
                tsum[1:2] += jnp.sum(ddiag * r * k, axis=0, keepdims=True)
                d_l = jnp.sum(
                    (dec.i + 1.0) * kg * d_kg
                    - dec.i * rd * d_rd
                    - (CHUNK - 1.0 - dec.i) * kt * d_kt,
                    axis=0,
                    keepdims=True,
                )
                d_l = d_l - CHUNK * dec.span * jnp.sum(state * end, axis=0, keepdims=True)
                tsum[0:1] += d_l
                st[s] = dec.span * end + adds[s, n]

        for copy in held:
            pl.when(inner(me, H))(copy.start)
        loads[9].wait()
        landed(f1_got, f1r)

        @pl.loop(0, kk // 64)
        def _(q):
            at = rows_at(q, 64)
            f1[at] = (f1[at].astype(F32) + f1_got[at].astype(F32)).astype(BF)

        for dh in range(1, H):
            to = lax.rem(h + dh, H)
            cf.go(f1.at[rows_at(to, hk)], f_got.at[dh - 1, 1], fr.at[2 * dh - 1], {"h": to})
        chain.finish()

        cg = Copies(gs)
        units = [(step, k, jj) for step in range(A) for k in range(2) for jj in range(2)]

        def unit(v):
            step, k, jj = units[v]
            i = lax.rem(a + 1 + step, A)
            lo = pl.ds(pl.multiple_of((i * 2 + k) * kk, kk), kk)
            src = mixed.at[pl.ds(jj * 2, 2), :, lo]
            return pltpu.make_async_copy(src, mbuf.at[v % 2], ls.at[9 + v % 2])

        unit(0).start()
        for v, (step, k, jj) in enumerate(units):
            if v + 1 < len(units):
                unit(v + 1).start()
            unit(v).wait()
            i = lax.rem(a + 1 + step, A)
            for q in range(2):
                j = jj * 2 + q
                g = dot_tn(mbuf[v % 2, q], d_all[:, j * m : (j + 1) * m])
                g4[i * 2 + k, :, j * m : (j + 1) * m] = g.astype(BF)
            if step < A - 1 and jj == 1:
                cg.go(g4.at[i * 2 + k], got.at[k], gr.at[k], {"a": 1 - a})

        difs = [
            pltpu.make_async_copy(diff.at[:, pl.ds(i * kk, kk)], mbuf.at[i // 2, i % 2], ls.at[13 + i])
            for i in range(nk)
        ]
        for copy in difs:
            copy.start()
        sums[...] = jnp.zeros_like(sums)

        def chunk_of(i):
            lo = i * kk

            def chunk(t):
                at = rows_at(t, tile)
                return tuple(
                    dot_nt(d_all[at, j * m : (j + 1) * m], w4[i, :, j * m : (j + 1) * m])
                    for j in range(4)
                )

            def put(t, v):
                big[rows_at(t, tile), lo : lo + kk] = v.astype(BF)

            def put_first(s, v):
                first[s, :, lo : lo + kk] = v

            back_rows(
                T,
                tile,
                chunk,
                tuple(full[2 + j : 3 + j, lo : lo + kk] for j in range(4)),
                lambda t: mbuf[i // 2, i % 2, rows_at(t, tile)].astype(F32),
                put,
                put_first,
                [sums.at[j : j + 1, lo : lo + kk] for j in range(4)],
            )

        loads[10].wait()
        for i in range(nk):
            difs[i].wait()
            chunk_of(i)
        total = TeamSum(
            me, lambda p: big.at[rows_at(p, rows)], rn, ra, rm, rf, r_s, r_r, ("xz", "xz")
        )
        total.start()
        e = Edge(me, H, first, edge, es, er)
        e.start()

        def pass_on():
            if strided:
                landed(o_got, or_.at[0])

                @pl.loop(0, H)
                def _(j):
                    g_o[a, j] = (g_o[a, j].astype(F32) + o_got[j].astype(F32)).astype(BF)

                for dh in range(1, H):
                    to = lax.rem(h + dh, H)
                    co.go(g_o.at[a, to], o_late.at[dh - 1], or_.at[dh], {"h": to})
            for k in range(2):
                landed(got.at[k], gr.at[k])

                @pl.loop(0, kk // 64)
                def _(q):
                    at = rows_at(q, 64)
                    g4[a * 2 + k, at] = (g4[a * 2 + k, at].astype(F32) + got[k, at].astype(F32)).astype(BF)

                for dh in range(1, H):
                    to = lax.rem(h + dh, H)
                    v = (dh - 1) * 2 + k
                    cg.go(
                        g4.at[a * 2 + k, rows_at(to, hk)], late.at[dh - 1, k], gr.at[2 + v], {"h": to}
                    )

            loads[8].wait()
            for dh in range(1, H):
                for k in range(2):
                    landed(f_got.at[dh - 1, k], fr.at[2 * dh - 2 + k])
            for k in range(2):
                for q in range(4):
                    at = pl.ds(q * (hk // 4), hk // 4)
                    if k == 0:
                        v = f_own[at].astype(F32)
                    else:
                        v = f1[pl.ds(pl.multiple_of(h * hk + q * (hk // 4), hk // 4), hk // 4)].astype(F32)
                    for dh in range(1, H):
                        v = v + f_got[dh - 1, k, at].astype(F32)
                    t_f[k * 4 + q] = v.astype(BF)
            keep_f.start()
            gf.start()

        keep_f = pltpu.make_async_copy(t_f.at[mine], f_out.at[mine], ls.at[11])
        gf = Exchange(me, lambda p: t_f.at[p], lambda p: f_out.at[p], xs, xr)

        def put_dn(at, v):
            dn1[at] = v

        total.finish(put_dn, pass_on)
        e.finish(dn1)

        @pl.loop(0, rows // MIX)
        def _(t):
            at = rows_at(t, MIX)
            d = dn1[at]
            hat, rstd = norm_rows(x[at].astype(F32))
            sums[4:5] = sums[4:5] + jnp.sum(d * hat, axis=0, keepdims=True)
            sums[5:6] = sums[5:6] + jnp.sum(d, axis=0, keepdims=True)
            in_grad[at] = d_mid[at] + norm_back(d * full[0:1], hat, rstd)

        small[...] = jnp.zeros_like(small)
        per_lane = 128 // w_row
        for f in range(n_dev):
            g = pl.ds(f // per_lane * 128, 128)
            block = jnp.concatenate([sums[:, g], cm_sums[:, g]], axis=0)
            shift = (128 - w_row * (f % per_lane)) % 128
            small[f] = pltpu.roll(block, shift, axis=1) if shift else block

        if strided:
            for i in range(A):
                for j in range(H):
                    f = (((i * 2 + b) * H + j) * 2 + l) * 2 + c
                    v = (i * H + j) * w_row
                    block = tsum[:, v // 128 * 128 : v // 128 * 128 + 128]
                    shift = (128 - v % 128) % 128
                    block = pltpu.roll(block, shift, axis=1) if shift else block
                    small[f, 12:16] = block[:4]
        else:
            span = n_dev // 8
            for i in range(span):
                v = i * w_row
                block = tsum[:, v // 128 * 128 : v // 128 * 128 + 128]
                shift = (128 - v % 128) % 128
                block = pltpu.roll(block, shift, axis=1) if shift else block
                small[mine * span + i, 12:16] = block[:4]
        cv = Copies(ss)

        def flat(d):
            return (((d["a"] * 2 + d["b"]) * H + d["h"]) * 2 + d["l"]) * 2 + d["c"]

        for i, to in others:
            cv.go(small.at[flat(to)], s_got.at[i], sr.at[i], to)

        for k in range(2):
            for dh in range(1, H):
                landed(late.at[dh - 1, k], gr.at[2 + (dh - 1) * 2 + k])
            for q in range(4):
                at = pl.ds(pl.multiple_of(h * hk + q * (hk // 4), hk // 4), hk // 4)
                v = g4[a * 2 + k, at].astype(F32)
                for dh in range(1, H):
                    v = v + late[dh - 1, k, pl.ds(q * (hk // 4), hk // 4)].astype(F32)
                t4[k * 4 + q] = v.astype(BF)
        keep = [keep_f, pltpu.make_async_copy(t4.at[mine], g_out.at[mine], ls.at[12])]
        keep[1].start()
        gg = Exchange(me, lambda p: t4.at[p], lambda p: g_out.at[p], ys, yr)
        gg.start()
        if strided:
            v = g_o[a, h].astype(F32)
            for dh in range(1, H):
                landed(o_late.at[dh - 1], or_.at[dh])
                v = v + o_late[dh - 1].astype(F32)
            o_out[...] = v
        else:
            o_out[...] = g_o[...]
        acc = small[flat(me)]
        for i, _ in others:
            landed(s_got.at[i], sr.at[i])
            acc = acc + s_got[i]
        total_out[...] = acc
        if hop:

            @pl.when(last)
            def _():
                to_first.wait_send()
                kept.start()
                kept.wait()

            @pl.when(h == 0)
            def _():
                to_first.wait_recv()

        gf.finish()
        for copy in keep:
            copy.wait()

        def from_ranks(ref, lo, n, whole):
            parts = []
            for p in range(8):
                read = lambda i, j, p=p: ref[p, :, lo + i : lo + j]
                for src, dst, many in rank_columns(lay, n, whole, p):
                    parts.append((read, n // 8, dst, src, many))
            return parts

        def into(ref):
            def put(lo, v):
                ref[:, lo : lo + 128] = v

            return put

        lay_lanes(F, from_ranks(f_out, 0, F, 1), into(ck_out))
        for p in range(8):
            cr_out[:, p * m : (p + 1) * m] = f_out[p, :, F // 8 :].astype(F32)
        gg.finish()
        for j, ref in enumerate(four):
            lay_lanes(D, from_ranks(g_out, j * m, D, HEAD), into(ref))
        for copies in (c1, cf, co, cg, cv):
            copies.drain()

    o_shape = wo.shape[2:] if strided else wo.shape
    return comm_call(
        body,
        (
            jax.ShapeDtypeStruct((rows, D), F32),
            jax.ShapeDtypeStruct(o_shape, F32 if strided else BF),
            jax.ShapeDtypeStruct((16, 128), F32),
            jax.ShapeDtypeStruct((4, HEAD, 128), BF),
            jax.ShapeDtypeStruct((k_row, F), F32),
            *[jax.ShapeDtypeStruct((k_row, D), F32)] * 5,
        ),
        [ANY] + [VM] * 9 + [ANY] * 3 + [VM] * 3 + [ANY] * (3 if hop else 2),
        (VM, VM, VM, ANY, *[VM] * 6),
        [
            pltpu.VMEM((T, D), BF),
            pltpu.VMEM((T, m), F32),
            pltpu.VMEM((2, per, m, m), F32),
            pltpu.VMEM((2, m, m), F32),
            pltpu.VMEM((2, m, m), F32),
            pltpu.VMEM((m, 128), BF),
            pltpu.VMEM((m, 128), BF),
            pltpu.VMEM((T, 4 * m), BF),
            pltpu.VMEM((8, m), F32),
            pltpu.VMEM((8, D), F32),
            pltpu.VMEM((2, 2, T, kk), BF),
            pltpu.VMEM((nk, kk, 4 * m), BF),
            pltpu.VMEM((2, kk, 4 * m), BF),
            pltpu.VMEM((H1, 2, hk, 4 * m), BF),
            pltpu.VMEM((8, hk // 4, 4 * m), BF),
            pltpu.VMEM((2, 16, D), BF),
            pltpu.VMEM((8, 16, D), BF),
            pltpu.VMEM(wo.shape, BF),
            pltpu.VMEM(wo.shape[1:], BF),
            pltpu.VMEM((H1, *wo.shape[2:]), BF),
            pltpu.VMEM(s_f.shape[1:], BF),
            pltpu.VMEM((H1, 2, *s_f.shape[1:]), BF),
            pltpu.VMEM((8, hk // 4, nf), BF),
            pltpu.VMEM((n_dev, 16, 128), F32),
            pltpu.VMEM((n_dev, 16, 128), F32),
            *TeamSum.scratch(rows, D),
            DMA,
            DMA,
            DMA((2,)),
            DMA((8,)),
            DMA((2 + 2 * H1,)),
            DMA((2 + 2 * H1,)),
            DMA((H,)),
            DMA((H,)),
            DMA((2 * H1,)),
            DMA((2 * H1,)),
            DMA((7,)),
            DMA((8,)),
            DMA((7,)),
            DMA((8,)),
            DMA((n_dev,)),
            DMA((n_dev,)),
            DMA((15 + nk,)),
            pltpu.VMEM((8, k_row, nf), BF),
            pltpu.VMEM((8, k_row, 4 * m), BF),
            DMA,
            DMA,
            pltpu.VMEM((kk, nf), BF),
            pltpu.VMEM((kk, nf), BF),
            DMA((1,)),
            DMA,
            pltpu.VMEM(w4.shape, BF),
        ],
        3,
    )(d_br, wo, gated, ghat, grstd, gate, rkv, states, mv, full, mixed, diff, w4, x, d_mid, cm_sums, s_f, g_f, *([fin] if hop else []))


def dot(a, b, dims):
    return lax.dot_general(a, b, (dims, ((), ())), preferred_element_type=F32)


def mm(a, b):
    return dot(a, b, ((1,), (0,)))


def mm_nt(a, b):
    return dot(a, b, ((1,), (1,)))


def mm_tn(a, b):
    return dot(a, b, ((0,), (0,)))


class Layout:
    def __init__(self, mesh_shape):
        self.A, self.B, self.H, self.L, self.C = mesh_shape
        self.team = self.B * self.L * self.C
        self.n = self.team * self.A * self.H

    def of(self, D):
        self.strided = (D // self.n) % HEAD == 0
        return self

    def spread(self, v, whole):
        w = v.shape[-1] // self.n
        lead = v.shape[:-1]
        if w % whole:
            return v.reshape(*lead, self.team, -1)
        k = len(lead)
        v = v.reshape(*lead, self.A, self.B, self.H, self.L, self.C, w)
        v = v.transpose(*range(k), k + 1, k + 3, k + 4, k, k + 2, k + 5)
        return v.reshape(*lead, self.team, -1)

    def unspread(self, v, whole):
        lead = v.shape[:-2]
        w = v.shape[-1] * self.team // self.n
        if w % whole:
            return v.reshape(*lead, -1)
        k = len(lead)
        v = v.reshape(*lead, self.B, self.L, self.C, self.A, self.H, w)
        v = v.transpose(*range(k), k + 3, k, k + 4, k + 1, k + 2, k + 5)
        return v.reshape(*lead, -1)

    def rows_in(self, g):
        m = g.shape[-1]
        g = g.reshape(self.A, self.H, self.B, self.L, self.C, -1, m)
        return g.transpose(0, 2, 1, 3, 4, 5, 6).reshape(-1, m)

    def rows_out(self, g):
        m = g.shape[-1]
        g = g.reshape(self.A, self.B, self.H, self.L, self.C, -1, m)
        return g.transpose(0, 2, 1, 3, 4, 5, 6).reshape(self.A * self.H, self.team, -1, m)


def normed(v):
    mean = jnp.mean(v, axis=-1, keepdims=True)
    cent = v - mean
    rstd = lax.rsqrt(jnp.mean(cent * cent, axis=-1, keepdims=True) + EPS)
    return cent * rstd, rstd


def norm_back(e, xhat, rstd):
    m1 = jnp.mean(e, axis=-1, keepdims=True)
    m2 = jnp.mean(e * xhat, axis=-1, keepdims=True)
    return (e - m1 - xhat * m2) * rstd


def with_before(rows, halo, segs):
    v = rows.reshape(segs, -1, rows.shape[-1])
    return jnp.concatenate([halo, v[:, :-1]], axis=1).reshape(rows.shape)


def with_after(rows, segs):
    v = rows.reshape(segs, -1, rows.shape[-1])
    return (
        jnp.concatenate([v[:, 1:], jnp.zeros_like(v[:, :1])], axis=1).reshape(rows.shape),
        v[:, :1],
    )


def swap(v, axis):
    return lax.ppermute(v, axis, [(0, 1), (1, 0)])


def per_device(lay, *args):
    (x_in, up_in, start_in) = args[:3]
    vec = args[3:13]
    w_r, w_k, w_v, w_g, w_o = args[13:18]
    vec2 = args[18:22]
    w_ck, w_cv, w_cr = args[22:]
    a_at, b_at, h_at = (lax.axis_index(n) for n in ("a", "b", "h"))
    rank = (b_at * lay.L + lax.axis_index("l")) * lay.C + lax.axis_index("c")
    H = lay.H
    segs = lay.B
    D = x_in.shape[-1]
    x_own = x_in[0]
    rows = x_own.shape[0]
    T = rows * lay.team
    dcol = D // lay.team
    heads = dcol // HEAD
    half = lay.L * lay.C
    w_row = D // lay.n
    lay.of(D)
    hid = w_ck.shape[1] // lay.team

    stacked = jnp.stack([*vec, *vec2])
    nv = stacked.shape[0]
    stacked = jnp.pad(stacked, ((0, 16 - nv), (0, 128 - w_row)))
    o_own = w_o
    if not lay.strided:
        o_own = lax.all_gather(w_o, ALL, axis=0, tiled=True)
        o_own = lax.dynamic_slice_in_dim(o_own, rank * dcol, dcol, 0)
        o_own = o_own.reshape(lay.A, H, -1, D)
    (
        every, my_vecs, mixed, diff1, rkv, gate, upc, W4, W_o, gated, ghat, grstd, states, fin, middle, n2, halo_2,
        W_cv, ffn_all,
    ) = front(lay, stacked, x_own, up_in[0], (w_r, w_k, w_v, w_g), w_ck, w_cr, o_own, w_cv, start_in[0])
    W_cv = W_cv.reshape(hid, D)
    direct = lay.strided and H == 2 and lay.A == 2
    items = []
    if direct:
        blocks = fin.astype(BF).reshape(lay.A, H, HEAD, 128).transpose(1, 0, 2, 3)
        blocks = jnp.broadcast_to(blocks.reshape(H, lay.A * HEAD, 128), (4, H, lay.A * HEAD, 128))
        items = [(blocks.reshape(8, lay.A * HEAD, 128), "t")]
    else:
        nh = start_in.shape[1]
        head_ids = lay.spread(jnp.arange(nh * HEAD, dtype=jnp.int32), HEAD)
        my_heads = lax.dynamic_index_in_dim(head_ids, rank, 0, False)[::HEAD] // HEAD
        s_out = fin.reshape(heads, HEAD, 2, HEAD).transpose(2, 0, 3, 1)
        placed = jnp.zeros((segs, nh, HEAD, HEAD), BF)
        s_fin = jnp.where(h_at == lay.H - 1, s_out, 0.0).astype(BF)
        placed = placed.at[:, my_heads].set(s_fin)
        final = lax.psum_scatter(placed, "b", scatter_dimension=0, tiled=True)
        final = lax.psum_scatter(final, SEQ, scatter_dimension=1, tiled=True).astype(F32)

    wf = ffn_all.reshape(2 * lay.A, D // (2 * lay.A), -1)
    d_mid, d_br, moved, s_cv, got_cv, g_f, got_f, cm_sums, *got_fin = channel_mix(
        lay, n2, halo_2, every, W_cv, wf, upc.reshape(T, dcol), middle, up_in[0], items
    )
    layer_output = (middle + moved.transpose(1, 0, 2).reshape(rows, D).astype(F32)).astype(BF)
    g_cv = s_cv.astype(F32) + jnp.sum(got_cv.astype(F32), axis=0)

    s_f = lax.dynamic_slice(g_f, (a_at, 0, 0, 0), (1, 1, *g_f.shape[2:]))[0, 0]
    s_f = s_f.astype(F32) + got_f.astype(F32)
    s_f = s_f.astype(BF).reshape(H, -1, s_f.shape[-1])
    w4 = W4.reshape(2 * lay.A, D // (2 * lay.A), -1)
    input_grad, g_o, small, fin, g_ck, g_cr, g_r, g_k, g_v, g_w = time_back(
        lay, d_br, W_o, gated, ghat, grstd, gate, rkv, states, my_vecs, every, mixed, diff1, w4, x_own, d_mid,
        cm_sums, s_f, g_f, got_fin[0] if direct else None,
    )
    if direct:
        fin = jnp.where(b_at == 0, fin[:, :, :HEAD], fin[:, :, HEAD:])
        final = fin.transpose(0, 2, 1)[None].astype(F32)
    if not lay.strided:
        g_o = jnp.zeros((D, D), BF).at[rank * dcol + jnp.arange(dcol)].set(g_o.reshape(dcol, D))
        g_o = lax.psum_scatter(g_o, ALL, scatter_dimension=0, tiled=True).astype(F32)
    small = small[:, :w_row]
    order = (4, 5, 0, 1, 2, 3, 12, 13, 14, 15, 10, 11, 8, 9)
    small = [small[i] for i in order]

    return (
        layer_output[None],
        input_grad[None],
        final,
        *small[:10],
        g_r,
        g_k,
        g_v,
        g_w,
        g_o,
        *small[10:],
        g_ck,
        g_cv,
        g_cr,
    )


def solution(mesh):
    n_seg, n_seq = mesh.devices.shape
    shape = (n_seg // 2, 2, n_seq // 4, 2, 2)
    view = Mesh(mesh.devices.reshape(shape), ALL)
    lay = Layout(shape)
    seg = ("a", "b")
    vec, mat = P(ALL), P(ALL, None)
    tok = P(seg, SEQ, None)

    def step(*args):
        return per_device(lay, *args)

    return jax.shard_map(
        step,
        mesh=view,
        in_specs=(tok, tok, P(seg, None, None, None), *[vec] * 10, *[mat] * 5, *[vec] * 4, *[mat] * 3),
        out_specs=(tok, tok, P(seg, SEQ, None, None), *[vec] * 10, *[mat] * 5, *[vec] * 4, *[mat] * 3),
        check_vma=False,
    )
```
